32 devices in a mesh: gx: 8 (over z, x), gy: 4 (over y, core).
Axes of the slice: x: 2, y: 2, z: 4, core: 2. Of those that a mesh axis runs over, the one named last changes fastest.
Arguments:
- concentration: float32 [3, 128, 512, 128], P(None, 'gx', 'gy'), may hold values from 0.2 to 2
- influx: float32 [128, 512, 128], P('gx', 'gy'), may hold values from -8 to 8
- numbers: float32 [3, 3], replicated, may hold values from 0.5 to 196608, as said below
- cross_terms: float32 [3, 3], replicated, may hold values from -0.25 to 0.25
- kinetics: float32 [3], replicated, may hold values from 0.25 to 1.5
Outputs:
- updated: float32 [3, 128, 512, 128], P(None, 'gx', 'gy')
The draws below stay inside these ranges and needn't reach their ends.
Inputs may be any that keep to these rules, and one draw needn't show every extreme that they name: numbers[s, 0] and numbers[s, 1] lie between 3 * 128 ** 2 and 12 * 128 ** 2, numbers[s, 2] between 0.5 and 4.
All inputs are finite; a program needn't handle non-finite values.
Results may differ from the reference program's by a relative error of at most 0.0003.
Values sent between devices are 32-bit elements; how exact they have to be, the bound alone decides.
No kernel may reach another device: no remote copies, remote signals or barrier semaphores. Data moves between devices by JAX's collectives and lax.ppermute only.
A program may use at most 128 MiB of HBM per device.

```python
import math
import jax
import jax.numpy as jnp
from jax import lax

CY = 128
NZ = 128
NX = 128
NY = 512


def log_uniform(subkey, lowest, highest):
    sample = jax.random.uniform(subkey, (3,), jnp.float32)
    return jnp.exp(jnp.log(lowest) + sample * (jnp.log(highest) - jnp.log(lowest)))


def draw_numbers(key, part):
    subkeys = jax.random.split(jax.random.fold_in(key, 17), 3)
    along_x = log_uniform(subkeys[0], 3.0 * CY * CY, 12.0 * CY * CY)
    along_y = log_uniform(subkeys[1], 3.0 * CY * CY, 12.0 * CY * CY)
    along_z = log_uniform(subkeys[2], 0.5, 4.0)
    return jnp.stack([along_x, along_y, along_z], axis=1).astype(jnp.float32)


def draw_influx(key, part):
    subkeys = jax.random.split(jax.random.fold_in(key, 29), 1)
    values = jnp.clip(2.0 * jax.random.normal(subkeys[0], (NX, NY, NZ), jnp.float32), -8.0, 8.0)
    return values.astype(jnp.float32)


def block_levels(stream_key, shape, cuts, smallest, high):
    def one(dim, shards_of):
        heights = jax.random.uniform(jax.random.fold_in(jax.random.fold_in(stream_key, 6), dim), (shards_of,), jnp.float32, smallest / len(cuts), high / len(cuts))
        return jnp.repeat(jnp.exp(heights), shape[dim] // shards_of).reshape((-1,) + (1,) * (len(shape) - dim - 1))

    gain = one(*cuts[0])
    for cut in cuts[1:]:
        gain = gain * one(*cut)
    return gain


def setup_inputs(seed: int = 0) -> dict:
    key_of = jax.random.split(jax.random.key(seed), 6)
    return {
        "concentration": jnp.clip(jnp.exp(math.log(2.0) - 2.3025851 * jax.random.uniform(key_of[0], (3, NX, NY, NZ), jnp.float32) ** block_levels(key_of[0], (3, NX, NY, NZ), ((1, 8), (2, 4)), -0.2, 0.2)), 0.2, 2.0),
        "influx": draw_influx(jax.random.fold_in(key_of[5], 71), 0),
        "numbers": draw_numbers(jax.random.fold_in(key_of[5], 71), 0),
        "cross_terms": jnp.clip(jax.random.uniform(key_of[3], (3, 3), jnp.float32, -0.25, 0.25), -0.25, 0.25),
        "kinetics": jnp.clip(jnp.exp(jax.random.uniform(key_of[4], (3,), jnp.float32, math.log(0.25), math.log(1.5))), 0.25, 1.5),
    }


def second_diff(species_field, direction):
    return jnp.roll(species_field, 1, direction) + jnp.roll(species_field, -1, direction) - 2.0 * species_field


def periodic_solve(source, number, direction):
    length = source.shape[direction]
    wavenumber = jnp.arange(length // 2 + 1).astype(source.dtype)
    symbol = 1.0 + 2.0 * number * (1.0 - jnp.cos(2.0 * jnp.pi * wavenumber / length))
    layout = [1, 1, 1]
    layout[direction] = length // 2 + 1
    spectrum = jnp.fft.rfft(source, axis=direction) / symbol.reshape(layout)
    return jnp.fft.irfft(spectrum, n=length, axis=direction).astype(source.dtype)


def reference(concentration, influx, numbers, cross_terms, kinetics):
    def diffusion(members):
        species_field, number = members
        return (number[0] * second_diff(species_field, 0) + number[1] * second_diff(species_field, 1)
                + number[2] * second_diff(species_field, 2))

    diffusive = lax.map(diffusion, (concentration, numbers))
    identity = jnp.eye(3, dtype=concentration.dtype)
    mixing = identity + cross_terms * (1.0 - identity)
    calcium = concentration[0]
    calmodulin = concentration[1]
    complexed = concentration[2]
    binding = kinetics[0] * calcium * calmodulin - kinetics[1] * complexed
    pumping = kinetics[2] * calcium / (1.0 + calcium)
    coefficients = jnp.array([[1.0, -4.0, -1.0], [0.0, -1.0, 0.0], [0.0, 1.0, 0.0]], dtype=concentration.dtype)

    def implicit(members):
        weights, coefficient, number = members
        explicit = coefficient[0] * influx + coefficient[1] * binding + coefficient[2] * pumping
        explicit = explicit + weights[0] * diffusive[0] + weights[1] * diffusive[1] + weights[2] * diffusive[2]
        after_z = periodic_solve(explicit, number[2], 2)
        after_y = periodic_solve(after_z, number[1], 1)
        return periodic_solve(after_y, number[0], 0)

    return concentration + lax.map(implicit, (mixing, coefficients, numbers))
```

```python
import functools

import jax
import jax.numpy as jnp
from jax import lax
from jax.experimental import pallas as pl
from jax.experimental.pallas import tpu as pltpu
from jax.sharding import PartitionSpec as P

SPECIES = 3
ROWS = 8
SMEM = pl.BlockSpec(memory_space=pltpu.SMEM)
VMEM = pl.BlockSpec(memory_space=pltpu.VMEM)


def decay_rate(number):
    half = 0.5 * lax.rsqrt(number)
    square = half * half
    return 2.0 * jnp.log1p(half + square / (1.0 + jnp.sqrt(1.0 + square)))


def scaling(number):
    return lax.rsqrt(1.0 + 4.0 * number)


def splat(value, shape):
    return jnp.full(shape, value, jnp.float32)


def split(value):
    high = value.astype(jnp.bfloat16)
    return high, (value - high.astype(jnp.float32)).astype(jnp.bfloat16)


def product(left, right):
    wide = jnp.concatenate([left[0], left[1]], axis=1)
    deep = jnp.concatenate([right[0], right[0]], axis=0)
    return jnp.dot(wide, deep, preferred_element_type=jnp.float32) + jnp.dot(
        left[0], right[1], preferred_element_type=jnp.float32
    )


def distances(length):
    rows = lax.broadcasted_iota(jnp.int32, (length, length), 0)
    columns = lax.broadcasted_iota(jnp.int32, (length, length), 1)
    return jnp.abs(rows - columns).astype(jnp.float32)


def depth_table(number, length):
    number = splat(number, (length, length))
    theta = decay_rate(number)
    spread = distances(length)
    divisor = 1.0 - jnp.exp(-length * theta)
    return (jnp.exp(-spread * theta) + jnp.exp((spread - length) * theta)) * scaling(number) / divisor


def column_table(number, length):
    number = splat(number, (length, length))
    return jnp.exp(-distances(length) * decay_rate(number)) * scaling(number)


def row_position(length, width):
    return lax.broadcasted_iota(jnp.int32, (length, width), 0).astype(jnp.float32)


def source_kernel(columns, numbers, cross, kinetics, conc, influx, h_out, b_out, v_out, w_out, y_out, g_hold, b_hold, acc):
    step = pl.program_id(0)
    planes, chunk, width = conc.shape[1:]
    tile = (ROWS, width)

    @pl.when(step == 0)
    def _():
        acc[...] = jnp.zeros_like(acc)

    n = [[splat(numbers[s, d], tile) for d in range(3)] for s in range(SPECIES)]
    inner, double, single_a, single_b = [], [], [], []
    decay, scale, theta_y = [], [], []
    for s in range(SPECIES):
        scale.append(scaling(n[s][0]))
        decay.append(jnp.exp(-decay_rate(n[s][0])))
        theta_y.append(decay_rate(n[s][1]))
        per_x = 1.0 / n[s][0]
        per_y = 1.0 / n[s][1]
        for j in range(SPECIES):
            mix = 1.0 if j == s else cross[s, j]
            along_x = n[j][0] * per_x * mix
            along_y = n[j][1] * per_y * mix
            along_z = n[j][2] * mix
            single_a.append(along_x)
            single_b.append(along_y * scale[s])
            double.append(along_z * scale[s])
            inner.append((along_x + along_y - 2.0 * along_z) * scale[s])
    bind, unbind, pump = (splat(kinetics[i], tile) for i in range(3))

    def rows(k, carry):
        at = pl.multiple_of(k * ROWS, ROWS)
        here = pl.ds(at, ROWS)
        up_g = [jnp.zeros(tile, jnp.float32) for _ in range(SPECIES)]
        up_b = [jnp.zeros(tile, jnp.float32) for _ in range(SPECIES)]
        for i in range(planes):
            c = [conc[j, i, here, :] for j in range(SPECIES)]
            around = [pltpu.roll(value, 1, 1) + pltpu.roll(value, width - 1, 1) for value in c]
            binding = bind * c[0] * c[1] - unbind * c[2]
            pumping = pump * c[0] / (1.0 + c[0])
            change = (influx[i, here, :] - 4.0 * binding - pumping, -binding, binding)
            for s in range(SPECIES):
                a = b = None
                g = change[s] * scale[s]
                for j in range(SPECIES):
                    at_sj = s * SPECIES + j
                    g = g + inner[at_sj] * c[j] + double[at_sj] * around[j]
                    part_a = c[j] if s == j else single_a[at_sj] * c[j]
                    part_b = single_b[at_sj] * c[j]
                    a = part_a if a is None else a + part_a
                    b = part_b if b is None else b + part_b
                up_g[s] = g + decay[s] * up_g[s]
                up_b[s] = b + decay[s] * up_b[s]
                g_hold[s, i] = g
                b_hold[s, i] = b
                h_out[s, i, here, :] = up_g[s] - a
                b_out[s, i, here, :] = up_b[s]
        place = step * chunk + at
        position = place.astype(jnp.float32) + row_position(ROWS, width)
        rise = [jnp.exp((position - (columns - 1.0)) * theta_y[s]) for s in range(SPECIES)]
        fall = [jnp.exp(-position * theta_y[s]) for s in range(SPECIES)]

        def add_up(s, i, value):
            acc[0, s, i] += rise[s] * value
            acc[1, s, i] += fall[s] * value

        for s in range(SPECIES):
            v_out[0, s, here, :] = up_g[s]
            w_out[0, s, here, :] = up_b[s]
            add_up(s, planes, up_g[s])
            down_g = jnp.zeros(tile, jnp.float32)
            down_b = jnp.zeros(tile, jnp.float32)
            for i in reversed(range(planes)):
                down_g = decay[s] * down_g
                down_b = decay[s] * down_b
                h = h_out[s, i, here, :] + down_g
                h_out[s, i, here, :] = h
                b_out[s, i, here, :] += down_b
                add_up(s, i, h)
                down_g += g_hold[s, i]
                down_b += b_hold[s, i]
            v_out[1, s, here, :] = down_g
            w_out[1, s, here, :] = down_b
            add_up(s, planes + 1, down_g)
        return carry

    lax.fori_loop(0, chunk // ROWS, rows, 0)

    @pl.when(step == pl.num_programs(0) - 1)
    def _():
        y_out[...] = jnp.sum(acc[...], axis=3)


def sources(numbers, cross, kinetics, conc, influx):
    _, planes, columns, width = conc.shape
    chunk = 2 * ROWS
    field = jax.ShapeDtypeStruct(conc.shape, jnp.float32)
    edge = jax.ShapeDtypeStruct((2, SPECIES, columns, width), jnp.float32)
    sums = jax.ShapeDtypeStruct((2, SPECIES, planes + 2, width), jnp.float32)
    field_spec = pl.BlockSpec((SPECIES, planes, chunk, width), lambda i: (0, 0, i, 0))
    edge_spec = pl.BlockSpec((2, SPECIES, chunk, width), lambda i: (0, 0, i, 0))
    return pl.pallas_call(
        functools.partial(source_kernel, columns),
        grid=(columns // chunk,),
        in_specs=[SMEM, SMEM, SMEM, field_spec, pl.BlockSpec((planes, chunk, width), lambda i: (0, i, 0))],
        out_specs=[field_spec, field_spec, edge_spec, edge_spec, pl.BlockSpec(sums.shape, lambda i: (0, 0, 0, 0))],
        out_shape=[field, field, edge, edge, sums],
        scratch_shapes=[
            pltpu.VMEM((SPECIES, planes, ROWS, width), jnp.float32),
            pltpu.VMEM((SPECIES, planes, ROWS, width), jnp.float32),
            pltpu.VMEM((2, SPECIES, planes + 2, ROWS, width), jnp.float32),
        ],
        compiler_params=pltpu.CompilerParams(vmem_limit_bytes=16 * 2**20),
        cost_estimate=pl.CostEstimate(flops=40 * conc.size, bytes_accessed=14 * conc.size, transcendentals=0),
        name="sources",
    )(numbers, cross, kinetics, conc, influx)


def edge_kernel(group, rank, numbers, v, w, *refs):
    count = len(refs) - group - 2
    sums, (y_out, sent, hold) = refs[:count], (refs[count], refs[count + 1 : -1], refs[-1])
    columns, width = v.shape[2:]
    planes = sums[0].shape[2] - 2
    for s in range(SPECIES):
        theta = decay_rate(splat(numbers[s, 1], (1, width)))
        scale = scaling(splat(numbers[s, 1], (1, width)))
        closing = scale / (1.0 - jnp.exp(-(columns * count) * theta))
        into, out_of = 0.0, 0.0
        for k in range(count):
            rise = jnp.exp(-(columns * (k - 1 if k else count - 1)) * theta) * closing
            fall = jnp.exp(-(columns * (count - k - 1)) * theta) * closing
            into = into + rise * sums[k][0, s]
            out_of = out_of + fall * sums[k][1, s]
        y_out[0, s] = into[:planes]
        y_out[1, s] = out_of[:planes]
        row = row_position(columns, width)
        theta = decay_rate(splat(numbers[s, 1], (columns, width)))
        rise = jnp.exp(-(row + 1.0) * theta)
        fall = jnp.exp((row - columns) * theta)
        table = split(column_table(numbers[s, 1], columns))
        both = product(table, split(jnp.concatenate([v[0, s], v[1, s]], axis=1)))
        solved = []
        for e in range(2):
            at = planes + e
            solved.append(
                both[:, e * width : (e + 1) * width] + rise * into[at : at + 1] + fall * out_of[at : at + 1] - w[e, s]
            )
        done = product(split(jnp.concatenate(solved, axis=0)), split(depth_table(numbers[s, 2], width)))
        hold[0, s] = done[:columns]
        hold[1, s] = done[columns:]
    share = columns // group
    member = lax.rem(rank[0], group)
    for d in range(group):
        start = pl.multiple_of(lax.rem(member + d, group) * share, share)
        sent[d][...] = hold[:, :, pl.ds(start, share), :]


def edges(group, rank, numbers, v, w, sums):
    _, _, columns, width = v.shape
    planes = sums[0].shape[2] - 2
    part = jax.ShapeDtypeStruct((2, SPECIES, columns // group, width), jnp.float32)
    return pl.pallas_call(
        functools.partial(edge_kernel, group),
        in_specs=[SMEM, SMEM] + [VMEM] * (2 + len(sums)),
        out_specs=[VMEM] * (1 + group),
        out_shape=[jax.ShapeDtypeStruct((2, SPECIES, planes, width), jnp.float32)] + [part] * group,
        scratch_shapes=[pltpu.VMEM(v.shape, jnp.float32)],
        compiler_params=pltpu.CompilerParams(vmem_limit_bytes=16 * 2**20),
        name="edges",
    )(rank, numbers, v, w, *sums)


def group_kernel(group, planes, rank, numbers, *refs):
    parts, out = refs[:-1], refs[-1]
    member = lax.rem(rank[0], group)
    tile = parts[0].shape[2:]
    for s in range(SPECIES):
        theta = planes * decay_rate(splat(numbers[s, 0], tile))
        rising, falling = 0.0, 0.0
        for d in range(group):
            block = lax.rem(member - d + group, group).astype(jnp.float32)
            rising = rising + jnp.exp((block - (group - 1.0)) * theta) * parts[d][0, s]
            falling = falling + jnp.exp(-block * theta) * parts[d][1, s]
        out[0, s] = rising
        out[1, s] = falling


def group_sums(group, planes, rank, numbers, parts):
    return pl.pallas_call(
        functools.partial(group_kernel, group, planes),
        in_specs=[SMEM, SMEM] + [VMEM] * len(parts),
        out_specs=VMEM,
        out_shape=jax.ShapeDtypeStruct(parts[0].shape, jnp.float32),
        compiler_params=pltpu.CompilerParams(vmem_limit_bytes=8 * 2**20),
        name="group_sums",
    )(rank, numbers, *parts)


def enter_kernel(group, planes, rank, numbers, *refs):
    parts, wholes, outs = refs[:group], refs[group:-group], refs[-group:]
    groups = len(wholes)
    member = lax.rem(rank[0], group)
    tile = parts[0].shape[2:]
    for s in range(SPECIES):
        theta = planes * decay_rate(splat(numbers[s, 0], tile))
        closing = 1.0 / (1.0 - jnp.exp(-(group * groups) * theta))
        into, out_of = 0.0, 0.0
        for j in range(groups):
            rise = jnp.exp(-(group * (j - 1 if j else groups - 1)) * theta) * closing
            fall = jnp.exp(-(group * (groups - j - 1)) * theta) * closing
            into = into + rise * wholes[j][0, s]
            out_of = out_of + fall * wholes[j][1, s]
        held = [(parts[d][0, s], parts[d][1, s]) for d in range(group)]
        for d in range(group):
            target = lax.rem(member + d, group)
            rising = jnp.exp(-target.astype(jnp.float32) * theta) * into
            falling = jnp.exp((target - (group - 1)).astype(jnp.float32) * theta) * out_of
            for e in range(group):
                block = lax.rem(member - e + group, group)
                away = (target - block).astype(jnp.float32)
                weight = jnp.exp((1.0 - jnp.abs(away)) * theta)
                rising = rising + jnp.where(target > block, weight, 0.0) * held[e][0]
                falling = falling + jnp.where(target < block, weight, 0.0) * held[e][1]
            outs[d][0, s] = rising
            outs[d][1, s] = falling


def entering(group, planes, rank, numbers, parts, wholes):
    part = jax.ShapeDtypeStruct(parts[0].shape, jnp.float32)
    return pl.pallas_call(
        functools.partial(enter_kernel, group, planes),
        in_specs=[SMEM, SMEM] + [VMEM] * (len(parts) + len(wholes)),
        out_specs=[VMEM] * group,
        out_shape=[part] * group,
        compiler_params=pltpu.CompilerParams(vmem_limit_bytes=8 * 2**20),
        name="entering",
    )(rank, numbers, *parts, *wholes)


def bulk_kernel(numbers, h, b, conc, y_in, out, column_hold, depth_hold):
    s = pl.program_id(0)
    planes, columns, width = h.shape[1:]

    @pl.when(pl.program_id(1) == 0)
    def _():
        column_hold[0], column_hold[1] = split(column_table(numbers[s, 1], columns))
        depth_hold[0], depth_hold[1] = split(depth_table(numbers[s, 2], width))

    row = row_position(columns, width)
    theta = decay_rate(splat(numbers[s, 1], (columns, width)))
    rise = jnp.exp(-(row + 1.0) * theta)
    fall = jnp.exp((row - columns) * theta)
    table = (column_hold[0], column_hold[1])
    depth = (depth_hold[0], depth_hold[1])
    for i in range(planes):
        solved = product(table, split(h[0, i]))
        solved = solved + rise * y_in[0, 0, i : i + 1] + fall * y_in[1, 0, i : i + 1] - b[0, i]
        out[0, i] = conc[0, i] + product(split(solved), depth)


def bulk(numbers, h, b, conc, y_in):
    _, planes, columns, width = conc.shape
    step = min(planes, 8)
    field_spec = pl.BlockSpec((1, step, columns, width), lambda s, i: (s, i, 0, 0))
    return pl.pallas_call(
        bulk_kernel,
        grid=(SPECIES, planes // step),
        in_specs=[SMEM, field_spec, field_spec, field_spec, pl.BlockSpec((2, 1, step, width), lambda s, i: (0, s, i, 0))],
        out_specs=field_spec,
        out_shape=jax.ShapeDtypeStruct(conc.shape, jnp.float32),
        scratch_shapes=[
            pltpu.VMEM((2, columns, columns), jnp.bfloat16),
            pltpu.VMEM((2, width, width), jnp.bfloat16),
        ],
        compiler_params=pltpu.CompilerParams(vmem_limit_bytes=16 * 2**20),
        cost_estimate=pl.CostEstimate(
            flops=6 * conc.size * (columns + width), bytes_accessed=16 * conc.size, transcendentals=0
        ),
        name="bulk",
    )(numbers, h, b, conc, y_in)


def spread_kernel(group, rank, numbers, base, *refs):
    parts, out, hold = refs[:group], refs[group], refs[group + 1]
    s, i = pl.program_id(0), pl.program_id(1)
    step, columns, width = base.shape[1:]
    planes = step * pl.num_programs(1)
    share = columns // group
    member = lax.rem(rank[0], group)

    @pl.when(i == 0)
    def _():
        for d in range(group):
            start = pl.multiple_of(lax.rem(member - d + group, group) * share, share)
            for e in range(2):
                hold[e, pl.ds(start, share), :] = parts[d][e, s]

    theta = decay_rate(splat(numbers[s, 0], (columns, width)))
    for k in range(step):
        place = (i * step + k).astype(jnp.float32)
        rise = jnp.exp(-(place + 1.0) * theta)
        fall = jnp.exp((place - planes) * theta)
        out[0, k] = base[0, k] + rise * hold[0] + fall * hold[1]


def spread(group, rank, numbers, base, parts):
    _, planes, columns, width = base.shape
    step = min(planes, 4)
    field_spec = pl.BlockSpec((1, step, columns, width), lambda s, i: (s, i, 0, 0))
    return pl.pallas_call(
        functools.partial(spread_kernel, group),
        grid=(SPECIES, planes // step),
        in_specs=[SMEM, SMEM, field_spec] + [VMEM] * group,
        out_specs=field_spec,
        out_shape=jax.ShapeDtypeStruct(base.shape, jnp.float32),
        scratch_shapes=[pltpu.VMEM((2, columns, width), jnp.float32)],
        compiler_params=pltpu.CompilerParams(vmem_limit_bytes=16 * 2**20),
        name="spread",
    )(rank, numbers, base, *parts)


def group_size(devices):
    size = 1
    while 4 * size * size <= 2 * devices and devices % (2 * size) == 0:
        size *= 2
    return size


def body(conc, influx, numbers, cross, kinetics):
    planes = conc.shape[1]
    across, along = lax.axis_size("gx"), lax.axis_size("gy")
    group = group_size(across)
    rank = lax.axis_index("gx").astype(jnp.int32).reshape(1)

    def turned(value, by):
        return lax.ppermute(value, "gy", [(i, (i + by) % along) for i in range(along)])

    def in_group(value, by):
        return lax.ppermute(value, "gx", [(i, i - i % group + (i + by) % group) for i in range(across)])

    def over_groups(value, by):
        return lax.ppermute(value, "gx", [(i, (i + by * group) % across) for i in range(across)])

    h, b, v, w, sums = sources(numbers, cross, kinetics, conc, influx)
    sums = [sums] + [turned(sums, k) for k in range(1, along)]
    y_in, *parts = edges(group, rank, numbers, v, w, sums)
    parts = [parts[0]] + [in_group(parts[d], d) for d in range(1, group)]
    whole = group_sums(group, planes, rank, numbers, parts)
    wholes = [whole] + [over_groups(whole, j) for j in range(1, across // group)]
    outs = entering(group, planes, rank, numbers, parts, wholes)
    outs = [outs[0]] + [in_group(outs[d], d) for d in range(1, group)]
    base = bulk(numbers, h, b, conc, y_in)
    return spread(group, rank, numbers, base, outs)


def solution(mesh):
    placed = (P(None, "gx", "gy", None), P("gx", "gy", None), P(), P(), P())
    return jax.shard_map(
        body, mesh=mesh, in_specs=placed, out_specs=P(None, "gx", "gy", None), check_vma=False
    )
```

```python
import functools

import jax
import jax.numpy as jnp
from jax import lax
from jax.experimental import pallas as pl
from jax.experimental.pallas import tpu as pltpu
from jax.sharding import PartitionSpec as P

SPECIES = 3
ROWS = 8
SMEM = pl.BlockSpec(memory_space=pltpu.SMEM)
VMEM = pl.BlockSpec(memory_space=pltpu.VMEM)
ANY = pl.BlockSpec(memory_space=pl.ANY)


def decay_rate(number):
    half = 0.5 * lax.rsqrt(number)
    square = half * half
    return 2.0 * jnp.log1p(half + square / (1.0 + jnp.sqrt(1.0 + square)))


def scaling(number):
    return lax.rsqrt(1.0 + 4.0 * number)


def splat(value, shape):
    return jnp.full(shape, value, jnp.float32)


def split(value):
    high = value.astype(jnp.bfloat16)
    return high, (value - high.astype(jnp.float32)).astype(jnp.bfloat16)


def product(left, right):
    wide = jnp.concatenate([left[0], left[1]], axis=1)
    deep = jnp.concatenate([right[0], right[0]], axis=0)
    return jnp.dot(wide, deep, preferred_element_type=jnp.float32) + jnp.dot(
        left[0], right[1], preferred_element_type=jnp.float32
    )


def distances(length):
    rows = lax.broadcasted_iota(jnp.int32, (length, length), 0)
    columns = lax.broadcasted_iota(jnp.int32, (length, length), 1)
    return jnp.abs(rows - columns).astype(jnp.float32)


def depth_table(number, length):
    number = splat(number, (length, length))
    theta = decay_rate(number)
    spread = distances(length)
    divisor = 1.0 - jnp.exp(-length * theta)
    return (jnp.exp(-spread * theta) + jnp.exp((spread - length) * theta)) * scaling(number) / divisor


def column_table(number, length):
    number = splat(number, (length, length))
    return jnp.exp(-distances(length) * decay_rate(number)) * scaling(number)


def row_position(length, width):
    return lax.broadcasted_iota(jnp.int32, (length, width), 0).astype(jnp.float32)


def edge_kernel(group, rank, numbers, cross, kinetics, conc, influx, *refs):
    sent, corner, weights, v_hold, w_hold = refs[:group], *refs[group:]
    step = pl.program_id(0)
    planes, chunk, width = conc.shape[1:]
    columns = v_hold.shape[2]
    half = planes // 2
    tile = (ROWS, width)
    n = [[splat(numbers[s, d], tile) for d in range(3)] for s in range(SPECIES)]

    @pl.when(step == 0)
    def _():
        for s in range(SPECIES):
            theta = decay_rate(n[s][0])
            for i in range(half):
                near = jnp.exp(-i * theta)
                far = jnp.exp(-(planes - 1.0 - i) * theta)
                weights[s, i, 0] = 0.5 * (near + far)
                weights[s, i, 1] = 0.5 * (near - far)

    inner, double, single_b = [], [], []
    for s in range(SPECIES):
        scale = scaling(n[s][0])
        per_x = 1.0 / n[s][0]
        per_y = 1.0 / n[s][1]
        for j in range(SPECIES):
            mix = scale if j == s else scale * cross[s, j]
            along_y = n[j][1] * per_y * mix
            along_z = n[j][2] * mix
            single_b.append(along_y)
            double.append(along_z)
            inner.append(n[j][0] * per_x * mix + along_y - 2.0 * along_z)
    scales = [scaling(n[s][0]) for s in range(SPECIES)]
    bind, unbind, pump = (splat(kinetics[i], tile) for i in range(3))

    def rows(k, carry):
        at = pl.multiple_of(k * ROWS, ROWS)
        here = pl.ds(at, ROWS)

        def at_plane(i):
            c = [conc[j, i, here, :] for j in range(SPECIES)]
            binding = bind * c[0] * c[1] - unbind * c[2]
            pumping = pump * c[0] / (1.0 + c[0])
            return c, influx[i, here, :] - 4.0 * binding - pumping, binding

        zero = jnp.zeros(tile, jnp.float32)
        plus = [[zero] * (SPECIES + 1) for _ in range(SPECIES)]
        minus = [[zero] * (SPECIES + 1) for _ in range(SPECIES)]
        for i in range(half):
            low, low_first, low_binding = at_plane(i)
            high, high_first, high_binding = at_plane(planes - 1 - i)
            both = [x + y for x, y in zip(low, high)]
            apart = [x - y for x, y in zip(low, high)]
            change = (low_first + high_first, low_binding + high_binding)
            turn = (low_first - high_first, low_binding - high_binding)
            for s in range(SPECIES):
                even, odd = weights[s, i, 0], weights[s, i, 1]
                of = min(s, 1)
                for j, (p, m) in enumerate(zip(both + [change[of]], apart + [turn[of]])):
                    plus[s][j] = plus[s][j] + even * p
                    minus[s][j] = minus[s][j] + odd * m
        place = pl.ds(pl.multiple_of(step * chunk + at, ROWS), ROWS)
        for s in range(SPECIES):
            for e in range(2):
                sums = [p + m if e else p - m for p, m in zip(plus[s], minus[s])]
                v = sums[SPECIES] * scales[s]
                if s == 1:
                    v = -v
                w = 0.0
                for j in range(SPECIES):
                    at_sj = s * SPECIES + j
                    around = pltpu.roll(sums[j], 1, 1) + pltpu.roll(sums[j], width - 1, 1)
                    v = v + inner[at_sj] * sums[j] + double[at_sj] * around
                    w = w + single_b[at_sj] * sums[j]
                v_hold[e, s, place, :] = v
                w_hold[e, s, place, :] = w
        return carry

    lax.fori_loop(0, chunk // ROWS, rows, 0, unroll=True)

    @pl.when(step == pl.num_programs(0) - 1)
    def _():
        row = row_position(columns, width)
        for s in range(SPECIES):
            theta = decay_rate(splat(numbers[s, 1], (1, width)))
            rise = jnp.exp((row - (columns - 1.0)) * theta)
            fall = jnp.exp(-row * theta)
            table = split(column_table(numbers[s, 1], columns))
            both = product(table, split(jnp.concatenate([v_hold[0, s], v_hold[1, s]], axis=1)))
            stack = [both[:, e * width : (e + 1) * width] - w_hold[e, s] for e in range(2)]
            for weight in (rise, fall):
                for e in range(2):
                    stack.append(jnp.sum(weight * v_hold[e, s], axis=0, keepdims=True))
            stack.append(jnp.zeros((12, width), jnp.float32))
            done = product(split(jnp.concatenate(stack, axis=0)), split(depth_table(numbers[s, 2], width)))
            v_hold[0, s] = done[:columns]
            v_hold[1, s] = done[columns : 2 * columns]
            for k in range(4):
                corner[pl.ds(k * SPECIES + s, 1), :] = done[2 * columns + k : 2 * columns + k + 1]
        share = columns // group
        member = lax.rem(rank[0], group)
        for d in range(group):
            start = pl.multiple_of(lax.rem(member + d, group) * share, share)
            sent[d][...] = v_hold[:, :, pl.ds(start, share), :]


def edges(group, rank, numbers, cross, kinetics, conc, influx):
    _, planes, columns, width = conc.shape
    chunk = 2 * ROWS
    part = jax.ShapeDtypeStruct((2, SPECIES, columns // group, width), jnp.float32)
    corner = jax.ShapeDtypeStruct((4 * SPECIES, width), jnp.float32)
    hold = pltpu.VMEM((2, SPECIES, columns, width), jnp.float32)
    field_spec = pl.BlockSpec((SPECIES, planes, chunk, width), lambda i: (0, 0, i, 0))
    return pl.pallas_call(
        functools.partial(edge_kernel, group),
        grid=(columns // chunk,),
        in_specs=[SMEM, SMEM, SMEM, SMEM, field_spec, pl.BlockSpec((planes, chunk, width), lambda i: (0, i, 0))],
        out_specs=[pl.BlockSpec(part.shape, lambda i: (0, 0, 0, 0))] * group
        + [pl.BlockSpec(corner.shape, lambda i: (0, 0))],
        out_shape=[part] * group + [corner],
        scratch_shapes=[pltpu.VMEM((SPECIES, planes // 2, 2, ROWS, width), jnp.float32), hold, hold],
        compiler_params=pltpu.CompilerParams(vmem_limit_bytes=16 * 2**20),
        cost_estimate=pl.CostEstimate(flops=40 * conc.size, bytes_accessed=6 * conc.size, transcendentals=0),
        name="edges",
    )(rank, numbers, cross, kinetics, conc, influx)


def sweep_kernel(numbers, cross, kinetics, conc, influx, h_out, b_out, g_hold, b_hold):
    planes, chunk, width = conc.shape[1:]
    tile = (ROWS, width)
    n = [[splat(numbers[s, d], tile) for d in range(3)] for s in range(SPECIES)]
    inner, double, single_a, single_b = [], [], [], []
    decay, scale = [], []
    for s in range(SPECIES):
        scale.append(scaling(n[s][0]))
        decay.append(jnp.exp(-decay_rate(n[s][0])))
        per_x = 1.0 / n[s][0]
        per_y = 1.0 / n[s][1]
        for j in range(SPECIES):
            mix = 1.0 if j == s else cross[s, j]
            along_x = n[j][0] * per_x * mix
            along_y = n[j][1] * per_y * mix
            along_z = n[j][2] * mix
            single_a.append(along_x)
            single_b.append(along_y * scale[s])
            double.append(along_z * scale[s])
            inner.append((along_x + along_y - 2.0 * along_z) * scale[s])
    bind, unbind, pump = (splat(kinetics[i], tile) for i in range(3))

    def rows(k, carry):
        here = pl.ds(pl.multiple_of(k * ROWS, ROWS), ROWS)
        up_g = [jnp.zeros(tile, jnp.float32) for _ in range(SPECIES)]
        up_b = [jnp.zeros(tile, jnp.float32) for _ in range(SPECIES)]
        for i in range(planes):
            c = [conc[j, i, here, :] for j in range(SPECIES)]
            around = [pltpu.roll(value, 1, 1) + pltpu.roll(value, width - 1, 1) for value in c]
            binding = bind * c[0] * c[1] - unbind * c[2]
            pumping = pump * c[0] / (1.0 + c[0])
            change = (influx[i, here, :] - 4.0 * binding - pumping, -binding, binding)
            for s in range(SPECIES):
                a = b = None
                g = change[s] * scale[s]
                for j in range(SPECIES):
                    at_sj = s * SPECIES + j
                    g = g + inner[at_sj] * c[j] + double[at_sj] * around[j]
                    part_a = c[j] if s == j else single_a[at_sj] * c[j]
                    part_b = single_b[at_sj] * c[j]
                    a = part_a if a is None else a + part_a
                    b = part_b if b is None else b + part_b
                up_g[s] = g + decay[s] * up_g[s]
                up_b[s] = b + decay[s] * up_b[s]
                g_hold[s, i] = g
                b_hold[s, i] = b
                h_out[s, i, here, :] = up_g[s] - a
                b_out[s, i, here, :] = up_b[s]
        for s in range(SPECIES):
            down_g = jnp.zeros(tile, jnp.float32)
            down_b = jnp.zeros(tile, jnp.float32)
            for i in reversed(range(planes)):
                down_g = decay[s] * down_g
                down_b = decay[s] * down_b
                h_out[s, i, here, :] += down_g
                b_out[s, i, here, :] += down_b
                down_g += g_hold[s, i]
                down_b += b_hold[s, i]
        return carry

    lax.fori_loop(0, chunk // ROWS, rows, 0)


def sweeps(numbers, cross, kinetics, conc, influx):
    _, planes, columns, width = conc.shape
    chunk = 2 * ROWS
    field_spec = pl.BlockSpec((SPECIES, planes, chunk, width), lambda i: (0, 0, i, 0))
    hold = pltpu.VMEM((SPECIES, planes, ROWS, width), jnp.float32)
    return pl.pallas_call(
        sweep_kernel,
        grid=(columns // chunk,),
        in_specs=[SMEM, SMEM, SMEM, field_spec, pl.BlockSpec((planes, chunk, width), lambda i: (0, i, 0))],
        out_specs=[field_spec, field_spec],
        out_shape=[pltpu.HBM(conc.shape, jnp.float32)] * 2,
        scratch_shapes=[hold, hold],
        compiler_params=pltpu.CompilerParams(vmem_limit_bytes=16 * 2**20),
        cost_estimate=pl.CostEstimate(flops=100 * conc.size, bytes_accessed=14 * conc.size, transcendentals=0),
        name="sweeps",
    )(numbers, cross, kinetics, conc, influx)


def group_kernel(group, planes, rank, numbers, after, *refs):
    parts, out = refs[:-1], refs[-1]
    member = lax.rem(rank[0], group)
    tile = parts[0].shape[2:]
    for s in range(SPECIES):
        theta = planes * decay_rate(splat(numbers[s, 0], tile))
        rising, falling = 0.0, 0.0
        for d in range(group):
            block = lax.rem(member - d + group, group).astype(jnp.float32)
            rising = rising + jnp.exp((block - (group - 1.0)) * theta) * parts[d][0, s]
            falling = falling + jnp.exp(-block * theta) * parts[d][1, s]
        out[0, s] = rising
        out[1, s] = falling


def group_sums(group, planes, rank, numbers, after, parts):
    return pl.pallas_call(
        functools.partial(group_kernel, group, planes),
        in_specs=[SMEM, SMEM, ANY] + [VMEM] * len(parts),
        out_specs=VMEM,
        out_shape=jax.ShapeDtypeStruct(parts[0].shape, jnp.float32),
        compiler_params=pltpu.CompilerParams(vmem_limit_bytes=8 * 2**20),
        name="group_sums",
    )(rank, numbers, after, *parts)


def enter_kernel(group, planes, rank, numbers, after, *refs):
    parts, wholes, outs = refs[:group], refs[group:-group], refs[-group:]
    groups = len(wholes)
    member = lax.rem(rank[0], group)
    tile = parts[0].shape[2:]
    for s in range(SPECIES):
        theta = planes * decay_rate(splat(numbers[s, 0], tile))
        closing = 1.0 / (1.0 - jnp.exp(-(group * groups) * theta))
        into, out_of = 0.0, 0.0
        for j in range(groups):
            rise = jnp.exp(-(group * (j - 1 if j else groups - 1)) * theta) * closing
            fall = jnp.exp(-(group * (groups - j - 1)) * theta) * closing
            into = into + rise * wholes[j][0, s]
            out_of = out_of + fall * wholes[j][1, s]
        held = [(parts[d][0, s], parts[d][1, s]) for d in range(group)]
        for d in range(group):
            target = lax.rem(member + d, group)
            rising = jnp.exp(-target.astype(jnp.float32) * theta) * into
            falling = jnp.exp((target - (group - 1)).astype(jnp.float32) * theta) * out_of
            for e in range(group):
                block = lax.rem(member - e + group, group)
                away = (target - block).astype(jnp.float32)
                weight = jnp.exp((1.0 - jnp.abs(away)) * theta)
                rising = rising + jnp.where(target > block, weight, 0.0) * held[e][0]
                falling = falling + jnp.where(target < block, weight, 0.0) * held[e][1]
            outs[d][0, s] = rising
            outs[d][1, s] = falling


def entering(group, planes, rank, numbers, after, parts, wholes):
    part = jax.ShapeDtypeStruct(parts[0].shape, jnp.float32)
    return pl.pallas_call(
        functools.partial(enter_kernel, group, planes),
        in_specs=[SMEM, SMEM, ANY] + [VMEM] * (len(parts) + len(wholes)),
        out_specs=[VMEM] * group,
        out_shape=[part] * group,
        compiler_params=pltpu.CompilerParams(vmem_limit_bytes=8 * 2**20),
        name="entering",
    )(rank, numbers, after, *parts, *wholes)


def bulk_kernel(numbers, h, b, conc, out, y_out, column_hold, depth_hold):
    s = pl.program_id(0)
    planes, columns, width = h.shape[1:]

    @pl.when(pl.program_id(1) == 0)
    def _():
        row = lax.broadcasted_iota(jnp.int32, (2 * ROWS, columns), 0)
        position = lax.broadcasted_iota(jnp.int32, (2 * ROWS, columns), 1).astype(jnp.float32)
        theta = decay_rate(splat(numbers[s, 1], (2 * ROWS, columns)))
        rise = jnp.exp((position - (columns - 1.0)) * theta)
        fall = jnp.exp(-position * theta)
        sums = jnp.where(row == 0, rise, jnp.where(row == 1, fall, 0.0))
        table = jnp.concatenate([column_table(numbers[s, 1], columns), sums], axis=0)
        column_hold[0], column_hold[1] = split(table)
        depth_hold[0], depth_hold[1] = split(depth_table(numbers[s, 2], width))

    table = (column_hold[0], column_hold[1])
    depth = (depth_hold[0], depth_hold[1])
    for i in range(planes):
        solved = product(table, split(h[0, i]))
        solved = jnp.concatenate([solved[:columns] - b[0, i], solved[columns:]], axis=0)
        solved = product(split(solved), depth)
        out[0, i] = conc[0, i] + solved[:columns]
        y_out[0, 0, i : i + 1] = solved[columns : columns + 1]
        y_out[1, 0, i : i + 1] = solved[columns + 1 : columns + 2]


def bulk(numbers, h, b, conc):
    _, planes, columns, width = conc.shape
    step = min(planes, 8)
    field_spec = pl.BlockSpec((1, step, columns, width), lambda s, i: (s, i, 0, 0))
    return pl.pallas_call(
        bulk_kernel,
        grid=(SPECIES, planes // step),
        in_specs=[SMEM, field_spec, field_spec, field_spec],
        out_specs=[field_spec, pl.BlockSpec((2, 1, step, width), lambda s, i: (0, s, i, 0))],
        out_shape=[
            jax.ShapeDtypeStruct(conc.shape, jnp.float32),
            jax.ShapeDtypeStruct((2, SPECIES, planes, width), jnp.float32),
        ],
        scratch_shapes=[
            pltpu.VMEM((2, columns + 2 * ROWS, columns), jnp.bfloat16),
            pltpu.VMEM((2, width, width), jnp.bfloat16),
        ],
        compiler_params=pltpu.CompilerParams(vmem_limit_bytes=16 * 2**20),
        cost_estimate=pl.CostEstimate(
            flops=6 * conc.size * (columns + width), bytes_accessed=16 * conc.size, transcendentals=0
        ),
        name="bulk",
    )(numbers, h, b, conc)


def inflow_kernel(planes, columns, rank, numbers, corners, *refs):
    sums, (y_in, corner_in) = refs[:-2], refs[-2:]
    along = len(sums)
    across = corners.shape[0] // along
    width = corners.shape[2]
    for s in range(SPECIES):
        theta = decay_rate(splat(numbers[s, 1], (1, width)))
        closing = scaling(splat(numbers[s, 1], (1, width))) / (1.0 - jnp.exp(-(columns * along) * theta))
        into, out_of = 0.0, 0.0
        for k in range(along):
            rise = jnp.exp(-(columns * (k - 1 if k else along - 1)) * theta) * closing
            fall = jnp.exp(-(columns * (along - k - 1)) * theta) * closing
            into = into + rise * sums[k][0, s]
            out_of = out_of + fall * sums[k][1, s]
        y_in[0, s] = into
        y_in[1, s] = out_of

    tile = corners.shape[1:]
    row = lax.broadcasted_iota(jnp.int32, tile, 0)
    kind = row // SPECIES
    species = row - kind * SPECIES
    from_below_x = lax.rem(kind, 2) == 0
    from_below_y = kind < 2

    def by_species(d):
        first, second, third = (splat(numbers[s, d], tile) for s in range(SPECIES))
        return jnp.where(species == 0, first, jnp.where(species == 1, second, third))

    number_y = by_species(1)
    theta_x = planes * decay_rate(by_species(0))
    theta_y = columns * decay_rate(number_y)
    total = jnp.zeros(tile, jnp.float32)
    for k in range(across):
        up_x = lax.rem(rank[0] - k - 1 + 2 * across, across).astype(jnp.float32)
        down_x = lax.rem(k - rank[0] - 1 + 2 * across, across).astype(jnp.float32)
        steps_x = jnp.where(from_below_x, up_x, down_x) * theta_x
        part = jnp.zeros(tile, jnp.float32)
        for l in range(along):
            up_y = lax.rem(rank[1] - l - 1 + 2 * along, along).astype(jnp.float32)
            down_y = lax.rem(l - rank[1] - 1 + 2 * along, along).astype(jnp.float32)
            steps_y = jnp.where(from_below_y, up_y, down_y) * theta_y
            part = part + jnp.exp(-steps_y) * corners[k * along + l]
        total = total + jnp.exp(-steps_x) * part
    closing = scaling(number_y) / ((1.0 - jnp.exp(-across * theta_x)) * (1.0 - jnp.exp(-along * theta_y)))
    corner_in[...] = total * closing


def inflow(planes, columns, rank, numbers, corners, sums):
    return pl.pallas_call(
        functools.partial(inflow_kernel, planes, columns),
        in_specs=[SMEM, SMEM] + [VMEM] * (1 + len(sums)),
        out_specs=[VMEM, VMEM],
        out_shape=[
            jax.ShapeDtypeStruct(sums[0].shape, jnp.float32),
            jax.ShapeDtypeStruct(corners.shape[1:], jnp.float32),
        ],
        compiler_params=pltpu.CompilerParams(vmem_limit_bytes=8 * 2**20),
        name="inflow",
    )(rank, numbers, corners, *sums)


def spread_kernel(group, rank, numbers, base, y_in, corner_in, *refs):
    parts, out, hold, fade = refs[:group], *refs[group:]
    s, i = pl.program_id(0), pl.program_id(1)
    step, columns, width = base.shape[1:]
    planes = step * pl.num_programs(1)
    share = columns // group
    member = lax.rem(rank[0], group)

    @pl.when(i == 0)
    def _():
        row = row_position(columns, width)
        theta = decay_rate(splat(numbers[s, 1], (1, width)))
        fade[0] = jnp.exp(-(row + 1.0) * theta)
        fade[1] = jnp.exp((row - columns) * theta)
        for d in range(group):
            start = pl.multiple_of(lax.rem(member - d + group, group) * share, share)
            for e in range(2):
                hold[e, pl.ds(start, share), :] = parts[d][e, s]
        for e in range(2):
            rise = corner_in[pl.ds(e * SPECIES + s, 1), :]
            fall = corner_in[pl.ds((2 + e) * SPECIES + s, 1), :]
            hold[e] = hold[e] + fade[0] * rise + fade[1] * fall

    theta = decay_rate(splat(numbers[s, 0], (1, width)))
    for k in range(step):
        place = i * step + k
        position = place.astype(jnp.float32)
        rise = jnp.exp(-(position + 1.0) * theta)
        fall = jnp.exp((position - planes) * theta)
        along_x = rise * hold[0] + fall * hold[1]
        along_y = fade[0] * y_in[0, s, pl.ds(place, 1), :] + fade[1] * y_in[1, s, pl.ds(place, 1), :]
        out[0, k] = base[0, k] + along_x + along_y


def spread(group, rank, numbers, base, y_in, corner_in, parts):
    _, planes, columns, width = base.shape
    step = min(planes, 4)
    field_spec = pl.BlockSpec((1, step, columns, width), lambda s, i: (s, i, 0, 0))
    hold = pltpu.VMEM((2, columns, width), jnp.float32)
    return pl.pallas_call(
        functools.partial(spread_kernel, group),
        grid=(SPECIES, planes // step),
        in_specs=[SMEM, SMEM, field_spec] + [VMEM] * (2 + group),
        out_specs=field_spec,
        out_shape=jax.ShapeDtypeStruct(base.shape, jnp.float32),
        scratch_shapes=[hold, hold],
        compiler_params=pltpu.CompilerParams(vmem_limit_bytes=16 * 2**20),
        name="spread",
    )(rank, numbers, base, y_in, corner_in, *parts)


def group_size(devices):
    size = 1
    while 4 * size * size <= 2 * devices and devices % (2 * size) == 0:
        size *= 2
    return size


def body(conc, influx, numbers, cross, kinetics):
    _, planes, columns, _ = conc.shape
    across, along = lax.axis_size("gx"), lax.axis_size("gy")
    group = group_size(across)
    rank = jnp.stack([lax.axis_index("gx"), lax.axis_index("gy")]).astype(jnp.int32)
    conc, influx, numbers, cross, kinetics = (
        pltpu.with_memory_space_constraint(x, pltpu.HBM) for x in (conc, influx, numbers, cross, kinetics)
    )

    def turned(value, by):
        return lax.ppermute(value, "gy", [(i, (i + by) % along) for i in range(along)])

    def in_group(value, by):
        return lax.ppermute(value, "gx", [(i, i - i % group + (i + by) % group) for i in range(across)])

    def over_groups(value, by):
        return lax.ppermute(value, "gx", [(i, (i + by * group) % across) for i in range(across)])

    *parts, corner = edges(group, rank, numbers, cross, kinetics, conc, influx)
    parts = [parts[0]] + [in_group(parts[d], d) for d in range(1, group)]
    corners = lax.all_gather(corner, ("gx", "gy"))
    h, b = sweeps(numbers, cross, kinetics, conc, influx)
    whole = group_sums(group, planes, rank, numbers, b, parts)
    wholes = [whole] + [over_groups(whole, j) for j in range(1, across // group)]
    base, sums = bulk(numbers, h, b, conc)
    sums = [sums] + [turned(sums, k) for k in range(1, along)]
    outs = entering(group, planes, rank, numbers, base, parts, wholes)
    outs = [outs[0]] + [in_group(outs[d], d) for d in range(1, group)]
    y_in, corner_in = inflow(planes, columns, rank, numbers, corners, sums)
    return spread(group, rank, numbers, base, y_in, corner_in, outs)


def solution(mesh):
    placed = (P(None, "gx", "gy", None), P("gx", "gy", None), P(), P(), P())
    return jax.shard_map(
        body, mesh=mesh, in_specs=placed, out_specs=P(None, "gx", "gy", None), check_vma=False
    )
```

```python
import functools

import jax
import jax.numpy as jnp
from jax import lax
from jax.experimental import pallas as pl
from jax.experimental.pallas import tpu as pltpu
from jax.sharding import PartitionSpec as P

SPECIES = 3
ROWS = 8
SIDES = 2
CORNERS = SIDES * SIDES * SPECIES
SMEM = pl.BlockSpec(memory_space=pltpu.SMEM)
VMEM = pl.BlockSpec(memory_space=pltpu.VMEM)
ANY = pl.BlockSpec(memory_space=pl.ANY)

RATE_X, RATE_Y, SCALE_Y, MEMBER, RANK_Y, TABLE_ROWS = 0, 3, 6, 9, 10, 16


def padded(rows):
    return -(-rows // ROWS) * ROWS


def params(mebibytes):
    return pltpu.CompilerParams(vmem_limit_bytes=mebibytes * 2**20)


def struct(*shape):
    return jax.ShapeDtypeStruct(shape, jnp.float32)


def decay_rate(number):
    half = 0.5 * lax.rsqrt(number)
    square = half * half
    return 2.0 * jnp.log1p(half + square / (1.0 + jnp.sqrt(1.0 + square)))


def scaling(number):
    return lax.rsqrt(1.0 + 4.0 * number)


def splat(value, shape):
    return jnp.full(shape, value, jnp.float32)


def split(value):
    high = value.astype(jnp.bfloat16)
    return high, (value - high.astype(jnp.float32)).astype(jnp.bfloat16)


def left_pair(value):
    return jnp.concatenate(split(value), axis=1)


def right_pair(value):
    high, low = split(value)
    return jnp.concatenate(
        [jnp.concatenate([high, low], axis=1), jnp.concatenate([high, jnp.zeros_like(low)], axis=1)], axis=0
    )


def product(left, right):
    both = jnp.dot(left, right, preferred_element_type=jnp.float32)
    width = both.shape[1] // 2
    return both[:, :width] + both[:, width:]


def distances(length):
    rows = lax.broadcasted_iota(jnp.int32, (length, length), 0)
    columns = lax.broadcasted_iota(jnp.int32, (length, length), 1)
    return jnp.abs(rows - columns).astype(jnp.float32)


def depth_table(number, length):
    number = splat(number, (1, length))
    theta = decay_rate(number)
    spread = distances(length)
    factor = scaling(number) / (1.0 - jnp.exp(-length * theta))
    return (jnp.exp(-spread * theta) + jnp.exp((spread - length) * theta)) * factor


def column_table(number, length):
    number = splat(number, (1, length))
    return jnp.exp(-distances(length) * decay_rate(number)) * scaling(number)


def row_position(length, width):
    return lax.broadcasted_iota(jnp.int32, (length, width), 0).astype(jnp.float32)


def coefficients(numbers, cross, kinetics, tile):
    n = [[splat(numbers[s, d], tile) for d in range(3)] for s in range(SPECIES)]
    along_x, along_y, along_z = [], [], []
    for s in range(SPECIES):
        per_x, per_y = 1.0 / n[s][0], 1.0 / n[s][1]
        for j in range(SPECIES):
            mix = 1.0 if j == s else cross[s, j]
            along_x.append(n[j][0] * per_x * mix)
            along_y.append(n[j][1] * per_y * mix)
            along_z.append(n[j][2] * mix)
    scale = [scaling(n[s][0]) for s in range(SPECIES)]
    rate = [decay_rate(n[s][0]) for s in range(SPECIES)]
    return along_x, along_y, along_z, scale, rate, [splat(kinetics[i], tile) for i in range(3)]


def turned(value):
    width = value.shape[1]
    return pltpu.roll(value, 1, 1) + pltpu.roll(value, width - 1, 1)


def edge_kernel(
    group, rank, numbers, cross, kinetics, conc_far, influx_far,
    message, table, conc, influx, weights, v_hold, w_hold, y_table, z_table, arrived,
):
    planes, columns, width = influx.shape
    chunks = arrived.shape[1]
    chunk = columns // chunks
    half = planes // 2
    share = columns // group
    tile = (ROWS, width)

    def copies(k):
        part = pl.ds(k * chunk, chunk)
        return (
            pltpu.make_async_copy(conc_far.at[:, :, part, :], conc.at[:, :, part, :], arrived.at[0, k]),
            pltpu.make_async_copy(influx_far.at[:, part, :], influx.at[:, part, :], arrived.at[1, k]),
        )

    for k in range(chunks):
        for copy in copies(k):
            copy.start()

    along_x, along_y, along_z, scale, rate, (bind, unbind, pump) = coefficients(numbers, cross, kinetics, tile)
    inner, double, single = [], [], []
    for s in range(SPECIES):
        for at in range(s * SPECIES, (s + 1) * SPECIES):
            inner.append((along_x[at] + along_y[at] - 2.0 * along_z[at]) * scale[s])
            double.append(along_z[at] * scale[s])
            single.append(along_y[at] * scale[s])
        for i in range(half):
            near = jnp.exp(-i * rate[s])
            far = jnp.exp(-(planes - 1.0 - i) * rate[s])
            weights[s, i, 0] = 0.5 * (near + far)
            weights[s, i, 1] = 0.5 * (near - far)
        table[RATE_X + s : RATE_X + s + 1] = rate[s][:1]
        number = splat(numbers[s, 1], (1, width))
        table[RATE_Y + s : RATE_Y + s + 1] = decay_rate(number)
        table[SCALE_Y + s : SCALE_Y + s + 1] = scaling(number)
        y_table[s] = left_pair(column_table(numbers[s, 1], columns))
        z_table[s] = right_pair(depth_table(numbers[s, 2], width))
    member = lax.rem(rank[0], group).astype(jnp.float32)
    table[MEMBER : MEMBER + 1] = splat(member, (1, width))
    table[RANK_Y : RANK_Y + 1] = splat(rank[1].astype(jnp.float32), (1, width))

    def rows(k, carry):
        here = pl.ds(pl.multiple_of(k * ROWS, ROWS), ROWS)

        def at_plane(i):
            c = [conc[j, i, here, :] for j in range(SPECIES)]
            binding = bind * c[0] * c[1] - unbind * c[2]
            pumping = pump * c[0] / (1.0 + c[0])
            return c, influx[i, here, :] - 4.0 * binding - pumping, binding

        zero = jnp.zeros(tile, jnp.float32)
        plus = [[zero] * (SPECIES + 1) for _ in range(SPECIES)]
        minus = [[zero] * (SPECIES + 1) for _ in range(SPECIES)]
        for i in range(half):
            low, low_first, low_binding = at_plane(i)
            high, high_first, high_binding = at_plane(planes - 1 - i)
            both = [x + y for x, y in zip(low, high)]
            apart = [x - y for x, y in zip(low, high)]
            change = (low_first + high_first, low_binding + high_binding)
            turn = (low_first - high_first, low_binding - high_binding)
            for s in range(SPECIES):
                even, odd = weights[s, i, 0], weights[s, i, 1]
                of = min(s, 1)
                for j, (p, m) in enumerate(zip(both + [change[of]], apart + [turn[of]])):
                    plus[s][j] = plus[s][j] + even * p
                    minus[s][j] = minus[s][j] + odd * m
        for s in range(SPECIES):
            for e in range(SIDES):
                sums = [p + m if e else p - m for p, m in zip(plus[s], minus[s])]
                v = sums[SPECIES] * scale[s]
                if s == 1:
                    v = -v
                w = 0.0
                for j in range(SPECIES):
                    at = s * SPECIES + j
                    v = v + inner[at] * sums[j] + double[at] * turned(sums[j])
                    w = w + single[at] * sums[j]
                v_hold[e, s, here, :] = v
                w_hold[e, s, here, :] = w
        return carry

    for k in range(chunks):
        for copy in copies(k):
            copy.wait()
        lax.fori_loop(k * (chunk // ROWS), (k + 1) * (chunk // ROWS), rows, 0, unroll=True)

    row = row_position(columns, width)
    for s in range(SPECIES):
        theta = table[RATE_Y + s : RATE_Y + s + 1]
        rise = jnp.exp((row - (columns - 1.0)) * theta)
        fall = jnp.exp(-row * theta)
        both = product(y_table[s], right_pair(jnp.concatenate([v_hold[0, s], v_hold[1, s]], axis=1)))
        stack = [both[:, e * width : (e + 1) * width] - w_hold[e, s] for e in range(SIDES)]
        for weight in (rise, fall):
            for e in range(SIDES):
                stack.append(jnp.sum(weight * v_hold[e, s], axis=0, keepdims=True))
        stack.append(jnp.zeros((2 * ROWS - 2 * SIDES, width), jnp.float32))
        done = product(left_pair(jnp.concatenate(stack, axis=0)), z_table[s])
        for b in range(group):
            for e in range(SIDES):
                at = e * columns + b * share
                message[b, pl.ds((e * SPECIES + s) * share, share), :] = done[at : at + share]
            for k in range(SIDES * SIDES):
                at = SIDES * columns + k
                message[b, pl.ds(SIDES * SPECIES * share + k * SPECIES + s, 1), :] = done[at : at + 1]


def edges(group, rank, numbers, cross, kinetics, conc, influx):
    _, planes, columns, width = conc.shape
    chunks = columns // (2 * ROWS)
    hold = pltpu.VMEM((SIDES, SPECIES, columns, width), jnp.float32)
    rows = padded(SIDES * SPECIES * (columns // group) + CORNERS)
    return pl.pallas_call(
        functools.partial(edge_kernel, group),
        in_specs=[SMEM, SMEM, SMEM, SMEM, ANY, ANY],
        out_specs=[VMEM] * 4,
        out_shape=[
            struct(group, rows, width),
            pltpu.VMEM((TABLE_ROWS, width), jnp.float32),
            pltpu.VMEM(conc.shape, jnp.float32),
            pltpu.VMEM(influx.shape, jnp.float32),
        ],
        scratch_shapes=[
            pltpu.VMEM((SPECIES, planes // 2, 2, ROWS, width), jnp.float32),
            hold,
            hold,
            pltpu.VMEM((SPECIES, columns, 2 * columns), jnp.bfloat16),
            pltpu.VMEM((SPECIES, 2 * width, 2 * width), jnp.bfloat16),
            pltpu.SemaphoreType.DMA((2, chunks)),
        ],
        compiler_params=params(16),
        name="edges",
    )(rank, numbers, cross, kinetics, conc, influx)


def sweep_kernel(numbers, cross, kinetics, conc, influx, h_out, b_out, g_hold, b_hold):
    planes, columns, width = influx.shape
    tile = (ROWS, width)
    along_x, along_y, along_z, scale, rate, (bind, unbind, pump) = coefficients(numbers, cross, kinetics, tile)
    inner, double, single = [], [], []
    for s in range(SPECIES):
        for at in range(s * SPECIES, (s + 1) * SPECIES):
            inner.append((along_x[at] + along_y[at] - 2.0 * along_z[at]) * scale[s])
            double.append(along_z[at] * scale[s])
            single.append(along_y[at] * scale[s])
    decay = [jnp.exp(-value) for value in rate]

    def rows(k, carry):
        here = pl.ds(pl.multiple_of(k * ROWS, ROWS), ROWS)
        up_g = [jnp.zeros(tile, jnp.float32) for _ in range(SPECIES)]
        up_b = [jnp.zeros(tile, jnp.float32) for _ in range(SPECIES)]
        for i in range(planes):
            c = [conc[j, i, here, :] for j in range(SPECIES)]
            around = [turned(value) for value in c]
            binding = bind * c[0] * c[1] - unbind * c[2]
            pumping = pump * c[0] / (1.0 + c[0])
            change = (influx[i, here, :] - 4.0 * binding - pumping, -binding, binding)
            for s in range(SPECIES):
                a = b = None
                g = change[s] * scale[s]
                for j in range(SPECIES):
                    at = s * SPECIES + j
                    g = g + inner[at] * c[j] + double[at] * around[j]
                    part_a = c[j] if s == j else along_x[at] * c[j]
                    part_b = single[at] * c[j]
                    a = part_a if a is None else a + part_a
                    b = part_b if b is None else b + part_b
                up_g[s] = g + decay[s] * up_g[s]
                up_b[s] = b + decay[s] * up_b[s]
                g_hold[s, i] = g
                b_hold[s, i] = b
                h_out[s, i, here, :] = up_g[s] - a
                b_out[s, i, here, :] = up_b[s]
        for s in range(SPECIES):
            down_g = jnp.zeros(tile, jnp.float32)
            down_b = jnp.zeros(tile, jnp.float32)
            for i in reversed(range(planes)):
                down_g = decay[s] * down_g
                down_b = decay[s] * down_b
                h_out[s, i, here, :] += down_g
                b_out[s, i, here, :] += down_b
                down_g += g_hold[s, i]
                down_b += b_hold[s, i]
        return carry

    lax.fori_loop(0, columns // ROWS, rows, 0)


def sweeps(numbers, cross, kinetics, conc, influx):
    _, planes, columns, width = conc.shape
    hold = pltpu.VMEM((SPECIES, planes, ROWS, width), jnp.float32)
    return pl.pallas_call(
        sweep_kernel,
        in_specs=[SMEM, SMEM, SMEM, VMEM, VMEM],
        out_specs=[VMEM] * 2,
        out_shape=[pltpu.VMEM(conc.shape, jnp.float32)] * 2,
        scratch_shapes=[hold, hold],
        compiler_params=params(8),
        cost_estimate=pl.CostEstimate(flops=100 * conc.size, bytes_accessed=14 * conc.size, transcendentals=0),
        name="sweeps",
    )(numbers, cross, kinetics, conc, influx)


def group_kernel(planes, share, table, after, message, out):
    group = message.shape[0]
    corners = SIDES * SPECIES * share
    for s in range(SPECIES):
        theta = planes * table[RATE_X + s : RATE_X + s + 1]
        for e in range(SIDES):
            weight = [jnp.exp(-float(b if e else group - 1 - b) * theta) for b in range(group)]
            here = pl.ds((e * SPECIES + s) * share, share)
            out[here, :] = sum(weight[b] * message[b, here, :] for b in range(group))
            for k in range(SIDES):
                here = pl.ds(corners + (k * SIDES + e) * SPECIES + s, 1)
                out[here, :] = sum(weight[b] * message[b, here, :] for b in range(group))


def group_sums(planes, share, table, after, message):
    return pl.pallas_call(
        functools.partial(group_kernel, planes, share),
        in_specs=[VMEM, ANY, VMEM],
        out_specs=VMEM,
        out_shape=struct(*message.shape[1:]),
        compiler_params=params(8),
        name="group_sums",
    )(table, after, message)


def bulk_kernel(numbers, table, h, b, conc, out, y_out, weights, y_table, z_table, sums):
    _, planes, columns, width = h.shape
    row = row_position(columns, width)
    for s in range(SPECIES):
        theta = table[RATE_Y + s : RATE_Y + s + 1]
        weights[0] = jnp.exp((row - (columns - 1.0)) * theta)
        weights[1] = jnp.exp(-row * theta)
        y_table[...] = left_pair(column_table(numbers[s, 1], columns))
        z_table[...] = right_pair(depth_table(numbers[s, 2], width))

        def plane(i, carry):
            value = h[s, i]
            for e in range(SIDES):
                sums[e, pl.ds(i, 1), :] = jnp.sum(weights[e] * value, axis=0, keepdims=True)
            solved = product(y_table[...], right_pair(value)) - b[s, i]
            out[s, i] = conc[s, i] + product(left_pair(solved), z_table[...])
            return carry

        lax.fori_loop(0, planes, plane, 0, unroll=4)
        both = jnp.concatenate([sums[e] for e in range(SIDES)], axis=0)
        both = product(left_pair(both), z_table[...])
        for e in range(SIDES):
            y_out[pl.ds((e * SPECIES + s) * planes, planes), :] = both[e * planes : (e + 1) * planes]


def bulk(numbers, table, h, b, conc):
    _, planes, columns, width = conc.shape
    return pl.pallas_call(
        bulk_kernel,
        in_specs=[SMEM] + [VMEM] * 4,
        out_specs=[VMEM] * 2,
        out_shape=[
            pltpu.VMEM(conc.shape, jnp.float32),
            pltpu.VMEM((SIDES * SPECIES * planes, width), jnp.float32),
        ],
        scratch_shapes=[
            pltpu.VMEM((SIDES, columns, width), jnp.float32),
            pltpu.VMEM((columns, 2 * columns), jnp.bfloat16),
            pltpu.VMEM((2 * width, 2 * width), jnp.bfloat16),
            pltpu.VMEM((SIDES, planes, width), jnp.float32),
        ],
        compiler_params=params(8),
        cost_estimate=pl.CostEstimate(
            flops=6 * conc.size * (columns + width), bytes_accessed=16 * conc.size, transcendentals=0
        ),
        name="bulk",
    )(numbers, table, h, b, conc)


def enter_kernel(planes, share, table, sums, message, *refs):
    wholes, (out, y_out) = refs[:-2], refs[-2:]
    group, groups, along = message.shape[0], len(wholes), y_out.shape[0]
    corners = SIDES * SPECIES * share
    member = table[MEMBER : MEMBER + 1]
    for copy in range(along):
        y_out[copy, pl.ds(0, sums.shape[0]), :] = sums[...]

    for s in range(SPECIES):
        theta = planes * table[RATE_X + s : RATE_X + s + 1]
        power = [jnp.exp(-float(k) * theta) for k in range(group)]
        closing = 1.0 / (1.0 - jnp.exp(-float(group * groups) * theta))
        for e in range(SIDES):
            steps = [(groups - j - 1) if e else (j - 1 if j else groups - 1) for j in range(groups)]
            outside = [jnp.exp(-float(group * k) * theta) * closing for k in steps]

            def entering_group(here):
                return sum(weight * whole[here, :] for weight, whole in zip(outside, wholes))

            here = pl.ds((e * SPECIES + s) * share, share)
            whole = entering_group(here)
            held = [message[b, here, :] for b in range(group)]
            for target in range(group):
                total = power[group - 1 - target if e else target] * whole
                for b in range(group):
                    away = (b - target) if e else (target - b)
                    if away > 0:
                        total = total + power[away - 1] * held[b]
                out[target, here, :] = total

            from_outside = jnp.exp(-(group - 1 - member if e else member) * theta)
            inside = []
            for b in range(group):
                away = (b - member) if e else (member - b)
                inside.append(jnp.where(away > 0, jnp.exp((1.0 - jnp.abs(away)) * theta), 0.0))
            for k in range(SIDES):
                at = (k * SIDES + e) * SPECIES + s
                here = pl.ds(corners + at, 1)
                total = from_outside * entering_group(here)
                for b in range(group):
                    total = total + inside[b] * message[b, here, :]
                for copy in range(along):
                    y_out[copy, pl.ds(sums.shape[0] + at, 1), :] = total


def entering(planes, share, along, table, sums, message, wholes):
    group, _, width = message.shape
    return pl.pallas_call(
        functools.partial(enter_kernel, planes, share),
        in_specs=[VMEM] * (3 + len(wholes)),
        out_specs=[VMEM] * 2,
        out_shape=[
            struct(group, SIDES * SPECIES * share, width),
            struct(along, padded(sums.shape[0] + CORNERS), width),
        ],
        compiler_params=params(8),
        name="entering",
    )(table, sums, message, *wholes)


def inflow_kernel(table, base, message, out, lift, fades, weights):
    _, planes, columns, width = base.shape
    along = message.shape[0]
    corners = SIDES * SPECIES * planes
    rank = table[RANK_Y : RANK_Y + 1]
    row = row_position(columns, width)
    position = row_position(planes, width)
    for s in range(SPECIES):
        rate_x = table[RATE_X + s : RATE_X + s + 1]
        rate_y = table[RATE_Y + s : RATE_Y + s + 1]
        theta = columns * rate_y
        closing = table[SCALE_Y + s : SCALE_Y + s + 1] / (1.0 - jnp.exp(-float(along) * theta))
        weights[0] = jnp.exp(-(row + 1.0) * rate_y)
        weights[1] = jnp.exp((row - columns) * rate_y)
        fades[pl.ds(s * planes, planes), :] = jnp.exp(-(position + 1.0) * rate_x)
        fades[pl.ds((SPECIES + s) * planes, planes), :] = jnp.exp((position - planes) * rate_x)
        enter, corner = [], []
        for e in range(SIDES):
            arrive = []
            for l in range(along):
                steps = (l - rank - 1.0) if e else (rank - l - 1.0)
                steps = jnp.where(steps < 0.0, steps + along, steps)
                arrive.append(jnp.exp(-steps * theta) * closing)

            def entering_block(here):
                return sum(arrive[l] * message[l, here, :] for l in range(along))

            enter.append(entering_block(pl.ds((e * SPECIES + s) * planes, planes)))
            corner.append([entering_block(pl.ds(corners + (e * SIDES + k) * SPECIES + s, 1)) for k in range(SIDES)])
        for k in range(SIDES):
            lift[k, s] = weights[0] * corner[0][k] + weights[1] * corner[1][k]
        for i in range(planes):
            out[s, i] = base[s, i] + weights[0] * enter[0][i : i + 1] + weights[1] * enter[1][i : i + 1]


def inflow(table, base, message):
    _, planes, columns, width = base.shape
    return pl.pallas_call(
        inflow_kernel,
        in_specs=[VMEM] * 3,
        out_specs=[VMEM] * 3,
        out_shape=[
            pltpu.VMEM(base.shape, jnp.float32),
            pltpu.VMEM((SIDES, SPECIES, columns, width), jnp.float32),
            pltpu.VMEM((SIDES * SPECIES * planes, width), jnp.float32),
        ],
        scratch_shapes=[pltpu.VMEM((SIDES, columns, width), jnp.float32)],
        compiler_params=params(8),
        name="inflow",
    )(table, base, message)


def spread_kernel(share, fades, base, lift, message, out_far, out, hold, left):
    _, planes, columns, width = base.shape
    group = message.shape[0]
    at_once = planes // left.shape[1]
    copies = []
    for s in range(SPECIES):
        for e in range(SIDES):
            for b in range(group):
                there = pl.ds(b * share, share)
                hold[e, there, :] = lift[e, s, there, :] + message[b, pl.ds((e * SPECIES + s) * share, share), :]
        for i in range(planes):
            rise = fades[s * planes + i : s * planes + i + 1]
            fall = fades[(SPECIES + s) * planes + i : (SPECIES + s) * planes + i + 1]
            out[s, i] = base[s, i] + rise * hold[0] + fall * hold[1]
            if i % at_once == at_once - 1:
                k = i // at_once
                part = pl.ds(k * at_once, at_once)
                copies.append(pltpu.make_async_copy(out.at[s, part], out_far.at[s, part], left.at[s, k]))
                copies[-1].start()
    for copy in copies:
        copy.wait()


def spread(share, fades, base, lift, message):
    _, planes, columns, width = base.shape
    return pl.pallas_call(
        functools.partial(spread_kernel, share),
        in_specs=[VMEM] * 4,
        out_specs=ANY,
        out_shape=struct(*base.shape),
        scratch_shapes=[
            pltpu.VMEM(base.shape, jnp.float32),
            pltpu.VMEM((SIDES, columns, width), jnp.float32),
            pltpu.SemaphoreType.DMA((SPECIES, planes // 4)),
        ],
        compiler_params=params(8),
        name="spread",
    )(fades, base, lift, message)


def group_size(devices):
    size = 1
    while 4 * size * size <= 2 * devices and devices % (2 * size) == 0:
        size *= 2
    return size


def body(conc, influx, numbers, cross, kinetics):
    _, planes, columns, _ = conc.shape
    across, along = lax.axis_size("gx"), lax.axis_size("gy")
    group = group_size(across)
    share = columns // group
    rank = jnp.stack([lax.axis_index("gx"), lax.axis_index("gy")]).astype(jnp.int32)
    conc, influx, numbers, cross, kinetics = (
        pltpu.with_memory_space_constraint(x, pltpu.HBM) for x in (conc, influx, numbers, cross, kinetics)
    )
    members = [list(range(i, i + group)) for i in range(0, across, group)]

    def in_group(value):
        return lax.all_to_all(value, "gx", 0, 0, axis_index_groups=members, tiled=True)

    def over_groups(value, by):
        return lax.ppermute(value, "gx", [(i, (i + by * group) % across) for i in range(across)])

    message, table, conc, influx = edges(group, rank, numbers, cross, kinetics, conc, influx)
    message = in_group(message)
    h, b = sweeps(numbers, cross, kinetics, conc, influx)
    whole = group_sums(planes, share, table, b, message)
    wholes = [whole] + [over_groups(whole, j) for j in range(1, across // group)]
    base, sums = bulk(numbers, table, h, b, conc)
    outgoing, sums = entering(planes, share, along, table, sums, message, wholes)
    outgoing = in_group(outgoing)
    sums = lax.all_to_all(sums, "gy", 0, 0, tiled=True)
    base, lift, fades = inflow(table, base, sums)
    return spread(share, fades, base, lift, outgoing)


def solution(mesh):
    placed = (P(None, "gx", "gy", None), P("gx", "gy", None), P(), P(), P())
    return jax.shard_map(
        body, mesh=mesh, in_specs=placed, out_specs=P(None, "gx", "gy", None), check_vma=False
    )
```

```python
import functools

import jax
import jax.numpy as jnp
from jax import lax
from jax.experimental import pallas as pl
from jax.experimental.pallas import tpu as pltpu
from jax.sharding import PartitionSpec as P

SPECIES = 3
ROWS = 8
SIDES = 2
CORNERS = SIDES * SIDES * SPECIES
SMEM = pl.BlockSpec(memory_space=pltpu.SMEM)
VMEM = pl.BlockSpec(memory_space=pltpu.VMEM)
ANY = pl.BlockSpec(memory_space=pl.ANY)

RATE_X, RATE_Y, SCALE_Y, MEMBER, TABLE_ROWS = 0, 3, 6, 9, 16


def padded(rows):
    return -(-rows // ROWS) * ROWS


def params(mebibytes):
    return pltpu.CompilerParams(vmem_limit_bytes=mebibytes * 2**20)


def struct(*shape):
    return jax.ShapeDtypeStruct(shape, jnp.float32)


def decay_rate(number):
    half = 0.5 * lax.rsqrt(number)
    square = half * half
    return 2.0 * jnp.log1p(half + square / (1.0 + jnp.sqrt(1.0 + square)))


def scaling(number):
    return lax.rsqrt(1.0 + 4.0 * number)


def splat(value, shape):
    return jnp.full(shape, value, jnp.float32)


def split(value):
    high = value.astype(jnp.bfloat16)
    return high, (value - high.astype(jnp.float32)).astype(jnp.bfloat16)


def left_pair(value):
    return jnp.concatenate(split(value), axis=1)


def right_pair(value):
    high, low = split(value)
    return jnp.concatenate(
        [jnp.concatenate([high, low], axis=1), jnp.concatenate([high, jnp.zeros_like(low)], axis=1)], axis=0
    )


def product(left, right):
    both = jnp.dot(left, right, preferred_element_type=jnp.float32)
    width = both.shape[1] // 2
    return both[:, :width] + both[:, width:]


def distances(length):
    rows = lax.broadcasted_iota(jnp.int32, (length, length), 0)
    columns = lax.broadcasted_iota(jnp.int32, (length, length), 1)
    return jnp.abs(rows - columns).astype(jnp.float32)


def depth_table(number, length):
    number = splat(number, (1, length))
    theta = decay_rate(number)
    spread = distances(length)
    factor = scaling(number) / (1.0 - jnp.exp(-length * theta))
    return (jnp.exp(-spread * theta) + jnp.exp((spread - length) * theta)) * factor


def column_table(number, length):
    number = splat(number, (1, length))
    return jnp.exp(-distances(length) * decay_rate(number)) * scaling(number)


def row_position(length, width):
    return lax.broadcasted_iota(jnp.int32, (length, width), 0).astype(jnp.float32)


def coefficients(numbers, cross, kinetics, tile):
    n = [[splat(numbers[s, d], tile) for d in range(3)] for s in range(SPECIES)]
    along_x, along_y, along_z = [], [], []
    for s in range(SPECIES):
        per_x, per_y = 1.0 / n[s][0], 1.0 / n[s][1]
        for j in range(SPECIES):
            mix = 1.0 if j == s else cross[s, j]
            along_x.append(n[j][0] * per_x * mix)
            along_y.append(n[j][1] * per_y * mix)
            along_z.append(n[j][2] * mix)
    scale = [scaling(n[s][0]) for s in range(SPECIES)]
    rate = [decay_rate(n[s][0]) for s in range(SPECIES)]
    return along_x, along_y, along_z, scale, rate, [splat(kinetics[i], tile) for i in range(3)]


def turned(value):
    width = value.shape[1]
    return pltpu.roll(value, 1, 1) + pltpu.roll(value, width - 1, 1)


def edge_kernel(
    group, rank, numbers, cross, kinetics, conc_far, influx_far,
    *refs,
):
    sent, (table, conc, influx, weights, v_hold, w_hold, corners, y_table, z_table, arrived) = refs[:group], refs[group:]
    planes, columns, width = influx.shape
    chunks = arrived.shape[1]
    chunk = columns // chunks
    half = planes // 2
    share = columns // group
    tile = (ROWS, width)

    def copies(k):
        part = pl.ds(k * chunk, chunk)
        return (
            pltpu.make_async_copy(conc_far.at[:, :, part, :], conc.at[:, :, part, :], arrived.at[0, k]),
            pltpu.make_async_copy(influx_far.at[:, part, :], influx.at[:, part, :], arrived.at[1, k]),
        )

    for k in range(chunks):
        for copy in copies(k):
            copy.start()

    along_x, along_y, along_z, scale, rate, (bind, unbind, pump) = coefficients(numbers, cross, kinetics, tile)
    inner, double, single = [], [], []
    for s in range(SPECIES):
        for at in range(s * SPECIES, (s + 1) * SPECIES):
            inner.append((along_x[at] + along_y[at] - 2.0 * along_z[at]) * scale[s])
            double.append(along_z[at] * scale[s])
            single.append(along_y[at] * scale[s])
        for i in range(half):
            near = jnp.exp(-i * rate[s])
            far = jnp.exp(-(planes - 1.0 - i) * rate[s])
            weights[s, i, 0] = 0.5 * (near + far)
            weights[s, i, 1] = 0.5 * (near - far)
        table[RATE_X + s : RATE_X + s + 1] = rate[s][:1]
        number = splat(numbers[s, 1], (1, width))
        table[RATE_Y + s : RATE_Y + s + 1] = decay_rate(number)
        table[SCALE_Y + s : SCALE_Y + s + 1] = scaling(number)
        y_table[s] = left_pair(column_table(numbers[s, 1], columns))
        z_table[s] = right_pair(depth_table(numbers[s, 2], width))
    member = lax.rem(rank[0], group)
    table[MEMBER : MEMBER + 1] = splat(member.astype(jnp.float32), (1, width))

    def rows(k, carry):
        here = pl.ds(pl.multiple_of(k * ROWS, ROWS), ROWS)

        def at_plane(i):
            c = [conc[j, i, here, :] for j in range(SPECIES)]
            binding = bind * c[0] * c[1] - unbind * c[2]
            pumping = pump * c[0] / (1.0 + c[0])
            return c, influx[i, here, :] - 4.0 * binding - pumping, binding

        zero = jnp.zeros(tile, jnp.float32)
        plus = [[zero] * (SPECIES + 1) for _ in range(SPECIES)]
        minus = [[zero] * (SPECIES + 1) for _ in range(SPECIES)]
        for i in range(half):
            low, low_first, low_binding = at_plane(i)
            high, high_first, high_binding = at_plane(planes - 1 - i)
            both = [x + y for x, y in zip(low, high)]
            apart = [x - y for x, y in zip(low, high)]
            change = (low_first + high_first, low_binding + high_binding)
            turn = (low_first - high_first, low_binding - high_binding)
            for s in range(SPECIES):
                even, odd = weights[s, i, 0], weights[s, i, 1]
                of = min(s, 1)
                for j, (p, m) in enumerate(zip(both + [change[of]], apart + [turn[of]])):
                    plus[s][j] = plus[s][j] + even * p
                    minus[s][j] = minus[s][j] + odd * m
        for s in range(SPECIES):
            for e in range(SIDES):
                sums = [p + m if e else p - m for p, m in zip(plus[s], minus[s])]
                v = sums[SPECIES] * scale[s]
                if s == 1:
                    v = -v
                w = 0.0
                for j in range(SPECIES):
                    at = s * SPECIES + j
                    v = v + inner[at] * sums[j] + double[at] * turned(sums[j])
                    w = w + single[at] * sums[j]
                v_hold[e, s, here, :] = v
                w_hold[e, s, here, :] = w
        return carry

    for k in range(chunks):
        for copy in copies(k):
            copy.wait()
        lax.fori_loop(k * (chunk // ROWS), (k + 1) * (chunk // ROWS), rows, 0, unroll=True)

    row = row_position(columns, width)
    for s in range(SPECIES):
        theta = table[RATE_Y + s : RATE_Y + s + 1]
        rise = jnp.exp((row - (columns - 1.0)) * theta)
        fall = jnp.exp(-row * theta)
        both = product(y_table[s], right_pair(jnp.concatenate([v_hold[0, s], v_hold[1, s]], axis=1)))
        stack = [both[:, e * width : (e + 1) * width] - w_hold[e, s] for e in range(SIDES)]
        for weight in (rise, fall):
            for e in range(SIDES):
                stack.append(jnp.sum(weight * v_hold[e, s], axis=0, keepdims=True))
        stack.append(jnp.zeros((2 * ROWS - 2 * SIDES, width), jnp.float32))
        done = product(left_pair(jnp.concatenate(stack, axis=0)), z_table[s])
        for e in range(SIDES):
            v_hold[e, s] = done[e * columns : (e + 1) * columns]
        for k in range(SIDES * SIDES):
            at = SIDES * columns + k
            corners[k * SPECIES + s : k * SPECIES + s + 1] = done[at : at + 1]
    for d in range(group):
        start = pl.multiple_of(lax.rem(member + d, group) * share, share)
        for s in range(SPECIES):
            for e in range(SIDES):
                sent[d][pl.ds((e * SPECIES + s) * share, share), :] = v_hold[e, s, pl.ds(start, share), :]
        sent[d][pl.ds(SIDES * SPECIES * share, corners.shape[0]), :] = corners[...]


def edges(group, rank, numbers, cross, kinetics, conc, influx):
    _, planes, columns, width = conc.shape
    chunks = columns // (2 * ROWS)
    hold = pltpu.VMEM((SIDES, SPECIES, columns, width), jnp.float32)
    rows = padded(SIDES * SPECIES * (columns // group) + CORNERS)
    return pl.pallas_call(
        functools.partial(edge_kernel, group),
        in_specs=[SMEM, SMEM, SMEM, SMEM, ANY, ANY],
        out_specs=[VMEM] * (group + 3),
        out_shape=[struct(rows, width)] * group
        + [
            pltpu.VMEM((TABLE_ROWS, width), jnp.float32),
            pltpu.VMEM(conc.shape, jnp.float32),
            pltpu.VMEM(influx.shape, jnp.float32),
        ],
        scratch_shapes=[
            pltpu.VMEM((SPECIES, planes // 2, 2, ROWS, width), jnp.float32),
            hold,
            hold,
            pltpu.VMEM((padded(CORNERS), width), jnp.float32),
            pltpu.VMEM((SPECIES, columns, 2 * columns), jnp.bfloat16),
            pltpu.VMEM((SPECIES, 2 * width, 2 * width), jnp.bfloat16),
            pltpu.SemaphoreType.DMA((2, chunks)),
        ],
        compiler_params=params(16),
        name="edges",
    )(rank, numbers, cross, kinetics, conc, influx)


def sweep_kernel(numbers, cross, kinetics, conc, influx, h_out, b_out, g_hold, b_hold):
    planes, columns, width = influx.shape
    tile = (ROWS, width)
    along_x, along_y, along_z, scale, rate, (bind, unbind, pump) = coefficients(numbers, cross, kinetics, tile)
    inner, double, single = [], [], []
    for s in range(SPECIES):
        for at in range(s * SPECIES, (s + 1) * SPECIES):
            inner.append((along_x[at] + along_y[at] - 2.0 * along_z[at]) * scale[s])
            double.append(along_z[at] * scale[s])
            single.append(along_y[at] * scale[s])
    decay = [jnp.exp(-value) for value in rate]

    def rows(k, carry):
        here = pl.ds(pl.multiple_of(k * ROWS, ROWS), ROWS)
        up_g = [jnp.zeros(tile, jnp.float32) for _ in range(SPECIES)]
        up_b = [jnp.zeros(tile, jnp.float32) for _ in range(SPECIES)]
        for i in range(planes):
            c = [conc[j, i, here, :] for j in range(SPECIES)]
            around = [turned(value) for value in c]
            binding = bind * c[0] * c[1] - unbind * c[2]
            pumping = pump * c[0] / (1.0 + c[0])
            change = (influx[i, here, :] - 4.0 * binding - pumping, -binding, binding)
            for s in range(SPECIES):
                a = b = None
                g = change[s] * scale[s]
                for j in range(SPECIES):
                    at = s * SPECIES + j
                    g = g + inner[at] * c[j] + double[at] * around[j]
                    part_a = c[j] if s == j else along_x[at] * c[j]
                    part_b = single[at] * c[j]
                    a = part_a if a is None else a + part_a
                    b = part_b if b is None else b + part_b
                up_g[s] = g + decay[s] * up_g[s]
                up_b[s] = b + decay[s] * up_b[s]
                g_hold[s, i] = g
                b_hold[s, i] = b
                h_out[s, i, here, :] = up_g[s] - a
                b_out[s, i, here, :] = up_b[s]
        for s in range(SPECIES):
            down_g = jnp.zeros(tile, jnp.float32)
            down_b = jnp.zeros(tile, jnp.float32)
            for i in reversed(range(planes)):
                down_g = decay[s] * down_g
                down_b = decay[s] * down_b
                h_out[s, i, here, :] += down_g
                b_out[s, i, here, :] += down_b
                down_g += g_hold[s, i]
                down_b += b_hold[s, i]
        return carry

    lax.fori_loop(0, columns // ROWS, rows, 0)


def sweeps(numbers, cross, kinetics, conc, influx):
    _, planes, columns, width = conc.shape
    hold = pltpu.VMEM((SPECIES, planes, ROWS, width), jnp.float32)
    return pl.pallas_call(
        sweep_kernel,
        in_specs=[SMEM, SMEM, SMEM, VMEM, VMEM],
        out_specs=[VMEM] * 2,
        out_shape=[pltpu.VMEM(conc.shape, jnp.float32)] * 2,
        scratch_shapes=[hold, hold],
        compiler_params=params(8),
        cost_estimate=pl.CostEstimate(flops=100 * conc.size, bytes_accessed=14 * conc.size, transcendentals=0),
        name="sweeps",
    )(numbers, cross, kinetics, conc, influx)


def block_of(member, d, group):
    block = member - d
    return jnp.where(block < 0.0, block + group, block)


def group_kernel(planes, share, table, after, *refs):
    parts, out = refs[:-1], refs[-1]
    group = len(parts)
    corners = SIDES * SPECIES * share
    member = table[MEMBER : MEMBER + 1]
    blocks = [block_of(member, d, group) for d in range(group)]
    for s in range(SPECIES):
        theta = planes * table[RATE_X + s : RATE_X + s + 1]
        for e in range(SIDES):
            weight = [jnp.exp((-b if e else b - (group - 1.0)) * theta) for b in blocks]
            here = pl.ds((e * SPECIES + s) * share, share)
            out[here, :] = sum(weight[d] * parts[d][here, :] for d in range(group))
            for k in range(SIDES):
                here = pl.ds(corners + (k * SIDES + e) * SPECIES + s, 1)
                out[here, :] = sum(weight[d] * parts[d][here, :] for d in range(group))


def group_sums(planes, share, table, after, parts):
    return pl.pallas_call(
        functools.partial(group_kernel, planes, share),
        in_specs=[VMEM, ANY] + [VMEM] * len(parts),
        out_specs=VMEM,
        out_shape=struct(*parts[0].shape),
        compiler_params=params(8),
        name="group_sums",
    )(table, after, *parts)


def bulk_kernel(numbers, table, h, b, conc, out, y_out, weights, y_table, z_table, sums):
    _, planes, columns, width = h.shape
    row = row_position(columns, width)
    for s in range(SPECIES):
        theta = table[RATE_Y + s : RATE_Y + s + 1]
        weights[0] = jnp.exp((row - (columns - 1.0)) * theta)
        weights[1] = jnp.exp(-row * theta)
        y_table[...] = left_pair(column_table(numbers[s, 1], columns))
        z_table[...] = right_pair(depth_table(numbers[s, 2], width))

        def plane(i, carry):
            value = h[s, i]
            for e in range(SIDES):
                sums[e, pl.ds(i, 1), :] = jnp.sum(weights[e] * value, axis=0, keepdims=True)
            solved = product(y_table[...], right_pair(value)) - b[s, i]
            out[s, i] = conc[s, i] + product(left_pair(solved), z_table[...])
            return carry

        lax.fori_loop(0, planes, plane, 0, unroll=4)
        both = jnp.concatenate([sums[e] for e in range(SIDES)], axis=0)
        both = product(left_pair(both), z_table[...])
        for e in range(SIDES):
            y_out[pl.ds((e * SPECIES + s) * planes, planes), :] = both[e * planes : (e + 1) * planes]


def bulk(numbers, table, h, b, conc):
    _, planes, columns, width = conc.shape
    return pl.pallas_call(
        bulk_kernel,
        in_specs=[SMEM] + [VMEM] * 4,
        out_specs=[VMEM] * 2,
        out_shape=[
            pltpu.VMEM(conc.shape, jnp.float32),
            pltpu.VMEM((SIDES * SPECIES * planes, width), jnp.float32),
        ],
        scratch_shapes=[
            pltpu.VMEM((SIDES, columns, width), jnp.float32),
            pltpu.VMEM((columns, 2 * columns), jnp.bfloat16),
            pltpu.VMEM((2 * width, 2 * width), jnp.bfloat16),
            pltpu.VMEM((SIDES, planes, width), jnp.float32),
        ],
        compiler_params=params(8),
        cost_estimate=pl.CostEstimate(
            flops=6 * conc.size * (columns + width), bytes_accessed=16 * conc.size, transcendentals=0
        ),
        name="bulk",
    )(numbers, table, h, b, conc)


def enter_kernel(group, planes, share, table, sums, *refs):
    parts, wholes, outs, y_out = refs[:group], refs[group : -group - 1], refs[-group - 1 : -1], refs[-1]
    groups = len(wholes)
    corners = SIDES * SPECIES * share
    member = table[MEMBER : MEMBER + 1]
    blocks = [block_of(member, d, group) for d in range(group)]
    targets = [jnp.where(member + d >= group, member + d - group, member + d) for d in range(group)]
    y_out[pl.ds(0, sums.shape[0]), :] = sums[...]

    for s in range(SPECIES):
        theta = planes * table[RATE_X + s : RATE_X + s + 1]
        closing = 1.0 / (1.0 - jnp.exp(-float(group * groups) * theta))
        for e in range(SIDES):
            steps = [(groups - j - 1) if e else (j - 1 if j else groups - 1) for j in range(groups)]
            outside = [jnp.exp(-float(group * k) * theta) * closing for k in steps]
            to_target = [jnp.exp((t - (group - 1.0) if e else -t) * theta) for t in targets]
            inside = []
            for t in targets:
                away = [(b - t) if e else (t - b) for b in blocks]
                inside.append([jnp.where(k > 0.0, jnp.exp((1.0 - jnp.abs(k)) * theta), 0.0) for k in away])

            def entering_group(here):
                return sum(weight * whole[here, :] for weight, whole in zip(outside, wholes))

            here = pl.ds((e * SPECIES + s) * share, share)
            whole = entering_group(here)
            held = [part[here, :] for part in parts]
            for d in range(group):
                total = to_target[d] * whole
                for weight, part in zip(inside[d], held):
                    total = total + weight * part
                outs[d][here, :] = total

            for k in range(SIDES):
                at = (k * SIDES + e) * SPECIES + s
                here = pl.ds(corners + at, 1)
                total = to_target[0] * entering_group(here)
                for weight, part in zip(inside[0], parts):
                    total = total + weight * part[here, :]
                y_out[pl.ds(sums.shape[0] + at, 1), :] = total


def entering(planes, share, table, sums, parts, wholes):
    group, width = len(parts), parts[0].shape[1]
    return pl.pallas_call(
        functools.partial(enter_kernel, group, planes, share),
        in_specs=[VMEM] * (2 + group + len(wholes)),
        out_specs=[VMEM] * (group + 1),
        out_shape=[struct(SIDES * SPECIES * share, width)] * group + [struct(padded(sums.shape[0] + CORNERS), width)],
        compiler_params=params(8),
        name="entering",
    )(table, sums, *parts, *wholes)


def inflow_kernel(table, base, *refs):
    parts, (out, lift, fades, weights) = refs[:-4], refs[-4:]
    _, planes, columns, width = base.shape
    along = len(parts)
    corners = SIDES * SPECIES * planes
    row = row_position(columns, width)
    position = row_position(planes, width)
    for s in range(SPECIES):
        rate_x = table[RATE_X + s : RATE_X + s + 1]
        rate_y = table[RATE_Y + s : RATE_Y + s + 1]
        theta = columns * rate_y
        closing = table[SCALE_Y + s : SCALE_Y + s + 1] / (1.0 - jnp.exp(-float(along) * theta))
        weights[0] = jnp.exp(-(row + 1.0) * rate_y)
        weights[1] = jnp.exp((row - columns) * rate_y)
        fades[pl.ds(s * planes, planes), :] = jnp.exp(-(position + 1.0) * rate_x)
        fades[pl.ds((SPECIES + s) * planes, planes), :] = jnp.exp((position - planes) * rate_x)
        enter, corner = [], []
        for e in range(SIDES):
            steps = [(along - k - 1) if e else (k - 1 if k else along - 1) for k in range(along)]
            arrive = [jnp.exp(-float(k) * theta) * closing for k in steps]

            def entering_block(here):
                return sum(weight * part[here, :] for weight, part in zip(arrive, parts))

            enter.append(entering_block(pl.ds((e * SPECIES + s) * planes, planes)))
            corner.append([entering_block(pl.ds(corners + (e * SIDES + k) * SPECIES + s, 1)) for k in range(SIDES)])
        for k in range(SIDES):
            lift[k, s] = weights[0] * corner[0][k] + weights[1] * corner[1][k]
        for i in range(planes):
            out[s, i] = base[s, i] + weights[0] * enter[0][i : i + 1] + weights[1] * enter[1][i : i + 1]


def inflow(table, base, parts):
    _, planes, columns, width = base.shape
    return pl.pallas_call(
        inflow_kernel,
        in_specs=[VMEM] * (2 + len(parts)),
        out_specs=[VMEM] * 3,
        out_shape=[
            pltpu.VMEM(base.shape, jnp.float32),
            pltpu.VMEM((SIDES, SPECIES, columns, width), jnp.float32),
            pltpu.VMEM((SIDES * SPECIES * planes, width), jnp.float32),
        ],
        scratch_shapes=[pltpu.VMEM((SIDES, columns, width), jnp.float32)],
        compiler_params=params(8),
        name="inflow",
    )(table, base, *parts)


def spread_kernel(group, share, rank, fades, base, lift, *refs):
    parts, (out_far, out, hold, left) = refs[:group], refs[group:]
    _, planes, columns, width = base.shape
    member = lax.rem(rank[0], group)
    at_once = planes // left.shape[1]
    copies = []
    for s in range(SPECIES):
        for e in range(SIDES):
            for d in range(group):
                there = pl.ds(pl.multiple_of(lax.rem(member - d + group, group) * share, share), share)
                hold[e, there, :] = lift[e, s, there, :] + parts[d][pl.ds((e * SPECIES + s) * share, share), :]
        for i in range(planes):
            rise = fades[s * planes + i : s * planes + i + 1]
            fall = fades[(SPECIES + s) * planes + i : (SPECIES + s) * planes + i + 1]
            out[s, i] = base[s, i] + rise * hold[0] + fall * hold[1]
            if i % at_once == at_once - 1:
                k = i // at_once
                part = pl.ds(k * at_once, at_once)
                copies.append(pltpu.make_async_copy(out.at[s, part], out_far.at[s, part], left.at[s, k]))
                copies[-1].start()
    for copy in copies:
        copy.wait()


def spread(share, rank, fades, base, lift, parts):
    _, planes, columns, width = base.shape
    return pl.pallas_call(
        functools.partial(spread_kernel, len(parts), share),
        in_specs=[SMEM] + [VMEM] * (3 + len(parts)),
        out_specs=ANY,
        out_shape=struct(*base.shape),
        scratch_shapes=[
            pltpu.VMEM(base.shape, jnp.float32),
            pltpu.VMEM((SIDES, columns, width), jnp.float32),
            pltpu.SemaphoreType.DMA((SPECIES, planes // 4)),
        ],
        compiler_params=params(8),
        name="spread",
    )(rank, fades, base, lift, *parts)


def group_size(devices):
    size = 1
    while 4 * size * size <= 2 * devices and devices % (2 * size) == 0:
        size *= 2
    return size


def body(conc, influx, numbers, cross, kinetics):
    _, planes, columns, _ = conc.shape
    across, along = lax.axis_size("gx"), lax.axis_size("gy")
    group = group_size(across)
    share = columns // group
    rank = lax.axis_index("gx").astype(jnp.int32).reshape(1)
    conc, influx, numbers, cross, kinetics = (
        pltpu.with_memory_space_constraint(x, pltpu.HBM) for x in (conc, influx, numbers, cross, kinetics)
    )

    def turn(value, by):
        return lax.ppermute(value, "gy", [(i, (i + by) % along) for i in range(along)])

    def in_group(parts):
        turns = [[(i, i - i % group + (i + d) % group) for i in range(across)] for d in range(group)]
        return [parts[0]] + [lax.ppermute(parts[d], "gx", turns[d]) for d in range(1, group)]

    def over_groups(value, by):
        return lax.ppermute(value, "gx", [(i, (i + by * group) % across) for i in range(across)])

    *parts, table, conc, influx = edges(group, rank, numbers, cross, kinetics, conc, influx)
    parts = in_group(parts)
    h, b = sweeps(numbers, cross, kinetics, conc, influx)
    whole = group_sums(planes, share, table, b, parts)
    wholes = [whole] + [over_groups(whole, j) for j in range(1, across // group)]
    base, sums = bulk(numbers, table, h, b, conc)
    *outs, sums = entering(planes, share, table, sums, parts, wholes)
    outs = in_group(outs)
    base, lift, fades = inflow(table, base, [sums] + [turn(sums, k) for k in range(1, along)])
    return spread(share, rank, fades, base, lift, outs)


def solution(mesh):
    placed = (P(None, "gx", "gy", None), P("gx", "gy", None), P(), P(), P())
    return jax.shard_map(
        body, mesh=mesh, in_specs=placed, out_specs=P(None, "gx", "gy", None), check_vma=False
    )
```

```python
import functools

import jax
import jax.numpy as jnp
from jax import lax
from jax.experimental import pallas as pl
from jax.experimental.pallas import tpu as pltpu
from jax.sharding import PartitionSpec as P

SPECIES = 3
ROWS = 8
SIDES = 2
CORNERS = SIDES * SIDES * SPECIES
SMEM = pl.BlockSpec(memory_space=pltpu.SMEM)
VMEM = pl.BlockSpec(memory_space=pltpu.VMEM)
ANY = pl.BlockSpec(memory_space=pl.ANY)

RATE_X, RATE_Y, SCALE_Y, MEMBER, TABLE_ROWS = 0, 3, 6, 9, 16


def padded(rows):
    return -(-rows // ROWS) * ROWS


def params(mebibytes):
    return pltpu.CompilerParams(vmem_limit_bytes=mebibytes * 2**20)


def struct(*shape):
    return jax.ShapeDtypeStruct(shape, jnp.float32)


def decay_rate(number):
    half = 0.5 * lax.rsqrt(number)
    square = half * half
    return 2.0 * jnp.log1p(half + square / (1.0 + jnp.sqrt(1.0 + square)))


def scaling(number):
    return lax.rsqrt(1.0 + 4.0 * number)


def splat(value, shape):
    return jnp.full(shape, value, jnp.float32)


def split(value):
    high = value.astype(jnp.bfloat16)
    return high, (value - high.astype(jnp.float32)).astype(jnp.bfloat16)


def left_pair(value):
    return jnp.concatenate(split(value), axis=1)


def right_pair(value):
    high, low = split(value)
    return jnp.concatenate(
        [jnp.concatenate([high, low], axis=1), jnp.concatenate([high, jnp.zeros_like(low)], axis=1)], axis=0
    )


def product(left, right):
    both = jnp.dot(left, right, preferred_element_type=jnp.float32)
    width = both.shape[1] // 2
    return both[:, :width] + both[:, width:]


def distances(length):
    rows = lax.broadcasted_iota(jnp.int32, (length, length), 0)
    columns = lax.broadcasted_iota(jnp.int32, (length, length), 1)
    return jnp.abs(rows - columns).astype(jnp.float32)


def depth_table(number, length):
    number = splat(number, (1, length))
    theta = decay_rate(number)
    spread = distances(length)
    factor = scaling(number) / (1.0 - jnp.exp(-length * theta))
    return (jnp.exp(-spread * theta) + jnp.exp((spread - length) * theta)) * factor


def column_table(number, length):
    number = splat(number, (1, length))
    return jnp.exp(-distances(length) * decay_rate(number)) * scaling(number)


def row_position(length, width):
    return lax.broadcasted_iota(jnp.int32, (length, width), 0).astype(jnp.float32)


def coefficients(numbers, cross, kinetics, tile):
    n = [[splat(numbers[s, d], tile) for d in range(3)] for s in range(SPECIES)]
    along_x, along_y, along_z = [], [], []
    for s in range(SPECIES):
        per_x, per_y = 1.0 / n[s][0], 1.0 / n[s][1]
        for j in range(SPECIES):
            mix = 1.0 if j == s else cross[s, j]
            along_x.append(n[j][0] * per_x * mix)
            along_y.append(n[j][1] * per_y * mix)
            along_z.append(n[j][2] * mix)
    scale = [scaling(n[s][0]) for s in range(SPECIES)]
    rate = [decay_rate(n[s][0]) for s in range(SPECIES)]
    return along_x, along_y, along_z, scale, rate, [splat(kinetics[i], tile) for i in range(3)]


def turned(value):
    width = value.shape[1]
    return pltpu.roll(value, 1, 1) + pltpu.roll(value, width - 1, 1)


def edge_kernel(
    group, rank, numbers, cross, kinetics, conc_far, influx_far,
    *refs,
):
    sent, (table, conc, influx, weights, v_hold, w_hold, corners, y_table, z_table, arrived) = refs[:group], refs[group:]
    planes, columns, width = influx.shape
    chunks = arrived.shape[1]
    chunk = columns // chunks
    half = planes // 2
    share = columns // group
    tile = (ROWS, width)

    def copies(k):
        part = pl.ds(k * chunk, chunk)
        return (
            pltpu.make_async_copy(conc_far.at[:, :, part, :], conc.at[:, :, part, :], arrived.at[0, k]),
            pltpu.make_async_copy(influx_far.at[:, part, :], influx.at[:, part, :], arrived.at[1, k]),
        )

    for k in range(chunks):
        for copy in copies(k):
            copy.start()

    along_x, along_y, along_z, scale, rate, (bind, unbind, pump) = coefficients(numbers, cross, kinetics, tile)
    inner, double, single = [], [], []
    for s in range(SPECIES):
        for at in range(s * SPECIES, (s + 1) * SPECIES):
            inner.append((along_x[at] + along_y[at] - 2.0 * along_z[at]) * scale[s])
            double.append(along_z[at] * scale[s])
            single.append(along_y[at] * scale[s])
        for i in range(half):
            near = jnp.exp(-i * rate[s])
            far = jnp.exp(-(planes - 1.0 - i) * rate[s])
            weights[s, i, 0] = 0.5 * (near + far)
            weights[s, i, 1] = 0.5 * (near - far)
        table[RATE_X + s : RATE_X + s + 1] = rate[s][:1]
        number = splat(numbers[s, 1], (1, width))
        table[RATE_Y + s : RATE_Y + s + 1] = decay_rate(number)
        table[SCALE_Y + s : SCALE_Y + s + 1] = scaling(number)
        y_table[s] = left_pair(column_table(numbers[s, 1], columns))
        z_table[s] = right_pair(depth_table(numbers[s, 2], width))
    member = lax.rem(rank[0], group)
    table[MEMBER : MEMBER + 1] = splat(member.astype(jnp.float32), (1, width))

    def rows(k, carry):
        here = pl.ds(pl.multiple_of(k * ROWS, ROWS), ROWS)

        def at_plane(i):
            c = [conc[j, i, here, :] for j in range(SPECIES)]
            binding = bind * c[0] * c[1] - unbind * c[2]
            pumping = pump * c[0] / (1.0 + c[0])
            return c, influx[i, here, :] - 4.0 * binding - pumping, binding

        zero = jnp.zeros(tile, jnp.float32)
        plus = [[zero] * (SPECIES + 1) for _ in range(SPECIES)]
        minus = [[zero] * (SPECIES + 1) for _ in range(SPECIES)]
        for i in range(half):
            low, low_first, low_binding = at_plane(i)
            high, high_first, high_binding = at_plane(planes - 1 - i)
            both = [x + y for x, y in zip(low, high)]
            apart = [x - y for x, y in zip(low, high)]
            change = (low_first + high_first, low_binding + high_binding)
            turn = (low_first - high_first, low_binding - high_binding)
            for s in range(SPECIES):
                even, odd = weights[s, i, 0], weights[s, i, 1]
                of = min(s, 1)
                for j, (p, m) in enumerate(zip(both + [change[of]], apart + [turn[of]])):
                    plus[s][j] = plus[s][j] + even * p
                    minus[s][j] = minus[s][j] + odd * m
        for s in range(SPECIES):
            for e in range(SIDES):
                sums = [p + m if e else p - m for p, m in zip(plus[s], minus[s])]
                v = sums[SPECIES] * scale[s]
                if s == 1:
                    v = -v
                w = 0.0
                for j in range(SPECIES):
                    at = s * SPECIES + j
                    v = v + inner[at] * sums[j] + double[at] * turned(sums[j])
                    w = w + single[at] * sums[j]
                v_hold[e, s, here, :] = v
                w_hold[e, s, here, :] = w
        return carry

    for k in range(chunks):
        for copy in copies(k):
            copy.wait()
        lax.fori_loop(k * (chunk // ROWS), (k + 1) * (chunk // ROWS), rows, 0, unroll=True)

    row = row_position(columns, width)
    for s in range(SPECIES):
        theta = table[RATE_Y + s : RATE_Y + s + 1]
        rise = jnp.exp((row - (columns - 1.0)) * theta)
        fall = jnp.exp(-row * theta)
        both = product(y_table[s], right_pair(jnp.concatenate([v_hold[0, s], v_hold[1, s]], axis=1)))
        stack = [both[:, e * width : (e + 1) * width] - w_hold[e, s] for e in range(SIDES)]
        for weight in (rise, fall):
            for e in range(SIDES):
                stack.append(jnp.sum(weight * v_hold[e, s], axis=0, keepdims=True))
        stack.append(jnp.zeros((2 * ROWS - 2 * SIDES, width), jnp.float32))
        done = product(left_pair(jnp.concatenate(stack, axis=0)), z_table[s])
        for e in range(SIDES):
            v_hold[e, s] = done[e * columns : (e + 1) * columns]
        for k in range(SIDES * SIDES):
            at = SIDES * columns + k
            corners[k * SPECIES + s : k * SPECIES + s + 1] = done[at : at + 1]
    for d in range(group):
        start = pl.multiple_of(lax.rem(member + d, group) * share, share)
        for s in range(SPECIES):
            for e in range(SIDES):
                sent[d][pl.ds((e * SPECIES + s) * share, share), :] = v_hold[e, s, pl.ds(start, share), :]
        sent[d][pl.ds(SIDES * SPECIES * share, corners.shape[0]), :] = corners[...]


def edges(group, rank, numbers, cross, kinetics, conc, influx):
    _, planes, columns, width = conc.shape
    chunks = columns // (2 * ROWS)
    hold = pltpu.VMEM((SIDES, SPECIES, columns, width), jnp.float32)
    rows = padded(SIDES * SPECIES * (columns // group) + CORNERS)
    return pl.pallas_call(
        functools.partial(edge_kernel, group),
        in_specs=[SMEM, SMEM, SMEM, SMEM, ANY, ANY],
        out_specs=[VMEM] * (group + 3),
        out_shape=[struct(rows, width)] * group
        + [
            pltpu.VMEM((TABLE_ROWS, width), jnp.float32),
            pltpu.VMEM(conc.shape, jnp.float32),
            pltpu.VMEM(influx.shape, jnp.float32),
        ],
        scratch_shapes=[
            pltpu.VMEM((SPECIES, planes // 2, 2, ROWS, width), jnp.float32),
            hold,
            hold,
            pltpu.VMEM((padded(CORNERS), width), jnp.float32),
            pltpu.VMEM((SPECIES, columns, 2 * columns), jnp.bfloat16),
            pltpu.VMEM((SPECIES, 2 * width, 2 * width), jnp.bfloat16),
            pltpu.SemaphoreType.DMA((2, chunks)),
        ],
        compiler_params=params(16),
        name="edges",
    )(rank, numbers, cross, kinetics, conc, influx)


def sweep_kernel(numbers, cross, kinetics, conc, influx, h_out, g_hold):
    planes, columns, width = influx.shape
    tile = (ROWS, width)
    along_x, along_y, along_z, scale, rate, (bind, unbind, pump) = coefficients(numbers, cross, kinetics, tile)
    inner, double = [], []
    for s in range(SPECIES):
        for at in range(s * SPECIES, (s + 1) * SPECIES):
            inner.append((along_x[at] + along_y[at] - 2.0 * along_z[at]) * scale[s])
            double.append(along_z[at] * scale[s])
    decay = [jnp.exp(-value) for value in rate]

    def rows(k, carry):
        here = pl.ds(pl.multiple_of(k * ROWS, ROWS), ROWS)
        up = [jnp.zeros(tile, jnp.float32) for _ in range(SPECIES)]
        for i in range(planes):
            c = [conc[j, i, here, :] for j in range(SPECIES)]
            around = [turned(value) for value in c]
            binding = bind * c[0] * c[1] - unbind * c[2]
            pumping = pump * c[0] / (1.0 + c[0])
            change = (influx[i, here, :] - 4.0 * binding - pumping, -binding, binding)
            for s in range(SPECIES):
                g = change[s] * scale[s]
                a = c[s]
                for j in range(SPECIES):
                    at = s * SPECIES + j
                    g = g + inner[at] * c[j] + double[at] * around[j]
                    if j != s:
                        a = a + along_x[at] * c[j]
                up[s] = g + decay[s] * up[s]
                g_hold[s, i] = g
                h_out[s, i, here, :] = up[s] - a
        for s in range(SPECIES):
            down = jnp.zeros(tile, jnp.float32)
            for i in reversed(range(planes)):
                down = decay[s] * down
                h_out[s, i, here, :] += down
                down += g_hold[s, i]
        return carry

    lax.fori_loop(0, columns // ROWS, rows, 0)


def sweeps(numbers, cross, kinetics, conc, influx):
    _, planes, columns, width = conc.shape
    return pl.pallas_call(
        sweep_kernel,
        in_specs=[SMEM, SMEM, SMEM, VMEM, VMEM],
        out_specs=VMEM,
        out_shape=pltpu.VMEM(conc.shape, jnp.float32),
        scratch_shapes=[pltpu.VMEM((SPECIES, planes, ROWS, width), jnp.float32)],
        compiler_params=params(8),
        cost_estimate=pl.CostEstimate(flops=100 * conc.size, bytes_accessed=14 * conc.size, transcendentals=0),
        name="sweeps",
    )(numbers, cross, kinetics, conc, influx)


def block_of(member, d, group):
    block = member - d
    return jnp.where(block < 0.0, block + group, block)


def group_kernel(planes, share, table, after, *refs):
    parts, out = refs[:-1], refs[-1]
    group = len(parts)
    corners = SIDES * SPECIES * share
    member = table[MEMBER : MEMBER + 1]
    blocks = [block_of(member, d, group) for d in range(group)]
    for s in range(SPECIES):
        theta = planes * table[RATE_X + s : RATE_X + s + 1]
        for e in range(SIDES):
            weight = [jnp.exp((-b if e else b - (group - 1.0)) * theta) for b in blocks]
            here = pl.ds((e * SPECIES + s) * share, share)
            out[here, :] = sum(weight[d] * parts[d][here, :] for d in range(group))
            for k in range(SIDES):
                here = pl.ds(corners + (k * SIDES + e) * SPECIES + s, 1)
                out[here, :] = sum(weight[d] * parts[d][here, :] for d in range(group))


def group_sums(planes, share, table, after, parts):
    return pl.pallas_call(
        functools.partial(group_kernel, planes, share),
        in_specs=[VMEM, ANY] + [VMEM] * len(parts),
        out_specs=VMEM,
        out_shape=struct(*parts[0].shape),
        compiler_params=params(8),
        name="group_sums",
    )(table, after, *parts)


def column_kernel(numbers, table, h, out, y_out, weights, y_table, z_table, sums):
    _, planes, columns, width = h.shape
    row = row_position(columns, width)
    for s in range(SPECIES):
        theta = table[RATE_Y + s : RATE_Y + s + 1]
        weights[0] = jnp.exp((row - (columns - 1.0)) * theta)
        weights[1] = jnp.exp(-row * theta)
        y_table[...] = left_pair(column_table(numbers[s, 1], columns))
        z_table[...] = right_pair(depth_table(numbers[s, 2], width))

        def plane(i, carry):
            value = h[s, i]
            for e in range(SIDES):
                sums[e, pl.ds(i, 1), :] = jnp.sum(weights[e] * value, axis=0, keepdims=True)
            out[s, i] = product(y_table[...], right_pair(value))
            return carry

        lax.fori_loop(0, planes, plane, 0, unroll=4)
        both = jnp.concatenate([sums[e] for e in range(SIDES)], axis=0)
        both = product(left_pair(both), z_table[...])
        for e in range(SIDES):
            y_out[pl.ds((e * SPECIES + s) * planes, planes), :] = both[e * planes : (e + 1) * planes]


def column_parts(numbers, table, h):
    _, planes, columns, width = h.shape
    return pl.pallas_call(
        column_kernel,
        in_specs=[SMEM] + [VMEM] * 2,
        out_specs=[VMEM] * 2,
        out_shape=[
            pltpu.VMEM(h.shape, jnp.float32),
            pltpu.VMEM((SIDES * SPECIES * planes, width), jnp.float32),
        ],
        scratch_shapes=[
            pltpu.VMEM((SIDES, columns, width), jnp.float32),
            pltpu.VMEM((columns, 2 * columns), jnp.bfloat16),
            pltpu.VMEM((2 * width, 2 * width), jnp.bfloat16),
            pltpu.VMEM((SIDES, planes, width), jnp.float32),
        ],
        compiler_params=params(8),
        cost_estimate=pl.CostEstimate(flops=6 * h.size * columns, bytes_accessed=8 * h.size, transcendentals=0),
        name="column_parts",
    )(numbers, table, h)


def finish_kernel(numbers, cross, table, conc, solved, out, b_hold, z_table):
    _, planes, columns, width = conc.shape
    tile = (ROWS, width)
    weight, decay = [], []
    for s in range(SPECIES):
        number = splat(numbers[s, 1], tile)
        scale = scaling(splat(numbers[s, 0], tile))
        decay.append(jnp.exp(-table[RATE_X + s : RATE_X + s + 1]) + jnp.zeros(tile, jnp.float32))
        for j in range(SPECIES):
            mix = scale if j == s else scale * cross[s, j]
            weight.append(splat(numbers[j, 1], tile) / number * mix)

    def rows(k, carry):
        here = pl.ds(pl.multiple_of(k * ROWS, ROWS), ROWS)
        up = [jnp.zeros(tile, jnp.float32) for _ in range(SPECIES)]
        for i in range(planes):
            c = [conc[j, i, here, :] for j in range(SPECIES)]
            for s in range(SPECIES):
                at = s * SPECIES
                b = weight[at] * c[0] + weight[at + 1] * c[1] + weight[at + 2] * c[2]
                up[s] = b + decay[s] * up[s]
                b_hold[s, i] = b
                out[s, i, here, :] = solved[s, i, here, :] - up[s]
        for s in range(SPECIES):
            down = jnp.zeros(tile, jnp.float32)
            for i in reversed(range(planes)):
                down = decay[s] * down
                out[s, i, here, :] -= down
                down += b_hold[s, i]
        return carry

    lax.fori_loop(0, columns // ROWS, rows, 0)
    for s in range(SPECIES):
        z_table[...] = right_pair(depth_table(numbers[s, 2], width))

        def plane(i, carry):
            out[s, i] = conc[s, i] + product(left_pair(out[s, i]), z_table[...])
            return carry

        lax.fori_loop(0, planes, plane, 0, unroll=4)


def finish(numbers, cross, table, conc, solved):
    _, planes, columns, width = conc.shape
    return pl.pallas_call(
        finish_kernel,
        in_specs=[SMEM, SMEM] + [VMEM] * 3,
        out_specs=VMEM,
        out_shape=pltpu.VMEM(conc.shape, jnp.float32),
        scratch_shapes=[
            pltpu.VMEM((SPECIES, planes, ROWS, width), jnp.float32),
            pltpu.VMEM((2 * width, 2 * width), jnp.bfloat16),
        ],
        compiler_params=params(8),
        cost_estimate=pl.CostEstimate(flops=6 * conc.size * width, bytes_accessed=12 * conc.size, transcendentals=0),
        name="finish",
    )(numbers, cross, table, conc, solved)


def enter_kernel(group, planes, share, table, sums, *refs):
    parts, wholes, outs, y_out = refs[:group], refs[group : -group - 1], refs[-group - 1 : -1], refs[-1]
    groups = len(wholes)
    corners = SIDES * SPECIES * share
    member = table[MEMBER : MEMBER + 1]
    blocks = [block_of(member, d, group) for d in range(group)]
    targets = [jnp.where(member + d >= group, member + d - group, member + d) for d in range(group)]
    y_out[pl.ds(0, sums.shape[0]), :] = sums[...]

    for s in range(SPECIES):
        theta = planes * table[RATE_X + s : RATE_X + s + 1]
        closing = 1.0 / (1.0 - jnp.exp(-float(group * groups) * theta))
        for e in range(SIDES):
            steps = [(groups - j - 1) if e else (j - 1 if j else groups - 1) for j in range(groups)]
            outside = [jnp.exp(-float(group * k) * theta) * closing for k in steps]
            to_target = [jnp.exp((t - (group - 1.0) if e else -t) * theta) for t in targets]
            inside = []
            for t in targets:
                away = [(b - t) if e else (t - b) for b in blocks]
                inside.append([jnp.where(k > 0.0, jnp.exp((1.0 - jnp.abs(k)) * theta), 0.0) for k in away])

            def entering_group(here):
                return sum(weight * whole[here, :] for weight, whole in zip(outside, wholes))

            here = pl.ds((e * SPECIES + s) * share, share)
            whole = entering_group(here)
            held = [part[here, :] for part in parts]
            for d in range(group):
                total = to_target[d] * whole
                for weight, part in zip(inside[d], held):
                    total = total + weight * part
                outs[d][here, :] = total

            for k in range(SIDES):
                at = (k * SIDES + e) * SPECIES + s
                here = pl.ds(corners + at, 1)
                total = to_target[0] * entering_group(here)
                for weight, part in zip(inside[0], parts):
                    total = total + weight * part[here, :]
                y_out[pl.ds(sums.shape[0] + at, 1), :] = total


def entering(planes, share, table, sums, parts, wholes):
    group, width = len(parts), parts[0].shape[1]
    return pl.pallas_call(
        functools.partial(enter_kernel, group, planes, share),
        in_specs=[VMEM] * (2 + group + len(wholes)),
        out_specs=[VMEM] * (group + 1),
        out_shape=[struct(SIDES * SPECIES * share, width)] * group + [struct(padded(sums.shape[0] + CORNERS), width)],
        compiler_params=params(8),
        name="entering",
    )(table, sums, *parts, *wholes)


def inflow_kernel(table, base, *refs):
    parts, (out, lift, fades, weights) = refs[:-4], refs[-4:]
    _, planes, columns, width = base.shape
    along = len(parts)
    corners = SIDES * SPECIES * planes
    row = row_position(columns, width)
    position = row_position(planes, width)
    for s in range(SPECIES):
        rate_x = table[RATE_X + s : RATE_X + s + 1]
        rate_y = table[RATE_Y + s : RATE_Y + s + 1]
        theta = columns * rate_y
        closing = table[SCALE_Y + s : SCALE_Y + s + 1] / (1.0 - jnp.exp(-float(along) * theta))
        weights[0] = jnp.exp(-(row + 1.0) * rate_y)
        weights[1] = jnp.exp((row - columns) * rate_y)
        fades[pl.ds(s * planes, planes), :] = jnp.exp(-(position + 1.0) * rate_x)
        fades[pl.ds((SPECIES + s) * planes, planes), :] = jnp.exp((position - planes) * rate_x)
        enter, corner = [], []
        for e in range(SIDES):
            steps = [(along - k - 1) if e else (k - 1 if k else along - 1) for k in range(along)]
            arrive = [jnp.exp(-float(k) * theta) * closing for k in steps]

            def entering_block(here):
                return sum(weight * part[here, :] for weight, part in zip(arrive, parts))

            enter.append(entering_block(pl.ds((e * SPECIES + s) * planes, planes)))
            corner.append([entering_block(pl.ds(corners + (e * SIDES + k) * SPECIES + s, 1)) for k in range(SIDES)])
        for k in range(SIDES):
            lift[k, s] = weights[0] * corner[0][k] + weights[1] * corner[1][k]
        for i in range(planes):
            out[s, i] = base[s, i] + weights[0] * enter[0][i : i + 1] + weights[1] * enter[1][i : i + 1]


def inflow(table, base, parts):
    _, planes, columns, width = base.shape
    return pl.pallas_call(
        inflow_kernel,
        in_specs=[VMEM] * (2 + len(parts)),
        out_specs=[VMEM] * 3,
        out_shape=[
            pltpu.VMEM(base.shape, jnp.float32),
            pltpu.VMEM((SIDES, SPECIES, columns, width), jnp.float32),
            pltpu.VMEM((SIDES * SPECIES * planes, width), jnp.float32),
        ],
        scratch_shapes=[pltpu.VMEM((SIDES, columns, width), jnp.float32)],
        compiler_params=params(8),
        name="inflow",
    )(table, base, *parts)


def spread_kernel(group, share, rank, fades, base, lift, *refs):
    parts, (out_far, out, hold, left) = refs[:group], refs[group:]
    _, planes, columns, width = base.shape
    member = lax.rem(rank[0], group)
    at_once = planes // left.shape[1]
    copies = []
    for s in range(SPECIES):
        for e in range(SIDES):
            for d in range(group):
                there = pl.ds(pl.multiple_of(lax.rem(member - d + group, group) * share, share), share)
                hold[e, there, :] = lift[e, s, there, :] + parts[d][pl.ds((e * SPECIES + s) * share, share), :]
        for i in range(planes):
            rise = fades[s * planes + i : s * planes + i + 1]
            fall = fades[(SPECIES + s) * planes + i : (SPECIES + s) * planes + i + 1]
            out[s, i] = base[s, i] + rise * hold[0] + fall * hold[1]
            if i % at_once == at_once - 1:
                k = i // at_once
                part = pl.ds(k * at_once, at_once)
                copies.append(pltpu.make_async_copy(out.at[s, part], out_far.at[s, part], left.at[s, k]))
                copies[-1].start()
    for copy in copies:
        copy.wait()


def spread(share, rank, fades, base, lift, parts):
    _, planes, columns, width = base.shape
    return pl.pallas_call(
        functools.partial(spread_kernel, len(parts), share),
        in_specs=[SMEM] + [VMEM] * (3 + len(parts)),
        out_specs=ANY,
        out_shape=struct(*base.shape),
        scratch_shapes=[
            pltpu.VMEM(base.shape, jnp.float32),
            pltpu.VMEM((SIDES, columns, width), jnp.float32),
            pltpu.SemaphoreType.DMA((SPECIES, planes // 4)),
        ],
        compiler_params=params(8),
        name="spread",
    )(rank, fades, base, lift, *parts)


def group_size(devices):
    size = 1
    while 4 * size * size <= 2 * devices and devices % (2 * size) == 0:
        size *= 2
    return size


def body(conc, influx, numbers, cross, kinetics):
    _, planes, columns, _ = conc.shape
    across, along = lax.axis_size("gx"), lax.axis_size("gy")
    group = group_size(across)
    share = columns // group
    rank = lax.axis_index("gx").astype(jnp.int32).reshape(1)
    conc, influx, numbers, cross, kinetics = (
        pltpu.with_memory_space_constraint(x, pltpu.HBM) for x in (conc, influx, numbers, cross, kinetics)
    )

    def turn(value, by):
        return lax.ppermute(value, "gy", [(i, (i + by) % along) for i in range(along)])

    def in_group(parts):
        turns = [[(i, i - i % group + (i + d) % group) for i in range(across)] for d in range(group)]
        return [parts[0]] + [lax.ppermute(parts[d], "gx", turns[d]) for d in range(1, group)]

    def over_groups(value, by):
        return lax.ppermute(value, "gx", [(i, (i + by * group) % across) for i in range(across)])

    *parts, table, conc, influx = edges(group, rank, numbers, cross, kinetics, conc, influx)
    parts = in_group(parts)
    h = sweeps(numbers, cross, kinetics, conc, influx)
    whole = group_sums(planes, share, table, h, parts)
    wholes = [whole] + [over_groups(whole, j) for j in range(1, across // group)]
    solved, sums = column_parts(numbers, table, h)
    *outs, sums = entering(planes, share, table, sums, parts, wholes)
    outs = in_group(outs)
    base = finish(numbers, cross, table, conc, solved)
    base, lift, fades = inflow(table, base, [sums] + [turn(sums, k) for k in range(1, along)])
    return spread(share, rank, fades, base, lift, outs)


def solution(mesh):
    placed = (P(None, "gx", "gy", None), P("gx", "gy", None), P(), P(), P())
    return jax.shard_map(
        body, mesh=mesh, in_specs=placed, out_specs=P(None, "gx", "gy", None), check_vma=False
    )
```

```python
import functools

import jax
import jax.numpy as jnp
from jax import lax
from jax.experimental import pallas as pl
from jax.experimental.pallas import tpu as pltpu
from jax.sharding import PartitionSpec as P

SPECIES = 3
ROWS = 8
SIDES = 2
CORNERS = SIDES * SIDES * SPECIES
SMEM = pl.BlockSpec(memory_space=pltpu.SMEM)
VMEM = pl.BlockSpec(memory_space=pltpu.VMEM)
ANY = pl.BlockSpec(memory_space=pl.ANY)

RATE_X, RATE_Y, SCALE_Y, SCALE_X, DECAY, KINETICS, MEMBER = 0, 3, 6, 9, 12, 15, 18
INNER, DOUBLE, PART_A, PART_B, TABLE_ROWS = 19, 28, 37, 46, 56


def padded(rows):
    return -(-rows // ROWS) * ROWS


def params(mebibytes):
    return pltpu.CompilerParams(vmem_limit_bytes=mebibytes * 2**20)


def struct(*shape):
    return jax.ShapeDtypeStruct(shape, jnp.float32)


def decay_rate(number):
    half = 0.5 * lax.rsqrt(number)
    square = half * half
    return 2.0 * jnp.log1p(half + square / (1.0 + jnp.sqrt(1.0 + square)))


def scaling(number):
    return lax.rsqrt(1.0 + 4.0 * number)


def splat(value, shape):
    return jnp.full(shape, value, jnp.float32)


def split(value):
    high = value.astype(jnp.bfloat16)
    return high, (value - high.astype(jnp.float32)).astype(jnp.bfloat16)


def left_pair(value):
    return jnp.concatenate(split(value), axis=1)


def right_pair(value):
    high, low = split(value)
    return jnp.concatenate(
        [jnp.concatenate([high, low], axis=1), jnp.concatenate([high, jnp.zeros_like(low)], axis=1)], axis=0
    )


def product(left, right):
    both = jnp.dot(left, right, preferred_element_type=jnp.float32)
    width = both.shape[1] // 2
    return both[:, :width] + both[:, width:]


def distances(length):
    rows = lax.broadcasted_iota(jnp.int32, (length, length), 0)
    columns = lax.broadcasted_iota(jnp.int32, (length, length), 1)
    return jnp.abs(rows - columns).astype(jnp.float32)


def depth_table(number, length):
    number = splat(number, (1, length))
    theta = decay_rate(number)
    spread = distances(length)
    factor = scaling(number) / (1.0 - jnp.exp(-length * theta))
    return (jnp.exp(-spread * theta) + jnp.exp((spread - length) * theta)) * factor


def column_table(number, length):
    number = splat(number, (1, length))
    return jnp.exp(-distances(length) * decay_rate(number)) * scaling(number)


def row_position(length, width):
    return lax.broadcasted_iota(jnp.int32, (length, width), 0).astype(jnp.float32)


def coefficients(numbers, cross, kinetics, tile):
    n = [[splat(numbers[s, d], tile) for d in range(3)] for s in range(SPECIES)]
    along_x, along_y, along_z = [], [], []
    for s in range(SPECIES):
        per_x, per_y = 1.0 / n[s][0], 1.0 / n[s][1]
        for j in range(SPECIES):
            mix = 1.0 if j == s else cross[s, j]
            along_x.append(n[j][0] * per_x * mix)
            along_y.append(n[j][1] * per_y * mix)
            along_z.append(n[j][2] * mix)
    scale = [scaling(n[s][0]) for s in range(SPECIES)]
    rate = [decay_rate(n[s][0]) for s in range(SPECIES)]
    return along_x, along_y, along_z, scale, rate, [splat(kinetics[i], tile) for i in range(3)]


def turned(value):
    width = value.shape[1]
    return pltpu.roll(value, 1, 1) + pltpu.roll(value, width - 1, 1)


def tiles(table, first, count, tile):
    return [jnp.broadcast_to(table[at : at + 1], tile) for at in range(first, first + count)]


def rates(c, influx, kinetics):
    bind, unbind, pump = kinetics
    binding = bind * c[0] * c[1] - unbind * c[2]
    pumping = pump * c[0] / (1.0 + c[0])
    return influx - 4.0 * binding - pumping, binding


def side_by_side(counts, steps):
    common = min(counts)

    def together(k, carry):
        for step in steps:
            step(k)
        return carry

    lax.fori_loop(0, common, together, 0, unroll=2 if common % 2 == 0 else 1)
    for count, step in zip(counts, steps):
        if count > common:
            lax.fori_loop(common, count, lambda k, carry, step=step: (step(k), carry)[1], 0)


def edge_kernel(group, rank, numbers, cross, kinetics, conc_far, influx_far, *refs):
    sent, refs = refs[:group], refs[group:]
    table, conc, influx, y_table, z_table, weights, hold, deep, solved, corners, arrived = refs
    planes, columns, width = influx.shape
    chunks = arrived.shape[1]
    chunk = columns // chunks
    half = planes // 2
    share = columns // group
    tile = (ROWS, width)

    def copies(k):
        part = pl.ds(k * chunk, chunk)
        return (
            pltpu.make_async_copy(conc_far.at[:, :, part, :], conc.at[:, :, part, :], arrived.at[0, k]),
            pltpu.make_async_copy(influx_far.at[:, part, :], influx.at[:, part, :], arrived.at[1, k]),
        )

    for k in range(chunks):
        for copy in copies(k):
            copy.start()

    along_x, along_y, along_z, scale, rate, kinetic = coefficients(numbers, cross, kinetics, tile)
    inner, double, single = [], [], []
    for s in range(SPECIES):
        for at in range(s * SPECIES, (s + 1) * SPECIES):
            inner.append((along_x[at] + along_y[at] - 2.0 * along_z[at]) * scale[s])
            double.append(along_z[at] * scale[s])
            single.append(along_y[at] * scale[s])
        for i in range(half):
            near = jnp.exp(-i * rate[s])
            far = jnp.exp(-(planes - 1.0 - i) * rate[s])
            weights[s, i, 0] = 0.5 * (near + far)
            weights[s, i, 1] = 0.5 * (near - far)
        number = splat(numbers[s, 1], tile)
        table[RATE_Y + s : RATE_Y + s + 1] = decay_rate(number)[:1]
        table[SCALE_Y + s : SCALE_Y + s + 1] = scaling(number)[:1]
        y_table[s] = left_pair(column_table(numbers[s, 1], columns))
        z_table[s] = right_pair(depth_table(numbers[s, 2], width))
    member = lax.rem(rank[0], group)
    entries = (
        (RATE_X, rate),
        (SCALE_X, scale),
        (DECAY, [jnp.exp(-value) for value in rate]),
        (KINETICS, kinetic),
        (MEMBER, [splat(member.astype(jnp.float32), tile)]),
        (INNER, inner),
        (DOUBLE, double),
        (PART_A, along_x),
        (PART_B, single),
    )
    for first, values in entries:
        for k, value in enumerate(values):
            table[first + k : first + k + 1] = value[:1]

    def sums_of(start):
        here = slice(start, start + ROWS)

        def at_plane(i):
            c = [conc[j, i, here, :] for j in range(SPECIES)]
            return c, *rates(c, influx[i, here, :], kinetic)

        zero = jnp.zeros(tile, jnp.float32)
        plus = [[zero] * (SPECIES + 1) for _ in range(SPECIES)]
        minus = [[zero] * (SPECIES + 1) for _ in range(SPECIES)]
        for i in range(half):
            low, low_first, low_binding = at_plane(i)
            high, high_first, high_binding = at_plane(planes - 1 - i)
            both = [x + y for x, y in zip(low, high)]
            apart = [x - y for x, y in zip(low, high)]
            change = (low_first + high_first, low_binding + high_binding)
            turn = (low_first - high_first, low_binding - high_binding)
            for s in range(SPECIES):
                even, odd = weights[s, i, 0], weights[s, i, 1]
                of = min(s, 1)
                for j, (p, m) in enumerate(zip(both + [change[of]], apart + [turn[of]])):
                    plus[s][j] = plus[s][j] + even * p
                    minus[s][j] = minus[s][j] + odd * m
        for s in range(SPECIES):
            for e in range(SIDES):
                sums = [p + m if e else p - m for p, m in zip(plus[s], minus[s])]
                v = sums[SPECIES] * scale[s]
                if s == 1:
                    v = -v
                w = 0.0
                for j in range(SPECIES):
                    at = s * SPECIES + j
                    v = v + inner[at] * sums[j] + double[at] * turned(sums[j])
                    w = w + single[at] * sums[j]
                hold[s, e, here, :] = v
                hold[s, SIDES + e, here, :] = w

    def deepen(k):
        here = slice(k * chunk, (k + 1) * chunk)
        for s in range(SPECIES):
            stack = jnp.concatenate([hold[s, e, here, :] for e in range(2 * SIDES)], axis=0)
            done = product(left_pair(stack), z_table[s])
            for e in range(2 * SIDES):
                deep[s, e, here, :] = done[e * chunk : (e + 1) * chunk]

    for k in range(chunks):
        for copy in copies(k):
            copy.wait()
        if k:
            deepen(k - 1)
        for start in range(k * chunk, (k + 1) * chunk, ROWS):
            sums_of(start)
    deepen(chunks - 1)

    row = row_position(columns, width)
    for s in range(SPECIES):
        theta = table[RATE_Y + s : RATE_Y + s + 1]
        rise = jnp.exp((row - (columns - 1.0)) * theta)
        fall = jnp.exp(-row * theta)
        both = product(y_table[s], right_pair(jnp.concatenate([deep[s, e] for e in range(SIDES)], axis=1)))
        for e in range(SIDES):
            solved[e, s] = both[:, e * width : (e + 1) * width] - deep[s, SIDES + e]
            for f, weight in enumerate((rise, fall)):
                at = (f * SIDES + e) * SPECIES + s
                corners[at : at + 1] = jnp.sum(weight * deep[s, e], axis=0, keepdims=True)
    for d in range(group):
        start = pl.multiple_of(lax.rem(member + d, group) * share, share)
        for s in range(SPECIES):
            for e in range(SIDES):
                sent[d][pl.ds((e * SPECIES + s) * share, share), :] = solved[e, s, pl.ds(start, share), :]
        sent[d][pl.ds(SIDES * SPECIES * share, corners.shape[0]), :] = corners[...]


def edges(group, rank, numbers, cross, kinetics, conc, influx):
    _, planes, columns, width = conc.shape
    chunks = columns // (2 * ROWS)
    hold = pltpu.VMEM((SPECIES, 2 * SIDES, columns, width), jnp.float32)
    rows = SIDES * SPECIES * (columns // group) + padded(CORNERS)
    return pl.pallas_call(
        functools.partial(edge_kernel, group),
        in_specs=[SMEM, SMEM, SMEM, SMEM, ANY, ANY],
        out_specs=[VMEM] * (group + 5),
        out_shape=[struct(rows, width)] * group
        + [
            pltpu.VMEM((TABLE_ROWS, width), jnp.float32),
            pltpu.VMEM(conc.shape, jnp.float32),
            pltpu.VMEM(influx.shape, jnp.float32),
            pltpu.VMEM((SPECIES, columns, 2 * columns), jnp.bfloat16),
            pltpu.VMEM((SPECIES, 2 * width, 2 * width), jnp.bfloat16),
        ],
        scratch_shapes=[
            pltpu.VMEM((SPECIES, planes // 2, 2, ROWS, width), jnp.float32),
            hold,
            hold,
            pltpu.VMEM((SIDES, SPECIES, columns, width), jnp.float32),
            pltpu.VMEM((padded(CORNERS), width), jnp.float32),
            pltpu.SemaphoreType.DMA((2, chunks)),
        ],
        compiler_params=params(16),
        name="edges",
    )(rank, numbers, cross, kinetics, conc, influx)


def sweep_kernel(table, conc, influx, *refs):
    outs, g_hold = refs[:-1], refs[-1]
    planes, columns, width = influx.shape
    tile = (ROWS, width)
    count = len(outs)
    inner = tiles(table, INNER, count * SPECIES, tile)
    double = tiles(table, DOUBLE, count * SPECIES, tile)
    part_a = tiles(table, PART_A, count * SPECIES, tile)
    scale = tiles(table, SCALE_X, count, tile)
    decay = tiles(table, DECAY, count, tile)
    kinetic = tiles(table, KINETICS, 3, tile)

    def rows(k, carry):
        here = pl.ds(pl.multiple_of(k * ROWS, ROWS), ROWS)
        up = [jnp.zeros(tile, jnp.float32) for _ in range(count)]
        for i in range(planes):
            c = [conc[j, i, here, :] for j in range(SPECIES)]
            around = [turned(value) for value in c]
            first, binding = rates(c, influx[i, here, :], kinetic)
            change = (first, -binding, binding)
            for s in range(count):
                g = change[s] * scale[s]
                a = c[s]
                for j in range(SPECIES):
                    at = s * SPECIES + j
                    g = g + inner[at] * c[j] + double[at] * around[j]
                    if j != s:
                        a = a + part_a[at] * c[j]
                up[s] = g + decay[s] * up[s]
                g_hold[s, i] = g
                outs[s][i, here, :] = up[s] - a
        for s in range(count):
            down = jnp.zeros(tile, jnp.float32)
            for i in reversed(range(planes)):
                down = decay[s] * down
                outs[s][i, here, :] += down
                down += g_hold[s, i]
        return carry

    lax.fori_loop(0, columns // ROWS, rows, 0)


def sweeps(count, table, conc, influx):
    _, planes, columns, width = conc.shape
    return pl.pallas_call(
        sweep_kernel,
        in_specs=[VMEM] * 3,
        out_specs=[VMEM] * count,
        out_shape=[pltpu.VMEM(influx.shape, jnp.float32)] * count,
        scratch_shapes=[pltpu.VMEM((count, planes, ROWS, width), jnp.float32)],
        compiler_params=params(8),
        cost_estimate=pl.CostEstimate(flops=100 * conc.size, bytes_accessed=14 * conc.size, transcendentals=0),
        name="sweeps",
    )(table, conc, influx)


def block_of(member, d, group):
    block = member - d
    return jnp.where(block < 0.0, block + group, block)


def group_kernel(planes, share, table, after, *refs):
    parts, out = refs[:-1], refs[-1]
    group = len(parts)
    corners = SIDES * SPECIES * share
    member = table[MEMBER : MEMBER + 1]
    blocks = [block_of(member, d, group) for d in range(group)]
    for s in range(SPECIES):
        theta = planes * table[RATE_X + s : RATE_X + s + 1]
        for e in range(SIDES):
            weight = [jnp.exp((-b if e else b - (group - 1.0)) * theta) for b in blocks]
            here = pl.ds((e * SPECIES + s) * share, share)
            out[here, :] = sum(weight[d] * parts[d][here, :] for d in range(group))
            for k in range(SIDES):
                here = pl.ds(corners + (k * SIDES + e) * SPECIES + s, 1)
                out[here, :] = sum(weight[d] * parts[d][here, :] for d in range(group))


def group_sums(planes, share, table, after, parts):
    return pl.pallas_call(
        functools.partial(group_kernel, planes, share),
        in_specs=[VMEM, ANY] + [VMEM] * len(parts),
        out_specs=VMEM,
        out_shape=struct(*parts[0].shape),
        compiler_params=params(8),
        name="group_sums",
    )(table, after, *parts)


def column_kernel(table, y_table, z_table, conc, influx, *refs):
    count = SPECIES - 1
    h, u, (last, y_out, weights, sums) = refs[:count], refs[count : 2 * count], refs[2 * count :]
    planes, columns, width = influx.shape
    tile = (ROWS, width)
    row = row_position(columns, width)
    for s in range(SPECIES):
        theta = table[RATE_Y + s : RATE_Y + s + 1]
        weights[s, 0] = jnp.exp((row - (columns - 1.0)) * theta)
        weights[s, 1] = jnp.exp(-row * theta)
    inner = tiles(table, INNER + count * SPECIES, SPECIES, tile)
    double = tiles(table, DOUBLE + count * SPECIES, SPECIES, tile)
    part_a = tiles(table, PART_A + count * SPECIES, SPECIES, tile)
    (scale,) = tiles(table, SCALE_X + count, 1, tile)
    (decay,) = tiles(table, DECAY + count, 1, tile)
    bind, unbind, _ = tiles(table, KINETICS, 3, tile)

    def add_up(s, i, value):
        for e in range(SIDES):
            sums[s, e, pl.ds(i, 1), :] = jnp.sum(weights[s, e] * value, axis=0, keepdims=True)

    def plane(i):
        for s in range(count):
            value = h[s][i]
            add_up(s, i, value)
            u[s][i] = product(y_table[s], right_pair(value))

    def rows(k):
        here = pl.ds(pl.multiple_of(k * ROWS, ROWS), ROWS)
        up, sources, rising = 0.0, [], []
        for i in range(planes):
            c = [conc[j, i, here, :] for j in range(SPECIES)]
            g = (bind * c[0] * c[1] - unbind * c[2]) * scale
            a = c[count]
            for j in range(SPECIES):
                g = g + inner[j] * c[j] + double[j] * turned(c[j])
                if j != count:
                    a = a + part_a[j] * c[j]
            up = g + decay * up
            sources.append(g)
            rising.append(up - a)
        down = jnp.zeros(tile, jnp.float32)
        for i in reversed(range(planes)):
            down = decay * down
            last[i, here, :] = rising[i] + down
            down = down + sources[i]

    side_by_side((planes, columns // ROWS), (plane, rows))
    side_by_side((planes,), (lambda i: add_up(count, i, last[i]),))
    for s in range(SPECIES):
        both = jnp.concatenate([sums[s, e] for e in range(SIDES)], axis=0)
        both = product(left_pair(both), z_table[s])
        for e in range(SIDES):
            y_out[pl.ds((e * SPECIES + s) * planes, planes), :] = both[e * planes : (e + 1) * planes]


def column_parts(table, y_table, z_table, conc, influx, h):
    planes, columns, width = influx.shape
    return pl.pallas_call(
        column_kernel,
        in_specs=[VMEM] * (5 + len(h)),
        out_specs=[VMEM] * (len(h) + 2),
        out_shape=[pltpu.VMEM(influx.shape, jnp.float32)] * (len(h) + 1)
        + [pltpu.VMEM((SIDES * SPECIES * planes, width), jnp.float32)],
        scratch_shapes=[
            pltpu.VMEM((SPECIES, SIDES, columns, width), jnp.float32),
            pltpu.VMEM((SPECIES, SIDES, planes, width), jnp.float32),
        ],
        compiler_params=params(8),
        cost_estimate=pl.CostEstimate(flops=6 * conc.size * columns, bytes_accessed=8 * conc.size, transcendentals=0),
        name="column_parts",
    )(table, y_table, z_table, conc, influx, *h)


def finish_kernel(table, y_table, z_table, conc, last, *refs):
    count = SPECIES - 1
    u, (out, rough, solved) = refs[:count], refs[count:]
    _, planes, columns, width = conc.shape
    tile = (ROWS, width)
    weight = tiles(table, PART_B, SPECIES * SPECIES, tile)
    decay = tiles(table, DECAY, SPECIES, tile)

    def plane(i):
        solved[i] = product(y_table[count], right_pair(last[i]))

    def rows(k):
        here = pl.ds(pl.multiple_of(k * ROWS, ROWS), ROWS)
        for s in range(SPECIES):
            up, sources, rising = 0.0, [], []
            for i in range(planes):
                b = sum(weight[s * SPECIES + j] * conc[j, i, here, :] for j in range(SPECIES))
                up = b + decay[s] * up
                sources.append(b)
                rising.append(up)
            down = jnp.zeros(tile, jnp.float32)
            for i in reversed(range(planes)):
                down = decay[s] * down
                rough[s, i, here, :] = rising[i] + down
                down = down + sources[i]

    def deepen(i):
        for s in range(SPECIES):
            value = (u[s][i] if s < count else solved[i]) - rough[s, i]
            out[s, i] = conc[s, i] + product(left_pair(value), z_table[s])

    side_by_side((planes, columns // ROWS), (plane, rows))
    side_by_side((planes,), (deepen,))


def finish(table, y_table, z_table, conc, last, u):
    _, planes, columns, width = conc.shape
    return pl.pallas_call(
        finish_kernel,
        in_specs=[VMEM] * (5 + len(u)),
        out_specs=VMEM,
        out_shape=pltpu.VMEM(conc.shape, jnp.float32),
        scratch_shapes=[pltpu.VMEM(conc.shape, jnp.float32), pltpu.VMEM(last.shape, jnp.float32)],
        compiler_params=params(8),
        cost_estimate=pl.CostEstimate(flops=6 * conc.size * width, bytes_accessed=12 * conc.size, transcendentals=0),
        name="finish",
    )(table, y_table, z_table, conc, last, *u)


def enter_kernel(group, planes, share, table, sums, *refs):
    parts, wholes, outs, y_out = refs[:group], refs[group : -group - 1], refs[-group - 1 : -1], refs[-1]
    groups = len(wholes)
    corners = SIDES * SPECIES * share
    member = table[MEMBER : MEMBER + 1]
    blocks = [block_of(member, d, group) for d in range(group)]
    targets = [jnp.where(member + d >= group, member + d - group, member + d) for d in range(group)]
    y_out[pl.ds(0, sums.shape[0]), :] = sums[...]

    for s in range(SPECIES):
        theta = planes * table[RATE_X + s : RATE_X + s + 1]
        closing = 1.0 / (1.0 - jnp.exp(-float(group * groups) * theta))
        for e in range(SIDES):
            steps = [(groups - j - 1) if e else (j - 1 if j else groups - 1) for j in range(groups)]
            outside = [jnp.exp(-float(group * k) * theta) * closing for k in steps]
            to_target = [jnp.exp((t - (group - 1.0) if e else -t) * theta) for t in targets]
            inside = []
            for t in targets:
                away = [(b - t) if e else (t - b) for b in blocks]
                inside.append([jnp.where(k > 0.0, jnp.exp((1.0 - jnp.abs(k)) * theta), 0.0) for k in away])

            def entering_group(here):
                return sum(weight * whole[here, :] for weight, whole in zip(outside, wholes))

            here = pl.ds((e * SPECIES + s) * share, share)
            whole = entering_group(here)
            held = [part[here, :] for part in parts]
            for d in range(group):
                total = to_target[d] * whole
                for weight, part in zip(inside[d], held):
                    total = total + weight * part
                outs[d][here, :] = total

            for k in range(SIDES):
                at = (k * SIDES + e) * SPECIES + s
                here = pl.ds(corners + at, 1)
                total = to_target[0] * entering_group(here)
                for weight, part in zip(inside[0], parts):
                    total = total + weight * part[here, :]
                y_out[pl.ds(sums.shape[0] + at, 1), :] = total


def entering(planes, share, table, sums, parts, wholes):
    group, width = len(parts), parts[0].shape[1]
    return pl.pallas_call(
        functools.partial(enter_kernel, group, planes, share),
        in_specs=[VMEM] * (2 + group + len(wholes)),
        out_specs=[VMEM] * (group + 1),
        out_shape=[struct(SIDES * SPECIES * share, width)] * group + [struct(padded(sums.shape[0] + CORNERS), width)],
        compiler_params=params(8),
        name="entering",
    )(table, sums, *parts, *wholes)


def inflow_kernel(table, base, *refs):
    parts, (out, lift, fades, weights) = refs[:-4], refs[-4:]
    _, planes, columns, width = base.shape
    along = len(parts)
    corners = SIDES * SPECIES * planes
    row = row_position(columns, width)
    position = row_position(planes, width)
    for s in range(SPECIES):
        rate_x = table[RATE_X + s : RATE_X + s + 1]
        rate_y = table[RATE_Y + s : RATE_Y + s + 1]
        theta = columns * rate_y
        closing = table[SCALE_Y + s : SCALE_Y + s + 1] / (1.0 - jnp.exp(-float(along) * theta))
        weights[0] = jnp.exp(-(row + 1.0) * rate_y)
        weights[1] = jnp.exp((row - columns) * rate_y)
        fades[pl.ds(s * planes, planes), :] = jnp.exp(-(position + 1.0) * rate_x)
        fades[pl.ds((SPECIES + s) * planes, planes), :] = jnp.exp((position - planes) * rate_x)
        enter, corner = [], []
        for e in range(SIDES):
            steps = [(along - k - 1) if e else (k - 1 if k else along - 1) for k in range(along)]
            arrive = [jnp.exp(-float(k) * theta) * closing for k in steps]

            def entering_block(here):
                return sum(weight * part[here, :] for weight, part in zip(arrive, parts))

            enter.append(entering_block(pl.ds((e * SPECIES + s) * planes, planes)))
            corner.append([entering_block(pl.ds(corners + (e * SIDES + k) * SPECIES + s, 1)) for k in range(SIDES)])
        for k in range(SIDES):
            lift[k, s] = weights[0] * corner[0][k] + weights[1] * corner[1][k]
        for i in range(planes):
            out[s, i] = base[s, i] + weights[0] * enter[0][i : i + 1] + weights[1] * enter[1][i : i + 1]


def inflow(table, base, parts):
    _, planes, columns, width = base.shape
    return pl.pallas_call(
        inflow_kernel,
        in_specs=[VMEM] * (2 + len(parts)),
        out_specs=[VMEM] * 3,
        out_shape=[
            pltpu.VMEM(base.shape, jnp.float32),
            pltpu.VMEM((SIDES, SPECIES, columns, width), jnp.float32),
            pltpu.VMEM((SIDES * SPECIES * planes, width), jnp.float32),
        ],
        scratch_shapes=[pltpu.VMEM((SIDES, columns, width), jnp.float32)],
        compiler_params=params(8),
        name="inflow",
    )(table, base, *parts)


def spread_kernel(group, share, table, fades, base, lift, *refs):
    parts, (out_far, out, hold, left) = refs[:group], refs[group:]
    _, planes, columns, width = base.shape
    blocks = [block_of(table[MEMBER : MEMBER + 1], d, group) for d in range(group)]
    at_once = planes // left.shape[1]
    copies = []
    for s in range(SPECIES):
        for e in range(SIDES):
            held = [part[pl.ds((e * SPECIES + s) * share, share), :] for part in parts]
            for b in range(group):
                there = pl.ds(b * share, share)
                mine = held[0]
                for d in range(1, group):
                    mine = jnp.where(blocks[d] == b, held[d], mine)
                hold[e, there, :] = lift[e, s, there, :] + mine
        for i in range(planes):
            rise = fades[s * planes + i : s * planes + i + 1]
            fall = fades[(SPECIES + s) * planes + i : (SPECIES + s) * planes + i + 1]
            out[s, i] = base[s, i] + rise * hold[0] + fall * hold[1]
            if i % at_once == at_once - 1:
                k = i // at_once
                part = pl.ds(k * at_once, at_once)
                copies.append(pltpu.make_async_copy(out.at[s, part], out_far.at[s, part], left.at[s, k]))
                copies[-1].start()
    for copy in copies:
        copy.wait()


def spread(share, table, fades, base, lift, parts):
    _, planes, columns, width = base.shape
    return pl.pallas_call(
        functools.partial(spread_kernel, len(parts), share),
        in_specs=[VMEM] * (4 + len(parts)),
        out_specs=ANY,
        out_shape=struct(*base.shape),
        scratch_shapes=[
            pltpu.VMEM(base.shape, jnp.float32),
            pltpu.VMEM((SIDES, columns, width), jnp.float32),
            pltpu.SemaphoreType.DMA((SPECIES, planes // 4)),
        ],
        compiler_params=params(8),
        name="spread",
    )(table, fades, base, lift, *parts)


def group_size(devices):
    size = 1
    while 4 * size * size <= 2 * devices and devices % (2 * size) == 0:
        size *= 2
    return size


def body(conc, influx, numbers, cross, kinetics):
    _, planes, columns, _ = conc.shape
    across, along = lax.axis_size("gx"), lax.axis_size("gy")
    group = group_size(across)
    share = columns // group
    rank = lax.axis_index("gx").astype(jnp.int32).reshape(1)
    conc, influx, numbers, cross, kinetics = (
        pltpu.with_memory_space_constraint(x, pltpu.HBM) for x in (conc, influx, numbers, cross, kinetics)
    )

    def turn(value, by):
        return lax.ppermute(value, "gy", [(i, (i + by) % along) for i in range(along)])

    def in_group(parts):
        turns = [[(i, i - i % group + (i + d) % group) for i in range(across)] for d in range(group)]
        return [parts[0]] + [lax.ppermute(parts[d], "gx", turns[d]) for d in range(1, group)]

    def over_groups(value, by):
        return lax.ppermute(value, "gx", [(i, (i + by * group) % across) for i in range(across)])

    *parts, table, conc, influx, y_table, z_table = edges(group, rank, numbers, cross, kinetics, conc, influx)
    parts = in_group(parts)
    h = sweeps(SPECIES - 1, table, conc, influx)
    whole = group_sums(planes, share, table, h[0], parts)
    wholes = [whole] + [over_groups(whole, j) for j in range(1, across // group)]
    *u, last, sums = column_parts(table, y_table, z_table, conc, influx, h)
    *outs, sums = entering(planes, share, table, sums, parts, wholes)
    outs = in_group(outs)
    base = finish(table, y_table, z_table, conc, last, u)
    base, lift, fades = inflow(table, base, [sums] + [turn(sums, k) for k in range(1, along)])
    return spread(share, table, fades, base, lift, outs)


def solution(mesh):
    placed = (P(None, "gx", "gy", None), P("gx", "gy", None), P(), P(), P())
    return jax.shard_map(
        body, mesh=mesh, in_specs=placed, out_specs=P(None, "gx", "gy", None), check_vma=False
    )
```

```python
import functools

import jax
import jax.numpy as jnp
from jax import lax
from jax.experimental import pallas as pl
from jax.experimental.pallas import tpu as pltpu
from jax.sharding import PartitionSpec as P

SPECIES = 3
ROWS = 8
SIDES = 2
CORNERS = SIDES * SIDES * SPECIES
SMEM = pl.BlockSpec(memory_space=pltpu.SMEM)
VMEM = pl.BlockSpec(memory_space=pltpu.VMEM)
ANY = pl.BlockSpec(memory_space=pl.ANY)

RATE_X, RATE_Y, SCALE_Y, SCALE_X, DECAY, KINETICS, MEMBER = 0, 3, 6, 9, 12, 15, 18
INNER, DOUBLE, PART_A, PART_B, TABLE_ROWS = 19, 28, 37, 46, 56


def padded(rows):
    return -(-rows // ROWS) * ROWS


def params(mebibytes):
    return pltpu.CompilerParams(vmem_limit_bytes=mebibytes * 2**20)


def struct(*shape):
    return jax.ShapeDtypeStruct(shape, jnp.float32)


def decay_rate(number):
    half = 0.5 * lax.rsqrt(number)
    square = half * half
    return 2.0 * jnp.log1p(half + square / (1.0 + jnp.sqrt(1.0 + square)))


def scaling(number):
    return lax.rsqrt(1.0 + 4.0 * number)


def splat(value, shape):
    return jnp.full(shape, value, jnp.float32)


def split(value):
    high = value.astype(jnp.bfloat16)
    return high, (value - high.astype(jnp.float32)).astype(jnp.bfloat16)


def left_pair(value):
    return jnp.concatenate(split(value), axis=1)


def right_pair(value):
    high, low = split(value)
    return jnp.concatenate(
        [jnp.concatenate([high, low], axis=1), jnp.concatenate([high, jnp.zeros_like(low)], axis=1)], axis=0
    )


def product(left, right):
    both = jnp.dot(left, right, preferred_element_type=jnp.float32)
    width = both.shape[1] // 2
    return both[:, :width] + both[:, width:]


def distances(length):
    rows = lax.broadcasted_iota(jnp.int32, (length, length), 0)
    columns = lax.broadcasted_iota(jnp.int32, (length, length), 1)
    return jnp.abs(rows - columns).astype(jnp.float32)


def depth_table(number, length):
    number = splat(number, (1, length))
    theta = decay_rate(number)
    spread = distances(length)
    factor = scaling(number) / (1.0 - jnp.exp(-length * theta))
    return (jnp.exp(-spread * theta) + jnp.exp((spread - length) * theta)) * factor


def column_table(number, length):
    number = splat(number, (1, length))
    return jnp.exp(-distances(length) * decay_rate(number)) * scaling(number)


def row_position(length, width):
    return lax.broadcasted_iota(jnp.int32, (length, width), 0).astype(jnp.float32)


def coefficients(numbers, cross, kinetics, tile):
    n = [[splat(numbers[s, d], tile) for d in range(3)] for s in range(SPECIES)]
    along_x, along_y, along_z = [], [], []
    for s in range(SPECIES):
        per_x, per_y = 1.0 / n[s][0], 1.0 / n[s][1]
        for j in range(SPECIES):
            mix = 1.0 if j == s else cross[s, j]
            along_x.append(n[j][0] * per_x * mix)
            along_y.append(n[j][1] * per_y * mix)
            along_z.append(n[j][2] * mix)
    scale = [scaling(n[s][0]) for s in range(SPECIES)]
    rate = [decay_rate(n[s][0]) for s in range(SPECIES)]
    return along_x, along_y, along_z, scale, rate, [splat(kinetics[i], tile) for i in range(3)]


def turned(value):
    width = value.shape[1]
    return pltpu.roll(value, 1, 1) + pltpu.roll(value, width - 1, 1)


def tiles(table, first, count, tile):
    return [jnp.broadcast_to(table[at : at + 1], tile) for at in range(first, first + count)]


def rates(c, influx, kinetics):
    bind, unbind, pump = kinetics
    binding = bind * c[0] * c[1] - unbind * c[2]
    pumping = pump * c[0] / (1.0 + c[0])
    return influx - 4.0 * binding - pumping, binding


def side_by_side(counts, steps):
    common = min(counts)

    def together(k, carry):
        for step in steps:
            step(k)
        return carry

    lax.fori_loop(0, common, together, 0, unroll=2 if common % 2 == 0 else 1)
    for count, step in zip(counts, steps):
        if count > common:
            lax.fori_loop(common, count, lambda k, carry, step=step: (step(k), carry)[1], 0)


def sweep_of_b(s, table, conc, out, k):
    _, planes, _, width = conc.shape
    tile = (ROWS, width)
    here = pl.ds(pl.multiple_of(k * ROWS, ROWS), ROWS)
    weight = tiles(table, PART_B + s * SPECIES, SPECIES, tile)
    (decay,) = tiles(table, DECAY + s, 1, tile)
    up, sources, rising = jnp.zeros(tile, jnp.float32), [], []
    for i in range(planes):
        b = weight[0] * conc[0, i, here, :] + weight[1] * conc[1, i, here, :] + weight[2] * conc[2, i, here, :]
        up = b + decay * up
        sources.append(b)
        rising.append(up)
    down = jnp.zeros(tile, jnp.float32)
    for i in reversed(range(planes)):
        down = decay * down
        out[i, here, :] = rising[i] + down
        down = down + sources[i]


def edge_kernel(group, rank_far, numbers_far, cross_far, kinetics_far, conc_far, influx_far, *refs):
    sent, refs = refs[:group], refs[group:]
    table, conc, influx, y_table, z_table, weights, hold, deep, solved, corners, arrived = refs[:11]
    rank, numbers, cross, kinetics, small = refs[11:]
    planes, columns, width = influx.shape
    chunks = arrived.shape[1]
    chunk = columns // chunks
    half = planes // 2
    share = columns // group
    tile = (ROWS, width)

    def copies(k):
        part = pl.ds(k * chunk, chunk)
        return (
            pltpu.make_async_copy(conc_far.at[:, :, part, :], conc.at[:, :, part, :], arrived.at[0, k]),
            pltpu.make_async_copy(influx_far.at[:, part, :], influx.at[:, part, :], arrived.at[1, k]),
        )

    for k in range(chunks):
        for copy in copies(k):
            copy.start()
    fars = (rank_far, numbers_far, cross_far, kinetics_far)
    nears = (rank, numbers, cross, kinetics)
    scalars = [pltpu.make_async_copy(far, near, small.at[k]) for k, (far, near) in enumerate(zip(fars, nears))]
    for copy in scalars:
        copy.start()
    for copy in scalars:
        copy.wait()

    along_x, along_y, along_z, scale, rate, kinetic = coefficients(numbers, cross, kinetics, tile)
    inner, double, single = [], [], []
    for s in range(SPECIES):
        for at in range(s * SPECIES, (s + 1) * SPECIES):
            inner.append((along_x[at] + along_y[at] - 2.0 * along_z[at]) * scale[s])
            double.append(along_z[at] * scale[s])
            single.append(along_y[at] * scale[s])
        for i in range(half):
            near = jnp.exp(-i * rate[s])
            far = jnp.exp(-(planes - 1.0 - i) * rate[s])
            weights[s, i, 0] = 0.5 * (near + far)
            weights[s, i, 1] = 0.5 * (near - far)
        number = splat(numbers[s, 1], tile)
        table[RATE_Y + s : RATE_Y + s + 1] = decay_rate(number)[:1]
        table[SCALE_Y + s : SCALE_Y + s + 1] = scaling(number)[:1]
        y_table[s] = left_pair(column_table(numbers[s, 1], columns))
        z_table[s] = right_pair(depth_table(numbers[s, 2], width))
    member = lax.rem(rank[0], group)
    entries = (
        (RATE_X, rate),
        (SCALE_X, scale),
        (DECAY, [jnp.exp(-value) for value in rate]),
        (KINETICS, kinetic),
        (MEMBER, [splat(member.astype(jnp.float32), tile)]),
        (INNER, inner),
        (DOUBLE, double),
        (PART_A, along_x),
        (PART_B, single),
    )
    for first, values in entries:
        for k, value in enumerate(values):
            table[first + k : first + k + 1] = value[:1]

    def sums_of(start):
        here = slice(start, start + ROWS)

        def at_plane(i):
            c = [conc[j, i, here, :] for j in range(SPECIES)]
            return c, *rates(c, influx[i, here, :], kinetic)

        zero = jnp.zeros(tile, jnp.float32)
        plus = [[zero] * (SPECIES + 1) for _ in range(SPECIES)]
        minus = [[zero] * (SPECIES + 1) for _ in range(SPECIES)]
        for i in range(half):
            low, low_first, low_binding = at_plane(i)
            high, high_first, high_binding = at_plane(planes - 1 - i)
            both = [x + y for x, y in zip(low, high)]
            apart = [x - y for x, y in zip(low, high)]
            change = (low_first + high_first, low_binding + high_binding)
            turn = (low_first - high_first, low_binding - high_binding)
            for s in range(SPECIES):
                even, odd = weights[s, i, 0], weights[s, i, 1]
                of = min(s, 1)
                for j, (p, m) in enumerate(zip(both + [change[of]], apart + [turn[of]])):
                    plus[s][j] = plus[s][j] + even * p
                    minus[s][j] = minus[s][j] + odd * m
        for s in range(SPECIES):
            for e in range(SIDES):
                sums = [p + m if e else p - m for p, m in zip(plus[s], minus[s])]
                v = sums[SPECIES] * scale[s]
                if s == 1:
                    v = -v
                w = 0.0
                for j in range(SPECIES):
                    at = s * SPECIES + j
                    v = v + inner[at] * sums[j] + double[at] * turned(sums[j])
                    w = w + single[at] * sums[j]
                hold[s, e, here, :] = v
                hold[s, SIDES + e, here, :] = w

    def deepen(k):
        here = slice(k * chunk, (k + 1) * chunk)
        for s in range(SPECIES):
            stack = jnp.concatenate([hold[s, e, here, :] for e in range(2 * SIDES)], axis=0)
            done = product(left_pair(stack), z_table[s])
            for e in range(2 * SIDES):
                deep[s, e, here, :] = done[e * chunk : (e + 1) * chunk]

    for k in range(chunks):
        for copy in copies(k):
            copy.wait()
        if k:
            deepen(k - 1)
        for start in range(k * chunk, (k + 1) * chunk, ROWS):
            sums_of(start)
    deepen(chunks - 1)

    row = row_position(columns, width)
    for s in range(SPECIES):
        theta = table[RATE_Y + s : RATE_Y + s + 1]
        rise = jnp.exp((row - (columns - 1.0)) * theta)
        fall = jnp.exp(-row * theta)
        both = product(y_table[s], right_pair(jnp.concatenate([deep[s, e] for e in range(SIDES)], axis=1)))
        for e in range(SIDES):
            solved[e, s] = both[:, e * width : (e + 1) * width] - deep[s, SIDES + e]
            for f, weight in enumerate((rise, fall)):
                at = (f * SIDES + e) * SPECIES + s
                corners[at : at + 1] = jnp.sum(weight * deep[s, e], axis=0, keepdims=True)
    for d in range(group):
        start = pl.multiple_of(lax.rem(member + d, group) * share, share)
        for s in range(SPECIES):
            for e in range(SIDES):
                sent[d][pl.ds((e * SPECIES + s) * share, share), :] = solved[e, s, pl.ds(start, share), :]
        sent[d][pl.ds(SIDES * SPECIES * share, corners.shape[0]), :] = corners[...]


def edges(group, rank, numbers, cross, kinetics, conc, influx):
    _, planes, columns, width = conc.shape
    chunks = columns // (2 * ROWS)
    hold = pltpu.VMEM((SPECIES, 2 * SIDES, columns, width), jnp.float32)
    rows = SIDES * SPECIES * (columns // group) + padded(CORNERS)
    return pl.pallas_call(
        functools.partial(edge_kernel, group),
        in_specs=[ANY] * 6,
        out_specs=[VMEM] * (group + 5),
        out_shape=[struct(rows, width)] * group
        + [
            pltpu.VMEM((TABLE_ROWS, width), jnp.float32),
            pltpu.VMEM(conc.shape, jnp.float32),
            pltpu.VMEM(influx.shape, jnp.float32),
            pltpu.VMEM((SPECIES, columns, 2 * columns), jnp.bfloat16),
            pltpu.VMEM((SPECIES, 2 * width, 2 * width), jnp.bfloat16),
        ],
        scratch_shapes=[
            pltpu.VMEM((SPECIES, planes // 2, 2, ROWS, width), jnp.float32),
            hold,
            hold,
            pltpu.VMEM((SIDES, SPECIES, columns, width), jnp.float32),
            pltpu.VMEM((padded(CORNERS), width), jnp.float32),
            pltpu.SemaphoreType.DMA((2, chunks)),
            pltpu.SMEM(rank.shape, rank.dtype),
            pltpu.SMEM(numbers.shape, numbers.dtype),
            pltpu.SMEM(cross.shape, cross.dtype),
            pltpu.SMEM(kinetics.shape, kinetics.dtype),
            pltpu.SemaphoreType.DMA((4,)),
        ],
        compiler_params=params(16),
        name="edges",
    )(rank, numbers, cross, kinetics, conc, influx)


def sweep_kernel(table, conc, influx, *refs):
    outs, g_hold = refs[:-1], refs[-1]
    planes, columns, width = influx.shape
    tile = (ROWS, width)
    count = len(outs)
    inner = tiles(table, INNER, count * SPECIES, tile)
    double = tiles(table, DOUBLE, count * SPECIES, tile)
    part_a = tiles(table, PART_A, count * SPECIES, tile)
    scale = tiles(table, SCALE_X, count, tile)
    decay = tiles(table, DECAY, count, tile)
    kinetic = tiles(table, KINETICS, 3, tile)

    def rows(k, carry):
        here = pl.ds(pl.multiple_of(k * ROWS, ROWS), ROWS)
        up = [jnp.zeros(tile, jnp.float32) for _ in range(count)]
        for i in range(planes):
            c = [conc[j, i, here, :] for j in range(SPECIES)]
            around = [turned(value) for value in c]
            first, binding = rates(c, influx[i, here, :], kinetic)
            change = (first, -binding, binding)
            for s in range(count):
                g = change[s] * scale[s]
                a = c[s]
                for j in range(SPECIES):
                    at = s * SPECIES + j
                    g = g + inner[at] * c[j] + double[at] * around[j]
                    if j != s:
                        a = a + part_a[at] * c[j]
                up[s] = g + decay[s] * up[s]
                g_hold[s, i] = g
                outs[s][i, here, :] = up[s] - a
        for s in range(count):
            down = jnp.zeros(tile, jnp.float32)
            for i in reversed(range(planes)):
                down = decay[s] * down
                outs[s][i, here, :] += down
                down += g_hold[s, i]
        return carry

    lax.fori_loop(0, columns // ROWS, rows, 0)


def sweeps(count, table, conc, influx):
    _, planes, columns, width = conc.shape
    return pl.pallas_call(
        sweep_kernel,
        in_specs=[VMEM] * 3,
        out_specs=[VMEM] * count,
        out_shape=[pltpu.VMEM(influx.shape, jnp.float32)] * count,
        scratch_shapes=[pltpu.VMEM((count, planes, ROWS, width), jnp.float32)],
        compiler_params=params(8),
        cost_estimate=pl.CostEstimate(flops=100 * conc.size, bytes_accessed=14 * conc.size, transcendentals=0),
        name="sweeps",
    )(table, conc, influx)


def block_of(member, d, group):
    block = member - d
    return jnp.where(block < 0.0, block + group, block)


def group_kernel(planes, share, table, after, *refs):
    parts, out = refs[:-1], refs[-1]
    group = len(parts)
    corners = SIDES * SPECIES * share
    member = table[MEMBER : MEMBER + 1]
    blocks = [block_of(member, d, group) for d in range(group)]
    for s in range(SPECIES):
        theta = planes * table[RATE_X + s : RATE_X + s + 1]
        for e in range(SIDES):
            weight = [jnp.exp((-b if e else b - (group - 1.0)) * theta) for b in blocks]
            here = pl.ds((e * SPECIES + s) * share, share)
            out[here, :] = sum(weight[d] * parts[d][here, :] for d in range(group))
            for k in range(SIDES):
                here = pl.ds(corners + (k * SIDES + e) * SPECIES + s, 1)
                out[here, :] = sum(weight[d] * parts[d][here, :] for d in range(group))


def group_sums(planes, share, table, after, parts):
    return pl.pallas_call(
        functools.partial(group_kernel, planes, share),
        in_specs=[VMEM, ANY] + [VMEM] * len(parts),
        out_specs=VMEM,
        out_shape=struct(*parts[0].shape),
        compiler_params=params(8),
        name="group_sums",
    )(table, after, *parts)


def column_kernel(table, y_table, z_table, conc, influx, *refs):
    count = SPECIES - 1
    h, u, (rough, y_out, last, weights, sums) = refs[:count], refs[count : count + SPECIES], refs[count + SPECIES :]
    planes, columns, width = influx.shape
    tile = (ROWS, width)
    row = row_position(columns, width)
    for s in range(SPECIES):
        theta = table[RATE_Y + s : RATE_Y + s + 1]
        weights[s, 0] = jnp.exp((row - (columns - 1.0)) * theta)
        weights[s, 1] = jnp.exp(-row * theta)
    inner = tiles(table, INNER + count * SPECIES, SPECIES, tile)
    double = tiles(table, DOUBLE + count * SPECIES, SPECIES, tile)
    part_a = tiles(table, PART_A + count * SPECIES, SPECIES, tile)
    (scale,) = tiles(table, SCALE_X + count, 1, tile)
    (decay,) = tiles(table, DECAY + count, 1, tile)
    bind, unbind, _ = tiles(table, KINETICS, 3, tile)

    def plane_of(s, value, i):
        for e in range(SIDES):
            sums[s, e, pl.ds(i, 1), :] = jnp.sum(weights[s, e] * value, axis=0, keepdims=True)
        u[s][i] = product(y_table[s], right_pair(value))

    def plane(i):
        for s in range(count):
            plane_of(s, h[s][i], i)

    def rows(k):
        here = pl.ds(pl.multiple_of(k * ROWS, ROWS), ROWS)
        up, sources, rising = jnp.zeros(tile, jnp.float32), [], []
        for i in range(planes):
            c = [conc[j, i, here, :] for j in range(SPECIES)]
            g = (bind * c[0] * c[1] - unbind * c[2]) * scale
            a = c[count]
            for j in range(SPECIES):
                g = g + inner[j] * c[j] + double[j] * turned(c[j])
                if j != count:
                    a = a + part_a[j] * c[j]
            up = g + decay * up
            sources.append(g)
            rising.append(up - a)
        down = jnp.zeros(tile, jnp.float32)
        for i in reversed(range(planes)):
            down = decay * down
            last[i, here, :] = rising[i] + down
            down = down + sources[i]

    side_by_side((planes, columns // ROWS), (plane, rows))
    side_by_side(
        (planes, columns // ROWS),
        (lambda i: plane_of(count, last[i], i), lambda k: sweep_of_b(0, table, conc, rough, k)),
    )
    for s in range(SPECIES):
        both = jnp.concatenate([sums[s, e] for e in range(SIDES)], axis=0)
        both = product(left_pair(both), z_table[s])
        for e in range(SIDES):
            y_out[pl.ds((e * SPECIES + s) * planes, planes), :] = both[e * planes : (e + 1) * planes]


def column_parts(table, y_table, z_table, conc, influx, h):
    planes, columns, width = influx.shape
    return pl.pallas_call(
        column_kernel,
        in_specs=[VMEM] * (5 + len(h)),
        out_specs=[VMEM] * (SPECIES + 2),
        out_shape=[pltpu.VMEM(influx.shape, jnp.float32)] * (SPECIES + 1)
        + [pltpu.VMEM((SIDES * SPECIES * planes, width), jnp.float32)],
        scratch_shapes=[
            pltpu.VMEM(influx.shape, jnp.float32),
            pltpu.VMEM((SPECIES, SIDES, columns, width), jnp.float32),
            pltpu.VMEM((SPECIES, SIDES, planes, width), jnp.float32),
        ],
        compiler_params=params(8),
        cost_estimate=pl.CostEstimate(flops=6 * conc.size * columns, bytes_accessed=8 * conc.size, transcendentals=0),
        name="column_parts",
    )(table, y_table, z_table, conc, influx, *h)


def finish_kernel(table, z_table, conc, *refs):
    u, (rough, out), roughs = refs[:SPECIES], refs[SPECIES : SPECIES + 2], refs[SPECIES + 2 :]
    _, planes, columns, width = conc.shape
    at_once = 4 if planes % 4 == 0 else 1
    blocks, chunks = planes // at_once, columns // ROWS
    roughs = [rough, *roughs]

    for s in range(SPECIES):
        each = chunks // blocks if chunks % blocks == 0 else chunks

        def sweep(k, carry):
            sweep_of_b(s + 1, table, conc, roughs[s + 1], k)
            return carry

        if s + 1 < SPECIES and each == chunks:
            lax.fori_loop(0, chunks, sweep, 0)

        def block(k, carry):
            here = pl.ds(pl.multiple_of(k * at_once, at_once), at_once)
            value = (u[s][here] - roughs[s][here]).reshape(at_once * columns, width)
            done = product(left_pair(value), z_table[s])
            out[s, here] = conc[s, here] + done.reshape(at_once, columns, width)
            if s + 1 < SPECIES and each < chunks:
                for n in range(each):
                    sweep(k * each + n, 0)
            return carry

        lax.fori_loop(0, blocks, block, 0)


def finish(table, z_table, conc, u, rough):
    return pl.pallas_call(
        finish_kernel,
        in_specs=[VMEM] * (4 + len(u)),
        out_specs=VMEM,
        out_shape=pltpu.VMEM(conc.shape, jnp.float32),
        scratch_shapes=[pltpu.VMEM(rough.shape, jnp.float32)] * (SPECIES - 1),
        compiler_params=params(8),
        cost_estimate=pl.CostEstimate(
            flops=6 * conc.size * conc.shape[3], bytes_accessed=12 * conc.size, transcendentals=0
        ),
        name="finish",
    )(table, z_table, conc, *u, rough)


def enter_kernel(group, planes, share, table, sums, *refs):
    parts, wholes, outs, y_out = refs[:group], refs[group : -group - 1], refs[-group - 1 : -1], refs[-1]
    groups = len(wholes)
    corners = SIDES * SPECIES * share
    member = table[MEMBER : MEMBER + 1]
    blocks = [block_of(member, d, group) for d in range(group)]
    targets = [jnp.where(member + d >= group, member + d - group, member + d) for d in range(group)]
    y_out[pl.ds(0, sums.shape[0]), :] = sums[...]

    for s in range(SPECIES):
        theta = planes * table[RATE_X + s : RATE_X + s + 1]
        closing = 1.0 / (1.0 - jnp.exp(-float(group * groups) * theta))
        for e in range(SIDES):
            steps = [(groups - j - 1) if e else (j - 1 if j else groups - 1) for j in range(groups)]
            outside = [jnp.exp(-float(group * k) * theta) * closing for k in steps]
            to_target = [jnp.exp((t - (group - 1.0) if e else -t) * theta) for t in targets]
            inside = []
            for t in targets:
                away = [(b - t) if e else (t - b) for b in blocks]
                inside.append([jnp.where(k > 0.0, jnp.exp((1.0 - jnp.abs(k)) * theta), 0.0) for k in away])

            def entering_group(here):
                return sum(weight * whole[here, :] for weight, whole in zip(outside, wholes))

            here = pl.ds((e * SPECIES + s) * share, share)
            whole = entering_group(here)
            held = [part[here, :] for part in parts]
            for d in range(group):
                total = to_target[d] * whole
                for weight, part in zip(inside[d], held):
                    total = total + weight * part
                outs[d][here, :] = total

            for k in range(SIDES):
                at = (k * SIDES + e) * SPECIES + s
                here = pl.ds(corners + at, 1)
                total = to_target[0] * entering_group(here)
                for weight, part in zip(inside[0], parts):
                    total = total + weight * part[here, :]
                y_out[pl.ds(sums.shape[0] + at, 1), :] = total


def entering(planes, share, table, sums, parts, wholes):
    group, width = len(parts), parts[0].shape[1]
    return pl.pallas_call(
        functools.partial(enter_kernel, group, planes, share),
        in_specs=[VMEM] * (2 + group + len(wholes)),
        out_specs=[VMEM] * (group + 1),
        out_shape=[struct(SIDES * SPECIES * share, width)] * group + [struct(padded(sums.shape[0] + CORNERS), width)],
        compiler_params=params(8),
        name="entering",
    )(table, sums, *parts, *wholes)


def inflow_kernel(table, base, *refs):
    parts, (out, lift, fades, weights) = refs[:-4], refs[-4:]
    _, planes, columns, width = base.shape
    along = len(parts)
    corners = SIDES * SPECIES * planes
    row = row_position(columns, width)
    position = row_position(planes, width)
    for s in range(SPECIES):
        rate_x = table[RATE_X + s : RATE_X + s + 1]
        rate_y = table[RATE_Y + s : RATE_Y + s + 1]
        theta = columns * rate_y
        closing = table[SCALE_Y + s : SCALE_Y + s + 1] / (1.0 - jnp.exp(-float(along) * theta))
        weights[0] = jnp.exp(-(row + 1.0) * rate_y)
        weights[1] = jnp.exp((row - columns) * rate_y)
        fades[pl.ds(s * planes, planes), :] = jnp.exp(-(position + 1.0) * rate_x)
        fades[pl.ds((SPECIES + s) * planes, planes), :] = jnp.exp((position - planes) * rate_x)
        enter, corner = [], []
        for e in range(SIDES):
            steps = [(along - k - 1) if e else (k - 1 if k else along - 1) for k in range(along)]
            arrive = [jnp.exp(-float(k) * theta) * closing for k in steps]

            def entering_block(here):
                return sum(weight * part[here, :] for weight, part in zip(arrive, parts))

            enter.append(entering_block(pl.ds((e * SPECIES + s) * planes, planes)))
            corner.append([entering_block(pl.ds(corners + (e * SIDES + k) * SPECIES + s, 1)) for k in range(SIDES)])
        for k in range(SIDES):
            lift[k, s] = weights[0] * corner[0][k] + weights[1] * corner[1][k]
        for i in range(planes):
            out[s, i] = base[s, i] + weights[0] * enter[0][i : i + 1] + weights[1] * enter[1][i : i + 1]


def inflow(table, base, parts):
    _, planes, columns, width = base.shape
    return pl.pallas_call(
        inflow_kernel,
        in_specs=[VMEM] * (2 + len(parts)),
        out_specs=[VMEM] * 3,
        out_shape=[
            pltpu.VMEM(base.shape, jnp.float32),
            pltpu.VMEM((SIDES, SPECIES, columns, width), jnp.float32),
            pltpu.VMEM((SIDES * SPECIES * planes, width), jnp.float32),
        ],
        scratch_shapes=[pltpu.VMEM((SIDES, columns, width), jnp.float32)],
        compiler_params=params(8),
        name="inflow",
    )(table, base, *parts)


def spread_kernel(group, share, table, fades, base, lift, *refs):
    parts, (out_far, out, hold, left) = refs[:group], refs[group:]
    _, planes, columns, width = base.shape
    blocks = [block_of(table[MEMBER : MEMBER + 1], d, group) for d in range(group)]
    at_once = planes // left.shape[1]
    copies = []
    for s in range(SPECIES):
        for e in range(SIDES):
            held = [part[pl.ds((e * SPECIES + s) * share, share), :] for part in parts]
            for b in range(group):
                there = pl.ds(b * share, share)
                mine = held[0]
                for d in range(1, group):
                    mine = jnp.where(blocks[d] == b, held[d], mine)
                hold[e, there, :] = lift[e, s, there, :] + mine
        for i in range(planes):
            rise = fades[s * planes + i : s * planes + i + 1]
            fall = fades[(SPECIES + s) * planes + i : (SPECIES + s) * planes + i + 1]
            out[s, i] = base[s, i] + rise * hold[0] + fall * hold[1]
            if i % at_once == at_once - 1:
                k = i // at_once
                part = pl.ds(k * at_once, at_once)
                copies.append(pltpu.make_async_copy(out.at[s, part], out_far.at[s, part], left.at[s, k]))
                copies[-1].start()
    for copy in copies:
        copy.wait()


def spread(share, table, fades, base, lift, parts):
    _, planes, columns, width = base.shape
    return pl.pallas_call(
        functools.partial(spread_kernel, len(parts), share),
        in_specs=[VMEM] * (4 + len(parts)),
        out_specs=ANY,
        out_shape=struct(*base.shape),
        scratch_shapes=[
            pltpu.VMEM(base.shape, jnp.float32),
            pltpu.VMEM((SIDES, columns, width), jnp.float32),
            pltpu.SemaphoreType.DMA((SPECIES, planes // 4)),
        ],
        compiler_params=params(8),
        name="spread",
    )(table, fades, base, lift, *parts)


def group_size(devices):
    size = 1
    while 4 * size * size <= 2 * devices and devices % (2 * size) == 0:
        size *= 2
    return size


def body(conc, influx, numbers, cross, kinetics):
    _, planes, columns, _ = conc.shape
    across, along = lax.axis_size("gx"), lax.axis_size("gy")
    group = group_size(across)
    share = columns // group
    rank = lax.axis_index("gx").astype(jnp.int32).reshape(1)
    conc, influx, numbers, cross, kinetics = (
        pltpu.with_memory_space_constraint(x, pltpu.HBM) for x in (conc, influx, numbers, cross, kinetics)
    )

    def turn(value, by):
        return lax.ppermute(value, "gy", [(i, (i + by) % along) for i in range(along)])

    def in_group(parts):
        turns = [[(i, i - i % group + (i + d) % group) for i in range(across)] for d in range(group)]
        return [parts[0]] + [lax.ppermute(parts[d], "gx", turns[d]) for d in range(1, group)]

    def over_groups(value, by):
        return lax.ppermute(value, "gx", [(i, (i + by * group) % across) for i in range(across)])

    *parts, table, conc, influx, y_table, z_table = edges(group, rank, numbers, cross, kinetics, conc, influx)
    parts = in_group(parts)
    h = sweeps(SPECIES - 1, table, conc, influx)
    whole = group_sums(planes, share, table, h[0], parts)
    wholes = [whole] + [over_groups(whole, j) for j in range(1, across // group)]
    *u, rough, sums = column_parts(table, y_table, z_table, conc, influx, h)
    *outs, sums = entering(planes, share, table, sums, parts, wholes)
    outs = in_group(outs)
    base = finish(table, z_table, conc, u, rough)
    base, lift, fades = inflow(table, base, [sums] + [turn(sums, k) for k in range(1, along)])
    return spread(share, table, fades, base, lift, outs)


def solution(mesh):
    placed = (P(None, "gx", "gy", None), P("gx", "gy", None), P(), P(), P())
    return jax.shard_map(
        body, mesh=mesh, in_specs=placed, out_specs=P(None, "gx", "gy", None), check_vma=False
    )
```

```python
import functools

import jax
import jax.numpy as jnp
from jax import lax
from jax.experimental import pallas as pl
from jax.experimental.pallas import tpu as pltpu
from jax.sharding import PartitionSpec as P

SPECIES = 3
ROWS = 8
SIDES = 2
CORNERS = SIDES * SIDES * SPECIES
SMEM = pl.BlockSpec(memory_space=pltpu.SMEM)
VMEM = pl.BlockSpec(memory_space=pltpu.VMEM)
ANY = pl.BlockSpec(memory_space=pl.ANY)

RATE_X, RATE_Y, SCALE_Y, SCALE_X, DECAY, KINETICS, MEMBER = 0, 3, 6, 9, 12, 15, 18
INNER, DOUBLE, PART_A, PART_B, TABLE_ROWS = 19, 28, 37, 46, 56


def padded(rows):
    return -(-rows // ROWS) * ROWS


def params(mebibytes):
    return pltpu.CompilerParams(vmem_limit_bytes=mebibytes * 2**20)


def struct(*shape):
    return jax.ShapeDtypeStruct(shape, jnp.float32)


def decay_rate(number):
    half = 0.5 * lax.rsqrt(number)
    square = half * half
    return 2.0 * jnp.log1p(half + square / (1.0 + jnp.sqrt(1.0 + square)))


def scaling(number):
    return lax.rsqrt(1.0 + 4.0 * number)


def splat(value, shape):
    return jnp.full(shape, value, jnp.float32)


def split(value):
    high = value.astype(jnp.bfloat16)
    return high, (value - high.astype(jnp.float32)).astype(jnp.bfloat16)


def left_pair(value):
    return jnp.concatenate(split(value), axis=1)


def right_pair(value):
    high, low = split(value)
    return jnp.concatenate(
        [jnp.concatenate([high, low], axis=1), jnp.concatenate([high, jnp.zeros_like(low)], axis=1)], axis=0
    )


def product(left, right):
    both = jnp.dot(left, right, preferred_element_type=jnp.float32)
    width = both.shape[1] // 2
    return both[:, :width] + both[:, width:]


def distances(length):
    rows = lax.broadcasted_iota(jnp.int32, (length, length), 0)
    columns = lax.broadcasted_iota(jnp.int32, (length, length), 1)
    return jnp.abs(rows - columns).astype(jnp.float32)


def depth_table(number, length):
    number = splat(number, (1, length))
    theta = decay_rate(number)
    spread = distances(length)
    factor = scaling(number) / (1.0 - jnp.exp(-length * theta))
    return (jnp.exp(-spread * theta) + jnp.exp((spread - length) * theta)) * factor


def column_table(number, length):
    number = splat(number, (1, length))
    return jnp.exp(-distances(length) * decay_rate(number)) * scaling(number)


def row_position(length, width):
    return lax.broadcasted_iota(jnp.int32, (length, width), 0).astype(jnp.float32)


def coefficients(numbers, cross, kinetics, tile):
    n = [[splat(numbers[s, d], tile) for d in range(3)] for s in range(SPECIES)]
    along_x, along_y, along_z = [], [], []
    for s in range(SPECIES):
        per_x, per_y = 1.0 / n[s][0], 1.0 / n[s][1]
        for j in range(SPECIES):
            mix = 1.0 if j == s else cross[s, j]
            along_x.append(n[j][0] * per_x * mix)
            along_y.append(n[j][1] * per_y * mix)
            along_z.append(n[j][2] * mix)
    scale = [scaling(n[s][0]) for s in range(SPECIES)]
    rate = [decay_rate(n[s][0]) for s in range(SPECIES)]
    return along_x, along_y, along_z, scale, rate, [splat(kinetics[i], tile) for i in range(3)]


def turned(value):
    width = value.shape[1]
    return pltpu.roll(value, 1, 1) + pltpu.roll(value, width - 1, 1)


def tiles(table, first, count, tile):
    return [jnp.broadcast_to(table[at : at + 1], tile) for at in range(first, first + count)]


def rates(c, influx, kinetics):
    bind, unbind, pump = kinetics
    binding = bind * c[0] * c[1] - unbind * c[2]
    pumping = pump * c[0] / (1.0 + c[0])
    return influx - 4.0 * binding - pumping, binding


def side_by_side(counts, steps):
    common = min(counts)

    def together(k, carry):
        for step in steps:
            step(k)
        return carry

    lax.fori_loop(0, common, together, 0, unroll=2 if common % 2 == 0 else 1)
    for count, step in zip(counts, steps):
        if count > common:
            lax.fori_loop(common, count, lambda k, carry, step=step: (step(k), carry)[1], 0)


def sweep_of_b(s, table, conc, out, k):
    _, planes, _, width = conc.shape
    tile = (ROWS, width)
    here = pl.ds(pl.multiple_of(k * ROWS, ROWS), ROWS)
    weight = tiles(table, PART_B + s * SPECIES, SPECIES, tile)
    (decay,) = tiles(table, DECAY + s, 1, tile)
    up, sources, rising = jnp.zeros(tile, jnp.float32), [], []
    for i in range(planes):
        b = weight[0] * conc[0, i, here, :] + weight[1] * conc[1, i, here, :] + weight[2] * conc[2, i, here, :]
        up = b + decay * up
        sources.append(b)
        rising.append(up)
    down = jnp.zeros(tile, jnp.float32)
    for i in reversed(range(planes)):
        down = decay * down
        out[i, here, :] = rising[i] + down
        down = down + sources[i]


def edge_kernel(group, rank_far, numbers_far, cross_far, kinetics_far, conc_far, influx_far, *refs):
    sent, refs = refs[:group], refs[group:]
    table, conc, influx, y_table, z_table, weights, hold, deep, solved, corners, arrived = refs[:11]
    rank, numbers, cross, kinetics, small = refs[11:]
    planes, columns, width = influx.shape
    chunks = arrived.shape[1]
    chunk = columns // chunks
    half = planes // 2
    share = columns // group
    tile = (ROWS, width)

    def copies(k):
        part = pl.ds(k * chunk, chunk)
        return (
            pltpu.make_async_copy(conc_far.at[:, :, part, :], conc.at[:, :, part, :], arrived.at[0, k]),
            pltpu.make_async_copy(influx_far.at[:, part, :], influx.at[:, part, :], arrived.at[1, k]),
        )

    for k in range(chunks):
        for copy in copies(k):
            copy.start()
    fars = (rank_far, numbers_far, cross_far, kinetics_far)
    nears = (rank, numbers, cross, kinetics)
    scalars = [pltpu.make_async_copy(far, near, small.at[k]) for k, (far, near) in enumerate(zip(fars, nears))]
    for copy in scalars:
        copy.start()
    for copy in scalars:
        copy.wait()

    along_x, along_y, along_z, scale, rate, kinetic = coefficients(numbers, cross, kinetics, tile)
    inner, double, single = [], [], []
    for s in range(SPECIES):
        for at in range(s * SPECIES, (s + 1) * SPECIES):
            inner.append((along_x[at] + along_y[at] - 2.0 * along_z[at]) * scale[s])
            double.append(along_z[at] * scale[s])
            single.append(along_y[at] * scale[s])
        for i in range(half):
            near = jnp.exp(-i * rate[s])
            far = jnp.exp(-(planes - 1.0 - i) * rate[s])
            weights[s, i, 0] = 0.5 * (near + far)
            weights[s, i, 1] = 0.5 * (near - far)
        number = splat(numbers[s, 1], tile)
        table[RATE_Y + s : RATE_Y + s + 1] = decay_rate(number)[:1]
        table[SCALE_Y + s : SCALE_Y + s + 1] = scaling(number)[:1]
        y_table[s] = left_pair(column_table(numbers[s, 1], columns))
        z_table[s] = right_pair(depth_table(numbers[s, 2], width))
    member = lax.rem(rank[0], group)
    entries = (
        (RATE_X, rate),
        (SCALE_X, scale),
        (DECAY, [jnp.exp(-value) for value in rate]),
        (KINETICS, kinetic),
        (MEMBER, [splat(member.astype(jnp.float32), tile)]),
        (INNER, inner),
        (DOUBLE, double),
        (PART_A, along_x),
        (PART_B, single),
    )
    for first, values in entries:
        for k, value in enumerate(values):
            table[first + k : first + k + 1] = value[:1]

    def sums_of(start):
        here = slice(start, start + ROWS)

        def at_plane(i):
            c = [conc[j, i, here, :] for j in range(SPECIES)]
            return c, *rates(c, influx[i, here, :], kinetic)

        zero = jnp.zeros(tile, jnp.float32)
        plus = [[zero] * (SPECIES + 1) for _ in range(SPECIES)]
        minus = [[zero] * (SPECIES + 1) for _ in range(SPECIES)]
        for i in range(half):
            low, low_first, low_binding = at_plane(i)
            high, high_first, high_binding = at_plane(planes - 1 - i)
            both = [x + y for x, y in zip(low, high)]
            apart = [x - y for x, y in zip(low, high)]
            change = (low_first + high_first, low_binding + high_binding)
            turn = (low_first - high_first, low_binding - high_binding)
            for s in range(SPECIES):
                even, odd = weights[s, i, 0], weights[s, i, 1]
                of = min(s, 1)
                for j, (p, m) in enumerate(zip(both + [change[of]], apart + [turn[of]])):
                    plus[s][j] = plus[s][j] + even * p
                    minus[s][j] = minus[s][j] + odd * m
        for s in range(SPECIES):
            for e in range(SIDES):
                sums = [p + m if e else p - m for p, m in zip(plus[s], minus[s])]
                v = sums[SPECIES] * scale[s]
                if s == 1:
                    v = -v
                w = 0.0
                for j in range(SPECIES):
                    at = s * SPECIES + j
                    v = v + inner[at] * sums[j] + double[at] * turned(sums[j])
                    w = w + single[at] * sums[j]
                hold[s, e, here, :] = v
                hold[s, SIDES + e, here, :] = w

    def deepen(k):
        here = slice(k * chunk, (k + 1) * chunk)
        for s in range(SPECIES):
            stack = jnp.concatenate([hold[s, e, here, :] for e in range(2 * SIDES)], axis=0)
            done = product(left_pair(stack), z_table[s])
            for e in range(2 * SIDES):
                deep[s, e, here, :] = done[e * chunk : (e + 1) * chunk]

    for k in range(chunks):
        for copy in copies(k):
            copy.wait()
        if k:
            deepen(k - 1)
        for start in range(k * chunk, (k + 1) * chunk, ROWS):
            sums_of(start)
    deepen(chunks - 1)

    row = row_position(columns, width)
    for s in range(SPECIES):
        theta = table[RATE_Y + s : RATE_Y + s + 1]
        rise = jnp.exp((row - (columns - 1.0)) * theta)
        fall = jnp.exp(-row * theta)
        both = product(y_table[s], right_pair(jnp.concatenate([deep[s, e] for e in range(SIDES)], axis=1)))
        for e in range(SIDES):
            solved[e, s] = both[:, e * width : (e + 1) * width] - deep[s, SIDES + e]
            for f, weight in enumerate((rise, fall)):
                at = (f * SIDES + e) * SPECIES + s
                corners[at : at + 1] = jnp.sum(weight * deep[s, e], axis=0, keepdims=True)
    for d in range(group):
        start = pl.multiple_of(lax.bitwise_xor(member, jnp.int32(d)) * share, share)
        for s in range(SPECIES):
            for e in range(SIDES):
                sent[d][pl.ds((e * SPECIES + s) * share, share), :] = solved[e, s, pl.ds(start, share), :]
        sent[d][pl.ds(SIDES * SPECIES * share, corners.shape[0]), :] = corners[...]


def edges(group, rank, numbers, cross, kinetics, conc, influx):
    _, planes, columns, width = conc.shape
    chunks = columns // (2 * ROWS)
    hold = pltpu.VMEM((SPECIES, 2 * SIDES, columns, width), jnp.float32)
    rows = SIDES * SPECIES * (columns // group) + padded(CORNERS)
    return pl.pallas_call(
        functools.partial(edge_kernel, group),
        in_specs=[ANY] * 6,
        out_specs=[VMEM] * (group + 5),
        out_shape=[struct(rows, width)] * group
        + [
            pltpu.VMEM((TABLE_ROWS, width), jnp.float32),
            pltpu.VMEM(conc.shape, jnp.float32),
            pltpu.VMEM(influx.shape, jnp.float32),
            pltpu.VMEM((SPECIES, columns, 2 * columns), jnp.bfloat16),
            pltpu.VMEM((SPECIES, 2 * width, 2 * width), jnp.bfloat16),
        ],
        scratch_shapes=[
            pltpu.VMEM((SPECIES, planes // 2, 2, ROWS, width), jnp.float32),
            hold,
            hold,
            pltpu.VMEM((SIDES, SPECIES, columns, width), jnp.float32),
            pltpu.VMEM((padded(CORNERS), width), jnp.float32),
            pltpu.SemaphoreType.DMA((2, chunks)),
            pltpu.SMEM(rank.shape, rank.dtype),
            pltpu.SMEM(numbers.shape, numbers.dtype),
            pltpu.SMEM(cross.shape, cross.dtype),
            pltpu.SMEM(kinetics.shape, kinetics.dtype),
            pltpu.SemaphoreType.DMA((4,)),
        ],
        compiler_params=params(16),
        name="edges",
    )(rank, numbers, cross, kinetics, conc, influx)


def sweep_kernel(table, conc, influx, *refs):
    outs, g_hold = refs[:-1], refs[-1]
    planes, columns, width = influx.shape
    tile = (ROWS, width)
    count = len(outs)
    inner = tiles(table, INNER, count * SPECIES, tile)
    double = tiles(table, DOUBLE, count * SPECIES, tile)
    part_a = tiles(table, PART_A, count * SPECIES, tile)
    scale = tiles(table, SCALE_X, count, tile)
    decay = tiles(table, DECAY, count, tile)
    kinetic = tiles(table, KINETICS, 3, tile)

    def rows(k, carry):
        here = pl.ds(pl.multiple_of(k * ROWS, ROWS), ROWS)
        up = [jnp.zeros(tile, jnp.float32) for _ in range(count)]
        for i in range(planes):
            c = [conc[j, i, here, :] for j in range(SPECIES)]
            around = [turned(value) for value in c]
            first, binding = rates(c, influx[i, here, :], kinetic)
            change = (first, -binding, binding)
            for s in range(count):
                g = change[s] * scale[s]
                a = c[s]
                for j in range(SPECIES):
                    at = s * SPECIES + j
                    g = g + inner[at] * c[j] + double[at] * around[j]
                    if j != s:
                        a = a + part_a[at] * c[j]
                up[s] = g + decay[s] * up[s]
                g_hold[s, i] = g
                outs[s][i, here, :] = up[s] - a
        for s in range(count):
            down = jnp.zeros(tile, jnp.float32)
            for i in reversed(range(planes)):
                down = decay[s] * down
                outs[s][i, here, :] += down
                down += g_hold[s, i]
        return carry

    lax.fori_loop(0, columns // ROWS, rows, 0)


def sweeps(count, table, conc, influx):
    _, planes, columns, width = conc.shape
    return pl.pallas_call(
        sweep_kernel,
        in_specs=[VMEM] * 3,
        out_specs=[VMEM] * count,
        out_shape=[pltpu.VMEM(influx.shape, jnp.float32)] * count,
        scratch_shapes=[pltpu.VMEM((count, planes, ROWS, width), jnp.float32)],
        compiler_params=params(8),
        cost_estimate=pl.CostEstimate(flops=100 * conc.size, bytes_accessed=14 * conc.size, transcendentals=0),
        name="sweeps",
    )(table, conc, influx)


def partner(member, d):
    return lax.bitwise_xor(member.astype(jnp.int32), jnp.int32(d)).astype(jnp.float32)


def group_kernel(planes, share, table, after, *refs):
    parts, out = refs[:-1], refs[-1]
    group = len(parts)
    corners = SIDES * SPECIES * share
    member = table[MEMBER : MEMBER + 1]
    blocks = [partner(member, d) for d in range(group)]
    for s in range(SPECIES):
        theta = planes * table[RATE_X + s : RATE_X + s + 1]
        for e in range(SIDES):
            weight = [jnp.exp((-b if e else b - (group - 1.0)) * theta) for b in blocks]
            here = pl.ds((e * SPECIES + s) * share, share)
            out[here, :] = sum(weight[d] * parts[d][here, :] for d in range(group))
            for k in range(SIDES):
                here = pl.ds(corners + (k * SIDES + e) * SPECIES + s, 1)
                out[here, :] = sum(weight[d] * parts[d][here, :] for d in range(group))


def group_sums(planes, share, table, after, parts):
    return pl.pallas_call(
        functools.partial(group_kernel, planes, share),
        in_specs=[VMEM, ANY] + [VMEM] * len(parts),
        out_specs=VMEM,
        out_shape=struct(*parts[0].shape),
        compiler_params=params(8),
        name="group_sums",
    )(table, after, *parts)


def column_kernel(table, y_table, z_table, conc, influx, *refs):
    count = SPECIES - 1
    h, u, (rough, y_out, last, weights, sums) = refs[:count], refs[count : count + SPECIES], refs[count + SPECIES :]
    planes, columns, width = influx.shape
    tile = (ROWS, width)
    row = row_position(columns, width)
    for s in range(SPECIES):
        theta = table[RATE_Y + s : RATE_Y + s + 1]
        weights[s, 0] = jnp.exp((row - (columns - 1.0)) * theta)
        weights[s, 1] = jnp.exp(-row * theta)
    inner = tiles(table, INNER + count * SPECIES, SPECIES, tile)
    double = tiles(table, DOUBLE + count * SPECIES, SPECIES, tile)
    part_a = tiles(table, PART_A + count * SPECIES, SPECIES, tile)
    (scale,) = tiles(table, SCALE_X + count, 1, tile)
    (decay,) = tiles(table, DECAY + count, 1, tile)
    bind, unbind, _ = tiles(table, KINETICS, 3, tile)

    def plane_of(s, value, i):
        for e in range(SIDES):
            sums[s, e, pl.ds(i, 1), :] = jnp.sum(weights[s, e] * value, axis=0, keepdims=True)
        u[s][i] = product(y_table[s], right_pair(value))

    def plane(i):
        for s in range(count):
            plane_of(s, h[s][i], i)

    def rows(k):
        here = pl.ds(pl.multiple_of(k * ROWS, ROWS), ROWS)
        up, sources, rising = jnp.zeros(tile, jnp.float32), [], []
        for i in range(planes):
            c = [conc[j, i, here, :] for j in range(SPECIES)]
            g = (bind * c[0] * c[1] - unbind * c[2]) * scale
            a = c[count]
            for j in range(SPECIES):
                g = g + inner[j] * c[j] + double[j] * turned(c[j])
                if j != count:
                    a = a + part_a[j] * c[j]
            up = g + decay * up
            sources.append(g)
            rising.append(up - a)
        down = jnp.zeros(tile, jnp.float32)
        for i in reversed(range(planes)):
            down = decay * down
            last[i, here, :] = rising[i] + down
            down = down + sources[i]

    side_by_side((planes, columns // ROWS), (plane, rows))
    side_by_side(
        (planes, columns // ROWS),
        (lambda i: plane_of(count, last[i], i), lambda k: sweep_of_b(0, table, conc, rough, k)),
    )
    for s in range(SPECIES):
        both = jnp.concatenate([sums[s, e] for e in range(SIDES)], axis=0)
        both = product(left_pair(both), z_table[s])
        for e in range(SIDES):
            y_out[pl.ds((e * SPECIES + s) * planes, planes), :] = both[e * planes : (e + 1) * planes]


def column_parts(table, y_table, z_table, conc, influx, h):
    planes, columns, width = influx.shape
    return pl.pallas_call(
        column_kernel,
        in_specs=[VMEM] * (5 + len(h)),
        out_specs=[VMEM] * (SPECIES + 2),
        out_shape=[pltpu.VMEM(influx.shape, jnp.float32)] * (SPECIES + 1)
        + [pltpu.VMEM((SIDES * SPECIES * planes, width), jnp.float32)],
        scratch_shapes=[
            pltpu.VMEM(influx.shape, jnp.float32),
            pltpu.VMEM((SPECIES, SIDES, columns, width), jnp.float32),
            pltpu.VMEM((SPECIES, SIDES, planes, width), jnp.float32),
        ],
        compiler_params=params(8),
        cost_estimate=pl.CostEstimate(flops=6 * conc.size * columns, bytes_accessed=8 * conc.size, transcendentals=0),
        name="column_parts",
    )(table, y_table, z_table, conc, influx, *h)


def finish_kernel(table, z_table, conc, *refs):
    u, (rough, out), roughs = refs[:SPECIES], refs[SPECIES : SPECIES + 2], refs[SPECIES + 2 :]
    _, planes, columns, width = conc.shape
    at_once = 4 if planes % 4 == 0 else 1
    blocks, chunks = planes // at_once, columns // ROWS
    roughs = [rough, *roughs]

    for s in range(SPECIES):
        each = chunks // blocks if chunks % blocks == 0 else chunks

        def sweep(k, carry):
            sweep_of_b(s + 1, table, conc, roughs[s + 1], k)
            return carry

        if s + 1 < SPECIES and each == chunks:
            lax.fori_loop(0, chunks, sweep, 0)

        def block(k, carry):
            here = pl.ds(pl.multiple_of(k * at_once, at_once), at_once)
            value = (u[s][here] - roughs[s][here]).reshape(at_once * columns, width)
            done = product(left_pair(value), z_table[s])
            out[s, here] = conc[s, here] + done.reshape(at_once, columns, width)
            if s + 1 < SPECIES and each < chunks:
                for n in range(each):
                    sweep(k * each + n, 0)
            return carry

        lax.fori_loop(0, blocks, block, 0)


def finish(table, z_table, conc, u, rough):
    return pl.pallas_call(
        finish_kernel,
        in_specs=[VMEM] * (4 + len(u)),
        out_specs=VMEM,
        out_shape=pltpu.VMEM(conc.shape, jnp.float32),
        scratch_shapes=[pltpu.VMEM(rough.shape, jnp.float32)] * (SPECIES - 1),
        compiler_params=params(8),
        cost_estimate=pl.CostEstimate(
            flops=6 * conc.size * conc.shape[3], bytes_accessed=12 * conc.size, transcendentals=0
        ),
        name="finish",
    )(table, z_table, conc, *u, rough)


def enter_kernel(group, planes, share, table, sums, *refs):
    parts, wholes, outs, y_out = refs[:group], refs[group : -group - 1], refs[-group - 1 : -1], refs[-1]
    groups = len(wholes)
    corners = SIDES * SPECIES * share
    member = table[MEMBER : MEMBER + 1]
    blocks = [partner(member, d) for d in range(group)]
    y_out[pl.ds(0, sums.shape[0]), :] = sums[...]

    for s in range(SPECIES):
        theta = planes * table[RATE_X + s : RATE_X + s + 1]
        closing = 1.0 / (1.0 - jnp.exp(-float(group * groups) * theta))
        for e in range(SIDES):
            steps = [(groups - j - 1) if e else (j - 1 if j else groups - 1) for j in range(groups)]
            outside = [jnp.exp(-float(group * k) * theta) * closing for k in steps]
            to_target = [jnp.exp((t - (group - 1.0) if e else -t) * theta) for t in blocks]
            inside = []
            for t in blocks:
                away = [(b - t) if e else (t - b) for b in blocks]
                inside.append([jnp.where(k > 0.0, jnp.exp((1.0 - jnp.abs(k)) * theta), 0.0) for k in away])

            def entering_group(here):
                return sum(weight * whole[here, :] for weight, whole in zip(outside, wholes))

            here = pl.ds((e * SPECIES + s) * share, share)
            whole = entering_group(here)
            held = [part[here, :] for part in parts]
            for d in range(group):
                total = to_target[d] * whole
                for weight, part in zip(inside[d], held):
                    total = total + weight * part
                outs[d][here, :] = total

            for k in range(SIDES):
                at = (k * SIDES + e) * SPECIES + s
                here = pl.ds(corners + at, 1)
                total = to_target[0] * entering_group(here)
                for weight, part in zip(inside[0], parts):
                    total = total + weight * part[here, :]
                y_out[pl.ds(sums.shape[0] + at, 1), :] = total


def entering(planes, share, table, sums, parts, wholes):
    group, width = len(parts), parts[0].shape[1]
    return pl.pallas_call(
        functools.partial(enter_kernel, group, planes, share),
        in_specs=[VMEM] * (2 + group + len(wholes)),
        out_specs=[VMEM] * (group + 1),
        out_shape=[struct(SIDES * SPECIES * share, width)] * group + [struct(padded(sums.shape[0] + CORNERS), width)],
        compiler_params=params(8),
        name="entering",
    )(table, sums, *parts, *wholes)


def inflow_kernel(turns, table, base, *refs):
    parts, (out, lift, fades, weights) = refs[:-4], refs[-4:]
    _, planes, columns, width = base.shape
    along = len(parts)
    corners = SIDES * SPECIES * planes
    row = row_position(columns, width)
    position = row_position(planes, width)
    for s in range(SPECIES):
        rate_x = table[RATE_X + s : RATE_X + s + 1]
        rate_y = table[RATE_Y + s : RATE_Y + s + 1]
        theta = columns * rate_y
        closing = table[SCALE_Y + s : SCALE_Y + s + 1] / (1.0 - jnp.exp(-float(along) * theta))
        weights[0] = jnp.exp(-(row + 1.0) * rate_y)
        weights[1] = jnp.exp((row - columns) * rate_y)
        fades[pl.ds(s * planes, planes), :] = jnp.exp(-(position + 1.0) * rate_x)
        fades[pl.ds((SPECIES + s) * planes, planes), :] = jnp.exp((position - planes) * rate_x)
        enter, corner = [], []
        for e in range(SIDES):
            steps = [(along - k - 1) if e else (k - 1 if k else along - 1) for k in turns]
            arrive = [jnp.exp(-float(k) * theta) * closing for k in steps]

            def entering_block(here):
                return sum(weight * part[here, :] for weight, part in zip(arrive, parts))

            enter.append(entering_block(pl.ds((e * SPECIES + s) * planes, planes)))
            corner.append([entering_block(pl.ds(corners + (e * SIDES + k) * SPECIES + s, 1)) for k in range(SIDES)])
        for k in range(SIDES):
            lift[k, s] = weights[0] * corner[0][k] + weights[1] * corner[1][k]
        for i in range(planes):
            out[s, i] = base[s, i] + weights[0] * enter[0][i : i + 1] + weights[1] * enter[1][i : i + 1]


def inflow(turns, table, base, parts):
    _, planes, columns, width = base.shape
    return pl.pallas_call(
        functools.partial(inflow_kernel, turns),
        in_specs=[VMEM] * (2 + len(parts)),
        out_specs=[VMEM] * 3,
        out_shape=[
            pltpu.VMEM(base.shape, jnp.float32),
            pltpu.VMEM((SIDES, SPECIES, columns, width), jnp.float32),
            pltpu.VMEM((SIDES * SPECIES * planes, width), jnp.float32),
        ],
        scratch_shapes=[pltpu.VMEM((SIDES, columns, width), jnp.float32)],
        compiler_params=params(8),
        name="inflow",
    )(table, base, *parts)


def spread_kernel(group, share, table, fades, base, lift, *refs):
    parts, (out_far, out, hold, left) = refs[:group], refs[group:]
    _, planes, columns, width = base.shape
    blocks = [partner(table[MEMBER : MEMBER + 1], d) for d in range(group)]
    at_once = planes // left.shape[1]
    copies = []
    for s in range(SPECIES):
        for e in range(SIDES):
            held = [part[pl.ds((e * SPECIES + s) * share, share), :] for part in parts]
            for b in range(group):
                there = pl.ds(b * share, share)
                mine = held[0]
                for d in range(1, group):
                    mine = jnp.where(blocks[d] == b, held[d], mine)
                hold[e, there, :] = lift[e, s, there, :] + mine
        for i in range(planes):
            rise = fades[s * planes + i : s * planes + i + 1]
            fall = fades[(SPECIES + s) * planes + i : (SPECIES + s) * planes + i + 1]
            out[s, i] = base[s, i] + rise * hold[0] + fall * hold[1]
            if i % at_once == at_once - 1:
                k = i // at_once
                part = pl.ds(k * at_once, at_once)
                copies.append(pltpu.make_async_copy(out.at[s, part], out_far.at[s, part], left.at[s, k]))
                copies[-1].start()
    for copy in copies:
        copy.wait()


def spread(share, table, fades, base, lift, parts):
    _, planes, columns, width = base.shape
    return pl.pallas_call(
        functools.partial(spread_kernel, len(parts), share),
        in_specs=[VMEM] * (4 + len(parts)),
        out_specs=ANY,
        out_shape=struct(*base.shape),
        scratch_shapes=[
            pltpu.VMEM(base.shape, jnp.float32),
            pltpu.VMEM((SIDES, columns, width), jnp.float32),
            pltpu.SemaphoreType.DMA((SPECIES, planes // 4)),
        ],
        compiler_params=params(8),
        name="spread",
    )(table, fades, base, lift, *parts)


def group_size(devices):
    size = 1
    while 4 * size * size <= 2 * devices and devices % (2 * size) == 0:
        size *= 2
    return size


def body(conc, influx, numbers, cross, kinetics):
    _, planes, columns, _ = conc.shape
    across, along = lax.axis_size("gx"), lax.axis_size("gy")
    group = group_size(across)
    share = columns // group
    rank = lax.axis_index("gx").astype(jnp.int32).reshape(1)
    conc, influx, numbers, cross, kinetics = (
        pltpu.with_memory_space_constraint(x, pltpu.HBM) for x in (conc, influx, numbers, cross, kinetics)
    )

    def turn(value, by):
        return lax.ppermute(value, "gy", [(i, (i + by) % along) for i in range(along)])

    def in_group(parts):
        pairs = [[(i, i ^ d) for i in range(across)] for d in range(group)]
        return [parts[0]] + [lax.ppermute(parts[d], "gx", pairs[d]) for d in range(1, group)]

    def over_groups(value, by):
        return lax.ppermute(value, "gx", [(i, (i + by * group) % across) for i in range(across)])

    *parts, table, conc, influx, y_table, z_table = edges(group, rank, numbers, cross, kinetics, conc, influx)
    parts = in_group(parts)
    h = sweeps(SPECIES - 1, table, conc, influx)
    whole = group_sums(planes, share, table, h[0], parts)
    wholes = [whole] + [over_groups(whole, j) for j in range(1, across // group)]
    *u, rough, sums = column_parts(table, y_table, z_table, conc, influx, h)
    *outs, sums = entering(planes, share, table, sums, parts, wholes)
    outs = in_group(outs)
    base = finish(table, z_table, conc, u, rough)
    turns = [0] + [k for k in range(1, along) if k % 2] + [k for k in range(1, along) if k % 2 == 0]
    base, lift, fades = inflow(turns, table, base, [turn(sums, k) if k else sums for k in turns])
    return spread(share, table, fades, base, lift, outs)


def solution(mesh):
    placed = (P(None, "gx", "gy", None), P("gx", "gy", None), P(), P(), P())
    return jax.shard_map(
        body, mesh=mesh, in_specs=placed, out_specs=P(None, "gx", "gy", None), check_vma=False
    )
```

```python
import functools

import jax
import jax.numpy as jnp
from jax import lax
from jax.experimental import pallas as pl
from jax.experimental.pallas import tpu as pltpu
from jax.sharding import PartitionSpec as P

SPECIES = 3
ROWS = 8
SIDES = 2
CORNERS = SIDES * SIDES * SPECIES
SMEM = pl.BlockSpec(memory_space=pltpu.SMEM)
VMEM = pl.BlockSpec(memory_space=pltpu.VMEM)
ANY = pl.BlockSpec(memory_space=pl.ANY)

RATE_X, RATE_Y, SCALE_Y, SCALE_X, DECAY, KINETICS, MEMBER = 0, 3, 6, 9, 12, 15, 18
INNER, DOUBLE, PART_A, PART_B, TABLE_ROWS = 19, 28, 37, 46, 56


def padded(rows):
    return -(-rows // ROWS) * ROWS


def params(mebibytes):
    return pltpu.CompilerParams(vmem_limit_bytes=mebibytes * 2**20)


def struct(*shape):
    return jax.ShapeDtypeStruct(shape, jnp.float32)


def decay_rate(number):
    half = 0.5 * lax.rsqrt(number)
    square = half * half
    return 2.0 * jnp.log1p(half + square / (1.0 + jnp.sqrt(1.0 + square)))


def scaling(number):
    return lax.rsqrt(1.0 + 4.0 * number)


def splat(value, shape):
    return jnp.full(shape, value, jnp.float32)


def split(value):
    high = value.astype(jnp.bfloat16)
    return high, (value - high.astype(jnp.float32)).astype(jnp.bfloat16)


def left_pair(value):
    return jnp.concatenate(split(value), axis=1)


def right_pair(value):
    high, low = split(value)
    return jnp.concatenate(
        [jnp.concatenate([high, low], axis=1), jnp.concatenate([high, jnp.zeros_like(low)], axis=1)], axis=0
    )


def product(left, right):
    both = jnp.dot(left, right, preferred_element_type=jnp.float32)
    width = both.shape[1] // 2
    return both[:, :width] + both[:, width:]


def distances(length):
    rows = lax.broadcasted_iota(jnp.int32, (length, length), 0)
    columns = lax.broadcasted_iota(jnp.int32, (length, length), 1)
    return jnp.abs(rows - columns).astype(jnp.float32)


def depth_table(number, length):
    number = splat(number, (1, length))
    theta = decay_rate(number)
    spread = distances(length)
    factor = scaling(number) / (1.0 - jnp.exp(-length * theta))
    return (jnp.exp(-spread * theta) + jnp.exp((spread - length) * theta)) * factor


def column_table(number, length):
    number = splat(number, (1, length))
    return jnp.exp(-distances(length) * decay_rate(number)) * scaling(number)


def row_position(length, width):
    return lax.broadcasted_iota(jnp.int32, (length, width), 0).astype(jnp.float32)


def coefficients(numbers, cross, kinetics, tile):
    n = [[splat(numbers[s, d], tile) for d in range(3)] for s in range(SPECIES)]
    along_x, along_y, along_z = [], [], []
    for s in range(SPECIES):
        per_x, per_y = 1.0 / n[s][0], 1.0 / n[s][1]
        for j in range(SPECIES):
            mix = 1.0 if j == s else cross[s, j]
            along_x.append(n[j][0] * per_x * mix)
            along_y.append(n[j][1] * per_y * mix)
            along_z.append(n[j][2] * mix)
    scale = [scaling(n[s][0]) for s in range(SPECIES)]
    rate = [decay_rate(n[s][0]) for s in range(SPECIES)]
    return along_x, along_y, along_z, scale, rate, [splat(kinetics[i], tile) for i in range(3)]


def turned(value):
    width = value.shape[1]
    return pltpu.roll(value, 1, 1) + pltpu.roll(value, width - 1, 1)


def weighted(weights, refs, here):
    return sum(weight * ref[here, :] for weight, ref in zip(weights, refs))


def tiles(table, first, count, tile):
    return [jnp.broadcast_to(table[at : at + 1], tile) for at in range(first, first + count)]


def rates(c, influx, kinetics):
    bind, unbind, pump = kinetics
    binding = bind * c[0] * c[1] - unbind * c[2]
    pumping = pump * c[0] / (1.0 + c[0])
    return influx - 4.0 * binding - pumping, binding


def side_by_side(counts, steps):
    common = min(counts)

    def together(k, carry):
        for step in steps:
            step(k)
        return carry

    lax.fori_loop(0, common, together, 0, unroll=2 if common % 2 == 0 else 1)
    for count, step in zip(counts, steps):
        if count > common:
            lax.fori_loop(common, count, lambda k, carry, step=step: (step(k), carry)[1], 0)


def sweep_of_b(s, table, conc, out, k):
    _, planes, _, width = conc.shape
    tile = (ROWS, width)
    here = pl.ds(pl.multiple_of(k * ROWS, ROWS), ROWS)
    weight = tiles(table, PART_B + s * SPECIES, SPECIES, tile)
    (decay,) = tiles(table, DECAY + s, 1, tile)
    up, sources, rising = jnp.zeros(tile, jnp.float32), [], []
    for i in range(planes):
        b = weight[0] * conc[0, i, here, :] + weight[1] * conc[1, i, here, :] + weight[2] * conc[2, i, here, :]
        up = b + decay * up
        sources.append(b)
        rising.append(up)
    down = jnp.zeros(tile, jnp.float32)
    for i in reversed(range(planes)):
        down = decay * down
        out[i, here, :] = rising[i] + down
        down = down + sources[i]


def edge_kernel(group, rank_far, numbers_far, cross_far, kinetics_far, conc_far, influx_far, *refs):
    sent, refs = refs[:group], refs[group:]
    table, conc, influx, y_table, z_table, weights, hold, deep, solved, corners, arrived = refs[:11]
    rank, numbers, cross, kinetics, small = refs[11:]
    planes, columns, width = influx.shape
    chunks = arrived.shape[1]
    chunk = columns // chunks
    half = planes // 2
    share = columns // group
    tile = (ROWS, width)

    def copies(k):
        part = pl.ds(k * chunk, chunk)
        return (
            pltpu.make_async_copy(conc_far.at[:, :, part, :], conc.at[:, :, part, :], arrived.at[0, k]),
            pltpu.make_async_copy(influx_far.at[:, part, :], influx.at[:, part, :], arrived.at[1, k]),
        )

    for k in range(chunks):
        for copy in copies(k):
            copy.start()
    fars = (rank_far, numbers_far, cross_far, kinetics_far)
    nears = (rank, numbers, cross, kinetics)
    scalars = [pltpu.make_async_copy(far, near, small.at[k]) for k, (far, near) in enumerate(zip(fars, nears))]
    for copy in scalars:
        copy.start()
    for copy in scalars:
        copy.wait()

    along_x, along_y, along_z, scale, rate, kinetic = coefficients(numbers, cross, kinetics, tile)
    inner, double, single = [], [], []
    for s in range(SPECIES):
        for at in range(s * SPECIES, (s + 1) * SPECIES):
            inner.append((along_x[at] + along_y[at] - 2.0 * along_z[at]) * scale[s])
            double.append(along_z[at] * scale[s])
            single.append(along_y[at] * scale[s])
        for i in range(half):
            near = jnp.exp(-i * rate[s])
            far = jnp.exp(-(planes - 1.0 - i) * rate[s])
            weights[s, i, 0] = 0.5 * (near + far)
            weights[s, i, 1] = 0.5 * (near - far)
        number = splat(numbers[s, 1], tile)
        table[RATE_Y + s : RATE_Y + s + 1] = decay_rate(number)[:1]
        table[SCALE_Y + s : SCALE_Y + s + 1] = scaling(number)[:1]
        y_table[s] = left_pair(column_table(numbers[s, 1], columns))
        z_table[s] = right_pair(depth_table(numbers[s, 2], width))
    member = lax.rem(rank[0], group)
    entries = (
        (RATE_X, rate),
        (SCALE_X, scale),
        (DECAY, [jnp.exp(-value) for value in rate]),
        (KINETICS, kinetic),
        (MEMBER, [splat(member.astype(jnp.float32), tile)]),
        (INNER, inner),
        (DOUBLE, double),
        (PART_A, along_x),
        (PART_B, single),
    )
    for first, values in entries:
        for k, value in enumerate(values):
            table[first + k : first + k + 1] = value[:1]

    def sums_of(start):
        here = slice(start, start + ROWS)

        def at_plane(i):
            c = [conc[j, i, here, :] for j in range(SPECIES)]
            return c, *rates(c, influx[i, here, :], kinetic)

        zero = jnp.zeros(tile, jnp.float32)
        plus = [[zero] * (SPECIES + 1) for _ in range(SPECIES)]
        minus = [[zero] * (SPECIES + 1) for _ in range(SPECIES)]
        for i in range(half):
            low, low_first, low_binding = at_plane(i)
            high, high_first, high_binding = at_plane(planes - 1 - i)
            both = [x + y for x, y in zip(low, high)]
            apart = [x - y for x, y in zip(low, high)]
            change = (low_first + high_first, low_binding + high_binding)
            turn = (low_first - high_first, low_binding - high_binding)
            for s in range(SPECIES):
                even, odd = weights[s, i, 0], weights[s, i, 1]
                of = min(s, 1)
                for j, (p, m) in enumerate(zip(both + [change[of]], apart + [turn[of]])):
                    plus[s][j] = plus[s][j] + even * p
                    minus[s][j] = minus[s][j] + odd * m
        for s in range(SPECIES):
            for e in range(SIDES):
                sums = [p + m if e else p - m for p, m in zip(plus[s], minus[s])]
                v = sums[SPECIES] * scale[s]
                if s == 1:
                    v = -v
                w = 0.0
                for j in range(SPECIES):
                    at = s * SPECIES + j
                    v = v + inner[at] * sums[j] + double[at] * turned(sums[j])
                    w = w + single[at] * sums[j]
                hold[s, e, here, :] = v
                hold[s, SIDES + e, here, :] = w

    def deepen(k):
        here = slice(k * chunk, (k + 1) * chunk)
        for s in range(SPECIES):
            stack = jnp.concatenate([hold[s, e, here, :] for e in range(2 * SIDES)], axis=0)
            done = product(left_pair(stack), z_table[s])
            for e in range(2 * SIDES):
                deep[s, e, here, :] = done[e * chunk : (e + 1) * chunk]

    for k in range(chunks):
        for copy in copies(k):
            copy.wait()
        if k:
            deepen(k - 1)
        for start in range(k * chunk, (k + 1) * chunk, ROWS):
            sums_of(start)
    deepen(chunks - 1)

    row = row_position(columns, width)
    for s in range(SPECIES):
        theta = table[RATE_Y + s : RATE_Y + s + 1]
        rise = jnp.exp((row - (columns - 1.0)) * theta)
        fall = jnp.exp(-row * theta)
        both = product(y_table[s], right_pair(jnp.concatenate([deep[s, e] for e in range(SIDES)], axis=1)))
        for e in range(SIDES):
            solved[e, s] = both[:, e * width : (e + 1) * width] - deep[s, SIDES + e]
            for f, weight in enumerate((rise, fall)):
                at = (f * SIDES + e) * SPECIES + s
                corners[at : at + 1] = jnp.sum(weight * deep[s, e], axis=0, keepdims=True)
    for d in range(group):
        start = pl.multiple_of(lax.bitwise_xor(member, jnp.int32(d)) * share, share)
        for s in range(SPECIES):
            for e in range(SIDES):
                sent[d][pl.ds((e * SPECIES + s) * share, share), :] = solved[e, s, pl.ds(start, share), :]
        sent[d][pl.ds(SIDES * SPECIES * share, corners.shape[0]), :] = corners[...]


def edges(group, rank, numbers, cross, kinetics, conc, influx):
    _, planes, columns, width = conc.shape
    chunks = columns // (2 * ROWS)
    hold = pltpu.VMEM((SPECIES, 2 * SIDES, columns, width), jnp.float32)
    rows = SIDES * SPECIES * (columns // group) + padded(CORNERS)
    return pl.pallas_call(
        functools.partial(edge_kernel, group),
        in_specs=[ANY] * 6,
        out_specs=[VMEM] * (group + 5),
        out_shape=[struct(rows, width)] * group
        + [
            pltpu.VMEM((TABLE_ROWS, width), jnp.float32),
            pltpu.VMEM(conc.shape, jnp.float32),
            pltpu.VMEM(influx.shape, jnp.float32),
            pltpu.VMEM((SPECIES, columns, 2 * columns), jnp.bfloat16),
            pltpu.VMEM((SPECIES, 2 * width, 2 * width), jnp.bfloat16),
        ],
        scratch_shapes=[
            pltpu.VMEM((SPECIES, planes // 2, 2, ROWS, width), jnp.float32),
            hold,
            hold,
            pltpu.VMEM((SIDES, SPECIES, columns, width), jnp.float32),
            pltpu.VMEM((padded(CORNERS), width), jnp.float32),
            pltpu.SemaphoreType.DMA((2, chunks)),
            pltpu.SMEM(rank.shape, rank.dtype),
            pltpu.SMEM(numbers.shape, numbers.dtype),
            pltpu.SMEM(cross.shape, cross.dtype),
            pltpu.SMEM(kinetics.shape, kinetics.dtype),
            pltpu.SemaphoreType.DMA((4,)),
        ],
        compiler_params=params(16),
        name="edges",
    )(rank, numbers, cross, kinetics, conc, influx)


def sweep_kernel(table, conc, influx, *refs):
    count = SPECIES - 1
    outs, roughs, g_hold = refs[:count], refs[count:-1], refs[-1]
    planes, columns, width = influx.shape
    tile = (ROWS, width)
    inner = tiles(table, INNER, count * SPECIES, tile)
    double = tiles(table, DOUBLE, count * SPECIES, tile)
    part_a = tiles(table, PART_A, count * SPECIES, tile)
    scale = tiles(table, SCALE_X, count, tile)
    decay = tiles(table, DECAY, count, tile)
    kinetic = tiles(table, KINETICS, 3, tile)

    def rows(k, carry):
        here = pl.ds(pl.multiple_of(k * ROWS, ROWS), ROWS)
        up = [jnp.zeros(tile, jnp.float32) for _ in range(count)]
        for i in range(planes):
            c = [conc[j, i, here, :] for j in range(SPECIES)]
            around = [turned(value) for value in c]
            first, binding = rates(c, influx[i, here, :], kinetic)
            change = (first, -binding, binding)
            for s in range(count):
                g = change[s] * scale[s]
                a = c[s]
                for j in range(SPECIES):
                    at = s * SPECIES + j
                    g = g + inner[at] * c[j] + double[at] * around[j]
                    if j != s:
                        a = a + part_a[at] * c[j]
                up[s] = g + decay[s] * up[s]
                g_hold[s, i] = g
                outs[s][i, here, :] = up[s] - a
        for s in range(count):
            down = jnp.zeros(tile, jnp.float32)
            for i in reversed(range(planes)):
                down = decay[s] * down
                outs[s][i, here, :] += down
                down += g_hold[s, i]
        for s, rough in enumerate(roughs, 1):
            sweep_of_b(s, table, conc, rough, k)
        return carry

    lax.fori_loop(0, columns // ROWS, rows, 0)


def sweeps(table, conc, influx):
    count, planes, width = SPECIES - 1, influx.shape[0], influx.shape[2]
    return pl.pallas_call(
        sweep_kernel,
        in_specs=[VMEM] * 3,
        out_specs=[VMEM] * (2 * count),
        out_shape=[pltpu.VMEM(influx.shape, jnp.float32)] * (2 * count),
        scratch_shapes=[pltpu.VMEM((count, planes, ROWS, width), jnp.float32)],
        compiler_params=params(8),
        cost_estimate=pl.CostEstimate(flops=100 * conc.size, bytes_accessed=14 * conc.size, transcendentals=0),
        name="sweeps",
    )(table, conc, influx)


def partner(member, d):
    return lax.bitwise_xor(member.astype(jnp.int32), jnp.int32(d)).astype(jnp.float32)


def group_kernel(planes, share, table, after, *refs):
    parts, out = refs[:-1], refs[-1]
    group = len(parts)
    corners = SIDES * SPECIES * share
    member = table[MEMBER : MEMBER + 1]
    blocks = [partner(member, d) for d in range(group)]
    for s in range(SPECIES):
        theta = planes * table[RATE_X + s : RATE_X + s + 1]
        for e in range(SIDES):
            weight = [jnp.exp((-b if e else b - (group - 1.0)) * theta) for b in blocks]
            here = pl.ds((e * SPECIES + s) * share, share)
            out[here, :] = sum(weight[d] * parts[d][here, :] for d in range(group))
            for k in range(SIDES):
                here = pl.ds(corners + (k * SIDES + e) * SPECIES + s, 1)
                out[here, :] = sum(weight[d] * parts[d][here, :] for d in range(group))


def group_sums(planes, share, table, after, parts):
    return pl.pallas_call(
        functools.partial(group_kernel, planes, share),
        in_specs=[VMEM, ANY] + [VMEM] * len(parts),
        out_specs=VMEM,
        out_shape=struct(*parts[0].shape),
        compiler_params=params(8),
        name="group_sums",
    )(table, after, *parts)


def column_kernel(table, y_table, z_table, conc, influx, *refs):
    count = SPECIES - 1
    h, u, (rough, y_out, last, weights, sums) = refs[:count], refs[count : count + SPECIES], refs[count + SPECIES :]
    planes, columns, width = influx.shape
    tile = (ROWS, width)
    row = row_position(columns, width)
    for s in range(SPECIES):
        theta = table[RATE_Y + s : RATE_Y + s + 1]
        weights[s, 0] = jnp.exp((row - (columns - 1.0)) * theta)
        weights[s, 1] = jnp.exp(-row * theta)
    inner = tiles(table, INNER + count * SPECIES, SPECIES, tile)
    double = tiles(table, DOUBLE + count * SPECIES, SPECIES, tile)
    part_a = tiles(table, PART_A + count * SPECIES, SPECIES, tile)
    (scale,) = tiles(table, SCALE_X + count, 1, tile)
    (decay,) = tiles(table, DECAY + count, 1, tile)
    bind, unbind, _ = tiles(table, KINETICS, 3, tile)

    def plane_of(s, value, i):
        for e in range(SIDES):
            sums[s, e, pl.ds(i, 1), :] = jnp.sum(weights[s, e] * value, axis=0, keepdims=True)
        u[s][i] = product(y_table[s], right_pair(value))

    def plane(i):
        for s in range(count):
            plane_of(s, h[s][i], i)

    def rows(k):
        here = pl.ds(pl.multiple_of(k * ROWS, ROWS), ROWS)
        up, sources, rising = jnp.zeros(tile, jnp.float32), [], []
        for i in range(planes):
            c = [conc[j, i, here, :] for j in range(SPECIES)]
            g = (bind * c[0] * c[1] - unbind * c[2]) * scale
            a = c[count]
            for j in range(SPECIES):
                g = g + inner[j] * c[j] + double[j] * turned(c[j])
                if j != count:
                    a = a + part_a[j] * c[j]
            up = g + decay * up
            sources.append(g)
            rising.append(up - a)
        down = jnp.zeros(tile, jnp.float32)
        for i in reversed(range(planes)):
            down = decay * down
            last[i, here, :] = rising[i] + down
            down = down + sources[i]

    side_by_side((planes, columns // ROWS), (plane, rows))
    side_by_side(
        (planes, columns // ROWS),
        (lambda i: plane_of(count, last[i], i), lambda k: sweep_of_b(0, table, conc, rough, k)),
    )
    for s in range(SPECIES):
        both = jnp.concatenate([sums[s, e] for e in range(SIDES)], axis=0)
        both = product(left_pair(both), z_table[s])
        for e in range(SIDES):
            y_out[pl.ds((e * SPECIES + s) * planes, planes), :] = both[e * planes : (e + 1) * planes]


def column_parts(table, y_table, z_table, conc, influx, h):
    planes, columns, width = influx.shape
    return pl.pallas_call(
        column_kernel,
        in_specs=[VMEM] * (5 + len(h)),
        out_specs=[VMEM] * (SPECIES + 2),
        out_shape=[pltpu.VMEM(influx.shape, jnp.float32)] * (SPECIES + 1)
        + [pltpu.VMEM((SIDES * SPECIES * planes, width), jnp.float32)],
        scratch_shapes=[
            pltpu.VMEM(influx.shape, jnp.float32),
            pltpu.VMEM((SPECIES, SIDES, columns, width), jnp.float32),
            pltpu.VMEM((SPECIES, SIDES, planes, width), jnp.float32),
        ],
        compiler_params=params(8),
        cost_estimate=pl.CostEstimate(flops=6 * conc.size * columns, bytes_accessed=8 * conc.size, transcendentals=0),
        name="column_parts",
    )(table, y_table, z_table, conc, influx, *h)


def finish_kernel(table, z_table, conc, *refs):
    u, rough, (out, weights, fades) = refs[:SPECIES], refs[SPECIES : 2 * SPECIES], refs[2 * SPECIES :]
    _, planes, columns, width = conc.shape
    at_once = 4 if planes % 4 == 0 else 1
    row = row_position(columns, width)
    position = row_position(planes, width)
    for s in range(SPECIES):
        rate_x = table[RATE_X + s : RATE_X + s + 1]
        rate_y = table[RATE_Y + s : RATE_Y + s + 1]
        weights[s, 0] = jnp.exp(-(row + 1.0) * rate_y)
        weights[s, 1] = jnp.exp((row - columns) * rate_y)
        fades[s, 0] = jnp.exp(-(position + 1.0) * rate_x)
        fades[s, 1] = jnp.exp((position - planes) * rate_x)
        for first in range(0, planes, at_once):
            here = slice(first, first + at_once)
            value = (u[s][here] - rough[s][here]).reshape(at_once * columns, width)
            done = product(left_pair(value), z_table[s])
            out[s, here] = conc[s, here] + done.reshape(at_once, columns, width)


def finish(table, z_table, conc, u, rough):
    _, planes, columns, width = conc.shape
    return pl.pallas_call(
        finish_kernel,
        in_specs=[VMEM] * (3 + len(u) + len(rough)),
        out_specs=[VMEM] * 3,
        out_shape=[
            pltpu.VMEM(conc.shape, jnp.float32),
            pltpu.VMEM((SPECIES, SIDES, columns, width), jnp.float32),
            pltpu.VMEM((SPECIES, SIDES, planes, width), jnp.float32),
        ],
        compiler_params=params(8),
        cost_estimate=pl.CostEstimate(flops=6 * conc.size * width, bytes_accessed=12 * conc.size, transcendentals=0),
        name="finish",
    )(table, z_table, conc, *u, *rough)


def enter_kernel(group, planes, share, table, sums, *refs):
    parts, wholes, outs, y_out = refs[:group], refs[group : -group - 1], refs[-group - 1 : -1], refs[-1]
    groups = len(wholes)
    corners = SIDES * SPECIES * share
    member = table[MEMBER : MEMBER + 1]
    blocks = [partner(member, d) for d in range(group)]
    y_out[pl.ds(0, sums.shape[0]), :] = sums[...]

    for s in range(SPECIES):
        theta = planes * table[RATE_X + s : RATE_X + s + 1]
        closing = 1.0 / (1.0 - jnp.exp(-float(group * groups) * theta))
        for e in range(SIDES):
            steps = [(groups - j - 1) if e else (j - 1 if j else groups - 1) for j in range(groups)]
            outside = [jnp.exp(-float(group * k) * theta) * closing for k in steps]
            to_target = [jnp.exp((t - (group - 1.0) if e else -t) * theta) for t in blocks]
            inside = []
            for t in blocks:
                away = [(b - t) if e else (t - b) for b in blocks]
                inside.append([jnp.where(k > 0.0, jnp.exp((1.0 - jnp.abs(k)) * theta), 0.0) for k in away])

            def entering_group(here):
                return sum(weight * whole[here, :] for weight, whole in zip(outside, wholes))

            here = pl.ds((e * SPECIES + s) * share, share)
            whole = entering_group(here)
            held = [part[here, :] for part in parts]
            for d in range(group):
                total = to_target[d] * whole
                for weight, part in zip(inside[d], held):
                    total = total + weight * part
                outs[d][here, :] = total

            for k in range(SIDES):
                at = (k * SIDES + e) * SPECIES + s
                here = pl.ds(corners + at, 1)
                total = to_target[0] * entering_group(here)
                for weight, part in zip(inside[0], parts):
                    total = total + weight * part[here, :]
                y_out[pl.ds(sums.shape[0] + at, 1), :] = total


def entering(planes, share, table, sums, parts, wholes):
    group, width = len(parts), parts[0].shape[1]
    return pl.pallas_call(
        functools.partial(enter_kernel, group, planes, share),
        in_specs=[VMEM] * (2 + group + len(wholes)),
        out_specs=[VMEM] * (group + 1),
        out_shape=[struct(SIDES * SPECIES * share, width)] * group + [struct(padded(sums.shape[0] + CORNERS), width)],
        compiler_params=params(8),
        name="entering",
    )(table, sums, *parts, *wholes)


def spread_kernel(turns, group, share, table, weights, fades, base, *refs):
    along = len(turns)
    parts, sums, (out_far, out, hold, enter, left) = refs[:group], refs[group : group + along], refs[group + along :]
    _, planes, columns, width = base.shape
    corners = SIDES * SPECIES * planes
    blocks = [partner(table[MEMBER : MEMBER + 1], d) for d in range(group)]
    at_once = planes // left.shape[1]
    copies = []
    for s in range(SPECIES):
        theta = columns * table[RATE_Y + s : RATE_Y + s + 1]
        closing = table[SCALE_Y + s : SCALE_Y + s + 1] / (1.0 - jnp.exp(-float(along) * theta))
        corner = []
        for e in range(SIDES):
            steps = [(along - k - 1) if e else (k - 1 if k else along - 1) for k in turns]
            arrive = [jnp.exp(-float(k) * theta) * closing for k in steps]
            enter[e] = weighted(arrive, sums, pl.ds((e * SPECIES + s) * planes, planes))
            corner.append([weighted(arrive, sums, pl.ds(corners + (e * SIDES + k) * SPECIES + s, 1)) for k in range(SIDES)])
        for e in range(SIDES):
            held = [part[pl.ds((e * SPECIES + s) * share, share), :] for part in parts]
            for b in range(group):
                there = pl.ds(b * share, share)
                mine = held[0]
                for d in range(1, group):
                    mine = jnp.where(blocks[d] == b, held[d], mine)
                lift = weights[s, 0, there, :] * corner[0][e] + weights[s, 1, there, :] * corner[1][e]
                hold[e, there, :] = mine + lift
        for first in range(0, planes, at_once):
            near = [[ref[i : i + 1] for i in range(first, first + at_once)] for ref in (fades.at[s, 0], fades.at[s, 1])]
            far = [[ref[i : i + 1] for i in range(first, first + at_once)] for ref in (enter.at[0], enter.at[1])]
            for start in range(0, columns, ROWS):
                here = slice(start, start + ROWS)
                x_low, x_high = hold[0, here, :], hold[1, here, :]
                y_low, y_high = weights[s, 0, here, :], weights[s, 1, here, :]
                for k in range(at_once):
                    added = near[0][k] * x_low + near[1][k] * x_high + far[0][k] * y_low + far[1][k] * y_high
                    out[s, first + k, here, :] = base[s, first + k, here, :] + added
            part = pl.ds(first, at_once)
            copies.append(pltpu.make_async_copy(out.at[s, part], out_far.at[s, part], left.at[s, first // at_once]))
            copies[-1].start()
    for copy in copies:
        copy.wait()


def spread(turns, share, table, weights, fades, base, sums, parts):
    _, planes, columns, width = base.shape
    return pl.pallas_call(
        functools.partial(spread_kernel, turns, len(parts), share),
        in_specs=[VMEM] * (4 + len(sums) + len(parts)),
        out_specs=ANY,
        out_shape=struct(*base.shape),
        scratch_shapes=[
            pltpu.VMEM(base.shape, jnp.float32),
            pltpu.VMEM((SIDES, columns, width), jnp.float32),
            pltpu.VMEM((SIDES, planes, width), jnp.float32),
            pltpu.SemaphoreType.DMA((SPECIES, planes // 4 if planes % 4 == 0 else planes)),
        ],
        compiler_params=params(8),
        name="spread",
    )(table, weights, fades, base, *parts, *sums)


def group_size(devices):
    size = 1
    while 4 * size * size <= 2 * devices and devices % (2 * size) == 0:
        size *= 2
    return size


def body(conc, influx, numbers, cross, kinetics):
    _, planes, columns, _ = conc.shape
    across, along = lax.axis_size("gx"), lax.axis_size("gy")
    group = group_size(across)
    share = columns // group
    rank = lax.axis_index("gx").astype(jnp.int32).reshape(1)
    conc, influx, numbers, cross, kinetics = (
        pltpu.with_memory_space_constraint(x, pltpu.HBM) for x in (conc, influx, numbers, cross, kinetics)
    )

    def turn(value, by):
        return lax.ppermute(value, "gy", [(i, (i + by) % along) for i in range(along)])

    def in_group(parts):
        pairs = [[(i, i ^ d) for i in range(across)] for d in range(group)]
        return [parts[0]] + [lax.ppermute(parts[d], "gx", pairs[d]) for d in range(1, group)]

    def over_groups(value, by):
        return lax.ppermute(value, "gx", [(i, (i + by * group) % across) for i in range(across)])

    *parts, table, conc, influx, y_table, z_table = edges(group, rank, numbers, cross, kinetics, conc, influx)
    parts = in_group(parts)
    swept = sweeps(table, conc, influx)
    h, rough = swept[: SPECIES - 1], swept[SPECIES - 1 :]
    whole = group_sums(planes, share, table, h[0], parts)
    wholes = [whole] + [over_groups(whole, j) for j in range(1, across // group)]
    *u, rough_first, sums = column_parts(table, y_table, z_table, conc, influx, h)
    *outs, sums = entering(planes, share, table, sums, parts, wholes)
    outs = in_group(outs)
    base, weights, fades = finish(table, z_table, conc, u, [rough_first, *rough])
    turns = [0] + [k for k in range(1, along) if k % 2] + [k for k in range(1, along) if k % 2 == 0]
    sums = [turn(sums, k) if k else sums for k in turns]
    return spread(turns, share, table, weights, fades, base, sums, outs)


def solution(mesh):
    placed = (P(None, "gx", "gy", None), P("gx", "gy", None), P(), P(), P())
    return jax.shard_map(
        body, mesh=mesh, in_specs=placed, out_specs=P(None, "gx", "gy", None), check_vma=False
    )
```

```python
import functools

import jax
import jax.numpy as jnp
from jax import lax
from jax.experimental import pallas as pl
from jax.experimental.pallas import tpu as pltpu
from jax.sharding import PartitionSpec as P

SPECIES = 3
ROWS = 8
SIDES = 2
CORNERS = SIDES * SIDES * SPECIES
SMEM = pl.BlockSpec(memory_space=pltpu.SMEM)
VMEM = pl.BlockSpec(memory_space=pltpu.VMEM)
ANY = pl.BlockSpec(memory_space=pl.ANY)

RATE_X, RATE_Y, SCALE_Y, SCALE_X, DECAY, KINETICS, MEMBER = 0, 3, 6, 9, 12, 15, 18
INNER, DOUBLE, PART_A, PART_B, RANK_Y, TABLE_ROWS = 19, 28, 37, 46, 55, 56


def padded(rows):
    return -(-rows // ROWS) * ROWS


def params(mebibytes):
    return pltpu.CompilerParams(vmem_limit_bytes=mebibytes * 2**20)


def struct(*shape):
    return jax.ShapeDtypeStruct(shape, jnp.float32)


def decay_rate(number):
    half = 0.5 * lax.rsqrt(number)
    square = half * half
    return 2.0 * jnp.log1p(half + square / (1.0 + jnp.sqrt(1.0 + square)))


def scaling(number):
    return lax.rsqrt(1.0 + 4.0 * number)


def splat(value, shape):
    return jnp.full(shape, value, jnp.float32)


def split(value):
    high = value.astype(jnp.bfloat16)
    return high, (value - high.astype(jnp.float32)).astype(jnp.bfloat16)


def left_pair(value):
    return jnp.concatenate(split(value), axis=1)


def right_pair(value):
    high, low = split(value)
    return jnp.concatenate(
        [jnp.concatenate([high, low], axis=1), jnp.concatenate([high, jnp.zeros_like(low)], axis=1)], axis=0
    )


def product(left, right):
    both = jnp.dot(left, right, preferred_element_type=jnp.float32)
    width = both.shape[1] // 2
    return both[:, :width] + both[:, width:]


def distances(length):
    rows = lax.broadcasted_iota(jnp.int32, (length, length), 0)
    columns = lax.broadcasted_iota(jnp.int32, (length, length), 1)
    return jnp.abs(rows - columns).astype(jnp.float32)


def depth_table(number, length):
    number = splat(number, (1, length))
    theta = decay_rate(number)
    spread = distances(length)
    factor = scaling(number) / (1.0 - jnp.exp(-length * theta))
    return (jnp.exp(-spread * theta) + jnp.exp((spread - length) * theta)) * factor


def column_table(number, length):
    number = splat(number, (1, length))
    return jnp.exp(-distances(length) * decay_rate(number)) * scaling(number)


def row_position(length, width):
    return lax.broadcasted_iota(jnp.int32, (length, width), 0).astype(jnp.float32)


def coefficients(numbers, cross, kinetics, tile):
    n = [[splat(numbers[s, d], tile) for d in range(3)] for s in range(SPECIES)]
    along_x, along_y, along_z = [], [], []
    for s in range(SPECIES):
        per_x, per_y = 1.0 / n[s][0], 1.0 / n[s][1]
        for j in range(SPECIES):
            mix = 1.0 if j == s else cross[s, j]
            along_x.append(n[j][0] * per_x * mix)
            along_y.append(n[j][1] * per_y * mix)
            along_z.append(n[j][2] * mix)
    scale = [scaling(n[s][0]) for s in range(SPECIES)]
    rate = [decay_rate(n[s][0]) for s in range(SPECIES)]
    return along_x, along_y, along_z, scale, rate, [splat(kinetics[i], tile) for i in range(3)]


def turned(value):
    width = value.shape[1]
    return pltpu.roll(value, 1, 1) + pltpu.roll(value, width - 1, 1)


def weighted(weights, refs, here):
    return sum(weight * ref[here, :] for weight, ref in zip(weights, refs))


def tile_rows(k):
    return pl.ds(k * ROWS if isinstance(k, int) else pl.multiple_of(k * ROWS, ROWS), ROWS)


def tiles(table, first, count, tile):
    return [jnp.broadcast_to(table[at : at + 1], tile) for at in range(first, first + count)]


def rates(c, influx, kinetics):
    bind, unbind, pump = kinetics
    binding = bind * c[0] * c[1] - unbind * c[2]
    pumping = pump * c[0] / (1.0 + c[0])
    return influx - 4.0 * binding - pumping, binding


def side_by_side(counts, steps):
    for k in range(max(counts)):
        for count, step in zip(counts, steps):
            if k < count:
                step(k)


def sweep_of_b(s, table, conc, out, k):
    _, planes, _, width = conc.shape
    tile = (ROWS, width)
    here = tile_rows(k)
    weight = tiles(table, PART_B + s * SPECIES, SPECIES, tile)
    (decay,) = tiles(table, DECAY + s, 1, tile)
    up, sources, rising = jnp.zeros(tile, jnp.float32), [], []
    for i in range(planes):
        b = weight[0] * conc[0, i, here, :] + weight[1] * conc[1, i, here, :] + weight[2] * conc[2, i, here, :]
        up = b + decay * up
        sources.append(b)
        rising.append(up)
    down = jnp.zeros(tile, jnp.float32)
    for i in reversed(range(planes)):
        down = decay * down
        out[i, here, :] = rising[i] + down
        down = down + sources[i]


def edge_kernel(group, rank_far, numbers_far, cross_far, kinetics_far, conc_far, influx_far, *refs):
    sent, refs = refs[:group], refs[group:]
    table, conc, influx, y_table, z_table, weights, hold, deep, solved, corners, arrived = refs[:11]
    rank, numbers, cross, kinetics, small = refs[11:]
    planes, columns, width = influx.shape
    chunks = arrived.shape[1]
    chunk = columns // chunks
    half = planes // 2
    share = columns // group
    tile = (ROWS, width)

    def copies(k):
        part = pl.ds(k * chunk, chunk)
        return (
            pltpu.make_async_copy(conc_far.at[:, :, part, :], conc.at[:, :, part, :], arrived.at[0, k]),
            pltpu.make_async_copy(influx_far.at[:, part, :], influx.at[:, part, :], arrived.at[1, k]),
        )

    for k in range(chunks):
        for copy in copies(k):
            copy.start()
    fars = (rank_far, numbers_far, cross_far, kinetics_far)
    nears = (rank, numbers, cross, kinetics)
    scalars = [pltpu.make_async_copy(far, near, small.at[k]) for k, (far, near) in enumerate(zip(fars, nears))]
    for copy in scalars:
        copy.start()
    for copy in scalars:
        copy.wait()

    along_x, along_y, along_z, scale, rate, kinetic = coefficients(numbers, cross, kinetics, tile)
    inner, double, single = [], [], []
    for s in range(SPECIES):
        for at in range(s * SPECIES, (s + 1) * SPECIES):
            inner.append((along_x[at] + along_y[at] - 2.0 * along_z[at]) * scale[s])
            double.append(along_z[at] * scale[s])
            single.append(along_y[at] * scale[s])
        for i in range(half):
            near = jnp.exp(-i * rate[s])
            far = jnp.exp(-(planes - 1.0 - i) * rate[s])
            weights[s, i, 0] = 0.5 * (near + far)
            weights[s, i, 1] = 0.5 * (near - far)
        number = splat(numbers[s, 1], tile)
        table[RATE_Y + s : RATE_Y + s + 1] = decay_rate(number)[:1]
        table[SCALE_Y + s : SCALE_Y + s + 1] = scaling(number)[:1]
        y_table[s] = left_pair(column_table(numbers[s, 1], columns))
        z_table[s] = right_pair(depth_table(numbers[s, 2], width))
    member = lax.rem(rank[0], group)
    entries = (
        (RATE_X, rate),
        (SCALE_X, scale),
        (DECAY, [jnp.exp(-value) for value in rate]),
        (KINETICS, kinetic),
        (MEMBER, [splat(member.astype(jnp.float32), tile)]),
        (RANK_Y, [splat(rank[1].astype(jnp.float32), tile)]),
        (INNER, inner),
        (DOUBLE, double),
        (PART_A, along_x),
        (PART_B, single),
    )
    for first, values in entries:
        for k, value in enumerate(values):
            table[first + k : first + k + 1] = value[:1]

    def sums_of(start):
        here = slice(start, start + ROWS)

        def at_plane(i):
            c = [conc[j, i, here, :] for j in range(SPECIES)]
            return c, *rates(c, influx[i, here, :], kinetic)

        zero = jnp.zeros(tile, jnp.float32)
        plus = [[zero] * (SPECIES + 1) for _ in range(SPECIES)]
        minus = [[zero] * (SPECIES + 1) for _ in range(SPECIES)]
        for i in range(half):
            low, low_first, low_binding = at_plane(i)
            high, high_first, high_binding = at_plane(planes - 1 - i)
            both = [x + y for x, y in zip(low, high)]
            apart = [x - y for x, y in zip(low, high)]
            change = (low_first + high_first, low_binding + high_binding)
            turn = (low_first - high_first, low_binding - high_binding)
            for s in range(SPECIES):
                even, odd = weights[s, i, 0], weights[s, i, 1]
                of = min(s, 1)
                for j, (p, m) in enumerate(zip(both + [change[of]], apart + [turn[of]])):
                    plus[s][j] = plus[s][j] + even * p
                    minus[s][j] = minus[s][j] + odd * m
        for s in range(SPECIES):
            for e in range(SIDES):
                sums = [p + m if e else p - m for p, m in zip(plus[s], minus[s])]
                v = sums[SPECIES] * scale[s]
                if s == 1:
                    v = -v
                w = 0.0
                for j in range(SPECIES):
                    at = s * SPECIES + j
                    v = v + inner[at] * sums[j] + double[at] * turned(sums[j])
                    w = w + single[at] * sums[j]
                hold[s, e, here, :] = v
                hold[s, SIDES + e, here, :] = w

    def deepen(k):
        here = slice(k * chunk, (k + 1) * chunk)
        for s in range(SPECIES):
            stack = jnp.concatenate([hold[s, e, here, :] for e in range(2 * SIDES)], axis=0)
            done = product(left_pair(stack), z_table[s])
            for e in range(2 * SIDES):
                deep[s, e, here, :] = done[e * chunk : (e + 1) * chunk]

    for k in range(chunks):
        for copy in copies(k):
            copy.wait()
        if k:
            deepen(k - 1)
        for start in range(k * chunk, (k + 1) * chunk, ROWS):
            sums_of(start)
    deepen(chunks - 1)

    row = row_position(columns, width)
    for s in range(SPECIES):
        theta = table[RATE_Y + s : RATE_Y + s + 1]
        rise = jnp.exp((row - (columns - 1.0)) * theta)
        fall = jnp.exp(-row * theta)
        both = product(y_table[s], right_pair(jnp.concatenate([deep[s, e] for e in range(SIDES)], axis=1)))
        for e in range(SIDES):
            solved[e, s] = both[:, e * width : (e + 1) * width] - deep[s, SIDES + e]
            for f, weight in enumerate((rise, fall)):
                at = (f * SIDES + e) * SPECIES + s
                corners[at : at + 1] = jnp.sum(weight * deep[s, e], axis=0, keepdims=True)
    for d in range(group):
        start = pl.multiple_of(lax.bitwise_xor(member, jnp.int32(d)) * share, share)
        for s in range(SPECIES):
            for e in range(SIDES):
                sent[d][pl.ds((e * SPECIES + s) * share, share), :] = solved[e, s, pl.ds(start, share), :]
        sent[d][pl.ds(SIDES * SPECIES * share, corners.shape[0]), :] = corners[...]


def edges(group, rank, numbers, cross, kinetics, conc, influx):
    _, planes, columns, width = conc.shape
    chunks = columns // (2 * ROWS)
    hold = pltpu.VMEM((SPECIES, 2 * SIDES, columns, width), jnp.float32)
    rows = SIDES * SPECIES * (columns // group) + padded(CORNERS)
    return pl.pallas_call(
        functools.partial(edge_kernel, group),
        in_specs=[ANY] * 6,
        out_specs=[VMEM] * (group + 5),
        out_shape=[struct(rows, width)] * group
        + [
            pltpu.VMEM((TABLE_ROWS, width), jnp.float32),
            pltpu.VMEM(conc.shape, jnp.float32),
            pltpu.VMEM(influx.shape, jnp.float32),
            pltpu.VMEM((SPECIES, columns, 2 * columns), jnp.bfloat16),
            pltpu.VMEM((SPECIES, 2 * width, 2 * width), jnp.bfloat16),
        ],
        scratch_shapes=[
            pltpu.VMEM((SPECIES, planes // 2, 2, ROWS, width), jnp.float32),
            hold,
            hold,
            pltpu.VMEM((SIDES, SPECIES, columns, width), jnp.float32),
            pltpu.VMEM((padded(CORNERS), width), jnp.float32),
            pltpu.SemaphoreType.DMA((2, chunks)),
            pltpu.SMEM(rank.shape, rank.dtype),
            pltpu.SMEM(numbers.shape, numbers.dtype),
            pltpu.SMEM(cross.shape, cross.dtype),
            pltpu.SMEM(kinetics.shape, kinetics.dtype),
            pltpu.SemaphoreType.DMA((4,)),
        ],
        compiler_params=params(16),
        name="edges",
    )(rank, numbers, cross, kinetics, conc, influx)


def sweep_kernel(table, conc, influx, *refs):
    count = SPECIES - 1
    outs, roughs, g_hold = refs[:count], refs[count:-1], refs[-1]
    planes, columns, width = influx.shape
    tile = (ROWS, width)
    inner = tiles(table, INNER, count * SPECIES, tile)
    double = tiles(table, DOUBLE, count * SPECIES, tile)
    part_a = tiles(table, PART_A, count * SPECIES, tile)
    scale = tiles(table, SCALE_X, count, tile)
    decay = tiles(table, DECAY, count, tile)
    kinetic = tiles(table, KINETICS, 3, tile)

    def rows(k, carry):
        here = pl.ds(pl.multiple_of(k * ROWS, ROWS), ROWS)
        up = [jnp.zeros(tile, jnp.float32) for _ in range(count)]
        for i in range(planes):
            c = [conc[j, i, here, :] for j in range(SPECIES)]
            around = [turned(value) for value in c]
            first, binding = rates(c, influx[i, here, :], kinetic)
            change = (first, -binding, binding)
            for s in range(count):
                g = change[s] * scale[s]
                a = c[s]
                for j in range(SPECIES):
                    at = s * SPECIES + j
                    g = g + inner[at] * c[j] + double[at] * around[j]
                    if j != s:
                        a = a + part_a[at] * c[j]
                up[s] = g + decay[s] * up[s]
                g_hold[s, i] = g
                outs[s][i, here, :] = up[s] - a
        for s in range(count):
            down = jnp.zeros(tile, jnp.float32)
            for i in reversed(range(planes)):
                down = decay[s] * down
                outs[s][i, here, :] += down
                down += g_hold[s, i]
        for s, rough in enumerate(roughs, 1):
            sweep_of_b(s, table, conc, rough, k)
        return carry

    lax.fori_loop(0, columns // ROWS, rows, 0)


def sweeps(table, conc, influx):
    count, planes, width = SPECIES - 1, influx.shape[0], influx.shape[2]
    return pl.pallas_call(
        sweep_kernel,
        in_specs=[VMEM] * 3,
        out_specs=[VMEM] * (2 * count),
        out_shape=[pltpu.VMEM(influx.shape, jnp.float32)] * (2 * count),
        scratch_shapes=[pltpu.VMEM((count, planes, ROWS, width), jnp.float32)],
        compiler_params=params(8),
        cost_estimate=pl.CostEstimate(flops=100 * conc.size, bytes_accessed=14 * conc.size, transcendentals=0),
        name="sweeps",
    )(table, conc, influx)


def partner(member, d):
    return lax.bitwise_xor(member.astype(jnp.int32), jnp.int32(d)).astype(jnp.float32)


def group_kernel(planes, share, table, after, *refs):
    parts, out = refs[:-1], refs[-1]
    group = len(parts)
    corners = SIDES * SPECIES * share
    member = table[MEMBER : MEMBER + 1]
    blocks = [partner(member, d) for d in range(group)]
    for s in range(SPECIES):
        theta = planes * table[RATE_X + s : RATE_X + s + 1]
        for e in range(SIDES):
            weight = [jnp.exp((-b if e else b - (group - 1.0)) * theta) for b in blocks]
            here = pl.ds((e * SPECIES + s) * share, share)
            out[here, :] = sum(weight[d] * parts[d][here, :] for d in range(group))
            for k in range(SIDES):
                here = pl.ds(corners + (k * SIDES + e) * SPECIES + s, 1)
                out[here, :] = sum(weight[d] * parts[d][here, :] for d in range(group))


def group_sums(planes, share, table, after, parts):
    return pl.pallas_call(
        functools.partial(group_kernel, planes, share),
        in_specs=[VMEM, ANY] + [VMEM] * len(parts),
        out_specs=VMEM,
        out_shape=struct(*parts[0].shape),
        compiler_params=params(8),
        name="group_sums",
    )(table, after, *parts)


def column_kernel(table, y_table, z_table, conc, influx, *refs):
    count = SPECIES - 1
    h, u, (rough, y_out, last, weights, sums) = refs[:count], refs[count : count + SPECIES], refs[count + SPECIES :]
    planes, columns, width = influx.shape
    tile = (ROWS, width)
    row = row_position(columns, width)
    for s in range(SPECIES):
        theta = table[RATE_Y + s : RATE_Y + s + 1]
        weights[s, 0] = jnp.exp((row - (columns - 1.0)) * theta)
        weights[s, 1] = jnp.exp(-row * theta)
    inner = tiles(table, INNER + count * SPECIES, SPECIES, tile)
    double = tiles(table, DOUBLE + count * SPECIES, SPECIES, tile)
    part_a = tiles(table, PART_A + count * SPECIES, SPECIES, tile)
    (scale,) = tiles(table, SCALE_X + count, 1, tile)
    (decay,) = tiles(table, DECAY + count, 1, tile)
    bind, unbind, _ = tiles(table, KINETICS, 3, tile)

    def plane_of(s, value, i):
        for e in range(SIDES):
            sums[s, e, i : i + 1, :] = jnp.sum(weights[s, e] * value, axis=0, keepdims=True)
        u[s][i] = product(y_table[s], right_pair(value))

    def plane(i):
        for s in range(count):
            plane_of(s, h[s][i], i)

    def rows(k):
        here = tile_rows(k)
        up, sources, rising = jnp.zeros(tile, jnp.float32), [], []
        for i in range(planes):
            c = [conc[j, i, here, :] for j in range(SPECIES)]
            g = (bind * c[0] * c[1] - unbind * c[2]) * scale
            a = c[count]
            for j in range(SPECIES):
                g = g + inner[j] * c[j] + double[j] * turned(c[j])
                if j != count:
                    a = a + part_a[j] * c[j]
            up = g + decay * up
            sources.append(g)
            rising.append(up - a)
        down = jnp.zeros(tile, jnp.float32)
        for i in reversed(range(planes)):
            down = decay * down
            last[i, here, :] = rising[i] + down
            down = down + sources[i]

    side_by_side((planes, columns // ROWS), (plane, rows))
    side_by_side(
        (planes, columns // ROWS),
        (lambda i: plane_of(count, last[i], i), lambda k: sweep_of_b(0, table, conc, rough, k)),
    )
    for s in range(SPECIES):
        both = jnp.concatenate([sums[s, e] for e in range(SIDES)], axis=0)
        both = product(left_pair(both), z_table[s])
        for e in range(SIDES):
            y_out[pl.ds((e * SPECIES + s) * planes, planes), :] = both[e * planes : (e + 1) * planes]


def column_parts(table, y_table, z_table, conc, influx, h):
    planes, columns, width = influx.shape
    return pl.pallas_call(
        column_kernel,
        in_specs=[VMEM] * (5 + len(h)),
        out_specs=[VMEM] * (SPECIES + 2),
        out_shape=[pltpu.VMEM(influx.shape, jnp.float32)] * (SPECIES + 1)
        + [pltpu.VMEM((SIDES * SPECIES * planes, width), jnp.float32)],
        scratch_shapes=[
            pltpu.VMEM(influx.shape, jnp.float32),
            pltpu.VMEM((SPECIES, SIDES, columns, width), jnp.float32),
            pltpu.VMEM((SPECIES, SIDES, planes, width), jnp.float32),
        ],
        compiler_params=params(8),
        cost_estimate=pl.CostEstimate(flops=6 * conc.size * columns, bytes_accessed=8 * conc.size, transcendentals=0),
        name="column_parts",
    )(table, y_table, z_table, conc, influx, *h)


def finish_kernel(table, z_table, conc, *refs):
    u, rough, (out, weights, fades) = refs[:SPECIES], refs[SPECIES : 2 * SPECIES], refs[2 * SPECIES :]
    _, planes, columns, width = conc.shape
    at_once = 4 if planes % 4 == 0 else 1
    row = row_position(columns, width)
    position = row_position(planes, width)
    for s in range(SPECIES):
        rate_x = table[RATE_X + s : RATE_X + s + 1]
        rate_y = table[RATE_Y + s : RATE_Y + s + 1]
        weights[s, 0] = jnp.exp(-(row + 1.0) * rate_y)
        weights[s, 1] = jnp.exp((row - columns) * rate_y)
        fades[s, 0] = jnp.exp(-(position + 1.0) * rate_x)
        fades[s, 1] = jnp.exp((position - planes) * rate_x)
        for first in range(0, planes, at_once):
            here = slice(first, first + at_once)
            value = (u[s][here] - rough[s][here]).reshape(at_once * columns, width)
            done = product(left_pair(value), z_table[s])
            out[s, here] = conc[s, here] + done.reshape(at_once, columns, width)


def finish(table, z_table, conc, u, rough):
    _, planes, columns, width = conc.shape
    return pl.pallas_call(
        finish_kernel,
        in_specs=[VMEM] * (3 + len(u) + len(rough)),
        out_specs=[VMEM] * 3,
        out_shape=[
            pltpu.VMEM(conc.shape, jnp.float32),
            pltpu.VMEM((SPECIES, SIDES, columns, width), jnp.float32),
            pltpu.VMEM((SPECIES, SIDES, planes, width), jnp.float32),
        ],
        compiler_params=params(8),
        cost_estimate=pl.CostEstimate(flops=6 * conc.size * width, bytes_accessed=12 * conc.size, transcendentals=0),
        name="finish",
    )(table, z_table, conc, *u, *rough)


def enter_kernel(group, planes, share, table, sums, *refs):
    parts, wholes, outs, y_out = refs[:group], refs[group : -group - 1], refs[-group - 1 : -1], refs[-1]
    groups = len(wholes)
    corners = SIDES * SPECIES * share
    member = table[MEMBER : MEMBER + 1]
    blocks = [partner(member, d) for d in range(group)]
    y_out[pl.ds(0, sums.shape[0]), :] = sums[...]

    for s in range(SPECIES):
        theta = planes * table[RATE_X + s : RATE_X + s + 1]
        closing = 1.0 / (1.0 - jnp.exp(-float(group * groups) * theta))
        for e in range(SIDES):
            steps = [(groups - j - 1) if e else (j - 1 if j else groups - 1) for j in range(groups)]
            outside = [jnp.exp(-float(group * k) * theta) * closing for k in steps]
            to_target = [jnp.exp((t - (group - 1.0) if e else -t) * theta) for t in blocks]
            inside = []
            for t in blocks:
                away = [(b - t) if e else (t - b) for b in blocks]
                inside.append([jnp.where(k > 0.0, jnp.exp((1.0 - jnp.abs(k)) * theta), 0.0) for k in away])

            def entering_group(here):
                return sum(weight * whole[here, :] for weight, whole in zip(outside, wholes))

            here = pl.ds((e * SPECIES + s) * share, share)
            whole = entering_group(here)
            held = [part[here, :] for part in parts]
            for d in range(group):
                total = to_target[d] * whole
                for weight, part in zip(inside[d], held):
                    total = total + weight * part
                outs[d][here, :] = total

            for k in range(SIDES):
                at = (k * SIDES + e) * SPECIES + s
                here = pl.ds(corners + at, 1)
                total = to_target[0] * entering_group(here)
                for weight, part in zip(inside[0], parts):
                    total = total + weight * part[here, :]
                y_out[pl.ds(sums.shape[0] + at, 1), :] = total


def entering(planes, share, table, sums, parts, wholes):
    group, width = len(parts), parts[0].shape[1]
    return pl.pallas_call(
        functools.partial(enter_kernel, group, planes, share),
        in_specs=[VMEM] * (2 + group + len(wholes)),
        out_specs=[VMEM] * (group + 1),
        out_shape=[struct(SIDES * SPECIES * share, width)] * group + [struct(padded(sums.shape[0] + CORNERS), width)],
        compiler_params=params(8),
        name="entering",
    )(table, sums, *parts, *wholes)


def y_rows(planes, s, e):
    corners = SIDES * SPECIES * planes
    return [pl.ds((e * SPECIES + s) * planes, planes)] + [
        pl.ds(corners + (e * SIDES + k) * SPECIES + s, 1) for k in range(SIDES)
    ]


def bits(table, stage):
    rank = table[RANK_Y : RANK_Y + 1].astype(jnp.int32)
    low = lax.bitwise_and(rank, jnp.int32(2**stage - 1)).astype(jnp.float32)
    return low, lax.bitwise_and(rank, jnp.int32(2**stage)) != 0


def pair_kernel(planes, columns, stage, table, mine, other, out):
    _, above = bits(table, stage)
    for s in range(SPECIES):
        far = jnp.exp(-float(columns * 2**stage) * table[RATE_Y + s : RATE_Y + s + 1])
        for e in range(SIDES):
            keep = jnp.where(above, far, 1.0) if e else jnp.where(above, 1.0, far)
            take = jnp.where(above, 1.0, far) if e else jnp.where(above, far, 1.0)
            for here in y_rows(planes, s, e):
                out[here, :] = keep * mine[here, :] + take * other[here, :]


def pair_sums(planes, columns, stage, table, mine, other):
    return pl.pallas_call(
        functools.partial(pair_kernel, planes, columns, stage),
        in_specs=[VMEM] * 3,
        out_specs=VMEM,
        out_shape=struct(*mine.shape),
        compiler_params=params(8),
        name="pair_sums",
    )(table, mine, other)


def y_weights(table, s, e, columns, stages):
    theta = columns * table[RATE_Y + s : RATE_Y + s + 1]
    along = 2**stages
    closing = table[SCALE_Y + s : SCALE_Y + s + 1] / (1.0 - jnp.exp(-float(along) * theta))
    weights = [jnp.exp(-(along - 1.0) * theta) * closing]
    for stage in range(stages):
        low, above = bits(table, stage)
        near = (2.0**stage - 1.0 - low) if e else low
        around = float(along - 2 ** (stage + 1))
        steps = near + (jnp.where(above, around, 0.0) if e else jnp.where(above, 0.0, around))
        weights.append(jnp.exp(-steps * theta) * closing)
    return weights


def spread_kernel(group, share, table, weights, fades, base, *refs):
    parts, sums, (out_far, out, hold, enter, left) = refs[:group], refs[group:-5], refs[-5:]
    _, planes, columns, width = base.shape
    blocks = [partner(table[MEMBER : MEMBER + 1], d) for d in range(group)]
    at_once = planes // left.shape[1]
    copies = []
    for s in range(SPECIES):
        corner = []
        for e in range(SIDES):
            arrive = y_weights(table, s, e, columns, len(sums) - 1)
            lines, *corner_lines = y_rows(planes, s, e)
            enter[e] = weighted(arrive, sums, lines)
            corner.append([weighted(arrive, sums, here) for here in corner_lines])
        for e in range(SIDES):
            held = [part[pl.ds((e * SPECIES + s) * share, share), :] for part in parts]
            for b in range(group):
                there = pl.ds(b * share, share)
                mine = held[0]
                for d in range(1, group):
                    mine = jnp.where(blocks[d] == b, held[d], mine)
                lift = weights[s, 0, there, :] * corner[0][e] + weights[s, 1, there, :] * corner[1][e]
                hold[e, there, :] = mine + lift
        for first in range(0, planes, at_once):
            near = [[ref[i : i + 1] for i in range(first, first + at_once)] for ref in (fades.at[s, 0], fades.at[s, 1])]
            far = [[ref[i : i + 1] for i in range(first, first + at_once)] for ref in (enter.at[0], enter.at[1])]
            for start in range(0, columns, ROWS):
                here = slice(start, start + ROWS)
                x_low, x_high = hold[0, here, :], hold[1, here, :]
                y_low, y_high = weights[s, 0, here, :], weights[s, 1, here, :]
                for k in range(at_once):
                    added = near[0][k] * x_low + near[1][k] * x_high + far[0][k] * y_low + far[1][k] * y_high
                    out[s, first + k, here, :] = base[s, first + k, here, :] + added
            part = pl.ds(first, at_once)
            copies.append(pltpu.make_async_copy(out.at[s, part], out_far.at[s, part], left.at[s, first // at_once]))
            copies[-1].start()
    for copy in copies:
        copy.wait()


def spread(share, table, weights, fades, base, sums, parts):
    _, planes, columns, width = base.shape
    return pl.pallas_call(
        functools.partial(spread_kernel, len(parts), share),
        in_specs=[VMEM] * (4 + len(sums) + len(parts)),
        out_specs=ANY,
        out_shape=struct(*base.shape),
        scratch_shapes=[
            pltpu.VMEM(base.shape, jnp.float32),
            pltpu.VMEM((SIDES, columns, width), jnp.float32),
            pltpu.VMEM((SIDES, planes, width), jnp.float32),
            pltpu.SemaphoreType.DMA((SPECIES, planes // 4 if planes % 4 == 0 else planes)),
        ],
        compiler_params=params(8),
        name="spread",
    )(table, weights, fades, base, *parts, *sums)


def group_size(devices):
    size = 1
    while 4 * size * size <= 2 * devices and devices % (2 * size) == 0:
        size *= 2
    return size


def body(conc, influx, numbers, cross, kinetics):
    _, planes, columns, _ = conc.shape
    across, along = lax.axis_size("gx"), lax.axis_size("gy")
    group = group_size(across)
    share = columns // group
    rank = jnp.stack([lax.axis_index("gx"), lax.axis_index("gy")]).astype(jnp.int32)
    conc, influx, numbers, cross, kinetics = (
        pltpu.with_memory_space_constraint(x, pltpu.HBM) for x in (conc, influx, numbers, cross, kinetics)
    )

    def beside(value, stage):
        return lax.ppermute(value, "gy", [(i, i ^ 2**stage) for i in range(along)])

    def in_group(parts):
        pairs = [[(i, i ^ d) for i in range(across)] for d in range(group)]
        return [parts[0]] + [lax.ppermute(parts[d], "gx", pairs[d]) for d in range(1, group)]

    def over_groups(value, by):
        return lax.ppermute(value, "gx", [(i, (i + by * group) % across) for i in range(across)])

    *parts, table, conc, influx, y_table, z_table = edges(group, rank, numbers, cross, kinetics, conc, influx)
    parts = in_group(parts)
    swept = sweeps(table, conc, influx)
    h, rough = swept[: SPECIES - 1], swept[SPECIES - 1 :]
    whole = group_sums(planes, share, table, h[0], parts)
    wholes = [whole] + [over_groups(whole, j) for j in range(1, across // group)]
    *u, rough_first, sums = column_parts(table, y_table, z_table, conc, influx, h)
    *outs, sums = entering(planes, share, table, sums, parts, wholes)
    gathered = [sums]
    for stage in range(along.bit_length() - 1):
        if stage:
            sums = pair_sums(planes, columns, stage - 1, table, sums, gathered[-1])
        gathered.append(beside(sums, stage))
    outs = in_group(outs)
    base, weights, fades = finish(table, z_table, conc, u, [rough_first, *rough])
    return spread(share, table, weights, fades, base, gathered, outs)


def solution(mesh):
    placed = (P(None, "gx", "gy", None), P("gx", "gy", None), P(), P(), P())
    return jax.shard_map(
        body, mesh=mesh, in_specs=placed, out_specs=P(None, "gx", "gy", None), check_vma=False
    )
```

```python
import functools

import jax
import jax.numpy as jnp
from jax import lax
from jax.experimental import pallas as pl
from jax.experimental.pallas import tpu as pltpu
from jax.sharding import PartitionSpec as P

SPECIES = 3
ROWS = 8
SIDES = 2
CORNERS = SIDES * SIDES * SPECIES
SMEM = pl.BlockSpec(memory_space=pltpu.SMEM)
VMEM = pl.BlockSpec(memory_space=pltpu.VMEM)
ANY = pl.BlockSpec(memory_space=pl.ANY)

RATE_X, RATE_Y, SCALE_Y, SCALE_X, DECAY, KINETICS, MEMBER = 0, 3, 6, 9, 12, 15, 18
INNER, DOUBLE, PART_A, PART_B, RANK_Y, TABLE_ROWS = 19, 28, 37, 46, 55, 56


def padded(rows):
    return -(-rows // ROWS) * ROWS


def params(mebibytes):
    return pltpu.CompilerParams(vmem_limit_bytes=mebibytes * 2**20)


def struct(*shape):
    return jax.ShapeDtypeStruct(shape, jnp.float32)


def decay_rate(number):
    half = 0.5 * lax.rsqrt(number)
    square = half * half
    return 2.0 * jnp.log1p(half + square / (1.0 + jnp.sqrt(1.0 + square)))


def scaling(number):
    return lax.rsqrt(1.0 + 4.0 * number)


def splat(value, shape):
    return jnp.full(shape, value, jnp.float32)


def split(value):
    high = value.astype(jnp.bfloat16)
    return high, (value - high.astype(jnp.float32)).astype(jnp.bfloat16)


def left_pair(value):
    return jnp.concatenate(split(value), axis=1)


def right_pair(value):
    high, low = split(value)
    return jnp.concatenate(
        [jnp.concatenate([high, low], axis=1), jnp.concatenate([high, jnp.zeros_like(low)], axis=1)], axis=0
    )


def product(left, right):
    both = jnp.dot(left, right, preferred_element_type=jnp.float32)
    width = both.shape[1] // 2
    return both[:, :width] + both[:, width:]


def distances(length):
    rows = lax.broadcasted_iota(jnp.int32, (length, length), 0)
    columns = lax.broadcasted_iota(jnp.int32, (length, length), 1)
    return jnp.abs(rows - columns).astype(jnp.float32)


def depth_table(number, length):
    number = splat(number, (1, length))
    theta = decay_rate(number)
    spread = distances(length)
    factor = scaling(number) / (1.0 - jnp.exp(-length * theta))
    return (jnp.exp(-spread * theta) + jnp.exp((spread - length) * theta)) * factor


def column_table(number, length):
    number = splat(number, (1, length))
    return jnp.exp(-distances(length) * decay_rate(number)) * scaling(number)


def row_position(length, width):
    return lax.broadcasted_iota(jnp.int32, (length, width), 0).astype(jnp.float32)


def coefficients(numbers, cross, kinetics, tile):
    n = [[splat(numbers[s, d], tile) for d in range(3)] for s in range(SPECIES)]
    along_x, along_y, along_z = [], [], []
    for s in range(SPECIES):
        per_x, per_y = 1.0 / n[s][0], 1.0 / n[s][1]
        for j in range(SPECIES):
            mix = 1.0 if j == s else cross[s, j]
            along_x.append(n[j][0] * per_x * mix)
            along_y.append(n[j][1] * per_y * mix)
            along_z.append(n[j][2] * mix)
    scale = [scaling(n[s][0]) for s in range(SPECIES)]
    rate = [decay_rate(n[s][0]) for s in range(SPECIES)]
    return along_x, along_y, along_z, scale, rate, [splat(kinetics[i], tile) for i in range(3)]


def turned(value):
    width = value.shape[1]
    return pltpu.roll(value, 1, 1) + pltpu.roll(value, width - 1, 1)


def weighted(weights, refs, here):
    return sum(weight * ref[here, :] for weight, ref in zip(weights, refs))


def tile_rows(k):
    return pl.ds(k * ROWS if isinstance(k, int) else pl.multiple_of(k * ROWS, ROWS), ROWS)


def tiles(table, first, count, tile):
    return [jnp.broadcast_to(table[at : at + 1], tile) for at in range(first, first + count)]


def rates(c, influx, kinetics):
    bind, unbind, pump = kinetics
    binding = bind * c[0] * c[1] - unbind * c[2]
    pumping = pump * c[0] / (1.0 + c[0])
    return influx - 4.0 * binding - pumping, binding


def side_by_side(counts, steps):
    for k in range(max(counts)):
        for count, step in zip(counts, steps):
            if k < count:
                step(k)


def sweep_of_b(s, table, conc, out, k):
    _, planes, _, width = conc.shape
    tile = (ROWS, width)
    here = tile_rows(k)
    weight = tiles(table, PART_B + s * SPECIES, SPECIES, tile)
    (decay,) = tiles(table, DECAY + s, 1, tile)
    up, sources, rising = jnp.zeros(tile, jnp.float32), [], []
    for i in range(planes):
        b = weight[0] * conc[0, i, here, :] + weight[1] * conc[1, i, here, :] + weight[2] * conc[2, i, here, :]
        up = b + decay * up
        sources.append(b)
        rising.append(up)
    down = jnp.zeros(tile, jnp.float32)
    for i in reversed(range(planes)):
        down = decay * down
        out[i, here, :] = rising[i] + down
        down = down + sources[i]


def edge_kernel(group, rank_far, numbers_far, cross_far, kinetics_far, conc_far, influx_far, *refs):
    sent, refs = refs[:group], refs[group:]
    table, conc, influx, y_table, z_table, weights, hold, deep, solved, corners, arrived = refs[:11]
    rank, numbers, cross, kinetics, small = refs[11:]
    planes, columns, width = influx.shape
    chunks = arrived.shape[1]
    chunk = columns // chunks
    half = planes // 2
    share = columns // group
    tile = (ROWS, width)

    def copies(k):
        part = pl.ds(k * chunk, chunk)
        return (
            pltpu.make_async_copy(conc_far.at[:, :, part, :], conc.at[:, :, part, :], arrived.at[0, k]),
            pltpu.make_async_copy(influx_far.at[:, part, :], influx.at[:, part, :], arrived.at[1, k]),
        )

    for k in range(chunks):
        for copy in copies(k):
            copy.start()
    fars = (rank_far, numbers_far, cross_far, kinetics_far)
    nears = (rank, numbers, cross, kinetics)
    scalars = [pltpu.make_async_copy(far, near, small.at[k]) for k, (far, near) in enumerate(zip(fars, nears))]
    for copy in scalars:
        copy.start()
    for copy in scalars:
        copy.wait()

    along_x, along_y, along_z, scale, rate, kinetic = coefficients(numbers, cross, kinetics, tile)
    inner, double, single = [], [], []
    for s in range(SPECIES):
        for at in range(s * SPECIES, (s + 1) * SPECIES):
            inner.append((along_x[at] + along_y[at] - 2.0 * along_z[at]) * scale[s])
            double.append(along_z[at] * scale[s])
            single.append(along_y[at] * scale[s])
        for i in range(half):
            near = jnp.exp(-i * rate[s])
            far = jnp.exp(-(planes - 1.0 - i) * rate[s])
            weights[s, i, 0] = 0.5 * (near + far)
            weights[s, i, 1] = 0.5 * (near - far)
        number = splat(numbers[s, 1], tile)
        table[RATE_Y + s : RATE_Y + s + 1] = decay_rate(number)[:1]
        table[SCALE_Y + s : SCALE_Y + s + 1] = scaling(number)[:1]
        y_table[s] = left_pair(column_table(numbers[s, 1], columns))
        z_table[s] = right_pair(depth_table(numbers[s, 2], width))
    member = lax.rem(rank[0], group)
    entries = (
        (RATE_X, rate),
        (SCALE_X, scale),
        (DECAY, [jnp.exp(-value) for value in rate]),
        (KINETICS, kinetic),
        (MEMBER, [splat(member.astype(jnp.float32), tile)]),
        (RANK_Y, [splat(rank[1].astype(jnp.float32), tile)]),
        (INNER, inner),
        (DOUBLE, double),
        (PART_A, along_x),
        (PART_B, single),
    )
    for first, values in entries:
        for k, value in enumerate(values):
            table[first + k : first + k + 1] = value[:1]

    def sums_of(start):
        here = slice(start, start + ROWS)

        def at_plane(i):
            c = [conc[j, i, here, :] for j in range(SPECIES)]
            return c, *rates(c, influx[i, here, :], kinetic)

        zero = jnp.zeros(tile, jnp.float32)
        plus = [[zero] * (SPECIES + 1) for _ in range(SPECIES)]
        minus = [[zero] * (SPECIES + 1) for _ in range(SPECIES)]
        for i in range(half):
            low, low_first, low_binding = at_plane(i)
            high, high_first, high_binding = at_plane(planes - 1 - i)
            both = [x + y for x, y in zip(low, high)]
            apart = [x - y for x, y in zip(low, high)]
            change = (low_first + high_first, low_binding + high_binding)
            turn = (low_first - high_first, low_binding - high_binding)
            for s in range(SPECIES):
                even, odd = weights[s, i, 0], weights[s, i, 1]
                of = min(s, 1)
                for j, (p, m) in enumerate(zip(both + [change[of]], apart + [turn[of]])):
                    plus[s][j] = plus[s][j] + even * p
                    minus[s][j] = minus[s][j] + odd * m
        for s in range(SPECIES):
            for e in range(SIDES):
                sums = [p + m if e else p - m for p, m in zip(plus[s], minus[s])]
                v = sums[SPECIES] * scale[s]
                if s == 1:
                    v = -v
                w = 0.0
                for j in range(SPECIES):
                    at = s * SPECIES + j
                    v = v + inner[at] * sums[j] + double[at] * turned(sums[j])
                    w = w + single[at] * sums[j]
                hold[s, e, here, :] = v
                hold[s, SIDES + e, here, :] = w

    def deepen(k):
        here = slice(k * chunk, (k + 1) * chunk)
        for s in range(SPECIES):
            stack = jnp.concatenate([hold[s, e, here, :] for e in range(2 * SIDES)], axis=0)
            done = product(left_pair(stack), z_table[s])
            for e in range(2 * SIDES):
                deep[s, e, here, :] = done[e * chunk : (e + 1) * chunk]

    for k in range(chunks):
        for copy in copies(k):
            copy.wait()
        if k:
            deepen(k - 1)
        for start in range(k * chunk, (k + 1) * chunk, ROWS):
            sums_of(start)
    deepen(chunks - 1)

    row = row_position(columns, width)
    for s in range(SPECIES):
        theta = table[RATE_Y + s : RATE_Y + s + 1]
        rise = jnp.exp((row - (columns - 1.0)) * theta)
        fall = jnp.exp(-row * theta)
        both = product(y_table[s], right_pair(jnp.concatenate([deep[s, e] for e in range(SIDES)], axis=1)))
        for e in range(SIDES):
            solved[e, s] = both[:, e * width : (e + 1) * width] - deep[s, SIDES + e]
            for f, weight in enumerate((rise, fall)):
                at = (f * SIDES + e) * SPECIES + s
                corners[at : at + 1] = jnp.sum(weight * deep[s, e], axis=0, keepdims=True)
    for d in range(group):
        start = pl.multiple_of(lax.bitwise_xor(member, jnp.int32(d)) * share, share)
        for s in range(SPECIES):
            for e in range(SIDES):
                sent[d][pl.ds((e * SPECIES + s) * share, share), :] = solved[e, s, pl.ds(start, share), :]
        sent[d][pl.ds(SIDES * SPECIES * share, corners.shape[0]), :] = corners[...]


def edges(group, rank, numbers, cross, kinetics, conc, influx):
    _, planes, columns, width = conc.shape
    chunks = columns // (2 * ROWS)
    hold = pltpu.VMEM((SPECIES, 2 * SIDES, columns, width), jnp.float32)
    rows = SIDES * SPECIES * (columns // group) + padded(CORNERS)
    return pl.pallas_call(
        functools.partial(edge_kernel, group),
        in_specs=[ANY] * 6,
        out_specs=[VMEM] * (group + 5),
        out_shape=[struct(rows, width)] * group
        + [
            pltpu.VMEM((TABLE_ROWS, width), jnp.float32),
            pltpu.VMEM(conc.shape, jnp.float32),
            pltpu.VMEM(influx.shape, jnp.float32),
            pltpu.VMEM((SPECIES, columns, 2 * columns), jnp.bfloat16),
            pltpu.VMEM((SPECIES, 2 * width, 2 * width), jnp.bfloat16),
        ],
        scratch_shapes=[
            pltpu.VMEM((SPECIES, planes // 2, 2, ROWS, width), jnp.float32),
            hold,
            hold,
            pltpu.VMEM((SIDES, SPECIES, columns, width), jnp.float32),
            pltpu.VMEM((padded(CORNERS), width), jnp.float32),
            pltpu.SemaphoreType.DMA((2, chunks)),
            pltpu.SMEM(rank.shape, rank.dtype),
            pltpu.SMEM(numbers.shape, numbers.dtype),
            pltpu.SMEM(cross.shape, cross.dtype),
            pltpu.SMEM(kinetics.shape, kinetics.dtype),
            pltpu.SemaphoreType.DMA((4,)),
        ],
        compiler_params=params(16),
        name="edges",
    )(rank, numbers, cross, kinetics, conc, influx)


def sweep_kernel(table, conc, influx, *refs):
    count = SPECIES - 1
    outs, roughs, g_hold = refs[:count], refs[count:-1], refs[-1]
    planes, columns, width = influx.shape
    tile = (ROWS, width)
    inner = tiles(table, INNER, count * SPECIES, tile)
    double = tiles(table, DOUBLE, count * SPECIES, tile)
    part_a = tiles(table, PART_A, count * SPECIES, tile)
    scale = tiles(table, SCALE_X, count, tile)
    decay = tiles(table, DECAY, count, tile)
    kinetic = tiles(table, KINETICS, 3, tile)

    def rows(k, carry):
        here = pl.ds(pl.multiple_of(k * ROWS, ROWS), ROWS)
        up = [jnp.zeros(tile, jnp.float32) for _ in range(count)]
        for i in range(planes):
            c = [conc[j, i, here, :] for j in range(SPECIES)]
            around = [turned(value) for value in c]
            first, binding = rates(c, influx[i, here, :], kinetic)
            change = (first, -binding, binding)
            for s in range(count):
                g = change[s] * scale[s]
                a = c[s]
                for j in range(SPECIES):
                    at = s * SPECIES + j
                    g = g + inner[at] * c[j] + double[at] * around[j]
                    if j != s:
                        a = a + part_a[at] * c[j]
                up[s] = g + decay[s] * up[s]
                g_hold[s, i] = g
                outs[s][i, here, :] = up[s] - a
        for s in range(count):
            down = jnp.zeros(tile, jnp.float32)
            for i in reversed(range(planes)):
                down = decay[s] * down
                outs[s][i, here, :] += down
                down += g_hold[s, i]
        for s, rough in enumerate(roughs, 1):
            sweep_of_b(s, table, conc, rough, k)
        return carry

    lax.fori_loop(0, columns // ROWS, rows, 0)


def sweeps(table, conc, influx):
    count, planes, width = SPECIES - 1, influx.shape[0], influx.shape[2]
    return pl.pallas_call(
        sweep_kernel,
        in_specs=[VMEM] * 3,
        out_specs=[VMEM] * (2 * count),
        out_shape=[pltpu.VMEM(influx.shape, jnp.float32)] * (2 * count),
        scratch_shapes=[pltpu.VMEM((count, planes, ROWS, width), jnp.float32)],
        compiler_params=params(8),
        cost_estimate=pl.CostEstimate(flops=100 * conc.size, bytes_accessed=14 * conc.size, transcendentals=0),
        name="sweeps",
    )(table, conc, influx)


def partner(member, d):
    return lax.bitwise_xor(member.astype(jnp.int32), jnp.int32(d)).astype(jnp.float32)


def group_kernel(planes, share, table, after, *refs):
    parts, out = refs[:-1], refs[-1]
    group = len(parts)
    corners = SIDES * SPECIES * share
    member = table[MEMBER : MEMBER + 1]
    blocks = [partner(member, d) for d in range(group)]
    for s in range(SPECIES):
        theta = planes * table[RATE_X + s : RATE_X + s + 1]
        for e in range(SIDES):
            weight = [jnp.exp((-b if e else b - (group - 1.0)) * theta) for b in blocks]
            here = pl.ds((e * SPECIES + s) * share, share)
            out[here, :] = sum(weight[d] * parts[d][here, :] for d in range(group))
            for k in range(SIDES):
                here = pl.ds(corners + (k * SIDES + e) * SPECIES + s, 1)
                out[here, :] = sum(weight[d] * parts[d][here, :] for d in range(group))


def group_sums(planes, share, table, after, parts):
    return pl.pallas_call(
        functools.partial(group_kernel, planes, share),
        in_specs=[VMEM, ANY] + [VMEM] * len(parts),
        out_specs=VMEM,
        out_shape=struct(*parts[0].shape),
        compiler_params=params(8),
        name="group_sums",
    )(table, after, *parts)


def column_kernel(table, y_table, z_table, conc, influx, *refs):
    count = SPECIES - 1
    h, u, (rough, y_out, last, weights, sums) = refs[:count], refs[count : count + SPECIES], refs[count + SPECIES :]
    planes, columns, width = influx.shape
    tile = (ROWS, width)
    row = row_position(columns, width)
    for s in range(SPECIES):
        theta = table[RATE_Y + s : RATE_Y + s + 1]
        weights[s, 0] = jnp.exp((row - (columns - 1.0)) * theta)
        weights[s, 1] = jnp.exp(-row * theta)
    inner = tiles(table, INNER + count * SPECIES, SPECIES, tile)
    double = tiles(table, DOUBLE + count * SPECIES, SPECIES, tile)
    part_a = tiles(table, PART_A + count * SPECIES, SPECIES, tile)
    (scale,) = tiles(table, SCALE_X + count, 1, tile)
    (decay,) = tiles(table, DECAY + count, 1, tile)
    bind, unbind, _ = tiles(table, KINETICS, 3, tile)

    def plane_of(s, value, i):
        for e in range(SIDES):
            sums[s, e, i : i + 1, :] = jnp.sum(weights[s, e] * value, axis=0, keepdims=True)
        u[s][i] = product(y_table[s], right_pair(value))

    def plane(i):
        for s in range(count):
            plane_of(s, h[s][i], i)

    def rows(k):
        here = tile_rows(k)
        up, sources, rising = jnp.zeros(tile, jnp.float32), [], []
        for i in range(planes):
            c = [conc[j, i, here, :] for j in range(SPECIES)]
            g = (bind * c[0] * c[1] - unbind * c[2]) * scale
            a = c[count]
            for j in range(SPECIES):
                g = g + inner[j] * c[j] + double[j] * turned(c[j])
                if j != count:
                    a = a + part_a[j] * c[j]
            up = g + decay * up
            sources.append(g)
            rising.append(up - a)
        down = jnp.zeros(tile, jnp.float32)
        for i in reversed(range(planes)):
            down = decay * down
            last[i, here, :] = rising[i] + down
            down = down + sources[i]

    side_by_side((planes, columns // ROWS), (plane, rows))
    side_by_side(
        (planes, columns // ROWS),
        (lambda i: plane_of(count, last[i], i), lambda k: sweep_of_b(0, table, conc, rough, k)),
    )
    for s in range(SPECIES):
        both = jnp.concatenate([sums[s, e] for e in range(SIDES)], axis=0)
        both = product(left_pair(both), z_table[s])
        for e in range(SIDES):
            y_out[pl.ds((e * SPECIES + s) * planes, planes), :] = both[e * planes : (e + 1) * planes]


def column_parts(table, y_table, z_table, conc, influx, h):
    planes, columns, width = influx.shape
    return pl.pallas_call(
        column_kernel,
        in_specs=[VMEM] * (5 + len(h)),
        out_specs=[VMEM] * (SPECIES + 2),
        out_shape=[pltpu.VMEM(influx.shape, jnp.float32)] * (SPECIES + 1)
        + [pltpu.VMEM((SIDES * SPECIES * planes, width), jnp.float32)],
        scratch_shapes=[
            pltpu.VMEM(influx.shape, jnp.float32),
            pltpu.VMEM((SPECIES, SIDES, columns, width), jnp.float32),
            pltpu.VMEM((SPECIES, SIDES, planes, width), jnp.float32),
        ],
        compiler_params=params(8),
        cost_estimate=pl.CostEstimate(flops=6 * conc.size * columns, bytes_accessed=8 * conc.size, transcendentals=0),
        name="column_parts",
    )(table, y_table, z_table, conc, influx, *h)


def finish_kernel(table, z_table, conc, *refs):
    u, rough, (out, weights, fades) = refs[:SPECIES], refs[SPECIES : 2 * SPECIES], refs[2 * SPECIES :]
    _, planes, columns, width = conc.shape
    at_once = 4 if planes % 4 == 0 else 1
    row = row_position(columns, width)
    position = row_position(planes, width)
    for s in range(SPECIES):
        rate_x = table[RATE_X + s : RATE_X + s + 1]
        rate_y = table[RATE_Y + s : RATE_Y + s + 1]
        weights[s, 0] = jnp.exp(-(row + 1.0) * rate_y)
        weights[s, 1] = jnp.exp((row - columns) * rate_y)
        fades[s, 0] = jnp.exp(-(position + 1.0) * rate_x)
        fades[s, 1] = jnp.exp((position - planes) * rate_x)
        for first in range(0, planes, at_once):
            here = slice(first, first + at_once)
            value = (u[s][here] - rough[s][here]).reshape(at_once * columns, width)
            done = product(left_pair(value), z_table[s])
            out[s, here] = conc[s, here] + done.reshape(at_once, columns, width)


def finish(table, z_table, conc, u, rough):
    _, planes, columns, width = conc.shape
    return pl.pallas_call(
        finish_kernel,
        in_specs=[VMEM] * (3 + len(u) + len(rough)),
        out_specs=[VMEM] * 3,
        out_shape=[
            pltpu.VMEM(conc.shape, jnp.float32),
            pltpu.VMEM((SPECIES, SIDES, columns, width), jnp.float32),
            pltpu.VMEM((SPECIES, SIDES, planes, width), jnp.float32),
        ],
        compiler_params=params(8),
        cost_estimate=pl.CostEstimate(flops=6 * conc.size * width, bytes_accessed=12 * conc.size, transcendentals=0),
        name="finish",
    )(table, z_table, conc, *u, *rough)


def enter_kernel(group, planes, share, table, sums, *refs):
    parts, wholes, outs, y_out = refs[:group], refs[group : -group - 1], refs[-group - 1 : -1], refs[-1]
    groups = len(wholes)
    corners = SIDES * SPECIES * share
    member = table[MEMBER : MEMBER + 1]
    blocks = [partner(member, d) for d in range(group)]
    y_out[pl.ds(0, sums.shape[0]), :] = sums[...]

    for s in range(SPECIES):
        theta = planes * table[RATE_X + s : RATE_X + s + 1]
        closing = 1.0 / (1.0 - jnp.exp(-float(group * groups) * theta))
        for e in range(SIDES):
            steps = [(groups - j - 1) if e else (j - 1 if j else groups - 1) for j in range(groups)]
            outside = [jnp.exp(-float(group * k) * theta) * closing for k in steps]
            to_target = [jnp.exp((t - (group - 1.0) if e else -t) * theta) for t in blocks]
            inside = []
            for t in blocks:
                away = [(b - t) if e else (t - b) for b in blocks]
                inside.append([jnp.where(k > 0.0, jnp.exp((1.0 - jnp.abs(k)) * theta), 0.0) for k in away])

            def entering_group(here):
                return sum(weight * whole[here, :] for weight, whole in zip(outside, wholes))

            here = pl.ds((e * SPECIES + s) * share, share)
            whole = entering_group(here)
            held = [part[here, :] for part in parts]
            for d in range(group):
                total = to_target[d] * whole
                for weight, part in zip(inside[d], held):
                    total = total + weight * part
                outs[d][here, :] = total

            for k in range(SIDES):
                at = (k * SIDES + e) * SPECIES + s
                here = pl.ds(corners + at, 1)
                total = to_target[0] * entering_group(here)
                for weight, part in zip(inside[0], parts):
                    total = total + weight * part[here, :]
                y_out[pl.ds(sums.shape[0] + at, 1), :] = total


def entering(planes, share, table, sums, parts, wholes):
    group, width = len(parts), parts[0].shape[1]
    return pl.pallas_call(
        functools.partial(enter_kernel, group, planes, share),
        in_specs=[VMEM] * (2 + group + len(wholes)),
        out_specs=[VMEM] * (group + 1),
        out_shape=[struct(SIDES * SPECIES * share, width)] * group + [struct(padded(sums.shape[0] + CORNERS), width)],
        compiler_params=params(8),
        name="entering",
    )(table, sums, *parts, *wholes)


def y_rows(planes, s, e):
    corners = SIDES * SPECIES * planes
    return [pl.ds((e * SPECIES + s) * planes, planes)] + [
        pl.ds(corners + (e * SIDES + k) * SPECIES + s, 1) for k in range(SIDES)
    ]


def bits(table, stage):
    rank = table[RANK_Y : RANK_Y + 1].astype(jnp.int32)
    low = lax.bitwise_and(rank, jnp.int32(2**stage - 1)).astype(jnp.float32)
    return low, lax.bitwise_and(rank, jnp.int32(2**stage)) != 0


def pair_kernel(planes, columns, stage, table, mine, other, out):
    _, above = bits(table, stage)
    for s in range(SPECIES):
        far = jnp.exp(-float(columns * 2**stage) * table[RATE_Y + s : RATE_Y + s + 1])
        for e in range(SIDES):
            keep = jnp.where(above, far, 1.0) if e else jnp.where(above, 1.0, far)
            take = jnp.where(above, 1.0, far) if e else jnp.where(above, far, 1.0)
            for here in y_rows(planes, s, e):
                out[here, :] = keep * mine[here, :] + take * other[here, :]


def pair_sums(planes, columns, stage, table, mine, other):
    return pl.pallas_call(
        functools.partial(pair_kernel, planes, columns, stage),
        in_specs=[VMEM] * 3,
        out_specs=VMEM,
        out_shape=struct(*mine.shape),
        compiler_params=params(8),
        name="pair_sums",
    )(table, mine, other)


def y_weights(table, s, e, columns, stages):
    theta = columns * table[RATE_Y + s : RATE_Y + s + 1]
    along = 2**stages
    closing = table[SCALE_Y + s : SCALE_Y + s + 1] / (1.0 - jnp.exp(-float(along) * theta))
    weights = [jnp.exp(-(along - 1.0) * theta) * closing]
    for stage in range(stages):
        low, above = bits(table, stage)
        near = (2.0**stage - 1.0 - low) if e else low
        around = float(along - 2 ** (stage + 1))
        steps = near + (jnp.where(above, around, 0.0) if e else jnp.where(above, 0.0, around))
        weights.append(jnp.exp(-steps * theta) * closing)
    return weights


def entry_kernel(table, weights, *refs):
    sums, (enter, corner) = refs[:-2], refs[-2:]
    planes, columns = enter.shape[2], weights.shape[2]
    for s in range(SPECIES):
        for e in range(SIDES):
            arrive = y_weights(table, s, e, columns, len(sums) - 1)
            lines, *corner_lines = y_rows(planes, s, e)
            enter[s, e] = weighted(arrive, sums, lines)
            for k, here in enumerate(corner_lines):
                corner[s, e, k : k + 1] = weighted(arrive, sums, here)


def spread_kernel(shares, group, share, first, rank, table, weights, fades, base, *refs):
    count = len(shares)
    parts, refs = refs[:count], refs[count:]
    if first:
        sums, (out_far, enter, corner, out, hold, near_rank, left) = refs[:-7], refs[-7:]
    else:
        enter, corner, _, out_far, out, hold, near_rank, left = refs
    _, planes, _, width = base.shape
    at_once = planes // left.shape[2]
    fetch = pltpu.make_async_copy(rank, near_rank, left.at[0, 0, 0])
    fetch.start()
    if first:
        entry_kernel(table, weights, *sums, enter, corner)
    fetch.wait()
    member = lax.rem(near_rank[0], group)
    copies = []
    for q, d in enumerate(shares):
        start = pl.multiple_of(lax.bitwise_xor(member, jnp.int32(d)) * share, share)
        for s in range(SPECIES):
            for e in range(SIDES):
                message = parts[q][pl.ds((e * SPECIES + s) * share, share), :]
                low, high = (weights[s, f, pl.ds(start, share), :] for f in range(SIDES))
                lift = low * corner[s, 0, e : e + 1] + high * corner[s, 1, e : e + 1]
                hold[e, :, :] = message + lift
            for block in range(planes // at_once):
                here = range(block * at_once, (block + 1) * at_once)
                rows_of = [[ref[i : i + 1] for i in here] for ref in (fades.at[s, 0], fades.at[s, 1], enter.at[s, 0], enter.at[s, 1])]
                for tile in range(0, share, ROWS):
                    at = pl.ds(pl.multiple_of(start + tile, ROWS), ROWS)
                    x_low, x_high = hold[0, tile : tile + ROWS, :], hold[1, tile : tile + ROWS, :]
                    y_low, y_high = weights[s, 0, at, :], weights[s, 1, at, :]
                    for k, i in enumerate(here):
                        x_rise, x_fall, y_rise, y_fall = (rows[k] for rows in rows_of)
                        added = x_rise * x_low + x_fall * x_high + y_rise * y_low + y_fall * y_high
                        out[q, s, i, tile : tile + ROWS, :] = base[s, i, at, :] + added
                part = pl.ds(block * at_once, at_once)
                there = out_far.at[s, part, pl.ds(start, share), :]
                copies.append(pltpu.make_async_copy(out.at[q, s, part], there, left.at[q, s, block]))
                copies[-1].start()
    for copy in copies:
        copy.wait()


def spread(shares, share, group, rank, table, weights, fades, base, parts, sums=None, before=None):
    _, planes, columns, width = base.shape
    blocks = planes // 4 if planes % 4 == 0 else planes
    first = before is None
    entries = [
        pltpu.VMEM((SPECIES, SIDES, planes, width), jnp.float32),
        pltpu.VMEM((SPECIES, SIDES, ROWS, width), jnp.float32),
    ]
    operands = [rank, table, weights, fades, base, *parts, *(sums if first else before)]
    return pl.pallas_call(
        functools.partial(spread_kernel, shares, group, share, first),
        in_specs=[ANY] + [VMEM] * (len(operands) - 1) if first else [ANY] + [VMEM] * (len(operands) - 2) + [ANY],
        out_specs=[ANY, VMEM, VMEM] if first else ANY,
        out_shape=[struct(*base.shape), *entries] if first else struct(*base.shape),
        input_output_aliases={} if first else {len(operands) - 1: 0},
        scratch_shapes=[
            pltpu.VMEM((len(shares), SPECIES, planes, share, width), jnp.float32),
            pltpu.VMEM((SIDES, share, width), jnp.float32),
            pltpu.SMEM(rank.shape, rank.dtype),
            pltpu.SemaphoreType.DMA((len(shares), SPECIES, blocks)),
        ],
        compiler_params=params(8),
        cost_estimate=pl.CostEstimate(flops=1000, bytes_accessed=1000, transcendentals=0),
        name="spread",
    )(*operands)


def group_size(devices):
    size = 1
    while 4 * size * size <= 2 * devices and devices % (2 * size) == 0:
        size *= 2
    return size


def body(conc, influx, numbers, cross, kinetics):
    _, planes, columns, _ = conc.shape
    across, along = lax.axis_size("gx"), lax.axis_size("gy")
    group = group_size(across)
    share = columns // group
    rank = jnp.stack([lax.axis_index("gx"), lax.axis_index("gy")]).astype(jnp.int32)
    conc, influx, numbers, cross, kinetics = (
        pltpu.with_memory_space_constraint(x, pltpu.HBM) for x in (conc, influx, numbers, cross, kinetics)
    )

    def beside(value, stage):
        return lax.ppermute(value, "gy", [(i, i ^ 2**stage) for i in range(along)])

    def in_group(parts):
        pairs = [[(i, i ^ d) for i in range(across)] for d in range(group)]
        return [parts[0]] + [lax.ppermute(parts[d], "gx", pairs[d]) for d in range(1, group)]

    def over_groups(value, by):
        return lax.ppermute(value, "gx", [(i, (i + by * group) % across) for i in range(across)])

    *parts, table, conc, influx, y_table, z_table = edges(group, rank, numbers, cross, kinetics, conc, influx)
    parts = in_group(parts)
    swept = sweeps(table, conc, influx)
    h, rough = swept[: SPECIES - 1], swept[SPECIES - 1 :]
    whole = group_sums(planes, share, table, h[0], parts)
    wholes = [whole] + [over_groups(whole, j) for j in range(1, across // group)]
    *u, rough_first, sums = column_parts(table, y_table, z_table, conc, influx, h)
    *outs, sums = entering(planes, share, table, sums, parts, wholes)
    gathered = [sums]
    for stage in range(along.bit_length() - 1):
        if stage:
            sums = pair_sums(planes, columns, stage - 1, table, sums, gathered[-1])
        gathered.append(beside(sums, stage))
    outs = in_group(outs)
    base, weights, fades = finish(table, z_table, conc, u, [rough_first, *rough])
    early = min(2, group)
    out, *entries = spread(
        range(early), share, group, rank, table, weights, fades, base, outs[:early], sums=gathered
    )
    for d in range(early, group):
        out = spread([d], share, group, rank, table, weights, fades, base, [outs[d]], before=[*entries, out])
    return out


def solution(mesh):
    placed = (P(None, "gx", "gy", None), P("gx", "gy", None), P(), P(), P())
    return jax.shard_map(
        body, mesh=mesh, in_specs=placed, out_specs=P(None, "gx", "gy", None), check_vma=False
    )
```

```python
import functools

import jax
import jax.numpy as jnp
from jax import lax
from jax.experimental import pallas as pl
from jax.experimental.pallas import tpu as pltpu
from jax.sharding import PartitionSpec as P

SPECIES = 3
ROWS = 8
SIDES = 2
CORNERS = SIDES * SIDES * SPECIES
SMEM = pl.BlockSpec(memory_space=pltpu.SMEM)
VMEM = pl.BlockSpec(memory_space=pltpu.VMEM)
ANY = pl.BlockSpec(memory_space=pl.ANY)

RATE_X, RATE_Y, SCALE_Y, SCALE_X, DECAY, KINETICS, MEMBER = 0, 3, 6, 9, 12, 15, 18
INNER, DOUBLE, PART_A, PART_B, RANK_Y, TABLE_ROWS = 19, 28, 37, 46, 55, 56


def padded(rows):
    return -(-rows // ROWS) * ROWS


def params(mebibytes):
    return pltpu.CompilerParams(vmem_limit_bytes=mebibytes * 2**20)


def struct(*shape):
    return jax.ShapeDtypeStruct(shape, jnp.float32)


def decay_rate(number):
    half = 0.5 * lax.rsqrt(number)
    square = half * half
    return 2.0 * jnp.log1p(half + square / (1.0 + jnp.sqrt(1.0 + square)))


def scaling(number):
    return lax.rsqrt(1.0 + 4.0 * number)


def splat(value, shape):
    return jnp.full(shape, value, jnp.float32)


def split(value):
    high = value.astype(jnp.bfloat16)
    return high, (value - high.astype(jnp.float32)).astype(jnp.bfloat16)


def left_pair(value):
    return jnp.concatenate(split(value), axis=1)


def right_pair(value):
    high, low = split(value)
    return jnp.concatenate(
        [jnp.concatenate([high, low], axis=1), jnp.concatenate([high, jnp.zeros_like(low)], axis=1)], axis=0
    )


def product(left, right):
    both = jnp.dot(left, right, preferred_element_type=jnp.float32)
    width = both.shape[1] // 2
    return both[:, :width] + both[:, width:]


def distances(length):
    rows = lax.broadcasted_iota(jnp.int32, (length, length), 0)
    columns = lax.broadcasted_iota(jnp.int32, (length, length), 1)
    return jnp.abs(rows - columns).astype(jnp.float32)


def depth_table(number, length):
    number = splat(number, (1, length))
    theta = decay_rate(number)
    spread = distances(length)
    factor = scaling(number) / (1.0 - jnp.exp(-length * theta))
    return (jnp.exp(-spread * theta) + jnp.exp((spread - length) * theta)) * factor


def column_table(number, length):
    number = splat(number, (1, length))
    return jnp.exp(-distances(length) * decay_rate(number)) * scaling(number)


def row_position(length, width):
    return lax.broadcasted_iota(jnp.int32, (length, width), 0).astype(jnp.float32)


def coefficients(numbers, cross, kinetics, tile):
    n = [[splat(numbers[s, d], tile) for d in range(3)] for s in range(SPECIES)]
    along_x, along_y, along_z = [], [], []
    for s in range(SPECIES):
        per_x, per_y = 1.0 / n[s][0], 1.0 / n[s][1]
        for j in range(SPECIES):
            mix = 1.0 if j == s else cross[s, j]
            along_x.append(n[j][0] * per_x * mix)
            along_y.append(n[j][1] * per_y * mix)
            along_z.append(n[j][2] * mix)
    scale = [scaling(n[s][0]) for s in range(SPECIES)]
    rate = [decay_rate(n[s][0]) for s in range(SPECIES)]
    return along_x, along_y, along_z, scale, rate, [splat(kinetics[i], tile) for i in range(3)]


def turned(value):
    width = value.shape[1]
    return pltpu.roll(value, 1, 1) + pltpu.roll(value, width - 1, 1)


def weighted(weights, refs, here):
    return sum(weight * ref[here, :] for weight, ref in zip(weights, refs))


def tile_rows(k):
    return pl.ds(k * ROWS if isinstance(k, int) else pl.multiple_of(k * ROWS, ROWS), ROWS)


def tiles(table, first, count, tile):
    return [jnp.broadcast_to(table[at : at + 1], tile) for at in range(first, first + count)]


def rates(c, influx, kinetics):
    bind, unbind, pump = kinetics
    binding = bind * c[0] * c[1] - unbind * c[2]
    pumping = pump * c[0] / (1.0 + c[0])
    return influx - 4.0 * binding - pumping, binding


def side_by_side(counts, steps):
    for k in range(max(counts)):
        for count, step in zip(counts, steps):
            if k < count:
                step(k)


def sweep_of_b(s, table, conc, out, k):
    _, planes, _, width = conc.shape
    tile = (ROWS, width)
    here = tile_rows(k)
    weight = tiles(table, PART_B + s * SPECIES, SPECIES, tile)
    (decay,) = tiles(table, DECAY + s, 1, tile)
    up, sources, rising = jnp.zeros(tile, jnp.float32), [], []
    for i in range(planes):
        b = weight[0] * conc[0, i, here, :] + weight[1] * conc[1, i, here, :] + weight[2] * conc[2, i, here, :]
        up = b + decay * up
        sources.append(b)
        rising.append(up)
    down = jnp.zeros(tile, jnp.float32)
    for i in reversed(range(planes)):
        down = decay * down
        out[i, here, :] = rising[i] + down
        down = down + sources[i]


def edge_kernel(group, rank_far, numbers_far, cross_far, kinetics_far, conc_far, influx_far, *refs):
    sent, refs = refs[:group], refs[group:]
    table, conc, influx, y_table, z_table, weights, hold, deep, solved, corners, arrived = refs[:11]
    rank, numbers, cross, kinetics, small = refs[11:]
    planes, columns, width = influx.shape
    chunks = arrived.shape[1]
    chunk = columns // chunks
    half = planes // 2
    share = columns // group
    tile = (ROWS, width)

    def copies(k):
        part = pl.ds(k * chunk, chunk)
        return (
            pltpu.make_async_copy(conc_far.at[:, :, part, :], conc.at[:, :, part, :], arrived.at[0, k]),
            pltpu.make_async_copy(influx_far.at[:, part, :], influx.at[:, part, :], arrived.at[1, k]),
        )

    for k in range(chunks):
        for copy in copies(k):
            copy.start()
    fars = (rank_far, numbers_far, cross_far, kinetics_far)
    nears = (rank, numbers, cross, kinetics)
    scalars = [pltpu.make_async_copy(far, near, small.at[k]) for k, (far, near) in enumerate(zip(fars, nears))]
    for copy in scalars:
        copy.start()
    for copy in scalars:
        copy.wait()

    along_x, along_y, along_z, scale, rate, kinetic = coefficients(numbers, cross, kinetics, tile)
    inner, double, single = [], [], []
    for s in range(SPECIES):
        for at in range(s * SPECIES, (s + 1) * SPECIES):
            inner.append((along_x[at] + along_y[at] - 2.0 * along_z[at]) * scale[s])
            double.append(along_z[at] * scale[s])
            single.append(along_y[at] * scale[s])
        for i in range(half):
            near = jnp.exp(-i * rate[s])
            far = jnp.exp(-(planes - 1.0 - i) * rate[s])
            weights[s, i, 0] = 0.5 * (near + far)
            weights[s, i, 1] = 0.5 * (near - far)
        number = splat(numbers[s, 1], tile)
        table[RATE_Y + s : RATE_Y + s + 1] = decay_rate(number)[:1]
        table[SCALE_Y + s : SCALE_Y + s + 1] = scaling(number)[:1]
        y_table[s] = left_pair(column_table(numbers[s, 1], columns))
        z_table[s] = right_pair(depth_table(numbers[s, 2], width))
    member = lax.rem(rank[0], group)
    entries = (
        (RATE_X, rate),
        (SCALE_X, scale),
        (DECAY, [jnp.exp(-value) for value in rate]),
        (KINETICS, kinetic),
        (MEMBER, [splat(member.astype(jnp.float32), tile)]),
        (RANK_Y, [splat(rank[1].astype(jnp.float32), tile)]),
        (INNER, inner),
        (DOUBLE, double),
        (PART_A, along_x),
        (PART_B, single),
    )
    for first, values in entries:
        for k, value in enumerate(values):
            table[first + k : first + k + 1] = value[:1]

    def sums_of(start):
        here = slice(start, start + ROWS)

        def at_plane(i):
            c = [conc[j, i, here, :] for j in range(SPECIES)]
            return c, *rates(c, influx[i, here, :], kinetic)

        zero = jnp.zeros(tile, jnp.float32)
        plus = [[zero] * (SPECIES + 1) for _ in range(SPECIES)]
        minus = [[zero] * (SPECIES + 1) for _ in range(SPECIES)]
        for i in range(half):
            low, low_first, low_binding = at_plane(i)
            high, high_first, high_binding = at_plane(planes - 1 - i)
            both = [x + y for x, y in zip(low, high)]
            apart = [x - y for x, y in zip(low, high)]
            change = (low_first + high_first, low_binding + high_binding)
            turn = (low_first - high_first, low_binding - high_binding)
            for s in range(SPECIES):
                even, odd = weights[s, i, 0], weights[s, i, 1]
                of = min(s, 1)
                for j, (p, m) in enumerate(zip(both + [change[of]], apart + [turn[of]])):
                    plus[s][j] = plus[s][j] + even * p
                    minus[s][j] = minus[s][j] + odd * m
        for s in range(SPECIES):
            for e in range(SIDES):
                sums = [p + m if e else p - m for p, m in zip(plus[s], minus[s])]
                v = sums[SPECIES] * scale[s]
                if s == 1:
                    v = -v
                w = 0.0
                for j in range(SPECIES):
                    at = s * SPECIES + j
                    v = v + inner[at] * sums[j] + double[at] * turned(sums[j])
                    w = w + single[at] * sums[j]
                hold[s, e, here, :] = v
                hold[s, SIDES + e, here, :] = w

    def deepen(k):
        here = slice(k * chunk, (k + 1) * chunk)
        for s in range(SPECIES):
            stack = jnp.concatenate([hold[s, e, here, :] for e in range(2 * SIDES)], axis=0)
            done = product(left_pair(stack), z_table[s])
            for e in range(2 * SIDES):
                deep[s, e, here, :] = done[e * chunk : (e + 1) * chunk]

    for k in range(chunks):
        for copy in copies(k):
            copy.wait()
        if k:
            deepen(k - 1)
        for start in range(k * chunk, (k + 1) * chunk, ROWS):
            sums_of(start)
    deepen(chunks - 1)

    row = row_position(columns, width)
    for s in range(SPECIES):
        theta = table[RATE_Y + s : RATE_Y + s + 1]
        rise = jnp.exp((row - (columns - 1.0)) * theta)
        fall = jnp.exp(-row * theta)
        both = product(y_table[s], right_pair(jnp.concatenate([deep[s, e] for e in range(SIDES)], axis=1)))
        for e in range(SIDES):
            solved[e, s] = both[:, e * width : (e + 1) * width] - deep[s, SIDES + e]
            for f, weight in enumerate((rise, fall)):
                at = (f * SIDES + e) * SPECIES + s
                corners[at : at + 1] = jnp.sum(weight * deep[s, e], axis=0, keepdims=True)
    for d in range(group):
        start = pl.multiple_of(lax.bitwise_xor(member, jnp.int32(turn_of(d, group))) * share, share)
        for s in range(SPECIES):
            for e in range(SIDES):
                sent[d][pl.ds((e * SPECIES + s) * share, share), :] = solved[e, s, pl.ds(start, share), :]
        sent[d][pl.ds(SIDES * SPECIES * share, corners.shape[0]), :] = corners[...]


def edges(group, rank, numbers, cross, kinetics, conc, influx):
    _, planes, columns, width = conc.shape
    chunks = columns // (2 * ROWS)
    hold = pltpu.VMEM((SPECIES, 2 * SIDES, columns, width), jnp.float32)
    rows = SIDES * SPECIES * (columns // group) + padded(CORNERS)
    return pl.pallas_call(
        functools.partial(edge_kernel, group),
        in_specs=[ANY] * 6,
        out_specs=[VMEM] * (group + 5),
        out_shape=[struct(rows, width)] * group
        + [
            pltpu.VMEM((TABLE_ROWS, width), jnp.float32),
            pltpu.VMEM(conc.shape, jnp.float32),
            pltpu.VMEM(influx.shape, jnp.float32),
            pltpu.VMEM((SPECIES, columns, 2 * columns), jnp.bfloat16),
            pltpu.VMEM((SPECIES, 2 * width, 2 * width), jnp.bfloat16),
        ],
        scratch_shapes=[
            pltpu.VMEM((SPECIES, planes // 2, 2, ROWS, width), jnp.float32),
            hold,
            hold,
            pltpu.VMEM((SIDES, SPECIES, columns, width), jnp.float32),
            pltpu.VMEM((padded(CORNERS), width), jnp.float32),
            pltpu.SemaphoreType.DMA((2, chunks)),
            pltpu.SMEM(rank.shape, rank.dtype),
            pltpu.SMEM(numbers.shape, numbers.dtype),
            pltpu.SMEM(cross.shape, cross.dtype),
            pltpu.SMEM(kinetics.shape, kinetics.dtype),
            pltpu.SemaphoreType.DMA((4,)),
        ],
        compiler_params=params(16),
        name="edges",
    )(rank, numbers, cross, kinetics, conc, influx)


def sweep_kernel(table, conc, influx, *refs):
    count = SPECIES - 1
    outs, roughs, g_hold = refs[:count], refs[count:-1], refs[-1]
    planes, columns, width = influx.shape
    tile = (ROWS, width)
    inner = tiles(table, INNER, count * SPECIES, tile)
    double = tiles(table, DOUBLE, count * SPECIES, tile)
    part_a = tiles(table, PART_A, count * SPECIES, tile)
    scale = tiles(table, SCALE_X, count, tile)
    decay = tiles(table, DECAY, count, tile)
    kinetic = tiles(table, KINETICS, 3, tile)

    def rows(k, carry):
        here = pl.ds(pl.multiple_of(k * ROWS, ROWS), ROWS)
        up = [jnp.zeros(tile, jnp.float32) for _ in range(count)]
        for i in range(planes):
            c = [conc[j, i, here, :] for j in range(SPECIES)]
            around = [turned(value) for value in c]
            first, binding = rates(c, influx[i, here, :], kinetic)
            change = (first, -binding, binding)
            for s in range(count):
                g = change[s] * scale[s]
                a = c[s]
                for j in range(SPECIES):
                    at = s * SPECIES + j
                    g = g + inner[at] * c[j] + double[at] * around[j]
                    if j != s:
                        a = a + part_a[at] * c[j]
                up[s] = g + decay[s] * up[s]
                g_hold[s, i] = g
                outs[s][i, here, :] = up[s] - a
        for s in range(count):
            down = jnp.zeros(tile, jnp.float32)
            for i in reversed(range(planes)):
                down = decay[s] * down
                outs[s][i, here, :] += down
                down += g_hold[s, i]
        for s, rough in enumerate(roughs, 1):
            sweep_of_b(s, table, conc, rough, k)
        return carry

    lax.fori_loop(0, columns // ROWS, rows, 0)


def sweeps(table, conc, influx):
    count, planes, width = SPECIES - 1, influx.shape[0], influx.shape[2]
    return pl.pallas_call(
        sweep_kernel,
        in_specs=[VMEM] * 3,
        out_specs=[VMEM] * (2 * count),
        out_shape=[pltpu.VMEM(influx.shape, jnp.float32)] * (2 * count),
        scratch_shapes=[pltpu.VMEM((count, planes, ROWS, width), jnp.float32)],
        compiler_params=params(8),
        cost_estimate=pl.CostEstimate(flops=100 * conc.size, bytes_accessed=14 * conc.size, transcendentals=0),
        name="sweeps",
    )(table, conc, influx)


def turn_of(d, group):
    return (0, group - 1, *range(1, group - 1))[d]


def partner(member, d, group):
    return lax.bitwise_xor(member.astype(jnp.int32), jnp.int32(turn_of(d, group))).astype(jnp.float32)


def group_kernel(planes, share, table, after, *refs):
    parts, out = refs[:-1], refs[-1]
    group = len(parts)
    corners = SIDES * SPECIES * share
    member = table[MEMBER : MEMBER + 1]
    blocks = [partner(member, d, group) for d in range(group)]
    for s in range(SPECIES):
        theta = planes * table[RATE_X + s : RATE_X + s + 1]
        for e in range(SIDES):
            weight = [jnp.exp((-b if e else b - (group - 1.0)) * theta) for b in blocks]
            here = pl.ds((e * SPECIES + s) * share, share)
            out[here, :] = sum(weight[d] * parts[d][here, :] for d in range(group))
            for k in range(SIDES):
                here = pl.ds(corners + (k * SIDES + e) * SPECIES + s, 1)
                out[here, :] = sum(weight[d] * parts[d][here, :] for d in range(group))


def group_sums(planes, share, table, after, parts):
    return pl.pallas_call(
        functools.partial(group_kernel, planes, share),
        in_specs=[VMEM, ANY] + [VMEM] * len(parts),
        out_specs=VMEM,
        out_shape=struct(*parts[0].shape),
        compiler_params=params(8),
        name="group_sums",
    )(table, after, *parts)


def column_kernel(table, y_table, z_table, conc, influx, *refs):
    count = SPECIES - 1
    h, u, (rough, y_out, last, weights, sums) = refs[:count], refs[count : count + SPECIES], refs[count + SPECIES :]
    planes, columns, width = influx.shape
    tile = (ROWS, width)
    row = row_position(columns, width)
    for s in range(SPECIES):
        theta = table[RATE_Y + s : RATE_Y + s + 1]
        weights[s, 0] = jnp.exp((row - (columns - 1.0)) * theta)
        weights[s, 1] = jnp.exp(-row * theta)
    inner = tiles(table, INNER + count * SPECIES, SPECIES, tile)
    double = tiles(table, DOUBLE + count * SPECIES, SPECIES, tile)
    part_a = tiles(table, PART_A + count * SPECIES, SPECIES, tile)
    (scale,) = tiles(table, SCALE_X + count, 1, tile)
    (decay,) = tiles(table, DECAY + count, 1, tile)
    bind, unbind, _ = tiles(table, KINETICS, 3, tile)

    def plane_of(s, value, i):
        for e in range(SIDES):
            sums[s, e, i : i + 1, :] = jnp.sum(weights[s, e] * value, axis=0, keepdims=True)
        u[s][i] = product(y_table[s], right_pair(value))

    def plane(i):
        for s in range(count):
            plane_of(s, h[s][i], i)

    def rows(k):
        here = tile_rows(k)
        up, sources, rising = jnp.zeros(tile, jnp.float32), [], []
        for i in range(planes):
            c = [conc[j, i, here, :] for j in range(SPECIES)]
            g = (bind * c[0] * c[1] - unbind * c[2]) * scale
            a = c[count]
            for j in range(SPECIES):
                g = g + inner[j] * c[j] + double[j] * turned(c[j])
                if j != count:
                    a = a + part_a[j] * c[j]
            up = g + decay * up
            sources.append(g)
            rising.append(up - a)
        down = jnp.zeros(tile, jnp.float32)
        for i in reversed(range(planes)):
            down = decay * down
            last[i, here, :] = rising[i] + down
            down = down + sources[i]

    side_by_side((planes, columns // ROWS), (plane, rows))
    side_by_side(
        (planes, columns // ROWS),
        (lambda i: plane_of(count, last[i], i), lambda k: sweep_of_b(0, table, conc, rough, k)),
    )
    for s in range(SPECIES):
        both = jnp.concatenate([sums[s, e] for e in range(SIDES)], axis=0)
        both = product(left_pair(both), z_table[s])
        for e in range(SIDES):
            y_out[pl.ds((e * SPECIES + s) * planes, planes), :] = both[e * planes : (e + 1) * planes]


def column_parts(table, y_table, z_table, conc, influx, h):
    planes, columns, width = influx.shape
    return pl.pallas_call(
        column_kernel,
        in_specs=[VMEM] * (5 + len(h)),
        out_specs=[VMEM] * (SPECIES + 2),
        out_shape=[pltpu.VMEM(influx.shape, jnp.float32)] * (SPECIES + 1)
        + [pltpu.VMEM((SIDES * SPECIES * planes, width), jnp.float32)],
        scratch_shapes=[
            pltpu.VMEM(influx.shape, jnp.float32),
            pltpu.VMEM((SPECIES, SIDES, columns, width), jnp.float32),
            pltpu.VMEM((SPECIES, SIDES, planes, width), jnp.float32),
        ],
        compiler_params=params(8),
        cost_estimate=pl.CostEstimate(flops=6 * conc.size * columns, bytes_accessed=8 * conc.size, transcendentals=0),
        name="column_parts",
    )(table, y_table, z_table, conc, influx, *h)


def finish_kernel(table, z_table, conc, *refs):
    u, rough, (out, weights, fades) = refs[:SPECIES], refs[SPECIES : 2 * SPECIES], refs[2 * SPECIES :]
    _, planes, columns, width = conc.shape
    at_once = 4 if planes % 4 == 0 else 1
    row = row_position(columns, width)
    position = row_position(planes, width)
    for s in range(SPECIES):
        rate_x = table[RATE_X + s : RATE_X + s + 1]
        rate_y = table[RATE_Y + s : RATE_Y + s + 1]
        weights[s, 0] = jnp.exp(-(row + 1.0) * rate_y)
        weights[s, 1] = jnp.exp((row - columns) * rate_y)
        fades[s, 0] = jnp.exp(-(position + 1.0) * rate_x)
        fades[s, 1] = jnp.exp((position - planes) * rate_x)
        for first in range(0, planes, at_once):
            here = slice(first, first + at_once)
            value = (u[s][here] - rough[s][here]).reshape(at_once * columns, width)
            done = product(left_pair(value), z_table[s])
            out[s, here] = conc[s, here] + done.reshape(at_once, columns, width)


def finish(table, z_table, conc, u, rough):
    _, planes, columns, width = conc.shape
    return pl.pallas_call(
        finish_kernel,
        in_specs=[VMEM] * (3 + len(u) + len(rough)),
        out_specs=[VMEM] * 3,
        out_shape=[
            pltpu.VMEM(conc.shape, jnp.float32),
            pltpu.VMEM((SPECIES, SIDES, columns, width), jnp.float32),
            pltpu.VMEM((SPECIES, SIDES, planes, width), jnp.float32),
        ],
        compiler_params=params(8),
        cost_estimate=pl.CostEstimate(flops=6 * conc.size * width, bytes_accessed=12 * conc.size, transcendentals=0),
        name="finish",
    )(table, z_table, conc, *u, *rough)


def enter_kernel(group, planes, share, table, sums, *refs):
    parts, wholes, outs, y_out = refs[:group], refs[group : -group - 1], refs[-group - 1 : -1], refs[-1]
    groups = len(wholes)
    corners = SIDES * SPECIES * share
    member = table[MEMBER : MEMBER + 1]
    blocks = [partner(member, d, group) for d in range(group)]
    y_out[pl.ds(0, sums.shape[0]), :] = sums[...]

    for s in range(SPECIES):
        theta = planes * table[RATE_X + s : RATE_X + s + 1]
        closing = 1.0 / (1.0 - jnp.exp(-float(group * groups) * theta))
        for e in range(SIDES):
            steps = [(groups - j - 1) if e else (j - 1 if j else groups - 1) for j in range(groups)]
            outside = [jnp.exp(-float(group * k) * theta) * closing for k in steps]
            to_target = [jnp.exp((t - (group - 1.0) if e else -t) * theta) for t in blocks]
            inside = []
            for t in blocks:
                away = [(b - t) if e else (t - b) for b in blocks]
                inside.append([jnp.where(k > 0.0, jnp.exp((1.0 - jnp.abs(k)) * theta), 0.0) for k in away])

            def entering_group(here):
                return sum(weight * whole[here, :] for weight, whole in zip(outside, wholes))

            here = pl.ds((e * SPECIES + s) * share, share)
            whole = entering_group(here)
            held = [part[here, :] for part in parts]
            for d in range(group):
                total = to_target[d] * whole
                for weight, part in zip(inside[d], held):
                    total = total + weight * part
                outs[d][here, :] = total

            for k in range(SIDES):
                at = (k * SIDES + e) * SPECIES + s
                here = pl.ds(corners + at, 1)
                total = to_target[0] * entering_group(here)
                for weight, part in zip(inside[0], parts):
                    total = total + weight * part[here, :]
                y_out[pl.ds(sums.shape[0] + at, 1), :] = total


def entering(planes, share, table, sums, parts, wholes):
    group, width = len(parts), parts[0].shape[1]
    return pl.pallas_call(
        functools.partial(enter_kernel, group, planes, share),
        in_specs=[VMEM] * (2 + group + len(wholes)),
        out_specs=[VMEM] * (group + 1),
        out_shape=[struct(SIDES * SPECIES * share, width)] * group + [struct(padded(sums.shape[0] + CORNERS), width)],
        compiler_params=params(8),
        name="entering",
    )(table, sums, *parts, *wholes)


def y_rows(planes, s, e):
    corners = SIDES * SPECIES * planes
    return [pl.ds((e * SPECIES + s) * planes, planes)] + [
        pl.ds(corners + (e * SIDES + k) * SPECIES + s, 1) for k in range(SIDES)
    ]


def bits(table, stage):
    rank = table[RANK_Y : RANK_Y + 1].astype(jnp.int32)
    low = lax.bitwise_and(rank, jnp.int32(2**stage - 1)).astype(jnp.float32)
    return low, lax.bitwise_and(rank, jnp.int32(2**stage)) != 0


def pair_kernel(planes, columns, stage, table, mine, other, out):
    _, above = bits(table, stage)
    for s in range(SPECIES):
        far = jnp.exp(-float(columns * 2**stage) * table[RATE_Y + s : RATE_Y + s + 1])
        for e in range(SIDES):
            keep = jnp.where(above, far, 1.0) if e else jnp.where(above, 1.0, far)
            take = jnp.where(above, 1.0, far) if e else jnp.where(above, far, 1.0)
            for here in y_rows(planes, s, e):
                out[here, :] = keep * mine[here, :] + take * other[here, :]


def pair_sums(planes, columns, stage, table, mine, other):
    return pl.pallas_call(
        functools.partial(pair_kernel, planes, columns, stage),
        in_specs=[VMEM] * 3,
        out_specs=VMEM,
        out_shape=struct(*mine.shape),
        compiler_params=params(8),
        name="pair_sums",
    )(table, mine, other)


def y_weights(table, s, e, columns, stages):
    theta = columns * table[RATE_Y + s : RATE_Y + s + 1]
    along = 2**stages
    closing = table[SCALE_Y + s : SCALE_Y + s + 1] / (1.0 - jnp.exp(-float(along) * theta))
    weights = [jnp.exp(-(along - 1.0) * theta) * closing]
    for stage in range(stages):
        low, above = bits(table, stage)
        near = (2.0**stage - 1.0 - low) if e else low
        around = float(along - 2 ** (stage + 1))
        steps = near + (jnp.where(above, around, 0.0) if e else jnp.where(above, 0.0, around))
        weights.append(jnp.exp(-steps * theta) * closing)
    return weights


def spread_kernel(group, share, table, weights, fades, base, *refs):
    parts, sums, (out_far, out, hold, enter, left) = refs[:group], refs[group:-5], refs[-5:]
    _, planes, columns, width = base.shape
    blocks = [partner(table[MEMBER : MEMBER + 1], d, group) for d in range(group)]
    at_once = planes // left.shape[1]
    copies = []
    for s in range(SPECIES):
        corner = []
        for e in range(SIDES):
            arrive = y_weights(table, s, e, columns, len(sums) - 1)
            lines, *corner_lines = y_rows(planes, s, e)
            enter[e] = weighted(arrive, sums, lines)
            corner.append([weighted(arrive, sums, here) for here in corner_lines])
        for e in range(SIDES):
            held = [part[pl.ds((e * SPECIES + s) * share, share), :] for part in parts]
            for b in range(group):
                there = pl.ds(b * share, share)
                mine = held[0]
                for d in range(1, group):
                    mine = jnp.where(blocks[d] == b, held[d], mine)
                lift = weights[s, 0, there, :] * corner[0][e] + weights[s, 1, there, :] * corner[1][e]
                hold[e, there, :] = mine + lift
        for first in range(0, planes, at_once):
            near = [[ref[i : i + 1] for i in range(first, first + at_once)] for ref in (fades.at[s, 0], fades.at[s, 1])]
            far = [[ref[i : i + 1] for i in range(first, first + at_once)] for ref in (enter.at[0], enter.at[1])]
            for start in range(0, columns, ROWS):
                here = slice(start, start + ROWS)
                x_low, x_high = hold[0, here, :], hold[1, here, :]
                y_low, y_high = weights[s, 0, here, :], weights[s, 1, here, :]
                for k in range(at_once):
                    added = near[0][k] * x_low + near[1][k] * x_high + far[0][k] * y_low + far[1][k] * y_high
                    out[s, first + k, here, :] = base[s, first + k, here, :] + added
            part = pl.ds(first, at_once)
            copies.append(pltpu.make_async_copy(out.at[s, part], out_far.at[s, part], left.at[s, first // at_once]))
            copies[-1].start()
    for copy in copies:
        copy.wait()


def spread(share, table, weights, fades, base, sums, parts):
    _, planes, columns, width = base.shape
    return pl.pallas_call(
        functools.partial(spread_kernel, len(parts), share),
        in_specs=[VMEM] * (4 + len(sums) + len(parts)),
        out_specs=ANY,
        out_shape=struct(*base.shape),
        scratch_shapes=[
            pltpu.VMEM(base.shape, jnp.float32),
            pltpu.VMEM((SIDES, columns, width), jnp.float32),
            pltpu.VMEM((SIDES, planes, width), jnp.float32),
            pltpu.SemaphoreType.DMA((SPECIES, planes // 4 if planes % 4 == 0 else planes)),
        ],
        compiler_params=params(8),
        name="spread",
    )(table, weights, fades, base, *parts, *sums)


def group_size(devices):
    size = 1
    while 4 * size * size <= 2 * devices and devices % (2 * size) == 0:
        size *= 2
    return size


def body(conc, influx, numbers, cross, kinetics):
    _, planes, columns, _ = conc.shape
    across, along = lax.axis_size("gx"), lax.axis_size("gy")
    group = group_size(across)
    share = columns // group
    rank = jnp.stack([lax.axis_index("gx"), lax.axis_index("gy")]).astype(jnp.int32)
    conc, influx, numbers, cross, kinetics = (
        pltpu.with_memory_space_constraint(x, pltpu.HBM) for x in (conc, influx, numbers, cross, kinetics)
    )

    def beside(value, stage):
        return lax.ppermute(value, "gy", [(i, i ^ 2**stage) for i in range(along)])

    def in_group(parts):
        pairs = [[(i, i ^ turn_of(d, group)) for i in range(across)] for d in range(group)]
        return [parts[0]] + [lax.ppermute(parts[d], "gx", pairs[d]) for d in range(1, group)]

    def over_groups(value, by):
        return lax.ppermute(value, "gx", [(i, (i + by * group) % across) for i in range(across)])

    *parts, table, conc, influx, y_table, z_table = edges(group, rank, numbers, cross, kinetics, conc, influx)
    parts = in_group(parts)
    swept = sweeps(table, conc, influx)
    h, rough = swept[: SPECIES - 1], swept[SPECIES - 1 :]
    whole = group_sums(planes, share, table, h[0], parts)
    wholes = [whole] + [over_groups(whole, j) for j in range(1, across // group)]
    *u, rough_first, sums = column_parts(table, y_table, z_table, conc, influx, h)
    *outs, sums = entering(planes, share, table, sums, parts, wholes)
    gathered = [sums]
    for stage in range(along.bit_length() - 1):
        if stage:
            sums = pair_sums(planes, columns, stage - 1, table, sums, gathered[-1])
        gathered.append(beside(sums, stage))
    outs = in_group(outs)
    base, weights, fades = finish(table, z_table, conc, u, [rough_first, *rough])
    return spread(share, table, weights, fades, base, gathered, outs)


def solution(mesh):
    placed = (P(None, "gx", "gy", None), P("gx", "gy", None), P(), P(), P())
    return jax.shard_map(
        body, mesh=mesh, in_specs=placed, out_specs=P(None, "gx", "gy", None), check_vma=False
    )
```

```python
import functools

import jax
import jax.numpy as jnp
from jax import lax
from jax.experimental import pallas as pl
from jax.experimental.pallas import tpu as pltpu
from jax.sharding import PartitionSpec as P

SPECIES = 3
ROWS = 8
SIDES = 2
CORNERS = SIDES * SIDES * SPECIES
SMEM = pl.BlockSpec(memory_space=pltpu.SMEM)
VMEM = pl.BlockSpec(memory_space=pltpu.VMEM)
ANY = pl.BlockSpec(memory_space=pl.ANY)

RATE_X, RATE_Y, SCALE_Y, SCALE_X, DECAY, KINETICS, MEMBER = 0, 3, 6, 9, 12, 15, 18
INNER, DOUBLE, PART_A, PART_B, RANK_Y, TABLE_ROWS = 19, 28, 37, 46, 55, 56


def padded(rows):
    return -(-rows // ROWS) * ROWS


def params(mebibytes):
    return pltpu.CompilerParams(vmem_limit_bytes=mebibytes * 2**20)


def struct(*shape):
    return jax.ShapeDtypeStruct(shape, jnp.float32)


def decay_rate(number):
    half = 0.5 * lax.rsqrt(number)
    square = half * half
    return 2.0 * jnp.log1p(half + square / (1.0 + jnp.sqrt(1.0 + square)))


def scaling(number):
    return lax.rsqrt(1.0 + 4.0 * number)


def splat(value, shape):
    return jnp.full(shape, value, jnp.float32)


def split(value):
    high = value.astype(jnp.bfloat16)
    return high, (value - high.astype(jnp.float32)).astype(jnp.bfloat16)


def left_pair(value):
    return jnp.concatenate(split(value), axis=1)


def right_pair(value):
    high, low = split(value)
    return jnp.concatenate(
        [jnp.concatenate([high, low], axis=1), jnp.concatenate([high, jnp.zeros_like(low)], axis=1)], axis=0
    )


def product(left, right):
    both = jnp.dot(left, right, preferred_element_type=jnp.float32)
    width = both.shape[1] // 2
    return both[:, :width] + both[:, width:]


def distances(length):
    rows = lax.broadcasted_iota(jnp.int32, (length, length), 0)
    columns = lax.broadcasted_iota(jnp.int32, (length, length), 1)
    return jnp.abs(rows - columns).astype(jnp.float32)


def depth_table(number, length):
    number = splat(number, (1, length))
    theta = decay_rate(number)
    spread = distances(length)
    factor = scaling(number) / (1.0 - jnp.exp(-length * theta))
    return (jnp.exp(-spread * theta) + jnp.exp((spread - length) * theta)) * factor


def column_table(number, length):
    number = splat(number, (1, length))
    return jnp.exp(-distances(length) * decay_rate(number)) * scaling(number)


def row_position(length, width):
    return lax.broadcasted_iota(jnp.int32, (length, width), 0).astype(jnp.float32)


def coefficients(numbers, cross, kinetics, tile):
    n = [[splat(numbers[s, d], tile) for d in range(3)] for s in range(SPECIES)]
    along_x, along_y, along_z = [], [], []
    for s in range(SPECIES):
        per_x, per_y = 1.0 / n[s][0], 1.0 / n[s][1]
        for j in range(SPECIES):
            mix = 1.0 if j == s else cross[s, j]
            along_x.append(n[j][0] * per_x * mix)
            along_y.append(n[j][1] * per_y * mix)
            along_z.append(n[j][2] * mix)
    scale = [scaling(n[s][0]) for s in range(SPECIES)]
    rate = [decay_rate(n[s][0]) for s in range(SPECIES)]
    return along_x, along_y, along_z, scale, rate, [splat(kinetics[i], tile) for i in range(3)]


def turned(value):
    width = value.shape[1]
    return pltpu.roll(value, 1, 1) + pltpu.roll(value, width - 1, 1)


def weighted(weights, refs, here):
    return sum(weight * ref[here, :] for weight, ref in zip(weights, refs))


def tile_rows(k):
    return pl.ds(k * ROWS if isinstance(k, int) else pl.multiple_of(k * ROWS, ROWS), ROWS)


def tiles(table, first, count, tile):
    return [jnp.broadcast_to(table[at : at + 1], tile) for at in range(first, first + count)]


def rates(c, influx, kinetics):
    bind, unbind, pump = kinetics
    binding = bind * c[0] * c[1] - unbind * c[2]
    pumping = pump * c[0] / (1.0 + c[0])
    return influx - 4.0 * binding - pumping, binding


def side_by_side(counts, steps):
    for k in range(max(counts)):
        for count, step in zip(counts, steps):
            if k < count:
                step(k)


def sweep_of_b(s, table, conc, out, k):
    _, planes, _, width = conc.shape
    tile = (ROWS, width)
    here = tile_rows(k)
    weight = tiles(table, PART_B + s * SPECIES, SPECIES, tile)
    (decay,) = tiles(table, DECAY + s, 1, tile)
    up, sources, rising = jnp.zeros(tile, jnp.float32), [], []
    for i in range(planes):
        b = weight[0] * conc[0, i, here, :] + weight[1] * conc[1, i, here, :] + weight[2] * conc[2, i, here, :]
        up = b + decay * up
        sources.append(b)
        rising.append(up)
    down = jnp.zeros(tile, jnp.float32)
    for i in reversed(range(planes)):
        down = decay * down
        out[i, here, :] = rising[i] + down
        down = down + sources[i]


def edge_kernel(group, rank_far, numbers_far, cross_far, kinetics_far, conc_far, influx_far, *refs):
    sent, refs = refs[:group], refs[group:]
    table, conc, influx, y_table, z_table, weights, hold, deep, solved, corners, arrived = refs[:11]
    rank, numbers, cross, kinetics, small = refs[11:]
    planes, columns, width = influx.shape
    chunks = arrived.shape[1]
    chunk = columns // chunks
    half = planes // 2
    share = columns // group
    tile = (ROWS, width)

    def copies(k):
        part = pl.ds(k * chunk, chunk)
        return (
            pltpu.make_async_copy(conc_far.at[:, :, part, :], conc.at[:, :, part, :], arrived.at[0, k]),
            pltpu.make_async_copy(influx_far.at[:, part, :], influx.at[:, part, :], arrived.at[1, k]),
        )

    for k in range(chunks):
        for copy in copies(k):
            copy.start()
    fars = (rank_far, numbers_far, cross_far, kinetics_far)
    nears = (rank, numbers, cross, kinetics)
    scalars = [pltpu.make_async_copy(far, near, small.at[k]) for k, (far, near) in enumerate(zip(fars, nears))]
    for copy in scalars:
        copy.start()
    for copy in scalars:
        copy.wait()

    along_x, along_y, along_z, scale, rate, kinetic = coefficients(numbers, cross, kinetics, tile)
    inner, double, single = [], [], []
    for s in range(SPECIES):
        for at in range(s * SPECIES, (s + 1) * SPECIES):
            inner.append((along_x[at] + along_y[at] - 2.0 * along_z[at]) * scale[s])
            double.append(along_z[at] * scale[s])
            single.append(along_y[at] * scale[s])
        for i in range(half):
            near = jnp.exp(-i * rate[s])
            far = jnp.exp(-(planes - 1.0 - i) * rate[s])
            weights[s, i, 0] = 0.5 * (near + far)
            weights[s, i, 1] = 0.5 * (near - far)
        number = splat(numbers[s, 1], tile)
        table[RATE_Y + s : RATE_Y + s + 1] = decay_rate(number)[:1]
        table[SCALE_Y + s : SCALE_Y + s + 1] = scaling(number)[:1]
        y_table[s] = left_pair(column_table(numbers[s, 1], columns))
        z_table[s] = right_pair(depth_table(numbers[s, 2], width))
    member = lax.rem(rank[0], group)
    entries = (
        (RATE_X, rate),
        (SCALE_X, scale),
        (DECAY, [jnp.exp(-value) for value in rate]),
        (KINETICS, kinetic),
        (MEMBER, [splat(member.astype(jnp.float32), tile)]),
        (RANK_Y, [splat(rank[1].astype(jnp.float32), tile)]),
        (INNER, inner),
        (DOUBLE, double),
        (PART_A, along_x),
        (PART_B, single),
    )
    for first, values in entries:
        for k, value in enumerate(values):
            table[first + k : first + k + 1] = value[:1]

    def sums_of(start):
        here = slice(start, start + ROWS)

        def at_plane(i):
            c = [conc[j, i, here, :] for j in range(SPECIES)]
            return c, *rates(c, influx[i, here, :], kinetic)

        zero = jnp.zeros(tile, jnp.float32)
        plus = [[zero] * (SPECIES + 1) for _ in range(SPECIES)]
        minus = [[zero] * (SPECIES + 1) for _ in range(SPECIES)]
        for i in range(half):
            low, low_first, low_binding = at_plane(i)
            high, high_first, high_binding = at_plane(planes - 1 - i)
            both = [x + y for x, y in zip(low, high)]
            apart = [x - y for x, y in zip(low, high)]
            change = (low_first + high_first, low_binding + high_binding)
            turn = (low_first - high_first, low_binding - high_binding)
            for s in range(SPECIES):
                even, odd = weights[s, i, 0], weights[s, i, 1]
                of = min(s, 1)
                for j, (p, m) in enumerate(zip(both + [change[of]], apart + [turn[of]])):
                    plus[s][j] = plus[s][j] + even * p
                    minus[s][j] = minus[s][j] + odd * m
        for s in range(SPECIES):
            for e in range(SIDES):
                sums = [p + m if e else p - m for p, m in zip(plus[s], minus[s])]
                v = sums[SPECIES] * scale[s]
                if s == 1:
                    v = -v
                w = 0.0
                for j in range(SPECIES):
                    at = s * SPECIES + j
                    v = v + inner[at] * sums[j] + double[at] * turned(sums[j])
                    w = w + single[at] * sums[j]
                hold[s, e, here, :] = v
                hold[s, SIDES + e, here, :] = w

    def deepen(k):
        here = slice(k * chunk, (k + 1) * chunk)
        for s in range(SPECIES):
            stack = jnp.concatenate([hold[s, e, here, :] for e in range(2 * SIDES)], axis=0)
            done = product(left_pair(stack), z_table[s])
            for e in range(2 * SIDES):
                deep[s, e, here, :] = done[e * chunk : (e + 1) * chunk]

    for k in range(chunks):
        for copy in copies(k):
            copy.wait()
        if k:
            deepen(k - 1)
        for start in range(k * chunk, (k + 1) * chunk, ROWS):
            sums_of(start)
    deepen(chunks - 1)

    row = row_position(columns, width)
    for s in range(SPECIES):
        theta = table[RATE_Y + s : RATE_Y + s + 1]
        rise = jnp.exp((row - (columns - 1.0)) * theta)
        fall = jnp.exp(-row * theta)
        both = product(y_table[s], right_pair(jnp.concatenate([deep[s, e] for e in range(SIDES)], axis=1)))
        for e in range(SIDES):
            solved[e, s] = both[:, e * width : (e + 1) * width] - deep[s, SIDES + e]
            for f, weight in enumerate((rise, fall)):
                at = (f * SIDES + e) * SPECIES + s
                corners[at : at + 1] = jnp.sum(weight * deep[s, e], axis=0, keepdims=True)
    for d in range(group):
        start = pl.multiple_of(lax.bitwise_xor(member, jnp.int32(turn_of(d, group))) * share, share)
        for s in range(SPECIES):
            for e in range(SIDES):
                sent[d][pl.ds((e * SPECIES + s) * share, share), :] = solved[e, s, pl.ds(start, share), :]
        sent[d][pl.ds(SIDES * SPECIES * share, corners.shape[0]), :] = corners[...]


def edges(group, rank, numbers, cross, kinetics, conc, influx):
    _, planes, columns, width = conc.shape
    chunks = columns // (2 * ROWS)
    hold = pltpu.VMEM((SPECIES, 2 * SIDES, columns, width), jnp.float32)
    rows = SIDES * SPECIES * (columns // group) + padded(CORNERS)
    return pl.pallas_call(
        functools.partial(edge_kernel, group),
        in_specs=[ANY] * 6,
        out_specs=[VMEM] * (group + 5),
        out_shape=[struct(rows, width)] * group
        + [
            pltpu.VMEM((TABLE_ROWS, width), jnp.float32),
            pltpu.VMEM(conc.shape, jnp.float32),
            pltpu.VMEM(influx.shape, jnp.float32),
            pltpu.VMEM((SPECIES, columns, 2 * columns), jnp.bfloat16),
            pltpu.VMEM((SPECIES, 2 * width, 2 * width), jnp.bfloat16),
        ],
        scratch_shapes=[
            pltpu.VMEM((SPECIES, planes // 2, 2, ROWS, width), jnp.float32),
            hold,
            hold,
            pltpu.VMEM((SIDES, SPECIES, columns, width), jnp.float32),
            pltpu.VMEM((padded(CORNERS), width), jnp.float32),
            pltpu.SemaphoreType.DMA((2, chunks)),
            pltpu.SMEM(rank.shape, rank.dtype),
            pltpu.SMEM(numbers.shape, numbers.dtype),
            pltpu.SMEM(cross.shape, cross.dtype),
            pltpu.SMEM(kinetics.shape, kinetics.dtype),
            pltpu.SemaphoreType.DMA((4,)),
        ],
        compiler_params=params(16),
        name="edges",
    )(rank, numbers, cross, kinetics, conc, influx)


def sweep_kernel(table, conc, influx, *refs):
    count = SPECIES - 1
    outs, roughs, holds = refs[:count], refs[count:-1], refs[-1]
    planes, columns, width = influx.shape
    tile = (ROWS, width)
    inner = tiles(table, INNER, count * SPECIES, tile)
    double = tiles(table, DOUBLE, count * SPECIES, tile)
    part_a = tiles(table, PART_A, count * SPECIES, tile)
    scale = tiles(table, SCALE_X, count, tile)
    decay = tiles(table, DECAY, count, tile)
    kinetic = tiles(table, KINETICS, 3, tile)

    def rows(k, g_hold):
        here = tile_rows(k)
        up = [jnp.zeros(tile, jnp.float32) for _ in range(count)]
        for i in range(planes):
            c = [conc[j, i, here, :] for j in range(SPECIES)]
            around = [turned(value) for value in c]
            first, binding = rates(c, influx[i, here, :], kinetic)
            change = (first, -binding, binding)
            for s in range(count):
                g = change[s] * scale[s]
                a = c[s]
                for j in range(SPECIES):
                    at = s * SPECIES + j
                    g = g + inner[at] * c[j] + double[at] * around[j]
                    if j != s:
                        a = a + part_a[at] * c[j]
                up[s] = g + decay[s] * up[s]
                g_hold[s, i] = g
                outs[s][i, here, :] = up[s] - a
        for s in range(count):
            down = jnp.zeros(tile, jnp.float32)
            for i in reversed(range(planes)):
                down = decay[s] * down
                outs[s][i, here, :] += down
                down += g_hold[s, i]
        for s, rough in enumerate(roughs, 1):
            sweep_of_b(s, table, conc, rough, k)

    together = holds.shape[0]

    def several(k, carry):
        for n in range(together):
            rows(k * together + n, holds.at[n])
        return carry

    lax.fori_loop(0, columns // ROWS // together, several, 0)


def sweeps(table, conc, influx):
    count = SPECIES - 1
    planes, columns, width = influx.shape
    together = 2 if columns // ROWS % 2 == 0 else 1
    return pl.pallas_call(
        sweep_kernel,
        in_specs=[VMEM] * 3,
        out_specs=[VMEM] * (2 * count),
        out_shape=[pltpu.VMEM(influx.shape, jnp.float32)] * (2 * count),
        scratch_shapes=[pltpu.VMEM((together, count, planes, ROWS, width), jnp.float32)],
        compiler_params=params(8),
        cost_estimate=pl.CostEstimate(flops=100 * conc.size, bytes_accessed=14 * conc.size, transcendentals=0),
        name="sweeps",
    )(table, conc, influx)


def turn_of(d, group):
    return (0, group - 1, *range(1, group - 1))[d]


def partner(member, d, group):
    return lax.bitwise_xor(member.astype(jnp.int32), jnp.int32(turn_of(d, group))).astype(jnp.float32)


def group_kernel(planes, share, table, after, *refs):
    parts, out = refs[:-1], refs[-1]
    group = len(parts)
    corners = SIDES * SPECIES * share
    member = table[MEMBER : MEMBER + 1]
    blocks = [partner(member, d, group) for d in range(group)]
    for s in range(SPECIES):
        theta = planes * table[RATE_X + s : RATE_X + s + 1]
        for e in range(SIDES):
            weight = [jnp.exp((-b if e else b - (group - 1.0)) * theta) for b in blocks]
            here = pl.ds((e * SPECIES + s) * share, share)
            out[here, :] = sum(weight[d] * parts[d][here, :] for d in range(group))
            for k in range(SIDES):
                here = pl.ds(corners + (k * SIDES + e) * SPECIES + s, 1)
                out[here, :] = sum(weight[d] * parts[d][here, :] for d in range(group))


def group_sums(planes, share, table, after, parts):
    return pl.pallas_call(
        functools.partial(group_kernel, planes, share),
        in_specs=[VMEM, ANY] + [VMEM] * len(parts),
        out_specs=VMEM,
        out_shape=struct(*parts[0].shape),
        compiler_params=params(8),
        name="group_sums",
    )(table, after, *parts)


def column_kernel(table, y_table, z_table, conc, influx, *refs):
    count = SPECIES - 1
    h, u, (rough, y_out, last, weights, sums) = refs[:count], refs[count : count + SPECIES], refs[count + SPECIES :]
    planes, columns, width = influx.shape
    tile = (ROWS, width)
    row = row_position(columns, width)
    for s in range(SPECIES):
        theta = table[RATE_Y + s : RATE_Y + s + 1]
        weights[s, 0] = jnp.exp((row - (columns - 1.0)) * theta)
        weights[s, 1] = jnp.exp(-row * theta)
    inner = tiles(table, INNER + count * SPECIES, SPECIES, tile)
    double = tiles(table, DOUBLE + count * SPECIES, SPECIES, tile)
    part_a = tiles(table, PART_A + count * SPECIES, SPECIES, tile)
    (scale,) = tiles(table, SCALE_X + count, 1, tile)
    (decay,) = tiles(table, DECAY + count, 1, tile)
    bind, unbind, _ = tiles(table, KINETICS, 3, tile)

    def plane_of(s, value, i):
        for e in range(SIDES):
            sums[s, e, i : i + 1, :] = jnp.sum(weights[s, e] * value, axis=0, keepdims=True)
        u[s][i] = product(y_table[s], right_pair(value))

    def plane(i):
        for s in range(count):
            plane_of(s, h[s][i], i)

    def rows(k):
        here = tile_rows(k)
        up, sources, rising = jnp.zeros(tile, jnp.float32), [], []
        for i in range(planes):
            c = [conc[j, i, here, :] for j in range(SPECIES)]
            g = (bind * c[0] * c[1] - unbind * c[2]) * scale
            a = c[count]
            for j in range(SPECIES):
                g = g + inner[j] * c[j] + double[j] * turned(c[j])
                if j != count:
                    a = a + part_a[j] * c[j]
            up = g + decay * up
            sources.append(g)
            rising.append(up - a)
        down = jnp.zeros(tile, jnp.float32)
        for i in reversed(range(planes)):
            down = decay * down
            last[i, here, :] = rising[i] + down
            down = down + sources[i]

    side_by_side((planes, columns // ROWS), (plane, rows))
    side_by_side(
        (planes, columns // ROWS),
        (lambda i: plane_of(count, last[i], i), lambda k: sweep_of_b(0, table, conc, rough, k)),
    )
    for s in range(SPECIES):
        both = jnp.concatenate([sums[s, e] for e in range(SIDES)], axis=0)
        both = product(left_pair(both), z_table[s])
        for e in range(SIDES):
            y_out[pl.ds((e * SPECIES + s) * planes, planes), :] = both[e * planes : (e + 1) * planes]


def column_parts(table, y_table, z_table, conc, influx, h):
    planes, columns, width = influx.shape
    return pl.pallas_call(
        column_kernel,
        in_specs=[VMEM] * (5 + len(h)),
        out_specs=[VMEM] * (SPECIES + 2),
        out_shape=[pltpu.VMEM(influx.shape, jnp.float32)] * (SPECIES + 1)
        + [pltpu.VMEM((SIDES * SPECIES * planes, width), jnp.float32)],
        scratch_shapes=[
            pltpu.VMEM(influx.shape, jnp.float32),
            pltpu.VMEM((SPECIES, SIDES, columns, width), jnp.float32),
            pltpu.VMEM((SPECIES, SIDES, planes, width), jnp.float32),
        ],
        compiler_params=params(8),
        cost_estimate=pl.CostEstimate(flops=6 * conc.size * columns, bytes_accessed=8 * conc.size, transcendentals=0),
        name="column_parts",
    )(table, y_table, z_table, conc, influx, *h)


def finish_kernel(table, z_table, conc, *refs):
    u, rough, (out, weights, fades) = refs[:SPECIES], refs[SPECIES : 2 * SPECIES], refs[2 * SPECIES :]
    _, planes, columns, width = conc.shape
    at_once = 4 if planes % 4 == 0 else 1
    row = row_position(columns, width)
    position = row_position(planes, width)
    for s in range(SPECIES):
        rate_x = table[RATE_X + s : RATE_X + s + 1]
        rate_y = table[RATE_Y + s : RATE_Y + s + 1]
        weights[s, 0] = jnp.exp(-(row + 1.0) * rate_y)
        weights[s, 1] = jnp.exp((row - columns) * rate_y)
        fades[s, 0] = jnp.exp(-(position + 1.0) * rate_x)
        fades[s, 1] = jnp.exp((position - planes) * rate_x)
        for first in range(0, planes, at_once):
            here = slice(first, first + at_once)
            value = (u[s][here] - rough[s][here]).reshape(at_once * columns, width)
            done = product(left_pair(value), z_table[s])
            out[s, here] = conc[s, here] + done.reshape(at_once, columns, width)


def finish(table, z_table, conc, u, rough):
    _, planes, columns, width = conc.shape
    return pl.pallas_call(
        finish_kernel,
        in_specs=[VMEM] * (3 + len(u) + len(rough)),
        out_specs=[VMEM] * 3,
        out_shape=[
            pltpu.VMEM(conc.shape, jnp.float32),
            pltpu.VMEM((SPECIES, SIDES, columns, width), jnp.float32),
            pltpu.VMEM((SPECIES, SIDES, planes, width), jnp.float32),
        ],
        compiler_params=params(8),
        cost_estimate=pl.CostEstimate(flops=6 * conc.size * width, bytes_accessed=12 * conc.size, transcendentals=0),
        name="finish",
    )(table, z_table, conc, *u, *rough)


def enter_kernel(group, planes, share, table, sums, *refs):
    parts, wholes, outs, y_out = refs[:group], refs[group : -group - 1], refs[-group - 1 : -1], refs[-1]
    groups = len(wholes)
    corners = SIDES * SPECIES * share
    member = table[MEMBER : MEMBER + 1]
    blocks = [partner(member, d, group) for d in range(group)]
    y_out[pl.ds(0, sums.shape[0]), :] = sums[...]

    for s in range(SPECIES):
        theta = planes * table[RATE_X + s : RATE_X + s + 1]
        closing = 1.0 / (1.0 - jnp.exp(-float(group * groups) * theta))
        for e in range(SIDES):
            steps = [(groups - j - 1) if e else (j - 1 if j else groups - 1) for j in range(groups)]
            outside = [jnp.exp(-float(group * k) * theta) * closing for k in steps]
            to_target = [jnp.exp((t - (group - 1.0) if e else -t) * theta) for t in blocks]
            inside = []
            for t in blocks:
                away = [(b - t) if e else (t - b) for b in blocks]
                inside.append([jnp.where(k > 0.0, jnp.exp((1.0 - jnp.abs(k)) * theta), 0.0) for k in away])

            def entering_group(here):
                return sum(weight * whole[here, :] for weight, whole in zip(outside, wholes))

            here = pl.ds((e * SPECIES + s) * share, share)
            whole = entering_group(here)
            held = [part[here, :] for part in parts]
            for d in range(group):
                total = to_target[d] * whole
                for weight, part in zip(inside[d], held):
                    total = total + weight * part
                outs[d][here, :] = total

            for k in range(SIDES):
                at = (k * SIDES + e) * SPECIES + s
                here = pl.ds(corners + at, 1)
                total = to_target[0] * entering_group(here)
                for weight, part in zip(inside[0], parts):
                    total = total + weight * part[here, :]
                y_out[pl.ds(sums.shape[0] + at, 1), :] = total


def entering(planes, share, table, sums, parts, wholes):
    group, width = len(parts), parts[0].shape[1]
    return pl.pallas_call(
        functools.partial(enter_kernel, group, planes, share),
        in_specs=[VMEM] * (2 + group + len(wholes)),
        out_specs=[VMEM] * (group + 1),
        out_shape=[struct(SIDES * SPECIES * share, width)] * group + [struct(padded(sums.shape[0] + CORNERS), width)],
        compiler_params=params(8),
        name="entering",
    )(table, sums, *parts, *wholes)


def y_rows(planes, s, e):
    corners = SIDES * SPECIES * planes
    return [pl.ds((e * SPECIES + s) * planes, planes)] + [
        pl.ds(corners + (e * SIDES + k) * SPECIES + s, 1) for k in range(SIDES)
    ]


def flipped(rank, d):
    return lax.bitwise_xor(rank.astype(jnp.int32), jnp.int32(d)).astype(jnp.float32)


def y_weight(table, s, e, columns, along, target, block):
    theta = columns * table[RATE_Y + s : RATE_Y + s + 1]
    closing = table[SCALE_Y + s : SCALE_Y + s + 1] / (1.0 - jnp.exp(-float(along) * theta))
    steps = (block - target - 1.0) if e else (target - block - 1.0)
    steps = jnp.where(steps < 0.0, steps + along, steps)
    return jnp.exp(-steps * theta) * closing


def pair_kernel(planes, columns, along, table, mine, other, *outs):
    rank = table[RANK_Y : RANK_Y + 1]
    across = flipped(rank, along // 2)
    for d, out in enumerate(outs, 1):
        target = flipped(rank, d)
        for s in range(SPECIES):
            for e in range(SIDES):
                keep = y_weight(table, s, e, columns, along, target, rank)
                take = y_weight(table, s, e, columns, along, target, across)
                for here in y_rows(planes, s, e):
                    out[here, :] = keep * mine[here, :] + take * other[here, :]


def pair_sums(planes, columns, along, table, mine, other):
    return pl.pallas_call(
        functools.partial(pair_kernel, planes, columns, along),
        in_specs=[VMEM] * 3,
        out_specs=[VMEM] * (along // 2 - 1),
        out_shape=[struct(*mine.shape)] * (along // 2 - 1),
        compiler_params=params(8),
        name="pair_sums",
    )(table, mine, other)


def spread_kernel(along, group, share, table, weights, fades, base, *refs):
    parts, sums, (out_far, out, hold, enter, left) = refs[:group], refs[group:-5], refs[-5:]
    _, planes, columns, width = base.shape
    blocks = [partner(table[MEMBER : MEMBER + 1], d, group) for d in range(group)]
    at_once = planes // left.shape[1]
    rank = table[RANK_Y : RANK_Y + 1]
    copies = []
    for s in range(SPECIES):
        corner = []
        for e in range(SIDES):
            sources = [rank, flipped(rank, along // 2)][: len(sums)]
            arrive = [y_weight(table, s, e, columns, along, rank, block) for block in sources]
            arrive += [1.0] * (len(sums) - len(arrive))
            lines, *corner_lines = y_rows(planes, s, e)
            enter[e] = weighted(arrive, sums, lines)
            corner.append([weighted(arrive, sums, here) for here in corner_lines])
        for e in range(SIDES):
            held = [part[pl.ds((e * SPECIES + s) * share, share), :] for part in parts]
            for b in range(group):
                there = pl.ds(b * share, share)
                mine = held[0]
                for d in range(1, group):
                    mine = jnp.where(blocks[d] == b, held[d], mine)
                lift = weights[s, 0, there, :] * corner[0][e] + weights[s, 1, there, :] * corner[1][e]
                hold[e, there, :] = mine + lift
        for first in range(0, planes, at_once):
            near = [[ref[i : i + 1] for i in range(first, first + at_once)] for ref in (fades.at[s, 0], fades.at[s, 1])]
            far = [[ref[i : i + 1] for i in range(first, first + at_once)] for ref in (enter.at[0], enter.at[1])]
            for start in range(0, columns, ROWS):
                here = slice(start, start + ROWS)
                x_low, x_high = hold[0, here, :], hold[1, here, :]
                y_low, y_high = weights[s, 0, here, :], weights[s, 1, here, :]
                for k in range(at_once):
                    added = near[0][k] * x_low + near[1][k] * x_high + far[0][k] * y_low + far[1][k] * y_high
                    out[s, first + k, here, :] = base[s, first + k, here, :] + added
            part = pl.ds(first, at_once)
            copies.append(pltpu.make_async_copy(out.at[s, part], out_far.at[s, part], left.at[s, first // at_once]))
            copies[-1].start()
    for copy in copies:
        copy.wait()


def spread(along, share, table, weights, fades, base, sums, parts):
    _, planes, columns, width = base.shape
    return pl.pallas_call(
        functools.partial(spread_kernel, along, len(parts), share),
        in_specs=[VMEM] * (4 + len(sums) + len(parts)),
        out_specs=ANY,
        out_shape=struct(*base.shape),
        scratch_shapes=[
            pltpu.VMEM(base.shape, jnp.float32),
            pltpu.VMEM((SIDES, columns, width), jnp.float32),
            pltpu.VMEM((SIDES, planes, width), jnp.float32),
            pltpu.SemaphoreType.DMA((SPECIES, planes // 4 if planes % 4 == 0 else planes)),
        ],
        compiler_params=params(8),
        name="spread",
    )(table, weights, fades, base, *parts, *sums)


def group_size(devices):
    size = 1
    while 4 * size * size <= 2 * devices and devices % (2 * size) == 0:
        size *= 2
    return size


def body(conc, influx, numbers, cross, kinetics):
    _, planes, columns, _ = conc.shape
    across, along = lax.axis_size("gx"), lax.axis_size("gy")
    group = group_size(across)
    share = columns // group
    rank = jnp.stack([lax.axis_index("gx"), lax.axis_index("gy")]).astype(jnp.int32)
    conc, influx, numbers, cross, kinetics = (
        pltpu.with_memory_space_constraint(x, pltpu.HBM) for x in (conc, influx, numbers, cross, kinetics)
    )

    def beside(value, d):
        return lax.ppermute(value, "gy", [(i, i ^ d) for i in range(along)])

    def in_group(parts):
        pairs = [[(i, i ^ turn_of(d, group)) for i in range(across)] for d in range(group)]
        return [parts[0]] + [lax.ppermute(parts[d], "gx", pairs[d]) for d in range(1, group)]

    def over_groups(value, by):
        return lax.ppermute(value, "gx", [(i, (i + by * group) % across) for i in range(across)])

    *parts, table, conc, influx, y_table, z_table = edges(group, rank, numbers, cross, kinetics, conc, influx)
    parts = in_group(parts)
    swept = sweeps(table, conc, influx)
    h, rough = swept[: SPECIES - 1], swept[SPECIES - 1 :]
    whole = group_sums(planes, share, table, h[0], parts)
    wholes = [whole] + [over_groups(whole, j) for j in range(1, across // group)]
    *u, rough_first, sums = column_parts(table, y_table, z_table, conc, influx, h)
    *outs, sums = entering(planes, share, table, sums, parts, wholes)
    gathered = [sums]
    if along > 1:
        gathered.append(beside(sums, along // 2))
    if along > 2:
        onward = pair_sums(planes, columns, along, table, *gathered)
        gathered += [beside(value, d) for d, value in enumerate(onward, 1)]
    outs = in_group(outs)
    base, weights, fades = finish(table, z_table, conc, u, [rough_first, *rough])
    return spread(along, share, table, weights, fades, base, gathered, outs)


def solution(mesh):
    placed = (P(None, "gx", "gy", None), P("gx", "gy", None), P(), P(), P())
    return jax.shard_map(
        body, mesh=mesh, in_specs=placed, out_specs=P(None, "gx", "gy", None), check_vma=False
    )
```

```python
import functools

import jax
import jax.numpy as jnp
from jax import lax
from jax.experimental import pallas as pl
from jax.experimental.pallas import tpu as pltpu
from jax.sharding import PartitionSpec as P

SPECIES = 3
ROWS = 8
SIDES = 2
CORNERS = SIDES * SIDES * SPECIES
SMEM = pl.BlockSpec(memory_space=pltpu.SMEM)
VMEM = pl.BlockSpec(memory_space=pltpu.VMEM)
ANY = pl.BlockSpec(memory_space=pl.ANY)

RATE_X, RATE_Y, SCALE_Y, SCALE_X, DECAY, KINETICS, MEMBER = 0, 3, 6, 9, 12, 15, 18
INNER, DOUBLE, PART_A, PART_B, RANK_Y, TABLE_ROWS = 19, 28, 37, 46, 55, 56


def padded(rows):
    return -(-rows // ROWS) * ROWS


def params(mebibytes):
    return pltpu.CompilerParams(vmem_limit_bytes=mebibytes * 2**20)


def struct(*shape):
    return jax.ShapeDtypeStruct(shape, jnp.float32)


def decay_rate(number):
    half = 0.5 * lax.rsqrt(number)
    square = half * half
    return 2.0 * jnp.log1p(half + square / (1.0 + jnp.sqrt(1.0 + square)))


def scaling(number):
    return lax.rsqrt(1.0 + 4.0 * number)


def splat(value, shape):
    return jnp.full(shape, value, jnp.float32)


def split(value):
    high = value.astype(jnp.bfloat16)
    return high, (value - high.astype(jnp.float32)).astype(jnp.bfloat16)


def left_pair(value):
    return jnp.concatenate(split(value), axis=1)


def right_pair(value):
    high, low = split(value)
    return jnp.concatenate(
        [jnp.concatenate([high, low], axis=1), jnp.concatenate([high, jnp.zeros_like(low)], axis=1)], axis=0
    )


def product(left, right):
    both = jnp.dot(left, right, preferred_element_type=jnp.float32)
    width = both.shape[1] // 2
    return both[:, :width] + both[:, width:]


def distances(length):
    rows = lax.broadcasted_iota(jnp.int32, (length, length), 0)
    columns = lax.broadcasted_iota(jnp.int32, (length, length), 1)
    return jnp.abs(rows - columns).astype(jnp.float32)


def depth_table(number, length):
    number = splat(number, (1, length))
    theta = decay_rate(number)
    spread = distances(length)
    factor = scaling(number) / (1.0 - jnp.exp(-length * theta))
    return (jnp.exp(-spread * theta) + jnp.exp((spread - length) * theta)) * factor


def column_table(number, length):
    number = splat(number, (1, length))
    return jnp.exp(-distances(length) * decay_rate(number)) * scaling(number)


def row_position(length, width):
    return lax.broadcasted_iota(jnp.int32, (length, width), 0).astype(jnp.float32)


def coefficients(numbers, cross, kinetics, tile):
    n = [[splat(numbers[s, d], tile) for d in range(3)] for s in range(SPECIES)]
    along_x, along_y, along_z = [], [], []
    for s in range(SPECIES):
        per_x, per_y = 1.0 / n[s][0], 1.0 / n[s][1]
        for j in range(SPECIES):
            mix = 1.0 if j == s else cross[s, j]
            along_x.append(n[j][0] * per_x * mix)
            along_y.append(n[j][1] * per_y * mix)
            along_z.append(n[j][2] * mix)
    scale = [scaling(n[s][0]) for s in range(SPECIES)]
    rate = [decay_rate(n[s][0]) for s in range(SPECIES)]
    return along_x, along_y, along_z, scale, rate, [splat(kinetics[i], tile) for i in range(3)]


def turned(value):
    width = value.shape[1]
    return pltpu.roll(value, 1, 1) + pltpu.roll(value, width - 1, 1)


def weighted(weights, refs, here):
    return sum(weight * ref[here, :] for weight, ref in zip(weights, refs))


def tile_rows(k):
    return pl.ds(k * ROWS if isinstance(k, int) else pl.multiple_of(k * ROWS, ROWS), ROWS)


def tiles(table, first, count, tile):
    return [jnp.broadcast_to(table[at : at + 1], tile) for at in range(first, first + count)]


def rates(c, influx, kinetics):
    bind, unbind, pump = kinetics
    binding = bind * c[0] * c[1] - unbind * c[2]
    pumping = pump * c[0] / (1.0 + c[0])
    return influx - 4.0 * binding - pumping, binding


def side_by_side(counts, steps):
    for k in range(max(counts)):
        for count, step in zip(counts, steps):
            if k < count:
                step(k)


def sweep_of_b(s, table, conc, out, k):
    _, planes, _, width = conc.shape
    tile = (ROWS, width)
    here = tile_rows(k)
    weight = tiles(table, PART_B + s * SPECIES, SPECIES, tile)
    (decay,) = tiles(table, DECAY + s, 1, tile)
    up, sources, rising = jnp.zeros(tile, jnp.float32), [], []
    for i in range(planes):
        b = weight[0] * conc[0, i, here, :] + weight[1] * conc[1, i, here, :] + weight[2] * conc[2, i, here, :]
        up = b + decay * up
        sources.append(b)
        rising.append(up)
    down = jnp.zeros(tile, jnp.float32)
    for i in reversed(range(planes)):
        down = decay * down
        out[i, here, :] = rising[i] + down
        down = down + sources[i]


def edge_kernel(group, x_far, y_far, numbers_far, cross_far, kinetics_far, conc_far, influx_far, *refs):
    sent, refs = refs[:group], refs[group:]
    table, conc, influx, y_table, z_table, weights, hold, deep, solved, corners, arrived = refs[:11]
    rank_x, rank_y, numbers, cross, kinetics, small = refs[11:]
    planes, columns, width = influx.shape
    chunks = arrived.shape[1]
    chunk = columns // chunks
    half = planes // 2
    share = columns // group
    tile = (ROWS, width)

    def copies(k):
        part = pl.ds(k * chunk, chunk)
        return (
            pltpu.make_async_copy(conc_far.at[:, :, part, :], conc.at[:, :, part, :], arrived.at[0, k]),
            pltpu.make_async_copy(influx_far.at[:, part, :], influx.at[:, part, :], arrived.at[1, k]),
        )

    for k in range(chunks):
        for copy in copies(k):
            copy.start()
    fars = (x_far, y_far, numbers_far, cross_far, kinetics_far)
    nears = (rank_x, rank_y, numbers, cross, kinetics)
    scalars = [pltpu.make_async_copy(far, near, small.at[k]) for k, (far, near) in enumerate(zip(fars, nears))]
    for copy in scalars:
        copy.start()
    for copy in scalars:
        copy.wait()

    along_x, along_y, along_z, scale, rate, kinetic = coefficients(numbers, cross, kinetics, tile)
    inner, double, single = [], [], []
    for s in range(SPECIES):
        for at in range(s * SPECIES, (s + 1) * SPECIES):
            inner.append((along_x[at] + along_y[at] - 2.0 * along_z[at]) * scale[s])
            double.append(along_z[at] * scale[s])
            single.append(along_y[at] * scale[s])
        for i in range(half):
            near = jnp.exp(-i * rate[s])
            far = jnp.exp(-(planes - 1.0 - i) * rate[s])
            weights[s, i, 0] = 0.5 * (near + far)
            weights[s, i, 1] = 0.5 * (near - far)
        number = splat(numbers[s, 1], tile)
        table[RATE_Y + s : RATE_Y + s + 1] = decay_rate(number)[:1]
        table[SCALE_Y + s : SCALE_Y + s + 1] = scaling(number)[:1]
        y_table[s] = left_pair(column_table(numbers[s, 1], columns))
        z_table[s] = right_pair(depth_table(numbers[s, 2], width))
    member = lax.rem(rank_x[0], group)
    entries = (
        (RATE_X, rate),
        (SCALE_X, scale),
        (DECAY, [jnp.exp(-value) for value in rate]),
        (KINETICS, kinetic),
        (MEMBER, [splat(member.astype(jnp.float32), tile)]),
        (RANK_Y, [splat(rank_y[0].astype(jnp.float32), tile)]),
        (INNER, inner),
        (DOUBLE, double),
        (PART_A, along_x),
        (PART_B, single),
    )
    for first, values in entries:
        for k, value in enumerate(values):
            table[first + k : first + k + 1] = value[:1]

    def sums_of(start):
        here = slice(start, start + ROWS)

        def at_plane(i):
            c = [conc[j, i, here, :] for j in range(SPECIES)]
            return c, *rates(c, influx[i, here, :], kinetic)

        zero = jnp.zeros(tile, jnp.float32)
        plus = [[zero] * (SPECIES + 1) for _ in range(SPECIES)]
        minus = [[zero] * (SPECIES + 1) for _ in range(SPECIES)]
        for i in range(half):
            low, low_first, low_binding = at_plane(i)
            high, high_first, high_binding = at_plane(planes - 1 - i)
            both = [x + y for x, y in zip(low, high)]
            apart = [x - y for x, y in zip(low, high)]
            change = (low_first + high_first, low_binding + high_binding)
            turn = (low_first - high_first, low_binding - high_binding)
            for s in range(SPECIES):
                even, odd = weights[s, i, 0], weights[s, i, 1]
                of = min(s, 1)
                for j, (p, m) in enumerate(zip(both + [change[of]], apart + [turn[of]])):
                    plus[s][j] = plus[s][j] + even * p
                    minus[s][j] = minus[s][j] + odd * m
        for s in range(SPECIES):
            for e in range(SIDES):
                sums = [p + m if e else p - m for p, m in zip(plus[s], minus[s])]
                v = sums[SPECIES] * scale[s]
                if s == 1:
                    v = -v
                w = 0.0
                for j in range(SPECIES):
                    at = s * SPECIES + j
                    v = v + inner[at] * sums[j] + double[at] * turned(sums[j])
                    w = w + single[at] * sums[j]
                hold[s, e, here, :] = v
                hold[s, SIDES + e, here, :] = w

    def deepen(k):
        here = slice(k * chunk, (k + 1) * chunk)
        for s in range(SPECIES):
            stack = jnp.concatenate([hold[s, e, here, :] for e in range(2 * SIDES)], axis=0)
            done = product(left_pair(stack), z_table[s])
            for e in range(2 * SIDES):
                deep[s, e, here, :] = done[e * chunk : (e + 1) * chunk]

    for k in range(chunks):
        for copy in copies(k):
            copy.wait()
        if k:
            deepen(k - 1)
        for start in range(k * chunk, (k + 1) * chunk, ROWS):
            sums_of(start)
    deepen(chunks - 1)

    row = row_position(columns, width)
    for s in range(SPECIES):
        theta = table[RATE_Y + s : RATE_Y + s + 1]
        rise = jnp.exp((row - (columns - 1.0)) * theta)
        fall = jnp.exp(-row * theta)
        both = product(y_table[s], right_pair(jnp.concatenate([deep[s, e] for e in range(SIDES)], axis=1)))
        for e in range(SIDES):
            solved[e, s] = both[:, e * width : (e + 1) * width] - deep[s, SIDES + e]
            for f, weight in enumerate((rise, fall)):
                at = (f * SIDES + e) * SPECIES + s
                corners[at : at + 1] = jnp.sum(weight * deep[s, e], axis=0, keepdims=True)
    for d in range(group):
        start = pl.multiple_of(lax.bitwise_xor(member, jnp.int32(turn_of(d, group))) * share, share)
        for s in range(SPECIES):
            for e in range(SIDES):
                sent[d][pl.ds((e * SPECIES + s) * share, share), :] = solved[e, s, pl.ds(start, share), :]
        sent[d][pl.ds(SIDES * SPECIES * share, corners.shape[0]), :] = corners[...]


def edges(group, rank_x, rank_y, numbers, cross, kinetics, conc, influx):
    _, planes, columns, width = conc.shape
    chunks = columns // (2 * ROWS)
    hold = pltpu.VMEM((SPECIES, 2 * SIDES, columns, width), jnp.float32)
    rows = SIDES * SPECIES * (columns // group) + padded(CORNERS)
    return pl.pallas_call(
        functools.partial(edge_kernel, group),
        in_specs=[ANY] * 7,
        out_specs=[VMEM] * (group + 5),
        out_shape=[struct(rows, width)] * group
        + [
            pltpu.VMEM((TABLE_ROWS, width), jnp.float32),
            pltpu.VMEM(conc.shape, jnp.float32),
            pltpu.VMEM(influx.shape, jnp.float32),
            pltpu.VMEM((SPECIES, columns, 2 * columns), jnp.bfloat16),
            pltpu.VMEM((SPECIES, 2 * width, 2 * width), jnp.bfloat16),
        ],
        scratch_shapes=[
            pltpu.VMEM((SPECIES, planes // 2, 2, ROWS, width), jnp.float32),
            hold,
            hold,
            pltpu.VMEM((SIDES, SPECIES, columns, width), jnp.float32),
            pltpu.VMEM((padded(CORNERS), width), jnp.float32),
            pltpu.SemaphoreType.DMA((2, chunks)),
            *(pltpu.SMEM(x.shape, x.dtype) for x in (rank_x, rank_y, numbers, cross, kinetics)),
            pltpu.SemaphoreType.DMA((5,)),
        ],
        compiler_params=params(16),
        name="edges",
    )(rank_x, rank_y, numbers, cross, kinetics, conc, influx)


def sweep_kernel(table, conc, influx, *refs):
    count = SPECIES - 1
    outs, roughs, holds = refs[:count], refs[count:-1], refs[-1]
    planes, columns, width = influx.shape
    tile = (ROWS, width)
    inner = tiles(table, INNER, count * SPECIES, tile)
    double = tiles(table, DOUBLE, count * SPECIES, tile)
    part_a = tiles(table, PART_A, count * SPECIES, tile)
    scale = tiles(table, SCALE_X, count, tile)
    decay = tiles(table, DECAY, count, tile)
    kinetic = tiles(table, KINETICS, 3, tile)

    def rows(k, g_hold):
        here = tile_rows(k)
        up = [jnp.zeros(tile, jnp.float32) for _ in range(count)]
        for i in range(planes):
            c = [conc[j, i, here, :] for j in range(SPECIES)]
            around = [turned(value) for value in c]
            first, binding = rates(c, influx[i, here, :], kinetic)
            change = (first, -binding, binding)
            for s in range(count):
                g = change[s] * scale[s]
                a = c[s]
                for j in range(SPECIES):
                    at = s * SPECIES + j
                    g = g + inner[at] * c[j] + double[at] * around[j]
                    if j != s:
                        a = a + part_a[at] * c[j]
                up[s] = g + decay[s] * up[s]
                g_hold[s, i] = g
                outs[s][i, here, :] = up[s] - a
        for s in range(count):
            down = jnp.zeros(tile, jnp.float32)
            for i in reversed(range(planes)):
                down = decay[s] * down
                outs[s][i, here, :] += down
                down += g_hold[s, i]
        for s, rough in enumerate(roughs, 1):
            sweep_of_b(s, table, conc, rough, k)

    together = holds.shape[0]

    def several(k, carry):
        for n in range(together):
            rows(k * together + n, holds.at[n])
        return carry

    lax.fori_loop(0, columns // ROWS // together, several, 0)


def sweeps(table, conc, influx):
    count = SPECIES - 1
    planes, columns, width = influx.shape
    together = 2 if columns // ROWS % 2 == 0 else 1
    return pl.pallas_call(
        sweep_kernel,
        in_specs=[VMEM] * 3,
        out_specs=[VMEM] * (2 * count),
        out_shape=[pltpu.VMEM(influx.shape, jnp.float32)] * (2 * count),
        scratch_shapes=[pltpu.VMEM((together, count, planes, ROWS, width), jnp.float32)],
        compiler_params=params(8),
        cost_estimate=pl.CostEstimate(flops=100 * conc.size, bytes_accessed=14 * conc.size, transcendentals=0),
        name="sweeps",
    )(table, conc, influx)


def turn_of(d, group):
    return (0, group - 1, *range(1, group - 1))[d]


def partner(member, d, group):
    return lax.bitwise_xor(member.astype(jnp.int32), jnp.int32(turn_of(d, group))).astype(jnp.float32)


def group_kernel(planes, share, table, after, *refs):
    parts, out = refs[:-1], refs[-1]
    group = len(parts)
    corners = SIDES * SPECIES * share
    member = table[MEMBER : MEMBER + 1]
    blocks = [partner(member, d, group) for d in range(group)]
    for s in range(SPECIES):
        theta = planes * table[RATE_X + s : RATE_X + s + 1]
        for e in range(SIDES):
            weight = [jnp.exp((-b if e else b - (group - 1.0)) * theta) for b in blocks]
            here = pl.ds((e * SPECIES + s) * share, share)
            out[here, :] = sum(weight[d] * parts[d][here, :] for d in range(group))
            for k in range(SIDES):
                here = pl.ds(corners + (k * SIDES + e) * SPECIES + s, 1)
                out[here, :] = sum(weight[d] * parts[d][here, :] for d in range(group))


def group_sums(planes, share, table, after, parts):
    return pl.pallas_call(
        functools.partial(group_kernel, planes, share),
        in_specs=[VMEM, ANY] + [VMEM] * len(parts),
        out_specs=VMEM,
        out_shape=struct(*parts[0].shape),
        compiler_params=params(8),
        name="group_sums",
    )(table, after, *parts)


def column_kernel(table, y_table, z_table, conc, influx, *refs):
    count = SPECIES - 1
    h, u, (rough, y_out, last, weights, sums) = refs[:count], refs[count : count + SPECIES], refs[count + SPECIES :]
    planes, columns, width = influx.shape
    tile = (ROWS, width)
    row = row_position(columns, width)
    for s in range(SPECIES):
        theta = table[RATE_Y + s : RATE_Y + s + 1]
        weights[s, 0] = jnp.exp((row - (columns - 1.0)) * theta)
        weights[s, 1] = jnp.exp(-row * theta)
    inner = tiles(table, INNER + count * SPECIES, SPECIES, tile)
    double = tiles(table, DOUBLE + count * SPECIES, SPECIES, tile)
    part_a = tiles(table, PART_A + count * SPECIES, SPECIES, tile)
    (scale,) = tiles(table, SCALE_X + count, 1, tile)
    (decay,) = tiles(table, DECAY + count, 1, tile)
    bind, unbind, _ = tiles(table, KINETICS, 3, tile)

    def plane_of(s, value, i):
        for e in range(SIDES):
            sums[s, e, i : i + 1, :] = jnp.sum(weights[s, e] * value, axis=0, keepdims=True)
        u[s][i] = product(y_table[s], right_pair(value))

    def plane(i):
        for s in range(count):
            plane_of(s, h[s][i], i)

    def rows(k):
        here = tile_rows(k)
        up, sources, rising = jnp.zeros(tile, jnp.float32), [], []
        for i in range(planes):
            c = [conc[j, i, here, :] for j in range(SPECIES)]
            g = (bind * c[0] * c[1] - unbind * c[2]) * scale
            a = c[count]
            for j in range(SPECIES):
                g = g + inner[j] * c[j] + double[j] * turned(c[j])
                if j != count:
                    a = a + part_a[j] * c[j]
            up = g + decay * up
            sources.append(g)
            rising.append(up - a)
        down = jnp.zeros(tile, jnp.float32)
        for i in reversed(range(planes)):
            down = decay * down
            last[i, here, :] = rising[i] + down
            down = down + sources[i]

    side_by_side((planes, columns // ROWS), (plane, rows))
    side_by_side(
        (planes, columns // ROWS),
        (lambda i: plane_of(count, last[i], i), lambda k: sweep_of_b(0, table, conc, rough, k)),
    )
    for s in range(SPECIES):
        both = jnp.concatenate([sums[s, e] for e in range(SIDES)], axis=0)
        both = product(left_pair(both), z_table[s])
        for e in range(SIDES):
            y_out[pl.ds((e * SPECIES + s) * planes, planes), :] = both[e * planes : (e + 1) * planes]


def column_parts(table, y_table, z_table, conc, influx, h):
    planes, columns, width = influx.shape
    return pl.pallas_call(
        column_kernel,
        in_specs=[VMEM] * (5 + len(h)),
        out_specs=[VMEM] * (SPECIES + 2),
        out_shape=[pltpu.VMEM(influx.shape, jnp.float32)] * (SPECIES + 1)
        + [pltpu.VMEM((SIDES * SPECIES * planes, width), jnp.float32)],
        scratch_shapes=[
            pltpu.VMEM(influx.shape, jnp.float32),
            pltpu.VMEM((SPECIES, SIDES, columns, width), jnp.float32),
            pltpu.VMEM((SPECIES, SIDES, planes, width), jnp.float32),
        ],
        compiler_params=params(8),
        cost_estimate=pl.CostEstimate(flops=6 * conc.size * columns, bytes_accessed=8 * conc.size, transcendentals=0),
        name="column_parts",
    )(table, y_table, z_table, conc, influx, *h)


def finish_kernel(table, z_table, conc, *refs):
    u, rough, (out, weights, fades) = refs[:SPECIES], refs[SPECIES : 2 * SPECIES], refs[2 * SPECIES :]
    _, planes, columns, width = conc.shape
    at_once = 4 if planes % 4 == 0 else 1
    row = row_position(columns, width)
    position = row_position(planes, width)
    for s in range(SPECIES):
        rate_x = table[RATE_X + s : RATE_X + s + 1]
        rate_y = table[RATE_Y + s : RATE_Y + s + 1]
        weights[s, 0] = jnp.exp(-(row + 1.0) * rate_y)
        weights[s, 1] = jnp.exp((row - columns) * rate_y)
        fades[s, 0] = jnp.exp(-(position + 1.0) * rate_x)
        fades[s, 1] = jnp.exp((position - planes) * rate_x)
        for first in range(0, planes, at_once):
            here = slice(first, first + at_once)
            value = (u[s][here] - rough[s][here]).reshape(at_once * columns, width)
            done = product(left_pair(value), z_table[s])
            out[s, here] = conc[s, here] + done.reshape(at_once, columns, width)


def finish(table, z_table, conc, u, rough):
    _, planes, columns, width = conc.shape
    return pl.pallas_call(
        finish_kernel,
        in_specs=[VMEM] * (3 + len(u) + len(rough)),
        out_specs=[VMEM] * 3,
        out_shape=[
            pltpu.VMEM(conc.shape, jnp.float32),
            pltpu.VMEM((SPECIES, SIDES, columns, width), jnp.float32),
            pltpu.VMEM((SPECIES, SIDES, planes, width), jnp.float32),
        ],
        compiler_params=params(8),
        cost_estimate=pl.CostEstimate(flops=6 * conc.size * width, bytes_accessed=12 * conc.size, transcendentals=0),
        name="finish",
    )(table, z_table, conc, *u, *rough)


def enter_kernel(group, planes, share, table, sums, *refs):
    parts, wholes, outs, y_out = refs[:group], refs[group : -group - 1], refs[-group - 1 : -1], refs[-1]
    groups = len(wholes)
    corners = SIDES * SPECIES * share
    member = table[MEMBER : MEMBER + 1]
    blocks = [partner(member, d, group) for d in range(group)]
    y_out[pl.ds(0, sums.shape[0]), :] = sums[...]

    for s in range(SPECIES):
        theta = planes * table[RATE_X + s : RATE_X + s + 1]
        closing = 1.0 / (1.0 - jnp.exp(-float(group * groups) * theta))
        for e in range(SIDES):
            steps = [(groups - j - 1) if e else (j - 1 if j else groups - 1) for j in range(groups)]
            outside = [jnp.exp(-float(group * k) * theta) * closing for k in steps]
            to_target = [jnp.exp((t - (group - 1.0) if e else -t) * theta) for t in blocks]
            inside = []
            for t in blocks:
                away = [(b - t) if e else (t - b) for b in blocks]
                inside.append([jnp.where(k > 0.0, jnp.exp((1.0 - jnp.abs(k)) * theta), 0.0) for k in away])

            def entering_group(here):
                return sum(weight * whole[here, :] for weight, whole in zip(outside, wholes))

            here = pl.ds((e * SPECIES + s) * share, share)
            whole = entering_group(here)
            held = [part[here, :] for part in parts]
            for d in range(group):
                total = to_target[d] * whole
                for weight, part in zip(inside[d], held):
                    total = total + weight * part
                outs[d][here, :] = total

            for k in range(SIDES):
                at = (k * SIDES + e) * SPECIES + s
                here = pl.ds(corners + at, 1)
                total = to_target[0] * entering_group(here)
                for weight, part in zip(inside[0], parts):
                    total = total + weight * part[here, :]
                y_out[pl.ds(sums.shape[0] + at, 1), :] = total


def entering(planes, share, table, sums, parts, wholes):
    group, width = len(parts), parts[0].shape[1]
    return pl.pallas_call(
        functools.partial(enter_kernel, group, planes, share),
        in_specs=[VMEM] * (2 + group + len(wholes)),
        out_specs=[VMEM] * (group + 1),
        out_shape=[struct(SIDES * SPECIES * share, width)] * group + [struct(padded(sums.shape[0] + CORNERS), width)],
        compiler_params=params(8),
        name="entering",
    )(table, sums, *parts, *wholes)


def y_rows(planes, s, e):
    corners = SIDES * SPECIES * planes
    return [pl.ds((e * SPECIES + s) * planes, planes)] + [
        pl.ds(corners + (e * SIDES + k) * SPECIES + s, 1) for k in range(SIDES)
    ]


def flipped(rank, d):
    return lax.bitwise_xor(rank.astype(jnp.int32), jnp.int32(d)).astype(jnp.float32)


def y_weight(table, s, e, columns, along, target, block):
    theta = columns * table[RATE_Y + s : RATE_Y + s + 1]
    closing = table[SCALE_Y + s : SCALE_Y + s + 1] / (1.0 - jnp.exp(-float(along) * theta))
    steps = (block - target - 1.0) if e else (target - block - 1.0)
    steps = jnp.where(steps < 0.0, steps + along, steps)
    return jnp.exp(-steps * theta) * closing


def pair_kernel(planes, columns, along, table, mine, other, *outs):
    rank = table[RANK_Y : RANK_Y + 1]
    across = flipped(rank, along // 2)
    for d, out in enumerate(outs, 1):
        target = flipped(rank, d)
        for s in range(SPECIES):
            for e in range(SIDES):
                keep = y_weight(table, s, e, columns, along, target, rank)
                take = y_weight(table, s, e, columns, along, target, across)
                for here in y_rows(planes, s, e):
                    out[here, :] = keep * mine[here, :] + take * other[here, :]


def pair_sums(planes, columns, along, table, mine, other):
    return pl.pallas_call(
        functools.partial(pair_kernel, planes, columns, along),
        in_specs=[VMEM] * 3,
        out_specs=[VMEM] * (along // 2 - 1),
        out_shape=[struct(*mine.shape)] * (along // 2 - 1),
        compiler_params=params(8),
        name="pair_sums",
    )(table, mine, other)


def gather_kernel(share, table, *refs):
    parts, out = refs[:-1], refs[-1]
    group = len(parts)
    blocks = [partner(table[MEMBER : MEMBER + 1], d, group) for d in range(group)]
    for s in range(SPECIES):
        for e in range(SIDES):
            held = [part[pl.ds((e * SPECIES + s) * share, share), :] for part in parts]
            for b in range(group):
                mine = held[0]
                for d in range(1, group):
                    mine = jnp.where(blocks[d] == b, held[d], mine)
                out[e, s, pl.ds(b * share, share), :] = mine


def gathered_shares(columns, share, table, parts):
    return pl.pallas_call(
        functools.partial(gather_kernel, share),
        in_specs=[VMEM] * (1 + len(parts)),
        out_specs=VMEM,
        out_shape=pltpu.VMEM((SIDES, SPECIES, columns, parts[0].shape[1]), jnp.float32),
        compiler_params=params(8),
        cost_estimate=pl.CostEstimate(flops=20000000000, bytes_accessed=200000000, transcendentals=0),
        name="gathered_shares",
    )(table, *parts)


def spread_kernel(along, table, weights, fades, base, entered, *refs):
    sums, (out_far, out, hold, enter, left) = refs[:-5], refs[-5:]
    _, planes, columns, width = base.shape
    at_once = planes // left.shape[1]
    rank = table[RANK_Y : RANK_Y + 1]
    copies = []
    for s in range(SPECIES):
        corner = []
        for e in range(SIDES):
            sources = [rank, flipped(rank, along // 2)][: len(sums)]
            arrive = [y_weight(table, s, e, columns, along, rank, block) for block in sources]
            arrive += [1.0] * (len(sums) - len(arrive))
            lines, *corner_lines = y_rows(planes, s, e)
            enter[e] = weighted(arrive, sums, lines)
            corner.append([weighted(arrive, sums, here) for here in corner_lines])
        for e in range(SIDES):
            hold[e] = entered[e, s] + weights[s, 0] * corner[0][e] + weights[s, 1] * corner[1][e]
        for first in range(0, planes, at_once):
            near = [[ref[i : i + 1] for i in range(first, first + at_once)] for ref in (fades.at[s, 0], fades.at[s, 1])]
            far = [[ref[i : i + 1] for i in range(first, first + at_once)] for ref in (enter.at[0], enter.at[1])]
            for start in range(0, columns, ROWS):
                here = slice(start, start + ROWS)
                x_low, x_high = hold[0, here, :], hold[1, here, :]
                y_low, y_high = weights[s, 0, here, :], weights[s, 1, here, :]
                for k in range(at_once):
                    added = near[0][k] * x_low + near[1][k] * x_high + far[0][k] * y_low + far[1][k] * y_high
                    out[s, first + k, here, :] = base[s, first + k, here, :] + added
            part = pl.ds(first, at_once)
            copies.append(pltpu.make_async_copy(out.at[s, part], out_far.at[s, part], left.at[s, first // at_once]))
            copies[-1].start()
    for copy in copies:
        copy.wait()


def spread(along, table, weights, fades, base, entered, sums):
    _, planes, columns, width = base.shape
    return pl.pallas_call(
        functools.partial(spread_kernel, along),
        in_specs=[VMEM] * (5 + len(sums)),
        out_specs=ANY,
        out_shape=struct(*base.shape),
        scratch_shapes=[
            pltpu.VMEM(base.shape, jnp.float32),
            pltpu.VMEM((SIDES, columns, width), jnp.float32),
            pltpu.VMEM((SIDES, planes, width), jnp.float32),
            pltpu.SemaphoreType.DMA((SPECIES, planes // 4 if planes % 4 == 0 else planes)),
        ],
        compiler_params=params(8),
        name="spread",
    )(table, weights, fades, base, entered, *sums)


def group_size(devices):
    size = 1
    while 4 * size * size <= 2 * devices and devices % (2 * size) == 0:
        size *= 2
    return size


def body(conc, influx, numbers, cross, kinetics):
    _, planes, columns, _ = conc.shape
    across, along = lax.axis_size("gx"), lax.axis_size("gy")
    group = group_size(across)
    share = columns // group
    rank_x, rank_y = (lax.axis_index(axis).astype(jnp.int32).reshape(1) for axis in ("gx", "gy"))
    conc, influx, numbers, cross, kinetics = (
        pltpu.with_memory_space_constraint(x, pltpu.HBM) for x in (conc, influx, numbers, cross, kinetics)
    )

    def beside(value, d):
        return lax.ppermute(value, "gy", [(i, i ^ d) for i in range(along)])

    def in_group(parts):
        pairs = [[(i, i ^ turn_of(d, group)) for i in range(across)] for d in range(group)]
        return [parts[0]] + [lax.ppermute(parts[d], "gx", pairs[d]) for d in range(1, group)]

    def over_groups(value, by):
        return lax.ppermute(value, "gx", [(i, (i + by * group) % across) for i in range(across)])

    *parts, table, conc, influx, y_table, z_table = edges(
        group, rank_x, rank_y, numbers, cross, kinetics, conc, influx
    )
    parts = in_group(parts)
    swept = sweeps(table, conc, influx)
    h, rough = swept[: SPECIES - 1], swept[SPECIES - 1 :]
    whole = group_sums(planes, share, table, h[0], parts)
    wholes = [whole] + [over_groups(whole, j) for j in range(1, across // group)]
    *u, rough_first, sums = column_parts(table, y_table, z_table, conc, influx, h)
    *outs, sums = entering(planes, share, table, sums, parts, wholes)
    gathered = [sums]
    if along > 1:
        gathered.append(beside(sums, along // 2))
    if along > 2:
        onward = pair_sums(planes, columns, along, table, *gathered)
        gathered += [beside(value, d) for d, value in enumerate(onward, 1)]
    outs = in_group(outs)
    base, weights, fades = finish(table, z_table, conc, u, [rough_first, *rough])
    entered = gathered_shares(columns, share, table, outs)
    return spread(along, table, weights, fades, base, entered, gathered)


def solution(mesh):
    placed = (P(None, "gx", "gy", None), P("gx", "gy", None), P(), P(), P())
    return jax.shard_map(
        body, mesh=mesh, in_specs=placed, out_specs=P(None, "gx", "gy", None), check_vma=False
    )
```

```python
import functools

import jax
import jax.numpy as jnp
from jax import lax
from jax.experimental import pallas as pl
from jax.experimental.pallas import tpu as pltpu
from jax.sharding import PartitionSpec as P

SPECIES = 3
ROWS = 8
SIDES = 2
CORNERS = SIDES * SIDES * SPECIES
SMEM = pl.BlockSpec(memory_space=pltpu.SMEM)
VMEM = pl.BlockSpec(memory_space=pltpu.VMEM)
ANY = pl.BlockSpec(memory_space=pl.ANY)

RATE_X, RATE_Y, SCALE_Y, SCALE_X, DECAY, KINETICS, MEMBER = 0, 3, 6, 9, 12, 15, 18
INNER, DOUBLE, PART_A, PART_B, RANK_Y, TABLE_ROWS = 19, 28, 37, 46, 55, 56


def padded(rows):
    return -(-rows // ROWS) * ROWS


def params(mebibytes):
    return pltpu.CompilerParams(vmem_limit_bytes=mebibytes * 2**20)


def struct(*shape):
    return jax.ShapeDtypeStruct(shape, jnp.float32)


def decay_rate(number):
    half = 0.5 * lax.rsqrt(number)
    square = half * half
    return 2.0 * jnp.log1p(half + square / (1.0 + jnp.sqrt(1.0 + square)))


def scaling(number):
    return lax.rsqrt(1.0 + 4.0 * number)


def splat(value, shape):
    return jnp.full(shape, value, jnp.float32)


def split(value):
    high = value.astype(jnp.bfloat16)
    return high, (value - high.astype(jnp.float32)).astype(jnp.bfloat16)


def left_pair(value):
    return jnp.concatenate(split(value), axis=1)


def right_pair(value):
    high, low = split(value)
    return jnp.concatenate(
        [jnp.concatenate([high, low], axis=1), jnp.concatenate([high, jnp.zeros_like(low)], axis=1)], axis=0
    )


def product(left, right):
    both = jnp.dot(left, right, preferred_element_type=jnp.float32)
    width = both.shape[1] // 2
    return both[:, :width] + both[:, width:]


def distances(length):
    rows = lax.broadcasted_iota(jnp.int32, (length, length), 0)
    columns = lax.broadcasted_iota(jnp.int32, (length, length), 1)
    return jnp.abs(rows - columns).astype(jnp.float32)


def depth_table(number, length):
    number = splat(number, (1, length))
    theta = decay_rate(number)
    spread = distances(length)
    factor = scaling(number) / (1.0 - jnp.exp(-length * theta))
    return (jnp.exp(-spread * theta) + jnp.exp((spread - length) * theta)) * factor


def column_table(number, length):
    number = splat(number, (1, length))
    return jnp.exp(-distances(length) * decay_rate(number)) * scaling(number)


def row_position(length, width):
    return lax.broadcasted_iota(jnp.int32, (length, width), 0).astype(jnp.float32)


def coefficients(numbers, cross, kinetics, tile):
    n = [[splat(numbers[s, d], tile) for d in range(3)] for s in range(SPECIES)]
    along_x, along_y, along_z = [], [], []
    for s in range(SPECIES):
        per_x, per_y = 1.0 / n[s][0], 1.0 / n[s][1]
        for j in range(SPECIES):
            mix = 1.0 if j == s else cross[s, j]
            along_x.append(n[j][0] * per_x * mix)
            along_y.append(n[j][1] * per_y * mix)
            along_z.append(n[j][2] * mix)
    scale = [scaling(n[s][0]) for s in range(SPECIES)]
    rate = [decay_rate(n[s][0]) for s in range(SPECIES)]
    return along_x, along_y, along_z, scale, rate, [splat(kinetics[i], tile) for i in range(3)]


def turned(value):
    width = value.shape[1]
    return pltpu.roll(value, 1, 1) + pltpu.roll(value, width - 1, 1)


def weighted(weights, refs, here):
    return sum(weight * ref[here, :] for weight, ref in zip(weights, refs))


def tile_rows(k):
    return pl.ds(k * ROWS if isinstance(k, int) else pl.multiple_of(k * ROWS, ROWS), ROWS)


def tiles(table, first, count, tile):
    return [jnp.broadcast_to(table[at : at + 1], tile) for at in range(first, first + count)]


def rates(c, influx, kinetics):
    bind, unbind, pump = kinetics
    binding = bind * c[0] * c[1] - unbind * c[2]
    pumping = pump * c[0] / (1.0 + c[0])
    return influx - 4.0 * binding - pumping, binding


def side_by_side(counts, steps):
    for k in range(max(counts)):
        for count, step in zip(counts, steps):
            if k < count:
                step(k)


def sweep_of_b(s, table, conc, out, k):
    _, planes, _, width = conc.shape
    tile = (ROWS, width)
    here = tile_rows(k)
    weight = tiles(table, PART_B + s * SPECIES, SPECIES, tile)
    (decay,) = tiles(table, DECAY + s, 1, tile)
    up, sources, rising = jnp.zeros(tile, jnp.float32), [], []
    for i in range(planes):
        b = weight[0] * conc[0, i, here, :] + weight[1] * conc[1, i, here, :] + weight[2] * conc[2, i, here, :]
        up = b + decay * up
        sources.append(b)
        rising.append(up)
    down = jnp.zeros(tile, jnp.float32)
    for i in reversed(range(planes)):
        down = decay * down
        out[i, here, :] = rising[i] + down
        down = down + sources[i]


def chunk_cuts(columns):
    small, large = 2 * ROWS, 4 * ROWS
    cuts = [0]
    while cuts[-1] < columns:
        left = columns - cuts[-1]
        cuts.append(cuts[-1] + (large if cuts[-1] and left > 2 * small and left >= large + small else min(small, left)))
    return cuts


def edge_kernel(group, x_far, y_far, numbers_far, cross_far, kinetics_far, conc_far, influx_far, *refs):
    sent, refs = refs[:group], refs[group:]
    table, conc, influx, y_table, z_table, weights, hold, deep, solved, corners, arrived = refs[:11]
    rank_x, rank_y, numbers, cross, kinetics, small = refs[11:]
    planes, columns, width = influx.shape
    cuts = chunk_cuts(columns)
    half = planes // 2
    share = columns // group
    tile = (ROWS, width)

    def copies(k):
        part = pl.ds(cuts[k], cuts[k + 1] - cuts[k])
        return (
            pltpu.make_async_copy(conc_far.at[:, :, part, :], conc.at[:, :, part, :], arrived.at[0, k]),
            pltpu.make_async_copy(influx_far.at[:, part, :], influx.at[:, part, :], arrived.at[1, k]),
        )

    fars = (x_far, y_far, numbers_far, cross_far, kinetics_far)
    nears = (rank_x, rank_y, numbers, cross, kinetics)
    scalars = [pltpu.make_async_copy(far, near, small.at[k]) for k, (far, near) in enumerate(zip(fars, nears))]
    for copy in scalars:
        copy.start()
    for k in range(len(cuts) - 1):
        for copy in copies(k):
            copy.start()
    for copy in scalars:
        copy.wait()

    along_x, along_y, along_z, scale, rate, kinetic = coefficients(numbers, cross, kinetics, tile)
    inner, double, single = [], [], []
    for s in range(SPECIES):
        for at in range(s * SPECIES, (s + 1) * SPECIES):
            inner.append((along_x[at] + along_y[at] - 2.0 * along_z[at]) * scale[s])
            double.append(along_z[at] * scale[s])
            single.append(along_y[at] * scale[s])
        for i in range(half):
            near = jnp.exp(-i * rate[s])
            far = jnp.exp(-(planes - 1.0 - i) * rate[s])
            weights[s, i, 0] = 0.5 * (near + far)
            weights[s, i, 1] = 0.5 * (near - far)
    member = lax.rem(rank_x[0], group)

    def make_tables():
        for s in range(SPECIES):
            y_table[s] = left_pair(column_table(numbers[s, 1], columns))
            z_table[s] = right_pair(depth_table(numbers[s, 2], width))
        number_y = [splat(numbers[s, 1], tile) for s in range(SPECIES)]
        entries = (
            (RATE_X, rate),
            (RATE_Y, [decay_rate(value) for value in number_y]),
            (SCALE_Y, [scaling(value) for value in number_y]),
            (SCALE_X, scale),
            (DECAY, [jnp.exp(-value) for value in rate]),
            (KINETICS, kinetic),
            (MEMBER, [splat(member.astype(jnp.float32), tile)]),
            (RANK_Y, [splat(rank_y[0].astype(jnp.float32), tile)]),
            (INNER, inner),
            (DOUBLE, double),
            (PART_A, along_x),
            (PART_B, single),
        )
        for first, values in entries:
            for k, value in enumerate(values):
                table[first + k : first + k + 1] = value[:1]

    def sums_of(start):
        here = slice(start, start + ROWS)

        def at_plane(i):
            c = [conc[j, i, here, :] for j in range(SPECIES)]
            return c, *rates(c, influx[i, here, :], kinetic)

        zero = jnp.zeros(tile, jnp.float32)
        plus = [[zero] * (SPECIES + 1) for _ in range(SPECIES)]
        minus = [[zero] * (SPECIES + 1) for _ in range(SPECIES)]
        for i in range(half):
            low, low_first, low_binding = at_plane(i)
            high, high_first, high_binding = at_plane(planes - 1 - i)
            both = [x + y for x, y in zip(low, high)]
            apart = [x - y for x, y in zip(low, high)]
            change = (low_first + high_first, low_binding + high_binding)
            turn = (low_first - high_first, low_binding - high_binding)
            for s in range(SPECIES):
                even, odd = weights[s, i, 0], weights[s, i, 1]
                of = min(s, 1)
                for j, (p, m) in enumerate(zip(both + [change[of]], apart + [turn[of]])):
                    plus[s][j] = plus[s][j] + even * p
                    minus[s][j] = minus[s][j] + odd * m
        for s in range(SPECIES):
            for e in range(SIDES):
                sums = [p + m if e else p - m for p, m in zip(plus[s], minus[s])]
                v = sums[SPECIES] * scale[s]
                if s == 1:
                    v = -v
                w = 0.0
                for j in range(SPECIES):
                    at = s * SPECIES + j
                    v = v + inner[at] * sums[j] + double[at] * turned(sums[j])
                    w = w + single[at] * sums[j]
                hold[s, e, here, :] = v
                hold[s, SIDES + e, here, :] = w

    def deepen(k):
        here = slice(cuts[k], cuts[k + 1])
        chunk = cuts[k + 1] - cuts[k]
        for s in range(SPECIES):
            stack = jnp.concatenate([hold[s, e, here, :] for e in range(2 * SIDES)], axis=0)
            done = product(left_pair(stack), z_table[s])
            for e in range(2 * SIDES):
                deep[s, e, here, :] = done[e * chunk : (e + 1) * chunk]

    for k in range(len(cuts) - 1):
        for copy in copies(k):
            copy.wait()
        if k:
            deepen(k - 1)
        for start in range(cuts[k], cuts[k + 1], ROWS):
            sums_of(start)
        if not k:
            make_tables()
    deepen(len(cuts) - 2)

    row = row_position(columns, width)
    for s in range(SPECIES):
        theta = table[RATE_Y + s : RATE_Y + s + 1]
        rise = jnp.exp((row - (columns - 1.0)) * theta)
        fall = jnp.exp(-row * theta)
        both = product(y_table[s], right_pair(jnp.concatenate([deep[s, e] for e in range(SIDES)], axis=1)))
        for e in range(SIDES):
            solved[e, s] = both[:, e * width : (e + 1) * width] - deep[s, SIDES + e]
            for f, weight in enumerate((rise, fall)):
                at = (f * SIDES + e) * SPECIES + s
                corners[at : at + 1] = jnp.sum(weight * deep[s, e], axis=0, keepdims=True)
    for d in range(group):
        start = pl.multiple_of(lax.bitwise_xor(member, jnp.int32(turn_of(d, group))) * share, share)
        for s in range(SPECIES):
            for e in range(SIDES):
                sent[d][pl.ds((e * SPECIES + s) * share, share), :] = solved[e, s, pl.ds(start, share), :]
        sent[d][pl.ds(SIDES * SPECIES * share, corners.shape[0]), :] = corners[...]


def edges(group, rank_x, rank_y, numbers, cross, kinetics, conc, influx):
    _, planes, columns, width = conc.shape
    chunks = len(chunk_cuts(columns)) - 1
    hold = pltpu.VMEM((SPECIES, 2 * SIDES, columns, width), jnp.float32)
    rows = SIDES * SPECIES * (columns // group) + padded(CORNERS)
    return pl.pallas_call(
        functools.partial(edge_kernel, group),
        in_specs=[ANY] * 7,
        out_specs=[VMEM] * (group + 5),
        out_shape=[struct(rows, width)] * group
        + [
            pltpu.VMEM((TABLE_ROWS, width), jnp.float32),
            pltpu.VMEM(conc.shape, jnp.float32),
            pltpu.VMEM(influx.shape, jnp.float32),
            pltpu.VMEM((SPECIES, columns, 2 * columns), jnp.bfloat16),
            pltpu.VMEM((SPECIES, 2 * width, 2 * width), jnp.bfloat16),
        ],
        scratch_shapes=[
            pltpu.VMEM((SPECIES, planes // 2, 2, ROWS, width), jnp.float32),
            hold,
            hold,
            pltpu.VMEM((SIDES, SPECIES, columns, width), jnp.float32),
            pltpu.VMEM((padded(CORNERS), width), jnp.float32),
            pltpu.SemaphoreType.DMA((2, chunks)),
            *(pltpu.SMEM(x.shape, x.dtype) for x in (rank_x, rank_y, numbers, cross, kinetics)),
            pltpu.SemaphoreType.DMA((5,)),
        ],
        compiler_params=params(16),
        name="edges",
    )(rank_x, rank_y, numbers, cross, kinetics, conc, influx)


def sweep_kernel(table, conc, influx, *refs):
    count = SPECIES - 1
    outs, roughs, g_hold = refs[:count], refs[count:-1], refs[-1]
    planes, columns, width = influx.shape
    tile = (ROWS, width)
    inner = tiles(table, INNER, count * SPECIES, tile)
    double = tiles(table, DOUBLE, count * SPECIES, tile)
    part_a = tiles(table, PART_A, count * SPECIES, tile)
    scale = tiles(table, SCALE_X, count, tile)
    decay = tiles(table, DECAY, count, tile)
    kinetic = tiles(table, KINETICS, 3, tile)

    def rows(k, carry):
        here = pl.ds(pl.multiple_of(k * ROWS, ROWS), ROWS)
        up = [jnp.zeros(tile, jnp.float32) for _ in range(count)]
        for i in range(planes):
            c = [conc[j, i, here, :] for j in range(SPECIES)]
            around = [turned(value) for value in c]
            first, binding = rates(c, influx[i, here, :], kinetic)
            change = (first, -binding, binding)
            for s in range(count):
                g = change[s] * scale[s]
                a = c[s]
                for j in range(SPECIES):
                    at = s * SPECIES + j
                    g = g + inner[at] * c[j] + double[at] * around[j]
                    if j != s:
                        a = a + part_a[at] * c[j]
                up[s] = g + decay[s] * up[s]
                g_hold[s, i] = g
                outs[s][i, here, :] = up[s] - a
        for s in range(count):
            down = jnp.zeros(tile, jnp.float32)
            for i in reversed(range(planes)):
                down = decay[s] * down
                outs[s][i, here, :] += down
                down += g_hold[s, i]
        for s, rough in enumerate(roughs, 1):
            sweep_of_b(s, table, conc, rough, k)
        return carry

    lax.fori_loop(0, columns // ROWS, rows, 0)


def sweeps(table, conc, influx):
    count, planes, width = SPECIES - 1, influx.shape[0], influx.shape[2]
    return pl.pallas_call(
        sweep_kernel,
        in_specs=[VMEM] * 3,
        out_specs=[VMEM] * (2 * count),
        out_shape=[pltpu.VMEM(influx.shape, jnp.float32)] * (2 * count),
        scratch_shapes=[pltpu.VMEM((count, planes, ROWS, width), jnp.float32)],
        compiler_params=params(8),
        cost_estimate=pl.CostEstimate(flops=100 * conc.size, bytes_accessed=14 * conc.size, transcendentals=0),
        name="sweeps",
    )(table, conc, influx)


def turn_of(d, group):
    return (0, group - 1, *range(1, group - 1))[d]


def partner(member, d, group):
    return lax.bitwise_xor(member.astype(jnp.int32), jnp.int32(turn_of(d, group))).astype(jnp.float32)


def group_kernel(planes, share, table, after, *refs):
    parts, out = refs[:-1], refs[-1]
    group = len(parts)
    corners = SIDES * SPECIES * share
    member = table[MEMBER : MEMBER + 1]
    blocks = [partner(member, d, group) for d in range(group)]
    for s in range(SPECIES):
        theta = planes * table[RATE_X + s : RATE_X + s + 1]
        for e in range(SIDES):
            weight = [jnp.exp((-b if e else b - (group - 1.0)) * theta) for b in blocks]
            here = pl.ds((e * SPECIES + s) * share, share)
            out[here, :] = sum(weight[d] * parts[d][here, :] for d in range(group))
            for k in range(SIDES):
                here = pl.ds(corners + (k * SIDES + e) * SPECIES + s, 1)
                out[here, :] = sum(weight[d] * parts[d][here, :] for d in range(group))


def group_sums(planes, share, table, after, parts):
    return pl.pallas_call(
        functools.partial(group_kernel, planes, share),
        in_specs=[VMEM, ANY] + [VMEM] * len(parts),
        out_specs=VMEM,
        out_shape=struct(*parts[0].shape),
        compiler_params=params(8),
        name="group_sums",
    )(table, after, *parts)


def column_kernel(table, y_table, z_table, conc, influx, *refs):
    count = SPECIES - 1
    h, u, (rough, y_out, last, weights, sums) = refs[:count], refs[count : count + SPECIES], refs[count + SPECIES :]
    planes, columns, width = influx.shape
    tile = (ROWS, width)
    row = row_position(columns, width)
    for s in range(SPECIES):
        theta = table[RATE_Y + s : RATE_Y + s + 1]
        weights[s, 0] = jnp.exp((row - (columns - 1.0)) * theta)
        weights[s, 1] = jnp.exp(-row * theta)
    inner = tiles(table, INNER + count * SPECIES, SPECIES, tile)
    double = tiles(table, DOUBLE + count * SPECIES, SPECIES, tile)
    part_a = tiles(table, PART_A + count * SPECIES, SPECIES, tile)
    (scale,) = tiles(table, SCALE_X + count, 1, tile)
    (decay,) = tiles(table, DECAY + count, 1, tile)
    bind, unbind, _ = tiles(table, KINETICS, 3, tile)

    def plane_of(s, value, i):
        for e in range(SIDES):
            sums[s, e, i : i + 1, :] = jnp.sum(weights[s, e] * value, axis=0, keepdims=True)
        u[s][i] = product(y_table[s], right_pair(value))

    def plane(i):
        for s in range(count):
            plane_of(s, h[s][i], i)

    def rows(k):
        here = tile_rows(k)
        up, sources, rising = jnp.zeros(tile, jnp.float32), [], []
        for i in range(planes):
            c = [conc[j, i, here, :] for j in range(SPECIES)]
            g = (bind * c[0] * c[1] - unbind * c[2]) * scale
            a = c[count]
            for j in range(SPECIES):
                g = g + inner[j] * c[j] + double[j] * turned(c[j])
                if j != count:
                    a = a + part_a[j] * c[j]
            up = g + decay * up
            sources.append(g)
            rising.append(up - a)
        down = jnp.zeros(tile, jnp.float32)
        for i in reversed(range(planes)):
            down = decay * down
            last[i, here, :] = rising[i] + down
            down = down + sources[i]

    side_by_side((planes, columns // ROWS), (plane, rows))
    side_by_side(
        (planes, columns // ROWS),
        (lambda i: plane_of(count, last[i], i), lambda k: sweep_of_b(0, table, conc, rough, k)),
    )
    for s in range(SPECIES):
        both = jnp.concatenate([sums[s, e] for e in range(SIDES)], axis=0)
        both = product(left_pair(both), z_table[s])
        for e in range(SIDES):
            y_out[pl.ds((e * SPECIES + s) * planes, planes), :] = both[e * planes : (e + 1) * planes]


def column_parts(table, y_table, z_table, conc, influx, h):
    planes, columns, width = influx.shape
    return pl.pallas_call(
        column_kernel,
        in_specs=[VMEM] * (5 + len(h)),
        out_specs=[VMEM] * (SPECIES + 2),
        out_shape=[pltpu.VMEM(influx.shape, jnp.float32)] * (SPECIES + 1)
        + [pltpu.VMEM((SIDES * SPECIES * planes, width), jnp.float32)],
        scratch_shapes=[
            pltpu.VMEM(influx.shape, jnp.float32),
            pltpu.VMEM((SPECIES, SIDES, columns, width), jnp.float32),
            pltpu.VMEM((SPECIES, SIDES, planes, width), jnp.float32),
        ],
        compiler_params=params(8),
        cost_estimate=pl.CostEstimate(flops=6 * conc.size * columns, bytes_accessed=8 * conc.size, transcendentals=0),
        name="column_parts",
    )(table, y_table, z_table, conc, influx, *h)


def finish_kernel(table, z_table, conc, *refs):
    u, rough, (out, weights, fades) = refs[:SPECIES], refs[SPECIES : 2 * SPECIES], refs[2 * SPECIES :]
    _, planes, columns, width = conc.shape
    at_once = 4 if planes % 4 == 0 else 1
    row = row_position(columns, width)
    position = row_position(planes, width)
    for s in range(SPECIES):
        rate_x = table[RATE_X + s : RATE_X + s + 1]
        rate_y = table[RATE_Y + s : RATE_Y + s + 1]
        weights[s, 0] = jnp.exp(-(row + 1.0) * rate_y)
        weights[s, 1] = jnp.exp((row - columns) * rate_y)
        fades[s, 0] = jnp.exp(-(position + 1.0) * rate_x)
        fades[s, 1] = jnp.exp((position - planes) * rate_x)
        for first in range(0, planes, at_once):
            here = slice(first, first + at_once)
            value = (u[s][here] - rough[s][here]).reshape(at_once * columns, width)
            done = product(left_pair(value), z_table[s])
            out[s, here] = conc[s, here] + done.reshape(at_once, columns, width)


def finish(table, z_table, conc, u, rough):
    _, planes, columns, width = conc.shape
    return pl.pallas_call(
        finish_kernel,
        in_specs=[VMEM] * (3 + len(u) + len(rough)),
        out_specs=[VMEM] * 3,
        out_shape=[
            pltpu.VMEM(conc.shape, jnp.float32),
            pltpu.VMEM((SPECIES, SIDES, columns, width), jnp.float32),
            pltpu.VMEM((SPECIES, SIDES, planes, width), jnp.float32),
        ],
        compiler_params=params(8),
        cost_estimate=pl.CostEstimate(flops=6 * conc.size * width, bytes_accessed=12 * conc.size, transcendentals=0),
        name="finish",
    )(table, z_table, conc, *u, *rough)


def enter_kernel(group, planes, share, table, sums, *refs):
    parts, wholes, outs, y_out = refs[:group], refs[group : -group - 1], refs[-group - 1 : -1], refs[-1]
    groups = len(wholes)
    corners = SIDES * SPECIES * share
    member = table[MEMBER : MEMBER + 1]
    blocks = [partner(member, d, group) for d in range(group)]
    y_out[pl.ds(0, sums.shape[0]), :] = sums[...]

    for s in range(SPECIES):
        theta = planes * table[RATE_X + s : RATE_X + s + 1]
        closing = 1.0 / (1.0 - jnp.exp(-float(group * groups) * theta))
        for e in range(SIDES):
            steps = [(groups - j - 1) if e else (j - 1 if j else groups - 1) for j in range(groups)]
            outside = [jnp.exp(-float(group * k) * theta) * closing for k in steps]
            to_target = [jnp.exp((t - (group - 1.0) if e else -t) * theta) for t in blocks]
            inside = []
            for t in blocks:
                away = [(b - t) if e else (t - b) for b in blocks]
                inside.append([jnp.where(k > 0.0, jnp.exp((1.0 - jnp.abs(k)) * theta), 0.0) for k in away])

            def entering_group(here):
                return sum(weight * whole[here, :] for weight, whole in zip(outside, wholes))

            here = pl.ds((e * SPECIES + s) * share, share)
            whole = entering_group(here)
            held = [part[here, :] for part in parts]
            for d in range(group):
                total = to_target[d] * whole
                for weight, part in zip(inside[d], held):
                    total = total + weight * part
                outs[d][here, :] = total

            for k in range(SIDES):
                at = (k * SIDES + e) * SPECIES + s
                here = pl.ds(corners + at, 1)
                total = to_target[0] * entering_group(here)
                for weight, part in zip(inside[0], parts):
                    total = total + weight * part[here, :]
                y_out[pl.ds(sums.shape[0] + at, 1), :] = total


def entering(planes, share, table, sums, parts, wholes):
    group, width = len(parts), parts[0].shape[1]
    return pl.pallas_call(
        functools.partial(enter_kernel, group, planes, share),
        in_specs=[VMEM] * (2 + group + len(wholes)),
        out_specs=[VMEM] * (group + 1),
        out_shape=[struct(SIDES * SPECIES * share, width)] * group + [struct(padded(sums.shape[0] + CORNERS), width)],
        compiler_params=params(8),
        name="entering",
    )(table, sums, *parts, *wholes)


def y_rows(planes, s, e):
    corners = SIDES * SPECIES * planes
    return [pl.ds((e * SPECIES + s) * planes, planes)] + [
        pl.ds(corners + (e * SIDES + k) * SPECIES + s, 1) for k in range(SIDES)
    ]


def bits(table, stage):
    rank = table[RANK_Y : RANK_Y + 1].astype(jnp.int32)
    low = lax.bitwise_and(rank, jnp.int32(2**stage - 1)).astype(jnp.float32)
    return low, lax.bitwise_and(rank, jnp.int32(2**stage)) != 0


def pair_kernel(planes, columns, stage, table, mine, other, out):
    _, above = bits(table, stage)
    for s in range(SPECIES):
        far = jnp.exp(-float(columns * 2**stage) * table[RATE_Y + s : RATE_Y + s + 1])
        for e in range(SIDES):
            keep = jnp.where(above, far, 1.0) if e else jnp.where(above, 1.0, far)
            take = jnp.where(above, 1.0, far) if e else jnp.where(above, far, 1.0)
            for here in y_rows(planes, s, e):
                out[here, :] = keep * mine[here, :] + take * other[here, :]


def pair_sums(planes, columns, stage, table, mine, other):
    return pl.pallas_call(
        functools.partial(pair_kernel, planes, columns, stage),
        in_specs=[VMEM] * 3,
        out_specs=VMEM,
        out_shape=struct(*mine.shape),
        compiler_params=params(8),
        name="pair_sums",
    )(table, mine, other)


def y_weights(table, s, e, columns, stages):
    theta = columns * table[RATE_Y + s : RATE_Y + s + 1]
    along = 2**stages
    closing = table[SCALE_Y + s : SCALE_Y + s + 1] / (1.0 - jnp.exp(-float(along) * theta))
    weights = [jnp.exp(-(along - 1.0) * theta) * closing]
    for stage in range(stages):
        low, above = bits(table, stage)
        near = (2.0**stage - 1.0 - low) if e else low
        around = float(along - 2 ** (stage + 1))
        steps = near + (jnp.where(above, around, 0.0) if e else jnp.where(above, 0.0, around))
        weights.append(jnp.exp(-steps * theta) * closing)
    return weights


def spread_kernel(group, share, table, weights, fades, base, *refs):
    parts, sums, (out_far, out, hold, enter, left) = refs[:group], refs[group:-5], refs[-5:]
    _, planes, columns, width = base.shape
    blocks = [partner(table[MEMBER : MEMBER + 1], d, group) for d in range(group)]
    at_once = planes // left.shape[1]
    copies = []
    for s in range(SPECIES):
        corner = []
        for e in range(SIDES):
            arrive = y_weights(table, s, e, columns, len(sums) - 1)
            lines, *corner_lines = y_rows(planes, s, e)
            enter[e] = weighted(arrive, sums, lines)
            corner.append([weighted(arrive, sums, here) for here in corner_lines])
        for e in range(SIDES):
            held = [part[pl.ds((e * SPECIES + s) * share, share), :] for part in parts]
            for b in range(group):
                there = pl.ds(b * share, share)
                mine = held[0]
                for d in range(1, group):
                    mine = jnp.where(blocks[d] == b, held[d], mine)
                lift = weights[s, 0, there, :] * corner[0][e] + weights[s, 1, there, :] * corner[1][e]
                hold[e, there, :] = mine + lift
        for first in range(0, planes, at_once):
            near = [[ref[i : i + 1] for i in range(first, first + at_once)] for ref in (fades.at[s, 0], fades.at[s, 1])]
            far = [[ref[i : i + 1] for i in range(first, first + at_once)] for ref in (enter.at[0], enter.at[1])]
            for start in range(0, columns, ROWS):
                here = slice(start, start + ROWS)
                x_low, x_high = hold[0, here, :], hold[1, here, :]
                y_low, y_high = weights[s, 0, here, :], weights[s, 1, here, :]
                for k in range(at_once):
                    added = near[0][k] * x_low + near[1][k] * x_high + far[0][k] * y_low + far[1][k] * y_high
                    out[s, first + k, here, :] = base[s, first + k, here, :] + added
            part = pl.ds(first, at_once)
            copies.append(pltpu.make_async_copy(out.at[s, part], out_far.at[s, part], left.at[s, first // at_once]))
            copies[-1].start()
    for copy in copies:
        copy.wait()


def spread(share, table, weights, fades, base, sums, parts):
    _, planes, columns, width = base.shape
    return pl.pallas_call(
        functools.partial(spread_kernel, len(parts), share),
        in_specs=[VMEM] * (4 + len(sums) + len(parts)),
        out_specs=ANY,
        out_shape=struct(*base.shape),
        scratch_shapes=[
            pltpu.VMEM(base.shape, jnp.float32),
            pltpu.VMEM((SIDES, columns, width), jnp.float32),
            pltpu.VMEM((SIDES, planes, width), jnp.float32),
            pltpu.SemaphoreType.DMA((SPECIES, planes // 4 if planes % 4 == 0 else planes)),
        ],
        compiler_params=params(8),
        name="spread",
    )(table, weights, fades, base, *parts, *sums)


def group_size(devices):
    size = 1
    while 4 * size * size <= 2 * devices and devices % (2 * size) == 0:
        size *= 2
    return size


def body(conc, influx, numbers, cross, kinetics):
    _, planes, columns, _ = conc.shape
    across, along = lax.axis_size("gx"), lax.axis_size("gy")
    group = group_size(across)
    share = columns // group
    rank_x, rank_y = (lax.axis_index(axis).astype(jnp.int32).reshape(1) for axis in ("gx", "gy"))
    conc, influx, numbers, cross, kinetics = (
        pltpu.with_memory_space_constraint(x, pltpu.HBM) for x in (conc, influx, numbers, cross, kinetics)
    )

    def beside(value, stage):
        return lax.ppermute(value, "gy", [(i, i ^ 2**stage) for i in range(along)])

    def in_group(parts):
        pairs = [[(i, i ^ turn_of(d, group)) for i in range(across)] for d in range(group)]
        return [parts[0]] + [lax.ppermute(parts[d], "gx", pairs[d]) for d in range(1, group)]

    def over_groups(value, by):
        return lax.ppermute(value, "gx", [(i, (i + by * group) % across) for i in range(across)])

    *parts, table, conc, influx, y_table, z_table = edges(
        group, rank_x, rank_y, numbers, cross, kinetics, conc, influx
    )
    parts = in_group(parts)
    swept = sweeps(table, conc, influx)
    h, rough = swept[: SPECIES - 1], swept[SPECIES - 1 :]
    whole = group_sums(planes, share, table, h[0], parts)
    wholes = [whole] + [over_groups(whole, j) for j in range(1, across // group)]
    *u, rough_first, sums = column_parts(table, y_table, z_table, conc, influx, h)
    *outs, sums = entering(planes, share, table, sums, parts, wholes)
    gathered = [sums]
    for stage in range(along.bit_length() - 1):
        if stage:
            sums = pair_sums(planes, columns, stage - 1, table, sums, gathered[-1])
        gathered.append(beside(sums, stage))
    outs = in_group(outs)
    base, weights, fades = finish(table, z_table, conc, u, [rough_first, *rough])
    return spread(share, table, weights, fades, base, gathered, outs)


def solution(mesh):
    placed = (P(None, "gx", "gy", None), P("gx", "gy", None), P(), P(), P())
    return jax.shard_map(
        body, mesh=mesh, in_specs=placed, out_specs=P(None, "gx", "gy", None), check_vma=False
    )
```

```python
import functools

import jax
import jax.numpy as jnp
from jax import lax
from jax.experimental import pallas as pl
from jax.experimental.pallas import tpu as pltpu
from jax.sharding import PartitionSpec as P

SPECIES = 3
ROWS = 8
SIDES = 2
CORNERS = SIDES * SIDES * SPECIES
SMEM = pl.BlockSpec(memory_space=pltpu.SMEM)
VMEM = pl.BlockSpec(memory_space=pltpu.VMEM)
ANY = pl.BlockSpec(memory_space=pl.ANY)

RATE_X, RATE_Y, SCALE_Y, SCALE_X, DECAY, KINETICS, MEMBER = 0, 3, 6, 9, 12, 15, 18
INNER, DOUBLE, PART_A, PART_B, RANK_Y, TABLE_ROWS = 19, 28, 37, 46, 55, 56


def padded(rows):
    return -(-rows // ROWS) * ROWS


def params(mebibytes):
    return pltpu.CompilerParams(vmem_limit_bytes=mebibytes * 2**20)


def struct(*shape):
    return jax.ShapeDtypeStruct(shape, jnp.float32)


def decay_rate(number):
    half = 0.5 * lax.rsqrt(number)
    square = half * half
    return 2.0 * jnp.log1p(half + square / (1.0 + jnp.sqrt(1.0 + square)))


def scaling(number):
    return lax.rsqrt(1.0 + 4.0 * number)


def splat(value, shape):
    return jnp.full(shape, value, jnp.float32)


def split(value):
    high = value.astype(jnp.bfloat16)
    return high, (value - high.astype(jnp.float32)).astype(jnp.bfloat16)


def left_pair(value):
    return jnp.concatenate(split(value), axis=1)


def right_pair(value):
    high, low = split(value)
    return jnp.concatenate(
        [jnp.concatenate([high, low], axis=1), jnp.concatenate([high, jnp.zeros_like(low)], axis=1)], axis=0
    )


def product(left, right):
    both = jnp.dot(left, right, preferred_element_type=jnp.float32)
    width = both.shape[1] // 2
    return both[:, :width] + both[:, width:]


def distances(length):
    rows = lax.broadcasted_iota(jnp.int32, (length, length), 0)
    columns = lax.broadcasted_iota(jnp.int32, (length, length), 1)
    return jnp.abs(rows - columns).astype(jnp.float32)


def depth_table(number, length):
    number = splat(number, (1, length))
    theta = decay_rate(number)
    spread = distances(length)
    factor = scaling(number) / (1.0 - jnp.exp(-length * theta))
    return (jnp.exp(-spread * theta) + jnp.exp((spread - length) * theta)) * factor


def column_table(number, length):
    number = splat(number, (1, length))
    return jnp.exp(-distances(length) * decay_rate(number)) * scaling(number)


def row_position(length, width):
    return lax.broadcasted_iota(jnp.int32, (length, width), 0).astype(jnp.float32)


def coefficients(numbers, cross, kinetics, tile):
    n = [[splat(numbers[s, d], tile) for d in range(3)] for s in range(SPECIES)]
    along_x, along_y, along_z = [], [], []
    for s in range(SPECIES):
        per_x, per_y = 1.0 / n[s][0], 1.0 / n[s][1]
        for j in range(SPECIES):
            mix = 1.0 if j == s else cross[s, j]
            along_x.append(n[j][0] * per_x * mix)
            along_y.append(n[j][1] * per_y * mix)
            along_z.append(n[j][2] * mix)
    scale = [scaling(n[s][0]) for s in range(SPECIES)]
    rate = [decay_rate(n[s][0]) for s in range(SPECIES)]
    return along_x, along_y, along_z, scale, rate, [splat(kinetics[i], tile) for i in range(3)]


def turned(value):
    width = value.shape[1]
    return pltpu.roll(value, 1, 1) + pltpu.roll(value, width - 1, 1)


def weighted(weights, refs, here):
    return sum(weight * ref[here, :] for weight, ref in zip(weights, refs))


def tile_rows(k):
    return pl.ds(k * ROWS if isinstance(k, int) else pl.multiple_of(k * ROWS, ROWS), ROWS)


def tiles(table, first, count, tile):
    return [jnp.broadcast_to(table[at : at + 1], tile) for at in range(first, first + count)]


def rates(c, influx, kinetics):
    bind, unbind, pump = kinetics
    binding = bind * c[0] * c[1] - unbind * c[2]
    pumping = pump * c[0] / (1.0 + c[0])
    return influx - 4.0 * binding - pumping, binding


def side_by_side(counts, steps):
    for k in range(max(counts)):
        for count, step in zip(counts, steps):
            if k < count:
                step(k)


def sweep_of_b(s, table, conc, out, k):
    _, planes, _, width = conc.shape
    tile = (ROWS, width)
    here = tile_rows(k)
    weight = tiles(table, PART_B + s * SPECIES, SPECIES, tile)
    (decay,) = tiles(table, DECAY + s, 1, tile)
    up, sources, rising = jnp.zeros(tile, jnp.float32), [], []
    for i in range(planes):
        b = weight[0] * conc[0, i, here, :] + weight[1] * conc[1, i, here, :] + weight[2] * conc[2, i, here, :]
        up = b + decay * up
        sources.append(b)
        rising.append(up)
    down = jnp.zeros(tile, jnp.float32)
    for i in reversed(range(planes)):
        down = decay * down
        out[i, here, :] = rising[i] + down
        down = down + sources[i]


def edge_kernel(group, x_far, y_far, numbers_far, cross_far, kinetics_far, conc_far, influx_far, *refs):
    sent, refs = refs[:group], refs[group:]
    table, conc, influx, y_table, z_table, weights, hold, deep, solved, corners, arrived = refs[:11]
    rank_x, rank_y, numbers, cross, kinetics, small = refs[11:]
    planes, columns, width = influx.shape
    chunks = arrived.shape[1]
    chunk = columns // chunks
    half = planes // 2
    share = columns // group
    tile = (ROWS, width)

    def copies(k):
        part = pl.ds(k * chunk, chunk)
        return (
            pltpu.make_async_copy(conc_far.at[:, :, part, :], conc.at[:, :, part, :], arrived.at[0, k]),
            pltpu.make_async_copy(influx_far.at[:, part, :], influx.at[:, part, :], arrived.at[1, k]),
        )

    for k in range(chunks):
        for copy in copies(k):
            copy.start()
    fars = (x_far, y_far, numbers_far, cross_far, kinetics_far)
    nears = (rank_x, rank_y, numbers, cross, kinetics)
    scalars = [pltpu.make_async_copy(far, near, small.at[k]) for k, (far, near) in enumerate(zip(fars, nears))]
    for copy in scalars:
        copy.start()
    for copy in scalars:
        copy.wait()

    along_x, along_y, along_z, scale, rate, kinetic = coefficients(numbers, cross, kinetics, tile)
    inner, double, single = [], [], []
    for s in range(SPECIES):
        for at in range(s * SPECIES, (s + 1) * SPECIES):
            inner.append((along_x[at] + along_y[at] - 2.0 * along_z[at]) * scale[s])
            double.append(along_z[at] * scale[s])
            single.append(along_y[at] * scale[s])
        for i in range(half):
            near = jnp.exp(-i * rate[s])
            far = jnp.exp(-(planes - 1.0 - i) * rate[s])
            weights[s, i, 0] = 0.5 * (near + far)
            weights[s, i, 1] = 0.5 * (near - far)
        number = splat(numbers[s, 1], tile)
        table[RATE_Y + s : RATE_Y + s + 1] = decay_rate(number)[:1]
        table[SCALE_Y + s : SCALE_Y + s + 1] = scaling(number)[:1]
        y_table[s] = left_pair(column_table(numbers[s, 1], columns))
        z_table[s] = right_pair(depth_table(numbers[s, 2], width))
    member = lax.rem(rank_x[0], group)
    entries = (
        (RATE_X, rate),
        (SCALE_X, scale),
        (DECAY, [jnp.exp(-value) for value in rate]),
        (KINETICS, kinetic),
        (MEMBER, [splat(member.astype(jnp.float32), tile)]),
        (RANK_Y, [splat(rank_y[0].astype(jnp.float32), tile)]),
        (INNER, inner),
        (DOUBLE, double),
        (PART_A, along_x),
        (PART_B, single),
    )
    for first, values in entries:
        for k, value in enumerate(values):
            table[first + k : first + k + 1] = value[:1]

    def sums_of(start):
        here = slice(start, start + ROWS)

        def at_plane(i):
            c = [conc[j, i, here, :] for j in range(SPECIES)]
            return c, *rates(c, influx[i, here, :], kinetic)

        zero = jnp.zeros(tile, jnp.float32)
        plus = [[zero] * (SPECIES + 1) for _ in range(SPECIES)]
        minus = [[zero] * (SPECIES + 1) for _ in range(SPECIES)]
        for i in range(half):
            low, low_first, low_binding = at_plane(i)
            high, high_first, high_binding = at_plane(planes - 1 - i)
            both = [x + y for x, y in zip(low, high)]
            apart = [x - y for x, y in zip(low, high)]
            change = (low_first + high_first, low_binding + high_binding)
            turn = (low_first - high_first, low_binding - high_binding)
            for s in range(SPECIES):
                even, odd = weights[s, i, 0], weights[s, i, 1]
                of = min(s, 1)
                for j, (p, m) in enumerate(zip(both + [change[of]], apart + [turn[of]])):
                    plus[s][j] = plus[s][j] + even * p
                    minus[s][j] = minus[s][j] + odd * m
        for s in range(SPECIES):
            for e in range(SIDES):
                sums = [p + m if e else p - m for p, m in zip(plus[s], minus[s])]
                v = sums[SPECIES] * scale[s]
                if s == 1:
                    v = -v
                w = 0.0
                for j in range(SPECIES):
                    at = s * SPECIES + j
                    v = v + inner[at] * sums[j] + double[at] * turned(sums[j])
                    w = w + single[at] * sums[j]
                hold[s, e, here, :] = v
                hold[s, SIDES + e, here, :] = w

    def deepen(k):
        here = slice(k * chunk, (k + 1) * chunk)
        for s in range(SPECIES):
            stack = jnp.concatenate([hold[s, e, here, :] for e in range(2 * SIDES)], axis=0)
            done = product(left_pair(stack), z_table[s])
            for e in range(2 * SIDES):
                deep[s, e, here, :] = done[e * chunk : (e + 1) * chunk]

    for k in range(chunks):
        for copy in copies(k):
            copy.wait()
        if k:
            deepen(k - 1)
        for start in range(k * chunk, (k + 1) * chunk, ROWS):
            sums_of(start)
    deepen(chunks - 1)

    row = row_position(columns, width)
    for s in range(SPECIES):
        theta = table[RATE_Y + s : RATE_Y + s + 1]
        rise = jnp.exp((row - (columns - 1.0)) * theta)
        fall = jnp.exp(-row * theta)
        both = product(y_table[s], right_pair(jnp.concatenate([deep[s, e] for e in range(SIDES)], axis=1)))
        for e in range(SIDES):
            solved[e, s] = both[:, e * width : (e + 1) * width] - deep[s, SIDES + e]
            for f, weight in enumerate((rise, fall)):
                at = (f * SIDES + e) * SPECIES + s
                corners[at : at + 1] = jnp.sum(weight * deep[s, e], axis=0, keepdims=True)
    for d in range(group):
        start = pl.multiple_of(lax.bitwise_xor(member, jnp.int32(turn_of(d, group))) * share, share)
        for s in range(SPECIES):
            for e in range(SIDES):
                sent[d][pl.ds((e * SPECIES + s) * share, share), :] = solved[e, s, pl.ds(start, share), :]
        sent[d][pl.ds(SIDES * SPECIES * share, corners.shape[0]), :] = corners[...]


def edges(group, rank_x, rank_y, numbers, cross, kinetics, conc, influx):
    _, planes, columns, width = conc.shape
    chunks = columns // (2 * ROWS)
    hold = pltpu.VMEM((SPECIES, 2 * SIDES, columns, width), jnp.float32)
    rows = SIDES * SPECIES * (columns // group) + padded(CORNERS)
    return pl.pallas_call(
        functools.partial(edge_kernel, group),
        in_specs=[ANY] * 7,
        out_specs=[VMEM] * (group + 5),
        out_shape=[struct(rows, width)] * group
        + [
            pltpu.VMEM((TABLE_ROWS, width), jnp.float32),
            pltpu.VMEM(conc.shape, jnp.float32),
            pltpu.VMEM(influx.shape, jnp.float32),
            pltpu.VMEM((SPECIES, columns, 2 * columns), jnp.bfloat16),
            pltpu.VMEM((SPECIES, 2 * width, 2 * width), jnp.bfloat16),
        ],
        scratch_shapes=[
            pltpu.VMEM((SPECIES, planes // 2, 2, ROWS, width), jnp.float32),
            hold,
            hold,
            pltpu.VMEM((SIDES, SPECIES, columns, width), jnp.float32),
            pltpu.VMEM((padded(CORNERS), width), jnp.float32),
            pltpu.SemaphoreType.DMA((2, chunks)),
            *(pltpu.SMEM(x.shape, x.dtype) for x in (rank_x, rank_y, numbers, cross, kinetics)),
            pltpu.SemaphoreType.DMA((5,)),
        ],
        compiler_params=params(16),
        name="edges",
    )(rank_x, rank_y, numbers, cross, kinetics, conc, influx)


def sweep_kernel(table, conc, influx, *refs):
    count = SPECIES - 1
    outs, roughs, g_hold = refs[:count], refs[count:-1], refs[-1]
    planes, columns, width = influx.shape
    tile = (ROWS, width)
    inner = tiles(table, INNER, count * SPECIES, tile)
    double = tiles(table, DOUBLE, count * SPECIES, tile)
    part_a = tiles(table, PART_A, count * SPECIES, tile)
    scale = tiles(table, SCALE_X, count, tile)
    decay = tiles(table, DECAY, count, tile)
    kinetic = tiles(table, KINETICS, 3, tile)

    def rows(k, carry):
        here = pl.ds(pl.multiple_of(k * ROWS, ROWS), ROWS)
        up = [jnp.zeros(tile, jnp.float32) for _ in range(count)]
        for i in range(planes):
            c = [conc[j, i, here, :] for j in range(SPECIES)]
            around = [turned(value) for value in c]
            first, binding = rates(c, influx[i, here, :], kinetic)
            change = (first, -binding, binding)
            for s in range(count):
                g = change[s] * scale[s]
                a = c[s]
                for j in range(SPECIES):
                    at = s * SPECIES + j
                    g = g + inner[at] * c[j] + double[at] * around[j]
                    if j != s:
                        a = a + part_a[at] * c[j]
                up[s] = g + decay[s] * up[s]
                g_hold[s, i] = g
                outs[s][i, here, :] = up[s] - a
        for s in range(count):
            down = jnp.zeros(tile, jnp.float32)
            for i in reversed(range(planes)):
                down = decay[s] * down
                outs[s][i, here, :] += down
                down += g_hold[s, i]
        for s, rough in enumerate(roughs, 1):
            sweep_of_b(s, table, conc, rough, k)
        return carry

    lax.fori_loop(0, columns // ROWS, rows, 0)


def sweeps(table, conc, influx):
    count, planes, width = SPECIES - 1, influx.shape[0], influx.shape[2]
    return pl.pallas_call(
        sweep_kernel,
        in_specs=[VMEM] * 3,
        out_specs=[VMEM] * (2 * count),
        out_shape=[pltpu.VMEM(influx.shape, jnp.float32)] * (2 * count),
        scratch_shapes=[pltpu.VMEM((count, planes, ROWS, width), jnp.float32)],
        compiler_params=params(8),
        cost_estimate=pl.CostEstimate(flops=100 * conc.size, bytes_accessed=14 * conc.size, transcendentals=0),
        name="sweeps",
    )(table, conc, influx)


def turn_of(d, group):
    return (0, group - 1, *range(1, group - 1))[d]


def partner(member, d, group):
    return lax.bitwise_xor(member.astype(jnp.int32), jnp.int32(turn_of(d, group))).astype(jnp.float32)


def group_kernel(planes, share, table, after, *refs):
    parts, out = refs[:-1], refs[-1]
    group = len(parts)
    corners = SIDES * SPECIES * share
    member = table[MEMBER : MEMBER + 1]
    blocks = [partner(member, d, group) for d in range(group)]
    for s in range(SPECIES):
        theta = planes * table[RATE_X + s : RATE_X + s + 1]
        for e in range(SIDES):
            weight = [jnp.exp((-b if e else b - (group - 1.0)) * theta) for b in blocks]
            here = pl.ds((e * SPECIES + s) * share, share)
            out[here, :] = sum(weight[d] * parts[d][here, :] for d in range(group))
            for k in range(SIDES):
                here = pl.ds(corners + (k * SIDES + e) * SPECIES + s, 1)
                out[here, :] = sum(weight[d] * parts[d][here, :] for d in range(group))


def group_sums(planes, share, table, after, parts):
    return pl.pallas_call(
        functools.partial(group_kernel, planes, share),
        in_specs=[VMEM, ANY] + [VMEM] * len(parts),
        out_specs=VMEM,
        out_shape=struct(*parts[0].shape),
        compiler_params=params(8),
        name="group_sums",
    )(table, after, *parts)


def column_kernel(table, y_table, z_table, conc, influx, *refs):
    count = SPECIES - 1
    h, u, (rough, y_out, last, weights, sums) = refs[:count], refs[count : count + SPECIES], refs[count + SPECIES :]
    planes, columns, width = influx.shape
    tile = (ROWS, width)
    row = row_position(columns, width)
    for s in range(SPECIES):
        theta = table[RATE_Y + s : RATE_Y + s + 1]
        weights[s, 0] = jnp.exp((row - (columns - 1.0)) * theta)
        weights[s, 1] = jnp.exp(-row * theta)
    inner = tiles(table, INNER + count * SPECIES, SPECIES, tile)
    double = tiles(table, DOUBLE + count * SPECIES, SPECIES, tile)
    part_a = tiles(table, PART_A + count * SPECIES, SPECIES, tile)
    (scale,) = tiles(table, SCALE_X + count, 1, tile)
    (decay,) = tiles(table, DECAY + count, 1, tile)
    bind, unbind, _ = tiles(table, KINETICS, 3, tile)

    def plane_of(s, value, i):
        for e in range(SIDES):
            sums[s, e, i : i + 1, :] = jnp.sum(weights[s, e] * value, axis=0, keepdims=True)
        u[s][i] = product(y_table[s], right_pair(value))

    def plane(i):
        for s in range(count):
            plane_of(s, h[s][i], i)

    def rows(k):
        here = tile_rows(k)
        up, sources, rising = jnp.zeros(tile, jnp.float32), [], []
        for i in range(planes):
            c = [conc[j, i, here, :] for j in range(SPECIES)]
            g = (bind * c[0] * c[1] - unbind * c[2]) * scale
            a = c[count]
            for j in range(SPECIES):
                g = g + inner[j] * c[j] + double[j] * turned(c[j])
                if j != count:
                    a = a + part_a[j] * c[j]
            up = g + decay * up
            sources.append(g)
            rising.append(up - a)
        down = jnp.zeros(tile, jnp.float32)
        for i in reversed(range(planes)):
            down = decay * down
            last[i, here, :] = rising[i] + down
            down = down + sources[i]

    side_by_side((planes, columns // ROWS), (plane, rows))
    side_by_side(
        (planes, columns // ROWS),
        (lambda i: plane_of(count, last[i], i), lambda k: sweep_of_b(0, table, conc, rough, k)),
    )
    for s in range(SPECIES):
        both = jnp.concatenate([sums[s, e] for e in range(SIDES)], axis=0)
        both = product(left_pair(both), z_table[s])
        for e in range(SIDES):
            y_out[pl.ds((e * SPECIES + s) * planes, planes), :] = both[e * planes : (e + 1) * planes]


def column_parts(table, y_table, z_table, conc, influx, h):
    planes, columns, width = influx.shape
    return pl.pallas_call(
        column_kernel,
        in_specs=[VMEM] * (5 + len(h)),
        out_specs=[VMEM] * (SPECIES + 2),
        out_shape=[pltpu.VMEM(influx.shape, jnp.float32)] * (SPECIES + 1)
        + [pltpu.VMEM((SIDES * SPECIES * planes, width), jnp.float32)],
        scratch_shapes=[
            pltpu.VMEM(influx.shape, jnp.float32),
            pltpu.VMEM((SPECIES, SIDES, columns, width), jnp.float32),
            pltpu.VMEM((SPECIES, SIDES, planes, width), jnp.float32),
        ],
        compiler_params=params(8),
        cost_estimate=pl.CostEstimate(flops=6 * conc.size * columns, bytes_accessed=8 * conc.size, transcendentals=0),
        name="column_parts",
    )(table, y_table, z_table, conc, influx, *h)


def finish_kernel(table, z_table, conc, *refs):
    u, rough, (out, weights, fades) = refs[:SPECIES], refs[SPECIES : 2 * SPECIES], refs[2 * SPECIES :]
    _, planes, columns, width = conc.shape
    at_once = 4 if planes % 4 == 0 else 1
    row = row_position(columns, width)
    position = row_position(planes, width)
    for s in range(SPECIES):
        rate_x = table[RATE_X + s : RATE_X + s + 1]
        rate_y = table[RATE_Y + s : RATE_Y + s + 1]
        weights[s, 0] = jnp.exp(-(row + 1.0) * rate_y)
        weights[s, 1] = jnp.exp((row - columns) * rate_y)
        fades[s, 0] = jnp.exp(-(position + 1.0) * rate_x)
        fades[s, 1] = jnp.exp((position - planes) * rate_x)
        for first in range(0, planes, at_once):
            here = slice(first, first + at_once)
            value = (u[s][here] - rough[s][here]).reshape(at_once * columns, width)
            done = product(left_pair(value), z_table[s])
            out[s, here] = conc[s, here] + done.reshape(at_once, columns, width)


def finish(table, z_table, conc, u, rough):
    _, planes, columns, width = conc.shape
    return pl.pallas_call(
        finish_kernel,
        in_specs=[VMEM] * (3 + len(u) + len(rough)),
        out_specs=[VMEM] * 3,
        out_shape=[
            pltpu.VMEM(conc.shape, jnp.float32),
            pltpu.VMEM((SPECIES, SIDES, columns, width), jnp.float32),
            pltpu.VMEM((SPECIES, SIDES, planes, width), jnp.float32),
        ],
        compiler_params=params(8),
        cost_estimate=pl.CostEstimate(flops=6 * conc.size * width, bytes_accessed=12 * conc.size, transcendentals=0),
        name="finish",
    )(table, z_table, conc, *u, *rough)


def enter_kernel(group, planes, share, table, sums, *refs):
    parts, wholes, outs, y_out = refs[:group], refs[group : -group - 1], refs[-group - 1 : -1], refs[-1]
    groups = len(wholes)
    corners = SIDES * SPECIES * share
    member = table[MEMBER : MEMBER + 1]
    blocks = [partner(member, d, group) for d in range(group)]
    y_out[pl.ds(0, sums.shape[0]), :] = sums[...]

    for s in range(SPECIES):
        theta = planes * table[RATE_X + s : RATE_X + s + 1]
        closing = 1.0 / (1.0 - jnp.exp(-float(group * groups) * theta))
        for e in range(SIDES):
            steps = [(groups - j - 1) if e else (j - 1 if j else groups - 1) for j in range(groups)]
            outside = [jnp.exp(-float(group * k) * theta) * closing for k in steps]
            to_target = [jnp.exp((t - (group - 1.0) if e else -t) * theta) for t in blocks]
            inside = []
            for t in blocks:
                away = [(b - t) if e else (t - b) for b in blocks]
                inside.append([jnp.where(k > 0.0, jnp.exp((1.0 - jnp.abs(k)) * theta), 0.0) for k in away])

            def entering_group(here):
                return sum(weight * whole[here, :] for weight, whole in zip(outside, wholes))

            here = pl.ds((e * SPECIES + s) * share, share)
            whole = entering_group(here)
            held = [part[here, :] for part in parts]
            for d in range(group):
                total = to_target[d] * whole
                for weight, part in zip(inside[d], held):
                    total = total + weight * part
                outs[d][here, :] = total

            for k in range(SIDES):
                at = (k * SIDES + e) * SPECIES + s
                here = pl.ds(corners + at, 1)
                total = to_target[0] * entering_group(here)
                for weight, part in zip(inside[0], parts):
                    total = total + weight * part[here, :]
                y_out[pl.ds(sums.shape[0] + at, 1), :] = total


def entering(planes, share, table, sums, parts, wholes):
    group, width = len(parts), parts[0].shape[1]
    return pl.pallas_call(
        functools.partial(enter_kernel, group, planes, share),
        in_specs=[VMEM] * (2 + group + len(wholes)),
        out_specs=[VMEM] * (group + 1),
        out_shape=[struct(SIDES * SPECIES * share, width)] * group + [struct(padded(sums.shape[0] + CORNERS), width)],
        compiler_params=params(8),
        name="entering",
    )(table, sums, *parts, *wholes)


def y_rows(planes, s, e):
    corners = SIDES * SPECIES * planes
    return [pl.ds((e * SPECIES + s) * planes, planes)] + [
        pl.ds(corners + (e * SIDES + k) * SPECIES + s, 1) for k in range(SIDES)
    ]


def bits(table, stage):
    rank = table[RANK_Y : RANK_Y + 1].astype(jnp.int32)
    low = lax.bitwise_and(rank, jnp.int32(2**stage - 1)).astype(jnp.float32)
    return low, lax.bitwise_and(rank, jnp.int32(2**stage)) != 0


def pair_kernel(planes, columns, stage, table, mine, other, out):
    _, above = bits(table, stage)
    for s in range(SPECIES):
        far = jnp.exp(-float(columns * 2**stage) * table[RATE_Y + s : RATE_Y + s + 1])
        for e in range(SIDES):
            keep = jnp.where(above, far, 1.0) if e else jnp.where(above, 1.0, far)
            take = jnp.where(above, 1.0, far) if e else jnp.where(above, far, 1.0)
            for here in y_rows(planes, s, e):
                out[here, :] = keep * mine[here, :] + take * other[here, :]


def pair_sums(planes, columns, stage, table, mine, other):
    return pl.pallas_call(
        functools.partial(pair_kernel, planes, columns, stage),
        in_specs=[VMEM] * 3,
        out_specs=VMEM,
        out_shape=struct(*mine.shape),
        compiler_params=params(8),
        name="pair_sums",
    )(table, mine, other)


def y_weights(table, s, e, columns, stages):
    theta = columns * table[RATE_Y + s : RATE_Y + s + 1]
    along = 2**stages
    closing = table[SCALE_Y + s : SCALE_Y + s + 1] / (1.0 - jnp.exp(-float(along) * theta))
    weights = [jnp.exp(-(along - 1.0) * theta) * closing]
    for stage in range(stages):
        low, above = bits(table, stage)
        near = (2.0**stage - 1.0 - low) if e else low
        around = float(along - 2 ** (stage + 1))
        steps = near + (jnp.where(above, around, 0.0) if e else jnp.where(above, 0.0, around))
        weights.append(jnp.exp(-steps * theta) * closing)
    return weights


def gather_kernel(share, table, *refs):
    parts, out = refs[:-1], refs[-1]
    group = len(parts)
    blocks = [partner(table[MEMBER : MEMBER + 1], d, group) for d in range(group)]
    for s in range(SPECIES):
        for e in range(SIDES):
            held = [part[pl.ds((e * SPECIES + s) * share, share), :] for part in parts]
            for b in range(group):
                mine = held[0]
                for d in range(1, group):
                    mine = jnp.where(blocks[d] == b, held[d], mine)
                out[e, s, pl.ds(b * share, share), :] = mine


def gathered_shares(columns, share, table, parts):
    return pl.pallas_call(
        functools.partial(gather_kernel, share),
        in_specs=[VMEM] * (1 + len(parts)),
        out_specs=VMEM,
        out_shape=pltpu.VMEM((SIDES, SPECIES, columns, parts[0].shape[1]), jnp.float32),
        compiler_params=params(8),
        cost_estimate=pl.CostEstimate(flops=20000000000, bytes_accessed=200000000, transcendentals=0),
        name="gathered_shares",
    )(table, *parts)


def spread_kernel(table, weights, fades, base, entered, *refs):
    sums, (out_far, out, hold, enter, left) = refs[:-5], refs[-5:]
    _, planes, columns, width = base.shape
    at_once = planes // left.shape[1]
    copies = []
    for s in range(SPECIES):
        corner = []
        for e in range(SIDES):
            arrive = y_weights(table, s, e, columns, len(sums) - 1)
            lines, *corner_lines = y_rows(planes, s, e)
            enter[e] = weighted(arrive, sums, lines)
            corner.append([weighted(arrive, sums, here) for here in corner_lines])
        for e in range(SIDES):
            hold[e] = entered[e, s] + weights[s, 0] * corner[0][e] + weights[s, 1] * corner[1][e]
        for first in range(0, planes, at_once):
            near = [[ref[i : i + 1] for i in range(first, first + at_once)] for ref in (fades.at[s, 0], fades.at[s, 1])]
            far = [[ref[i : i + 1] for i in range(first, first + at_once)] for ref in (enter.at[0], enter.at[1])]
            for start in range(0, columns, ROWS):
                here = slice(start, start + ROWS)
                x_low, x_high = hold[0, here, :], hold[1, here, :]
                y_low, y_high = weights[s, 0, here, :], weights[s, 1, here, :]
                for k in range(at_once):
                    added = near[0][k] * x_low + near[1][k] * x_high + far[0][k] * y_low + far[1][k] * y_high
                    out[s, first + k, here, :] = base[s, first + k, here, :] + added
            part = pl.ds(first, at_once)
            copies.append(pltpu.make_async_copy(out.at[s, part], out_far.at[s, part], left.at[s, first // at_once]))
            copies[-1].start()
    for copy in copies:
        copy.wait()


def spread(table, weights, fades, base, entered, sums):
    _, planes, columns, width = base.shape
    return pl.pallas_call(
        spread_kernel,
        in_specs=[VMEM] * (5 + len(sums)),
        out_specs=ANY,
        out_shape=struct(*base.shape),
        scratch_shapes=[
            pltpu.VMEM(base.shape, jnp.float32),
            pltpu.VMEM((SIDES, columns, width), jnp.float32),
            pltpu.VMEM((SIDES, planes, width), jnp.float32),
            pltpu.SemaphoreType.DMA((SPECIES, planes // 4 if planes % 4 == 0 else planes)),
        ],
        compiler_params=params(8),
        name="spread",
    )(table, weights, fades, base, entered, *sums)


def group_size(devices):
    size = 1
    while 4 * size * size <= 2 * devices and devices % (2 * size) == 0:
        size *= 2
    return size


def body(conc, influx, numbers, cross, kinetics):
    _, planes, columns, _ = conc.shape
    across, along = lax.axis_size("gx"), lax.axis_size("gy")
    group = group_size(across)
    share = columns // group
    rank_x, rank_y = (lax.axis_index(axis).astype(jnp.int32).reshape(1) for axis in ("gx", "gy"))
    conc, influx, numbers, cross, kinetics = (
        pltpu.with_memory_space_constraint(x, pltpu.HBM) for x in (conc, influx, numbers, cross, kinetics)
    )

    def beside(value, stage):
        return lax.ppermute(value, "gy", [(i, i ^ 2**stage) for i in range(along)])

    def in_group(parts):
        pairs = [[(i, i ^ turn_of(d, group)) for i in range(across)] for d in range(group)]
        return [parts[0]] + [lax.ppermute(parts[d], "gx", pairs[d]) for d in range(1, group)]

    def over_groups(value, by):
        return lax.ppermute(value, "gx", [(i, (i + by * group) % across) for i in range(across)])

    *parts, table, conc, influx, y_table, z_table = edges(
        group, rank_x, rank_y, numbers, cross, kinetics, conc, influx
    )
    parts = in_group(parts)
    swept = sweeps(table, conc, influx)
    h, rough = swept[: SPECIES - 1], swept[SPECIES - 1 :]
    whole = group_sums(planes, share, table, h[0], parts)
    wholes = [whole] + [over_groups(whole, j) for j in range(1, across // group)]
    *u, rough_first, sums = column_parts(table, y_table, z_table, conc, influx, h)
    *outs, sums = entering(planes, share, table, sums, parts, wholes)
    gathered = [sums]
    for stage in range(along.bit_length() - 1):
        if stage:
            sums = pair_sums(planes, columns, stage - 1, table, sums, gathered[-1])
        gathered.append(beside(sums, stage))
    outs = in_group(outs)
    base, weights, fades = finish(table, z_table, conc, u, [rough_first, *rough])
    entered = gathered_shares(columns, share, table, outs)
    return spread(table, weights, fades, base, entered, gathered)


def solution(mesh):
    placed = (P(None, "gx", "gy", None), P("gx", "gy", None), P(), P(), P())
    return jax.shard_map(
        body, mesh=mesh, in_specs=placed, out_specs=P(None, "gx", "gy", None), check_vma=False
    )
```

```python
import functools

import jax
import jax.numpy as jnp
from jax import lax
from jax.experimental import pallas as pl
from jax.experimental.pallas import tpu as pltpu
from jax.sharding import PartitionSpec as P

SPECIES = 3
ROWS = 8
SIDES = 2
CORNERS = SIDES * SIDES * SPECIES
SMEM = pl.BlockSpec(memory_space=pltpu.SMEM)
VMEM = pl.BlockSpec(memory_space=pltpu.VMEM)
ANY = pl.BlockSpec(memory_space=pl.ANY)

RATE_X, RATE_Y, SCALE_Y, SCALE_X, DECAY, KINETICS, MEMBER = 0, 3, 6, 9, 12, 15, 18
INNER, DOUBLE, PART_A, PART_B, RANK_Y, TABLE_ROWS = 19, 28, 37, 46, 55, 56


def padded(rows):
    return -(-rows // ROWS) * ROWS


def params(mebibytes):
    return pltpu.CompilerParams(vmem_limit_bytes=mebibytes * 2**20)


def struct(*shape):
    return jax.ShapeDtypeStruct(shape, jnp.float32)


def decay_rate(number):
    half = 0.5 * lax.rsqrt(number)
    square = half * half
    return 2.0 * jnp.log1p(half + square / (1.0 + jnp.sqrt(1.0 + square)))


def scaling(number):
    return lax.rsqrt(1.0 + 4.0 * number)


def splat(value, shape):
    return jnp.full(shape, value, jnp.float32)


def split(value):
    high = value.astype(jnp.bfloat16)
    return high, (value - high.astype(jnp.float32)).astype(jnp.bfloat16)


def left_pair(value):
    return jnp.concatenate(split(value), axis=1)


def right_pair(value):
    high, low = split(value)
    return jnp.concatenate(
        [jnp.concatenate([high, low], axis=1), jnp.concatenate([high, jnp.zeros_like(low)], axis=1)], axis=0
    )


def product(left, right):
    both = jnp.dot(left, right, preferred_element_type=jnp.float32)
    width = both.shape[1] // 2
    return both[:, :width] + both[:, width:]


def distances(length):
    rows = lax.broadcasted_iota(jnp.int32, (length, length), 0)
    columns = lax.broadcasted_iota(jnp.int32, (length, length), 1)
    return jnp.abs(rows - columns).astype(jnp.float32)


def depth_table(number, length):
    number = splat(number, (1, length))
    theta = decay_rate(number)
    spread = distances(length)
    factor = scaling(number) / (1.0 - jnp.exp(-length * theta))
    return (jnp.exp(-spread * theta) + jnp.exp((spread - length) * theta)) * factor


def column_table(number, length):
    number = splat(number, (1, length))
    return jnp.exp(-distances(length) * decay_rate(number)) * scaling(number)


def row_position(length, width):
    return lax.broadcasted_iota(jnp.int32, (length, width), 0).astype(jnp.float32)


def coefficients(numbers, cross, kinetics, tile):
    n = [[splat(numbers[s, d], tile) for d in range(3)] for s in range(SPECIES)]
    along_x, along_y, along_z = [], [], []
    for s in range(SPECIES):
        per_x, per_y = 1.0 / n[s][0], 1.0 / n[s][1]
        for j in range(SPECIES):
            mix = 1.0 if j == s else cross[s, j]
            along_x.append(n[j][0] * per_x * mix)
            along_y.append(n[j][1] * per_y * mix)
            along_z.append(n[j][2] * mix)
    scale = [scaling(n[s][0]) for s in range(SPECIES)]
    rate = [decay_rate(n[s][0]) for s in range(SPECIES)]
    return along_x, along_y, along_z, scale, rate, [splat(kinetics[i], tile) for i in range(3)]


def turned(value):
    width = value.shape[1]
    return pltpu.roll(value, 1, 1) + pltpu.roll(value, width - 1, 1)


def weighted(weights, refs, here):
    return sum(weight * ref[here, :] for weight, ref in zip(weights, refs))


def tile_rows(k):
    return pl.ds(k * ROWS if isinstance(k, int) else pl.multiple_of(k * ROWS, ROWS), ROWS)


def tiles(table, first, count, tile):
    return [jnp.broadcast_to(table[at : at + 1], tile) for at in range(first, first + count)]


def rates(c, influx, kinetics):
    bind, unbind, pump = kinetics
    binding = bind * c[0] * c[1] - unbind * c[2]
    pumping = pump * c[0] / (1.0 + c[0])
    return influx - 4.0 * binding - pumping, binding


def side_by_side(counts, steps):
    for k in range(max(counts)):
        for count, step in zip(counts, steps):
            if k < count:
                step(k)


def sweep_of_b(s, table, conc, out, k):
    _, planes, _, width = conc.shape
    tile = (ROWS, width)
    here = tile_rows(k)
    weight = tiles(table, PART_B + s * SPECIES, SPECIES, tile)
    (decay,) = tiles(table, DECAY + s, 1, tile)
    up, sources, rising = jnp.zeros(tile, jnp.float32), [], []
    for i in range(planes):
        b = weight[0] * conc[0, i, here, :] + weight[1] * conc[1, i, here, :] + weight[2] * conc[2, i, here, :]
        up = b + decay * up
        sources.append(b)
        rising.append(up)
    down = jnp.zeros(tile, jnp.float32)
    for i in reversed(range(planes)):
        down = decay * down
        out[i, here, :] = rising[i] + down
        down = down + sources[i]


def chunk_cuts(columns):
    small, large = 2 * ROWS, 4 * ROWS
    cuts = [0]
    while cuts[-1] < columns:
        left = columns - cuts[-1]
        cuts.append(cuts[-1] + (large if cuts[-1] and left > 2 * small and left >= large + small else min(small, left)))
    return cuts


def edge_kernel(group, x_far, y_far, numbers_far, cross_far, kinetics_far, conc_far, influx_far, *refs):
    sent, refs = refs[:group], refs[group:]
    table, conc, influx, y_table, z_table, weights, hold, deep, solved, corners, arrived = refs[:11]
    rank_x, rank_y, numbers, cross, kinetics, small = refs[11:]
    planes, columns, width = influx.shape
    cuts = chunk_cuts(columns)
    half = planes // 2
    share = columns // group
    tile = (ROWS, width)

    def copies(k):
        part = pl.ds(cuts[k], cuts[k + 1] - cuts[k])
        return (
            pltpu.make_async_copy(conc_far.at[:, :, part, :], conc.at[:, :, part, :], arrived.at[0, k]),
            pltpu.make_async_copy(influx_far.at[:, part, :], influx.at[:, part, :], arrived.at[1, k]),
        )

    fars = (x_far, y_far, numbers_far, cross_far, kinetics_far)
    nears = (rank_x, rank_y, numbers, cross, kinetics)
    scalars = [pltpu.make_async_copy(far, near, small.at[k]) for k, (far, near) in enumerate(zip(fars, nears))]
    for copy in scalars:
        copy.start()
    for k in range(len(cuts) - 1):
        for copy in copies(k):
            copy.start(priority=k % 2)
    for copy in scalars:
        copy.wait()

    along_x, along_y, along_z, scale, rate, kinetic = coefficients(numbers, cross, kinetics, tile)
    inner, double, single = [], [], []
    for s in range(SPECIES):
        for at in range(s * SPECIES, (s + 1) * SPECIES):
            inner.append((along_x[at] + along_y[at] - 2.0 * along_z[at]) * scale[s])
            double.append(along_z[at] * scale[s])
            single.append(along_y[at] * scale[s])
        for i in range(half):
            near = jnp.exp(-i * rate[s])
            far = jnp.exp(-(planes - 1.0 - i) * rate[s])
            weights[s, i, 0] = 0.5 * (near + far)
            weights[s, i, 1] = 0.5 * (near - far)
    member = lax.rem(rank_x[0], group)

    def make_tables():
        for s in range(SPECIES):
            y_table[s] = left_pair(column_table(numbers[s, 1], columns))
            z_table[s] = right_pair(depth_table(numbers[s, 2], width))
        number_y = [splat(numbers[s, 1], tile) for s in range(SPECIES)]
        entries = (
            (RATE_X, rate),
            (RATE_Y, [decay_rate(value) for value in number_y]),
            (SCALE_Y, [scaling(value) for value in number_y]),
            (SCALE_X, scale),
            (DECAY, [jnp.exp(-value) for value in rate]),
            (KINETICS, kinetic),
            (MEMBER, [splat(member.astype(jnp.float32), tile)]),
            (RANK_Y, [splat(rank_y[0].astype(jnp.float32), tile)]),
            (INNER, inner),
            (DOUBLE, double),
            (PART_A, along_x),
            (PART_B, single),
        )
        for first, values in entries:
            for k, value in enumerate(values):
                table[first + k : first + k + 1] = value[:1]

    def sums_of(start):
        here = slice(start, start + ROWS)

        def at_plane(i):
            c = [conc[j, i, here, :] for j in range(SPECIES)]
            return c, *rates(c, influx[i, here, :], kinetic)

        zero = jnp.zeros(tile, jnp.float32)
        plus = [[zero] * (SPECIES + 1) for _ in range(SPECIES)]
        minus = [[zero] * (SPECIES + 1) for _ in range(SPECIES)]
        for i in range(half):
            low, low_first, low_binding = at_plane(i)
            high, high_first, high_binding = at_plane(planes - 1 - i)
            both = [x + y for x, y in zip(low, high)]
            apart = [x - y for x, y in zip(low, high)]
            change = (low_first + high_first, low_binding + high_binding)
            turn = (low_first - high_first, low_binding - high_binding)
            for s in range(SPECIES):
                even, odd = weights[s, i, 0], weights[s, i, 1]
                of = min(s, 1)
                for j, (p, m) in enumerate(zip(both + [change[of]], apart + [turn[of]])):
                    plus[s][j] = plus[s][j] + even * p
                    minus[s][j] = minus[s][j] + odd * m
        for s in range(SPECIES):
            for e in range(SIDES):
                sums = [p + m if e else p - m for p, m in zip(plus[s], minus[s])]
                v = sums[SPECIES] * scale[s]
                if s == 1:
                    v = -v
                w = 0.0
                for j in range(SPECIES):
                    at = s * SPECIES + j
                    v = v + inner[at] * sums[j] + double[at] * turned(sums[j])
                    w = w + single[at] * sums[j]
                hold[s, e, here, :] = v
                hold[s, SIDES + e, here, :] = w

    def deepen(k):
        here = slice(cuts[k], cuts[k + 1])
        chunk = cuts[k + 1] - cuts[k]
        for s in range(SPECIES):
            stack = jnp.concatenate([hold[s, e, here, :] for e in range(2 * SIDES)], axis=0)
            done = product(left_pair(stack), z_table[s])
            for e in range(2 * SIDES):
                deep[s, e, here, :] = done[e * chunk : (e + 1) * chunk]

    for k in range(len(cuts) - 1):
        for copy in copies(k):
            copy.wait()
        if k:
            deepen(k - 1)
        for start in range(cuts[k], cuts[k + 1], ROWS):
            sums_of(start)
        if not k:
            make_tables()
    deepen(len(cuts) - 2)

    row = row_position(columns, width)
    for s in range(SPECIES):
        theta = table[RATE_Y + s : RATE_Y + s + 1]
        rise = jnp.exp((row - (columns - 1.0)) * theta)
        fall = jnp.exp(-row * theta)
        both = product(y_table[s], right_pair(jnp.concatenate([deep[s, e] for e in range(SIDES)], axis=1)))
        for e in range(SIDES):
            solved[e, s] = both[:, e * width : (e + 1) * width] - deep[s, SIDES + e]
            for f, weight in enumerate((rise, fall)):
                at = (f * SIDES + e) * SPECIES + s
                corners[at : at + 1] = jnp.sum(weight * deep[s, e], axis=0, keepdims=True)
    for d in range(group):
        start = pl.multiple_of(lax.bitwise_xor(member, jnp.int32(turn_of(d, group))) * share, share)
        for s in range(SPECIES):
            for e in range(SIDES):
                sent[d][pl.ds((e * SPECIES + s) * share, share), :] = solved[e, s, pl.ds(start, share), :]
        sent[d][pl.ds(SIDES * SPECIES * share, corners.shape[0]), :] = corners[...]


def edges(group, rank_x, rank_y, numbers, cross, kinetics, conc, influx):
    _, planes, columns, width = conc.shape
    chunks = len(chunk_cuts(columns)) - 1
    hold = pltpu.VMEM((SPECIES, 2 * SIDES, columns, width), jnp.float32)
    rows = SIDES * SPECIES * (columns // group) + padded(CORNERS)
    return pl.pallas_call(
        functools.partial(edge_kernel, group),
        in_specs=[ANY] * 7,
        out_specs=[VMEM] * (group + 5),
        out_shape=[struct(rows, width)] * group
        + [
            pltpu.VMEM((TABLE_ROWS, width), jnp.float32),
            pltpu.VMEM(conc.shape, jnp.float32),
            pltpu.VMEM(influx.shape, jnp.float32),
            pltpu.VMEM((SPECIES, columns, 2 * columns), jnp.bfloat16),
            pltpu.VMEM((SPECIES, 2 * width, 2 * width), jnp.bfloat16),
        ],
        scratch_shapes=[
            pltpu.VMEM((SPECIES, planes // 2, 2, ROWS, width), jnp.float32),
            hold,
            hold,
            pltpu.VMEM((SIDES, SPECIES, columns, width), jnp.float32),
            pltpu.VMEM((padded(CORNERS), width), jnp.float32),
            pltpu.SemaphoreType.DMA((2, chunks)),
            *(pltpu.SMEM(x.shape, x.dtype) for x in (rank_x, rank_y, numbers, cross, kinetics)),
            pltpu.SemaphoreType.DMA((5,)),
        ],
        compiler_params=params(16),
        name="edges",
    )(rank_x, rank_y, numbers, cross, kinetics, conc, influx)


def sweep_kernel(table, conc, influx, *refs):
    count = SPECIES - 1
    outs, roughs, g_hold = refs[:count], refs[count:-1], refs[-1]
    planes, columns, width = influx.shape
    tile = (ROWS, width)
    inner = tiles(table, INNER, count * SPECIES, tile)
    double = tiles(table, DOUBLE, count * SPECIES, tile)
    part_a = tiles(table, PART_A, count * SPECIES, tile)
    scale = tiles(table, SCALE_X, count, tile)
    decay = tiles(table, DECAY, count, tile)
    kinetic = tiles(table, KINETICS, 3, tile)

    def rows(k, carry):
        here = pl.ds(pl.multiple_of(k * ROWS, ROWS), ROWS)
        up = [jnp.zeros(tile, jnp.float32) for _ in range(count)]
        for i in range(planes):
            c = [conc[j, i, here, :] for j in range(SPECIES)]
            around = [turned(value) for value in c]
            first, binding = rates(c, influx[i, here, :], kinetic)
            change = (first, -binding, binding)
            for s in range(count):
                g = change[s] * scale[s]
                a = c[s]
                for j in range(SPECIES):
                    at = s * SPECIES + j
                    g = g + inner[at] * c[j] + double[at] * around[j]
                    if j != s:
                        a = a + part_a[at] * c[j]
                up[s] = g + decay[s] * up[s]
                g_hold[s, i] = g
                outs[s][i, here, :] = up[s] - a
        for s in range(count):
            down = jnp.zeros(tile, jnp.float32)
            for i in reversed(range(planes)):
                down = decay[s] * down
                outs[s][i, here, :] += down
                down += g_hold[s, i]
        for s, rough in enumerate(roughs, 1):
            sweep_of_b(s, table, conc, rough, k)
        return carry

    lax.fori_loop(0, columns // ROWS, rows, 0)


def sweeps(table, conc, influx):
    count, planes, width = SPECIES - 1, influx.shape[0], influx.shape[2]
    return pl.pallas_call(
        sweep_kernel,
        in_specs=[VMEM] * 3,
        out_specs=[VMEM] * (2 * count),
        out_shape=[pltpu.VMEM(influx.shape, jnp.float32)] * (2 * count),
        scratch_shapes=[pltpu.VMEM((count, planes, ROWS, width), jnp.float32)],
        compiler_params=params(8),
        cost_estimate=pl.CostEstimate(flops=100 * conc.size, bytes_accessed=14 * conc.size, transcendentals=0),
        name="sweeps",
    )(table, conc, influx)


def turn_of(d, group):
    return (0, group - 1, *range(1, group - 1))[d]


def partner(member, d, group):
    return lax.bitwise_xor(member.astype(jnp.int32), jnp.int32(turn_of(d, group))).astype(jnp.float32)


def group_kernel(planes, share, table, after, *refs):
    parts, out = refs[:-1], refs[-1]
    group = len(parts)
    corners = SIDES * SPECIES * share
    member = table[MEMBER : MEMBER + 1]
    blocks = [partner(member, d, group) for d in range(group)]
    for s in range(SPECIES):
        theta = planes * table[RATE_X + s : RATE_X + s + 1]
        for e in range(SIDES):
            weight = [jnp.exp((-b if e else b - (group - 1.0)) * theta) for b in blocks]
            here = pl.ds((e * SPECIES + s) * share, share)
            out[here, :] = sum(weight[d] * parts[d][here, :] for d in range(group))
            for k in range(SIDES):
                here = pl.ds(corners + (k * SIDES + e) * SPECIES + s, 1)
                out[here, :] = sum(weight[d] * parts[d][here, :] for d in range(group))


def group_sums(planes, share, table, after, parts):
    return pl.pallas_call(
        functools.partial(group_kernel, planes, share),
        in_specs=[VMEM, ANY] + [VMEM] * len(parts),
        out_specs=VMEM,
        out_shape=struct(*parts[0].shape),
        compiler_params=params(8),
        name="group_sums",
    )(table, after, *parts)


def column_kernel(table, y_table, z_table, conc, influx, *refs):
    count = SPECIES - 1
    h, u, (rough, y_out, last, weights, sums) = refs[:count], refs[count : count + SPECIES], refs[count + SPECIES :]
    planes, columns, width = influx.shape
    tile = (ROWS, width)
    row = row_position(columns, width)
    for s in range(SPECIES):
        theta = table[RATE_Y + s : RATE_Y + s + 1]
        weights[s, 0] = jnp.exp((row - (columns - 1.0)) * theta)
        weights[s, 1] = jnp.exp(-row * theta)
    inner = tiles(table, INNER + count * SPECIES, SPECIES, tile)
    double = tiles(table, DOUBLE + count * SPECIES, SPECIES, tile)
    part_a = tiles(table, PART_A + count * SPECIES, SPECIES, tile)
    (scale,) = tiles(table, SCALE_X + count, 1, tile)
    (decay,) = tiles(table, DECAY + count, 1, tile)
    bind, unbind, _ = tiles(table, KINETICS, 3, tile)

    def plane_of(s, value, i):
        for e in range(SIDES):
            sums[s, e, i : i + 1, :] = jnp.sum(weights[s, e] * value, axis=0, keepdims=True)
        u[s][i] = product(y_table[s], right_pair(value))

    def plane(i):
        for s in range(count):
            plane_of(s, h[s][i], i)

    def rows(k):
        here = tile_rows(k)
        up, sources, rising = jnp.zeros(tile, jnp.float32), [], []
        for i in range(planes):
            c = [conc[j, i, here, :] for j in range(SPECIES)]
            g = (bind * c[0] * c[1] - unbind * c[2]) * scale
            a = c[count]
            for j in range(SPECIES):
                g = g + inner[j] * c[j] + double[j] * turned(c[j])
                if j != count:
                    a = a + part_a[j] * c[j]
            up = g + decay * up
            sources.append(g)
            rising.append(up - a)
        down = jnp.zeros(tile, jnp.float32)
        for i in reversed(range(planes)):
            down = decay * down
            last[i, here, :] = rising[i] + down
            down = down + sources[i]

    side_by_side((planes, columns // ROWS), (plane, rows))
    side_by_side(
        (planes, columns // ROWS),
        (lambda i: plane_of(count, last[i], i), lambda k: sweep_of_b(0, table, conc, rough, k)),
    )
    for s in range(SPECIES):
        both = jnp.concatenate([sums[s, e] for e in range(SIDES)], axis=0)
        both = product(left_pair(both), z_table[s])
        for e in range(SIDES):
            y_out[pl.ds((e * SPECIES + s) * planes, planes), :] = both[e * planes : (e + 1) * planes]


def column_parts(table, y_table, z_table, conc, influx, h):
    planes, columns, width = influx.shape
    return pl.pallas_call(
        column_kernel,
        in_specs=[VMEM] * (5 + len(h)),
        out_specs=[VMEM] * (SPECIES + 2),
        out_shape=[pltpu.VMEM(influx.shape, jnp.float32)] * (SPECIES + 1)
        + [pltpu.VMEM((SIDES * SPECIES * planes, width), jnp.float32)],
        scratch_shapes=[
            pltpu.VMEM(influx.shape, jnp.float32),
            pltpu.VMEM((SPECIES, SIDES, columns, width), jnp.float32),
            pltpu.VMEM((SPECIES, SIDES, planes, width), jnp.float32),
        ],
        compiler_params=params(8),
        cost_estimate=pl.CostEstimate(flops=6 * conc.size * columns, bytes_accessed=8 * conc.size, transcendentals=0),
        name="column_parts",
    )(table, y_table, z_table, conc, influx, *h)


def finish_kernel(table, z_table, conc, *refs):
    u, rough, (out, weights, fades) = refs[:SPECIES], refs[SPECIES : 2 * SPECIES], refs[2 * SPECIES :]
    _, planes, columns, width = conc.shape
    at_once = 4 if planes % 4 == 0 else 1
    row = row_position(columns, width)
    position = row_position(planes, width)
    for s in range(SPECIES):
        rate_x = table[RATE_X + s : RATE_X + s + 1]
        rate_y = table[RATE_Y + s : RATE_Y + s + 1]
        weights[s, 0] = jnp.exp(-(row + 1.0) * rate_y)
        weights[s, 1] = jnp.exp((row - columns) * rate_y)
        fades[s, 0] = jnp.exp(-(position + 1.0) * rate_x)
        fades[s, 1] = jnp.exp((position - planes) * rate_x)
        for first in range(0, planes, at_once):
            here = slice(first, first + at_once)
            value = (u[s][here] - rough[s][here]).reshape(at_once * columns, width)
            done = product(left_pair(value), z_table[s])
            out[s, here] = conc[s, here] + done.reshape(at_once, columns, width)


def finish(table, z_table, conc, u, rough):
    _, planes, columns, width = conc.shape
    return pl.pallas_call(
        finish_kernel,
        in_specs=[VMEM] * (3 + len(u) + len(rough)),
        out_specs=[VMEM] * 3,
        out_shape=[
            pltpu.VMEM(conc.shape, jnp.float32),
            pltpu.VMEM((SPECIES, SIDES, columns, width), jnp.float32),
            pltpu.VMEM((SPECIES, SIDES, planes, width), jnp.float32),
        ],
        compiler_params=params(8),
        cost_estimate=pl.CostEstimate(flops=6 * conc.size * width, bytes_accessed=12 * conc.size, transcendentals=0),
        name="finish",
    )(table, z_table, conc, *u, *rough)


def enter_kernel(group, planes, share, table, sums, *refs):
    parts, wholes, outs, y_out = refs[:group], refs[group : -group - 1], refs[-group - 1 : -1], refs[-1]
    groups = len(wholes)
    corners = SIDES * SPECIES * share
    member = table[MEMBER : MEMBER + 1]
    blocks = [partner(member, d, group) for d in range(group)]
    y_out[pl.ds(0, sums.shape[0]), :] = sums[...]

    for s in range(SPECIES):
        theta = planes * table[RATE_X + s : RATE_X + s + 1]
        closing = 1.0 / (1.0 - jnp.exp(-float(group * groups) * theta))
        for e in range(SIDES):
            steps = [(groups - j - 1) if e else (j - 1 if j else groups - 1) for j in range(groups)]
            outside = [jnp.exp(-float(group * k) * theta) * closing for k in steps]
            to_target = [jnp.exp((t - (group - 1.0) if e else -t) * theta) for t in blocks]
            inside = []
            for t in blocks:
                away = [(b - t) if e else (t - b) for b in blocks]
                inside.append([jnp.where(k > 0.0, jnp.exp((1.0 - jnp.abs(k)) * theta), 0.0) for k in away])

            def entering_group(here):
                return sum(weight * whole[here, :] for weight, whole in zip(outside, wholes))

            here = pl.ds((e * SPECIES + s) * share, share)
            whole = entering_group(here)
            held = [part[here, :] for part in parts]
            for d in range(group):
                total = to_target[d] * whole
                for weight, part in zip(inside[d], held):
                    total = total + weight * part
                outs[d][here, :] = total

            for k in range(SIDES):
                at = (k * SIDES + e) * SPECIES + s
                here = pl.ds(corners + at, 1)
                total = to_target[0] * entering_group(here)
                for weight, part in zip(inside[0], parts):
                    total = total + weight * part[here, :]
                y_out[pl.ds(sums.shape[0] + at, 1), :] = total


def entering(planes, share, table, sums, parts, wholes):
    group, width = len(parts), parts[0].shape[1]
    return pl.pallas_call(
        functools.partial(enter_kernel, group, planes, share),
        in_specs=[VMEM] * (2 + group + len(wholes)),
        out_specs=[VMEM] * (group + 1),
        out_shape=[struct(SIDES * SPECIES * share, width)] * group + [struct(padded(sums.shape[0] + CORNERS), width)],
        compiler_params=params(8),
        name="entering",
    )(table, sums, *parts, *wholes)


def y_rows(planes, s, e):
    corners = SIDES * SPECIES * planes
    return [pl.ds((e * SPECIES + s) * planes, planes)] + [
        pl.ds(corners + (e * SIDES + k) * SPECIES + s, 1) for k in range(SIDES)
    ]


def bits(table, stage):
    rank = table[RANK_Y : RANK_Y + 1].astype(jnp.int32)
    low = lax.bitwise_and(rank, jnp.int32(2**stage - 1)).astype(jnp.float32)
    return low, lax.bitwise_and(rank, jnp.int32(2**stage)) != 0


def pair_kernel(planes, columns, stage, table, mine, other, out):
    _, above = bits(table, stage)
    for s in range(SPECIES):
        far = jnp.exp(-float(columns * 2**stage) * table[RATE_Y + s : RATE_Y + s + 1])
        for e in range(SIDES):
            keep = jnp.where(above, far, 1.0) if e else jnp.where(above, 1.0, far)
            take = jnp.where(above, 1.0, far) if e else jnp.where(above, far, 1.0)
            for here in y_rows(planes, s, e):
                out[here, :] = keep * mine[here, :] + take * other[here, :]


def pair_sums(planes, columns, stage, table, mine, other):
    return pl.pallas_call(
        functools.partial(pair_kernel, planes, columns, stage),
        in_specs=[VMEM] * 3,
        out_specs=VMEM,
        out_shape=struct(*mine.shape),
        compiler_params=params(8),
        name="pair_sums",
    )(table, mine, other)


def y_weights(table, s, e, columns, stages):
    theta = columns * table[RATE_Y + s : RATE_Y + s + 1]
    along = 2**stages
    closing = table[SCALE_Y + s : SCALE_Y + s + 1] / (1.0 - jnp.exp(-float(along) * theta))
    weights = [jnp.exp(-(along - 1.0) * theta) * closing]
    for stage in range(stages):
        low, above = bits(table, stage)
        near = (2.0**stage - 1.0 - low) if e else low
        around = float(along - 2 ** (stage + 1))
        steps = near + (jnp.where(above, around, 0.0) if e else jnp.where(above, 0.0, around))
        weights.append(jnp.exp(-steps * theta) * closing)
    return weights


def spread_kernel(group, share, table, weights, fades, base, *refs):
    parts, sums, (out_far, out, hold, enter, left) = refs[:group], refs[group:-5], refs[-5:]
    _, planes, columns, width = base.shape
    blocks = [partner(table[MEMBER : MEMBER + 1], d, group) for d in range(group)]
    at_once = planes // left.shape[1]
    copies = []
    for s in range(SPECIES):
        corner = []
        for e in range(SIDES):
            arrive = y_weights(table, s, e, columns, len(sums) - 1)
            lines, *corner_lines = y_rows(planes, s, e)
            enter[e] = weighted(arrive, sums, lines)
            corner.append([weighted(arrive, sums, here) for here in corner_lines])
        for e in range(SIDES):
            held = [part[pl.ds((e * SPECIES + s) * share, share), :] for part in parts]
            for b in range(group):
                there = pl.ds(b * share, share)
                mine = held[0]
                for d in range(1, group):
                    mine = jnp.where(blocks[d] == b, held[d], mine)
                lift = weights[s, 0, there, :] * corner[0][e] + weights[s, 1, there, :] * corner[1][e]
                hold[e, there, :] = mine + lift
        for first in range(0, planes, at_once):
            near = [[ref[i : i + 1] for i in range(first, first + at_once)] for ref in (fades.at[s, 0], fades.at[s, 1])]
            far = [[ref[i : i + 1] for i in range(first, first + at_once)] for ref in (enter.at[0], enter.at[1])]
            for start in range(0, columns, ROWS):
                here = slice(start, start + ROWS)
                x_low, x_high = hold[0, here, :], hold[1, here, :]
                y_low, y_high = weights[s, 0, here, :], weights[s, 1, here, :]
                for k in range(at_once):
                    added = near[0][k] * x_low + near[1][k] * x_high + far[0][k] * y_low + far[1][k] * y_high
                    out[s, first + k, here, :] = base[s, first + k, here, :] + added
            part = pl.ds(first, at_once)
            copies.append(pltpu.make_async_copy(out.at[s, part], out_far.at[s, part], left.at[s, first // at_once]))
            copies[-1].start(priority=len(copies) % 2)
    for copy in copies:
        copy.wait()


def spread(share, table, weights, fades, base, sums, parts):
    _, planes, columns, width = base.shape
    return pl.pallas_call(
        functools.partial(spread_kernel, len(parts), share),
        in_specs=[VMEM] * (4 + len(sums) + len(parts)),
        out_specs=ANY,
        out_shape=struct(*base.shape),
        scratch_shapes=[
            pltpu.VMEM(base.shape, jnp.float32),
            pltpu.VMEM((SIDES, columns, width), jnp.float32),
            pltpu.VMEM((SIDES, planes, width), jnp.float32),
            pltpu.SemaphoreType.DMA((SPECIES, planes // 4 if planes % 4 == 0 else planes)),
        ],
        compiler_params=params(8),
        name="spread",
    )(table, weights, fades, base, *parts, *sums)


def group_size(devices):
    size = 1
    while 4 * size * size <= 2 * devices and devices % (2 * size) == 0:
        size *= 2
    return size


def body(conc, influx, numbers, cross, kinetics):
    _, planes, columns, _ = conc.shape
    across, along = lax.axis_size("gx"), lax.axis_size("gy")
    group = group_size(across)
    share = columns // group
    rank_x, rank_y = (lax.axis_index(axis).astype(jnp.int32).reshape(1) for axis in ("gx", "gy"))
    conc, influx, numbers, cross, kinetics = (
        pltpu.with_memory_space_constraint(x, pltpu.HBM) for x in (conc, influx, numbers, cross, kinetics)
    )

    def beside(value, stage):
        return lax.ppermute(value, "gy", [(i, i ^ 2**stage) for i in range(along)])

    def in_group(parts):
        pairs = [[(i, i ^ turn_of(d, group)) for i in range(across)] for d in range(group)]
        return [parts[0]] + [lax.ppermute(parts[d], "gx", pairs[d]) for d in range(1, group)]

    def over_groups(value, by):
        return lax.ppermute(value, "gx", [(i, (i + by * group) % across) for i in range(across)])

    *parts, table, conc, influx, y_table, z_table = edges(
        group, rank_x, rank_y, numbers, cross, kinetics, conc, influx
    )
    parts = in_group(parts)
    swept = sweeps(table, conc, influx)
    h, rough = swept[: SPECIES - 1], swept[SPECIES - 1 :]
    whole = group_sums(planes, share, table, h[0], parts)
    wholes = [whole] + [over_groups(whole, j) for j in range(1, across // group)]
    *u, rough_first, sums = column_parts(table, y_table, z_table, conc, influx, h)
    *outs, sums = entering(planes, share, table, sums, parts, wholes)
    gathered = [sums]
    for stage in range(along.bit_length() - 1):
        if stage:
            sums = pair_sums(planes, columns, stage - 1, table, sums, gathered[-1])
        gathered.append(beside(sums, stage))
    outs = in_group(outs)
    base, weights, fades = finish(table, z_table, conc, u, [rough_first, *rough])
    return spread(share, table, weights, fades, base, gathered, outs)


def solution(mesh):
    placed = (P(None, "gx", "gy", None), P("gx", "gy", None), P(), P(), P())
    return jax.shard_map(
        body, mesh=mesh, in_specs=placed, out_specs=P(None, "gx", "gy", None), check_vma=False
    )
```

```python
import functools

import jax
import jax.numpy as jnp
from jax import lax
from jax.experimental import pallas as pl
from jax.experimental.pallas import tpu as pltpu
from jax.sharding import PartitionSpec as P

SPECIES = 3
ROWS = 8
SIDES = 2
CORNERS = SIDES * SIDES * SPECIES
SMEM = pl.BlockSpec(memory_space=pltpu.SMEM)
VMEM = pl.BlockSpec(memory_space=pltpu.VMEM)
ANY = pl.BlockSpec(memory_space=pl.ANY)

RATE_X, RATE_Y, SCALE_Y, SCALE_X, DECAY, KINETICS, MEMBER = 0, 3, 6, 9, 12, 15, 18
INNER, DOUBLE, PART_A, PART_B, RANK_Y, TABLE_ROWS = 19, 28, 37, 46, 55, 56


def padded(rows):
    return -(-rows // ROWS) * ROWS


def params(mebibytes):
    return pltpu.CompilerParams(vmem_limit_bytes=mebibytes * 2**20)


def struct(*shape):
    return jax.ShapeDtypeStruct(shape, jnp.float32)


def decay_rate(number):
    half = 0.5 * lax.rsqrt(number)
    square = half * half
    return 2.0 * jnp.log1p(half + square / (1.0 + jnp.sqrt(1.0 + square)))


def scaling(number):
    return lax.rsqrt(1.0 + 4.0 * number)


def splat(value, shape):
    return jnp.full(shape, value, jnp.float32)


def split(value):
    high = value.astype(jnp.bfloat16)
    return high, (value - high.astype(jnp.float32)).astype(jnp.bfloat16)


def left_pair(value):
    return jnp.concatenate(split(value), axis=1)


def right_pair(value):
    high, low = split(value)
    return jnp.concatenate(
        [jnp.concatenate([high, low], axis=1), jnp.concatenate([high, jnp.zeros_like(low)], axis=1)], axis=0
    )


def product(left, right):
    both = jnp.dot(left, right, preferred_element_type=jnp.float32)
    width = both.shape[1] // 2
    return both[:, :width] + both[:, width:]


def distances(length):
    rows = lax.broadcasted_iota(jnp.int32, (length, length), 0)
    columns = lax.broadcasted_iota(jnp.int32, (length, length), 1)
    return jnp.abs(rows - columns).astype(jnp.float32)


def depth_table(number, length):
    number = splat(number, (1, length))
    theta = decay_rate(number)
    spread = distances(length)
    factor = scaling(number) / (1.0 - jnp.exp(-length * theta))
    return (jnp.exp(-spread * theta) + jnp.exp((spread - length) * theta)) * factor


def column_table(number, length):
    number = splat(number, (1, length))
    return jnp.exp(-distances(length) * decay_rate(number)) * scaling(number)


def row_position(length, width):
    return lax.broadcasted_iota(jnp.int32, (length, width), 0).astype(jnp.float32)


def coefficients(numbers, cross, kinetics, tile):
    n = [[splat(numbers[s, d], tile) for d in range(3)] for s in range(SPECIES)]
    along_x, along_y, along_z = [], [], []
    for s in range(SPECIES):
        per_x, per_y = 1.0 / n[s][0], 1.0 / n[s][1]
        for j in range(SPECIES):
            mix = 1.0 if j == s else cross[s, j]
            along_x.append(n[j][0] * per_x * mix)
            along_y.append(n[j][1] * per_y * mix)
            along_z.append(n[j][2] * mix)
    scale = [scaling(n[s][0]) for s in range(SPECIES)]
    rate = [decay_rate(n[s][0]) for s in range(SPECIES)]
    return along_x, along_y, along_z, scale, rate, [splat(kinetics[i], tile) for i in range(3)]


def turned(value):
    width = value.shape[1]
    return pltpu.roll(value, 1, 1) + pltpu.roll(value, width - 1, 1)


def weighted(weights, refs, here):
    return sum(weight * ref[here, :] for weight, ref in zip(weights, refs))


def tile_rows(k):
    return pl.ds(k * ROWS if isinstance(k, int) else pl.multiple_of(k * ROWS, ROWS), ROWS)


def tiles(table, first, count, tile):
    return [jnp.broadcast_to(table[at : at + 1], tile) for at in range(first, first + count)]


def rates(c, influx, kinetics):
    bind, unbind, pump = kinetics
    binding = bind * c[0] * c[1] - unbind * c[2]
    pumping = pump * c[0] / (1.0 + c[0])
    return influx - 4.0 * binding - pumping, binding


def side_by_side(counts, steps):
    for k in range(max(counts)):
        for count, step in zip(counts, steps):
            if k < count:
                step(k)


def sweep_of_b(s, table, conc, out, k):
    _, planes, _, width = conc.shape
    tile = (ROWS, width)
    here = tile_rows(k)
    weight = tiles(table, PART_B + s * SPECIES, SPECIES, tile)
    (decay,) = tiles(table, DECAY + s, 1, tile)
    up, sources, rising = jnp.zeros(tile, jnp.float32), [], []
    for i in range(planes):
        b = weight[0] * conc[0, i, here, :] + weight[1] * conc[1, i, here, :] + weight[2] * conc[2, i, here, :]
        up = b + decay * up
        sources.append(b)
        rising.append(up)
    down = jnp.zeros(tile, jnp.float32)
    for i in reversed(range(planes)):
        down = decay * down
        out[i, here, :] = rising[i] + down
        down = down + sources[i]


def chunk_cuts(columns):
    small, large = 2 * ROWS, 4 * ROWS
    cuts = [0]
    while cuts[-1] < columns:
        left = columns - cuts[-1]
        cuts.append(cuts[-1] + (large if cuts[-1] and left > 2 * small and left >= large + small else min(small, left)))
    return cuts


def edge_kernel(group, x_far, y_far, numbers_far, cross_far, kinetics_far, conc_far, influx_far, *refs):
    sent, refs = refs[:group], refs[group:]
    table, conc, influx, y_table, z_table, weights, hold, deep, solved, corners, arrived = refs[:11]
    rank_x, rank_y, numbers, cross, kinetics, small = refs[11:]
    planes, columns, width = influx.shape
    cuts = chunk_cuts(columns)
    half = planes // 2
    share = columns // group
    tile = (ROWS, width)

    def copies(k):
        part = pl.ds(cuts[k], cuts[k + 1] - cuts[k])
        fields = [(conc_far.at[j], conc.at[j]) for j in range(SPECIES)] + [(influx_far, influx)]
        return [
            pltpu.make_async_copy(far.at[:, part, :], near.at[:, part, :], arrived.at[j, k])
            for j, (far, near) in enumerate(fields)
        ]

    fars = (x_far, y_far, numbers_far, cross_far, kinetics_far)
    nears = (rank_x, rank_y, numbers, cross, kinetics)
    scalars = [pltpu.make_async_copy(far, near, small.at[k]) for k, (far, near) in enumerate(zip(fars, nears))]
    for copy in scalars:
        copy.start()
    for k in range(len(cuts) - 1):
        for copy in copies(k):
            copy.start()
    for copy in scalars:
        copy.wait()

    along_x, along_y, along_z, scale, rate, kinetic = coefficients(numbers, cross, kinetics, tile)
    inner, double, single = [], [], []
    for s in range(SPECIES):
        for at in range(s * SPECIES, (s + 1) * SPECIES):
            inner.append((along_x[at] + along_y[at] - 2.0 * along_z[at]) * scale[s])
            double.append(along_z[at] * scale[s])
            single.append(along_y[at] * scale[s])
        for i in range(half):
            near = jnp.exp(-i * rate[s])
            far = jnp.exp(-(planes - 1.0 - i) * rate[s])
            weights[s, i, 0] = 0.5 * (near + far)
            weights[s, i, 1] = 0.5 * (near - far)
    member = lax.rem(rank_x[0], group)

    def make_tables():
        for s in range(SPECIES):
            y_table[s] = left_pair(column_table(numbers[s, 1], columns))
            z_table[s] = right_pair(depth_table(numbers[s, 2], width))
        number_y = [splat(numbers[s, 1], tile) for s in range(SPECIES)]
        entries = (
            (RATE_X, rate),
            (RATE_Y, [decay_rate(value) for value in number_y]),
            (SCALE_Y, [scaling(value) for value in number_y]),
            (SCALE_X, scale),
            (DECAY, [jnp.exp(-value) for value in rate]),
            (KINETICS, kinetic),
            (MEMBER, [splat(member.astype(jnp.float32), tile)]),
            (RANK_Y, [splat(rank_y[0].astype(jnp.float32), tile)]),
            (INNER, inner),
            (DOUBLE, double),
            (PART_A, along_x),
            (PART_B, single),
        )
        for first, values in entries:
            for k, value in enumerate(values):
                table[first + k : first + k + 1] = value[:1]

    def sums_of(start):
        here = slice(start, start + ROWS)

        def at_plane(i):
            c = [conc[j, i, here, :] for j in range(SPECIES)]
            return c, *rates(c, influx[i, here, :], kinetic)

        zero = jnp.zeros(tile, jnp.float32)
        plus = [[zero] * (SPECIES + 1) for _ in range(SPECIES)]
        minus = [[zero] * (SPECIES + 1) for _ in range(SPECIES)]
        for i in range(half):
            low, low_first, low_binding = at_plane(i)
            high, high_first, high_binding = at_plane(planes - 1 - i)
            both = [x + y for x, y in zip(low, high)]
            apart = [x - y for x, y in zip(low, high)]
            change = (low_first + high_first, low_binding + high_binding)
            turn = (low_first - high_first, low_binding - high_binding)
            for s in range(SPECIES):
                even, odd = weights[s, i, 0], weights[s, i, 1]
                of = min(s, 1)
                for j, (p, m) in enumerate(zip(both + [change[of]], apart + [turn[of]])):
                    plus[s][j] = plus[s][j] + even * p
                    minus[s][j] = minus[s][j] + odd * m
        for s in range(SPECIES):
            for e in range(SIDES):
                sums = [p + m if e else p - m for p, m in zip(plus[s], minus[s])]
                v = sums[SPECIES] * scale[s]
                if s == 1:
                    v = -v
                w = 0.0
                for j in range(SPECIES):
                    at = s * SPECIES + j
                    v = v + inner[at] * sums[j] + double[at] * turned(sums[j])
                    w = w + single[at] * sums[j]
                hold[s, e, here, :] = v
                hold[s, SIDES + e, here, :] = w

    def deepen(k):
        here = slice(cuts[k], cuts[k + 1])
        chunk = cuts[k + 1] - cuts[k]
        for s in range(SPECIES):
            stack = jnp.concatenate([hold[s, e, here, :] for e in range(2 * SIDES)], axis=0)
            done = product(left_pair(stack), z_table[s])
            for e in range(2 * SIDES):
                deep[s, e, here, :] = done[e * chunk : (e + 1) * chunk]

    for k in range(len(cuts) - 1):
        for copy in copies(k):
            copy.wait()
        if k:
            deepen(k - 1)
        for start in range(cuts[k], cuts[k + 1], ROWS):
            sums_of(start)
        if not k:
            make_tables()
    deepen(len(cuts) - 2)

    row = row_position(columns, width)
    for s in range(SPECIES):
        theta = table[RATE_Y + s : RATE_Y + s + 1]
        rise = jnp.exp((row - (columns - 1.0)) * theta)
        fall = jnp.exp(-row * theta)
        both = product(y_table[s], right_pair(jnp.concatenate([deep[s, e] for e in range(SIDES)], axis=1)))
        for e in range(SIDES):
            solved[e, s] = both[:, e * width : (e + 1) * width] - deep[s, SIDES + e]
            for f, weight in enumerate((rise, fall)):
                at = (f * SIDES + e) * SPECIES + s
                corners[at : at + 1] = jnp.sum(weight * deep[s, e], axis=0, keepdims=True)
    for d in range(group):
        start = pl.multiple_of(lax.bitwise_xor(member, jnp.int32(turn_of(d, group))) * share, share)
        for s in range(SPECIES):
            for e in range(SIDES):
                sent[d][pl.ds((e * SPECIES + s) * share, share), :] = solved[e, s, pl.ds(start, share), :]
        sent[d][pl.ds(SIDES * SPECIES * share, corners.shape[0]), :] = corners[...]


def edges(group, rank_x, rank_y, numbers, cross, kinetics, conc, influx):
    _, planes, columns, width = conc.shape
    chunks = len(chunk_cuts(columns)) - 1
    hold = pltpu.VMEM((SPECIES, 2 * SIDES, columns, width), jnp.float32)
    rows = SIDES * SPECIES * (columns // group) + padded(CORNERS)
    return pl.pallas_call(
        functools.partial(edge_kernel, group),
        in_specs=[ANY] * 7,
        out_specs=[VMEM] * (group + 5),
        out_shape=[struct(rows, width)] * group
        + [
            pltpu.VMEM((TABLE_ROWS, width), jnp.float32),
            pltpu.VMEM(conc.shape, jnp.float32),
            pltpu.VMEM(influx.shape, jnp.float32),
            pltpu.VMEM((SPECIES, columns, 2 * columns), jnp.bfloat16),
            pltpu.VMEM((SPECIES, 2 * width, 2 * width), jnp.bfloat16),
        ],
        scratch_shapes=[
            pltpu.VMEM((SPECIES, planes // 2, 2, ROWS, width), jnp.float32),
            hold,
            hold,
            pltpu.VMEM((SIDES, SPECIES, columns, width), jnp.float32),
            pltpu.VMEM((padded(CORNERS), width), jnp.float32),
            pltpu.SemaphoreType.DMA((SPECIES + 1, chunks)),
            *(pltpu.SMEM(x.shape, x.dtype) for x in (rank_x, rank_y, numbers, cross, kinetics)),
            pltpu.SemaphoreType.DMA((5,)),
        ],
        compiler_params=params(16),
        name="edges",
    )(rank_x, rank_y, numbers, cross, kinetics, conc, influx)


def sweep_kernel(table, conc, influx, *refs):
    count = SPECIES - 1
    outs, roughs, g_hold = refs[:count], refs[count:-1], refs[-1]
    planes, columns, width = influx.shape
    tile = (ROWS, width)
    inner = tiles(table, INNER, count * SPECIES, tile)
    double = tiles(table, DOUBLE, count * SPECIES, tile)
    part_a = tiles(table, PART_A, count * SPECIES, tile)
    scale = tiles(table, SCALE_X, count, tile)
    decay = tiles(table, DECAY, count, tile)
    kinetic = tiles(table, KINETICS, 3, tile)

    def rows(k, carry):
        here = pl.ds(pl.multiple_of(k * ROWS, ROWS), ROWS)
        up = [jnp.zeros(tile, jnp.float32) for _ in range(count)]
        for i in range(planes):
            c = [conc[j, i, here, :] for j in range(SPECIES)]
            around = [turned(value) for value in c]
            first, binding = rates(c, influx[i, here, :], kinetic)
            change = (first, -binding, binding)
            for s in range(count):
                g = change[s] * scale[s]
                a = c[s]
                for j in range(SPECIES):
                    at = s * SPECIES + j
                    g = g + inner[at] * c[j] + double[at] * around[j]
                    if j != s:
                        a = a + part_a[at] * c[j]
                up[s] = g + decay[s] * up[s]
                g_hold[s, i] = g
                outs[s][i, here, :] = up[s] - a
        for s in range(count):
            down = jnp.zeros(tile, jnp.float32)
            for i in reversed(range(planes)):
                down = decay[s] * down
                outs[s][i, here, :] += down
                down += g_hold[s, i]
        for s, rough in enumerate(roughs, 1):
            sweep_of_b(s, table, conc, rough, k)
        return carry

    lax.fori_loop(0, columns // ROWS, rows, 0)


def sweeps(table, conc, influx):
    count, planes, width = SPECIES - 1, influx.shape[0], influx.shape[2]
    return pl.pallas_call(
        sweep_kernel,
        in_specs=[VMEM] * 3,
        out_specs=[VMEM] * (2 * count),
        out_shape=[pltpu.VMEM(influx.shape, jnp.float32)] * (2 * count),
        scratch_shapes=[pltpu.VMEM((count, planes, ROWS, width), jnp.float32)],
        compiler_params=params(8),
        cost_estimate=pl.CostEstimate(flops=100 * conc.size, bytes_accessed=14 * conc.size, transcendentals=0),
        name="sweeps",
    )(table, conc, influx)


def turn_of(d, group):
    return (0, group - 1, *range(1, group - 1))[d]


def partner(member, d, group):
    return lax.bitwise_xor(member.astype(jnp.int32), jnp.int32(turn_of(d, group))).astype(jnp.float32)


def group_kernel(planes, share, table, after, *refs):
    parts, out = refs[:-1], refs[-1]
    group = len(parts)
    corners = SIDES * SPECIES * share
    member = table[MEMBER : MEMBER + 1]
    blocks = [partner(member, d, group) for d in range(group)]
    for s in range(SPECIES):
        theta = planes * table[RATE_X + s : RATE_X + s + 1]
        for e in range(SIDES):
            weight = [jnp.exp((-b if e else b - (group - 1.0)) * theta) for b in blocks]
            here = pl.ds((e * SPECIES + s) * share, share)
            out[here, :] = sum(weight[d] * parts[d][here, :] for d in range(group))
            for k in range(SIDES):
                here = pl.ds(corners + (k * SIDES + e) * SPECIES + s, 1)
                out[here, :] = sum(weight[d] * parts[d][here, :] for d in range(group))


def group_sums(planes, share, table, after, parts):
    return pl.pallas_call(
        functools.partial(group_kernel, planes, share),
        in_specs=[VMEM, ANY] + [VMEM] * len(parts),
        out_specs=VMEM,
        out_shape=struct(*parts[0].shape),
        compiler_params=params(8),
        name="group_sums",
    )(table, after, *parts)


def column_kernel(table, y_table, z_table, conc, influx, *refs):
    count = SPECIES - 1
    h, u, (rough, y_out, last, weights, sums) = refs[:count], refs[count : count + SPECIES], refs[count + SPECIES :]
    planes, columns, width = influx.shape
    tile = (ROWS, width)
    row = row_position(columns, width)
    for s in range(SPECIES):
        theta = table[RATE_Y + s : RATE_Y + s + 1]
        weights[s, 0] = jnp.exp((row - (columns - 1.0)) * theta)
        weights[s, 1] = jnp.exp(-row * theta)
    inner = tiles(table, INNER + count * SPECIES, SPECIES, tile)
    double = tiles(table, DOUBLE + count * SPECIES, SPECIES, tile)
    part_a = tiles(table, PART_A + count * SPECIES, SPECIES, tile)
    (scale,) = tiles(table, SCALE_X + count, 1, tile)
    (decay,) = tiles(table, DECAY + count, 1, tile)
    bind, unbind, _ = tiles(table, KINETICS, 3, tile)

    def plane_of(s, value, i):
        for e in range(SIDES):
            sums[s, e, i : i + 1, :] = jnp.sum(weights[s, e] * value, axis=0, keepdims=True)
        u[s][i] = product(y_table[s], right_pair(value))

    def plane(i):
        for s in range(count):
            plane_of(s, h[s][i], i)

    def rows(k):
        here = tile_rows(k)
        up, sources, rising = jnp.zeros(tile, jnp.float32), [], []
        for i in range(planes):
            c = [conc[j, i, here, :] for j in range(SPECIES)]
            g = (bind * c[0] * c[1] - unbind * c[2]) * scale
            a = c[count]
            for j in range(SPECIES):
                g = g + inner[j] * c[j] + double[j] * turned(c[j])
                if j != count:
                    a = a + part_a[j] * c[j]
            up = g + decay * up
            sources.append(g)
            rising.append(up - a)
        down = jnp.zeros(tile, jnp.float32)
        for i in reversed(range(planes)):
            down = decay * down
            last[i, here, :] = rising[i] + down
            down = down + sources[i]

    side_by_side((planes, columns // ROWS), (plane, rows))
    side_by_side(
        (planes, columns // ROWS),
        (lambda i: plane_of(count, last[i], i), lambda k: sweep_of_b(0, table, conc, rough, k)),
    )
    for s in range(SPECIES):
        both = jnp.concatenate([sums[s, e] for e in range(SIDES)], axis=0)
        both = product(left_pair(both), z_table[s])
        for e in range(SIDES):
            y_out[pl.ds((e * SPECIES + s) * planes, planes), :] = both[e * planes : (e + 1) * planes]


def column_parts(table, y_table, z_table, conc, influx, h):
    planes, columns, width = influx.shape
    return pl.pallas_call(
        column_kernel,
        in_specs=[VMEM] * (5 + len(h)),
        out_specs=[VMEM] * (SPECIES + 2),
        out_shape=[pltpu.VMEM(influx.shape, jnp.float32)] * (SPECIES + 1)
        + [pltpu.VMEM((SIDES * SPECIES * planes, width), jnp.float32)],
        scratch_shapes=[
            pltpu.VMEM(influx.shape, jnp.float32),
            pltpu.VMEM((SPECIES, SIDES, columns, width), jnp.float32),
            pltpu.VMEM((SPECIES, SIDES, planes, width), jnp.float32),
        ],
        compiler_params=params(8),
        cost_estimate=pl.CostEstimate(flops=6 * conc.size * columns, bytes_accessed=8 * conc.size, transcendentals=0),
        name="column_parts",
    )(table, y_table, z_table, conc, influx, *h)


def finish_kernel(table, z_table, conc, *refs):
    u, rough, (out, weights, fades) = refs[:SPECIES], refs[SPECIES : 2 * SPECIES], refs[2 * SPECIES :]
    _, planes, columns, width = conc.shape
    at_once = 4 if planes % 4 == 0 else 1
    row = row_position(columns, width)
    position = row_position(planes, width)
    for s in range(SPECIES):
        rate_x = table[RATE_X + s : RATE_X + s + 1]
        rate_y = table[RATE_Y + s : RATE_Y + s + 1]
        weights[s, 0] = jnp.exp(-(row + 1.0) * rate_y)
        weights[s, 1] = jnp.exp((row - columns) * rate_y)
        fades[s, 0] = jnp.exp(-(position + 1.0) * rate_x)
        fades[s, 1] = jnp.exp((position - planes) * rate_x)
        for first in range(0, planes, at_once):
            here = slice(first, first + at_once)
            value = (u[s][here] - rough[s][here]).reshape(at_once * columns, width)
            done = product(left_pair(value), z_table[s])
            out[s, here] = conc[s, here] + done.reshape(at_once, columns, width)


def finish(table, z_table, conc, u, rough):
    _, planes, columns, width = conc.shape
    return pl.pallas_call(
        finish_kernel,
        in_specs=[VMEM] * (3 + len(u) + len(rough)),
        out_specs=[VMEM] * 3,
        out_shape=[
            pltpu.VMEM(conc.shape, jnp.float32),
            pltpu.VMEM((SPECIES, SIDES, columns, width), jnp.float32),
            pltpu.VMEM((SPECIES, SIDES, planes, width), jnp.float32),
        ],
        compiler_params=params(8),
        cost_estimate=pl.CostEstimate(flops=6 * conc.size * width, bytes_accessed=12 * conc.size, transcendentals=0),
        name="finish",
    )(table, z_table, conc, *u, *rough)


def enter_kernel(group, planes, share, table, sums, *refs):
    parts, wholes, outs, y_out = refs[:group], refs[group : -group - 1], refs[-group - 1 : -1], refs[-1]
    groups = len(wholes)
    corners = SIDES * SPECIES * share
    member = table[MEMBER : MEMBER + 1]
    blocks = [partner(member, d, group) for d in range(group)]
    y_out[pl.ds(0, sums.shape[0]), :] = sums[...]

    for s in range(SPECIES):
        theta = planes * table[RATE_X + s : RATE_X + s + 1]
        closing = 1.0 / (1.0 - jnp.exp(-float(group * groups) * theta))
        for e in range(SIDES):
            steps = [(groups - j - 1) if e else (j - 1 if j else groups - 1) for j in range(groups)]
            outside = [jnp.exp(-float(group * k) * theta) * closing for k in steps]
            to_target = [jnp.exp((t - (group - 1.0) if e else -t) * theta) for t in blocks]
            inside = []
            for t in blocks:
                away = [(b - t) if e else (t - b) for b in blocks]
                inside.append([jnp.where(k > 0.0, jnp.exp((1.0 - jnp.abs(k)) * theta), 0.0) for k in away])

            def entering_group(here):
                return sum(weight * whole[here, :] for weight, whole in zip(outside, wholes))

            here = pl.ds((e * SPECIES + s) * share, share)
            whole = entering_group(here)
            held = [part[here, :] for part in parts]
            for d in range(group):
                total = to_target[d] * whole
                for weight, part in zip(inside[d], held):
                    total = total + weight * part
                outs[d][here, :] = total

            for k in range(SIDES):
                at = (k * SIDES + e) * SPECIES + s
                here = pl.ds(corners + at, 1)
                total = to_target[0] * entering_group(here)
                for weight, part in zip(inside[0], parts):
                    total = total + weight * part[here, :]
                y_out[pl.ds(sums.shape[0] + at, 1), :] = total


def entering(planes, share, table, sums, parts, wholes):
    group, width = len(parts), parts[0].shape[1]
    return pl.pallas_call(
        functools.partial(enter_kernel, group, planes, share),
        in_specs=[VMEM] * (2 + group + len(wholes)),
        out_specs=[VMEM] * (group + 1),
        out_shape=[struct(SIDES * SPECIES * share, width)] * group + [struct(padded(sums.shape[0] + CORNERS), width)],
        compiler_params=params(8),
        name="entering",
    )(table, sums, *parts, *wholes)


def y_rows(planes, s, e):
    corners = SIDES * SPECIES * planes
    return [pl.ds((e * SPECIES + s) * planes, planes)] + [
        pl.ds(corners + (e * SIDES + k) * SPECIES + s, 1) for k in range(SIDES)
    ]


def bits(table, stage):
    rank = table[RANK_Y : RANK_Y + 1].astype(jnp.int32)
    low = lax.bitwise_and(rank, jnp.int32(2**stage - 1)).astype(jnp.float32)
    return low, lax.bitwise_and(rank, jnp.int32(2**stage)) != 0


def pair_kernel(planes, columns, stage, table, mine, other, out):
    _, above = bits(table, stage)
    for s in range(SPECIES):
        far = jnp.exp(-float(columns * 2**stage) * table[RATE_Y + s : RATE_Y + s + 1])
        for e in range(SIDES):
            keep = jnp.where(above, far, 1.0) if e else jnp.where(above, 1.0, far)
            take = jnp.where(above, 1.0, far) if e else jnp.where(above, far, 1.0)
            for here in y_rows(planes, s, e):
                out[here, :] = keep * mine[here, :] + take * other[here, :]


def pair_sums(planes, columns, stage, table, mine, other):
    return pl.pallas_call(
        functools.partial(pair_kernel, planes, columns, stage),
        in_specs=[VMEM] * 3,
        out_specs=VMEM,
        out_shape=struct(*mine.shape),
        compiler_params=params(8),
        name="pair_sums",
    )(table, mine, other)


def y_weights(table, s, e, columns, stages):
    theta = columns * table[RATE_Y + s : RATE_Y + s + 1]
    along = 2**stages
    closing = table[SCALE_Y + s : SCALE_Y + s + 1] / (1.0 - jnp.exp(-float(along) * theta))
    weights = [jnp.exp(-(along - 1.0) * theta) * closing]
    for stage in range(stages):
        low, above = bits(table, stage)
        near = (2.0**stage - 1.0 - low) if e else low
        around = float(along - 2 ** (stage + 1))
        steps = near + (jnp.where(above, around, 0.0) if e else jnp.where(above, 0.0, around))
        weights.append(jnp.exp(-steps * theta) * closing)
    return weights


def spread_kernel(group, share, table, weights, fades, base, *refs):
    parts, sums, (out_far, out, hold, enter, left) = refs[:group], refs[group:-5], refs[-5:]
    _, planes, columns, width = base.shape
    blocks = [partner(table[MEMBER : MEMBER + 1], d, group) for d in range(group)]
    at_once = planes // left.shape[1]
    copies = []
    for s in range(SPECIES):
        corner = []
        for e in range(SIDES):
            arrive = y_weights(table, s, e, columns, len(sums) - 1)
            lines, *corner_lines = y_rows(planes, s, e)
            enter[e] = weighted(arrive, sums, lines)
            corner.append([weighted(arrive, sums, here) for here in corner_lines])
        for e in range(SIDES):
            held = [part[pl.ds((e * SPECIES + s) * share, share), :] for part in parts]
            for b in range(group):
                there = pl.ds(b * share, share)
                mine = held[0]
                for d in range(1, group):
                    mine = jnp.where(blocks[d] == b, held[d], mine)
                lift = weights[s, 0, there, :] * corner[0][e] + weights[s, 1, there, :] * corner[1][e]
                hold[e, there, :] = mine + lift
        for first in range(0, planes, at_once):
            near = [[ref[i : i + 1] for i in range(first, first + at_once)] for ref in (fades.at[s, 0], fades.at[s, 1])]
            far = [[ref[i : i + 1] for i in range(first, first + at_once)] for ref in (enter.at[0], enter.at[1])]
            for start in range(0, columns, ROWS):
                here = slice(start, start + ROWS)
                x_low, x_high = hold[0, here, :], hold[1, here, :]
                y_low, y_high = weights[s, 0, here, :], weights[s, 1, here, :]
                for k in range(at_once):
                    added = near[0][k] * x_low + near[1][k] * x_high + far[0][k] * y_low + far[1][k] * y_high
                    out[s, first + k, here, :] = base[s, first + k, here, :] + added
            part = pl.ds(first, at_once)
            copies.append(pltpu.make_async_copy(out.at[s, part], out_far.at[s, part], left.at[s, first // at_once]))
            copies[-1].start()
    for copy in copies:
        copy.wait()


def spread(share, table, weights, fades, base, sums, parts):
    _, planes, columns, width = base.shape
    return pl.pallas_call(
        functools.partial(spread_kernel, len(parts), share),
        in_specs=[VMEM] * (4 + len(sums) + len(parts)),
        out_specs=ANY,
        out_shape=struct(*base.shape),
        scratch_shapes=[
            pltpu.VMEM(base.shape, jnp.float32),
            pltpu.VMEM((SIDES, columns, width), jnp.float32),
            pltpu.VMEM((SIDES, planes, width), jnp.float32),
            pltpu.SemaphoreType.DMA((SPECIES, planes // 4 if planes % 4 == 0 else planes)),
        ],
        compiler_params=params(8),
        name="spread",
    )(table, weights, fades, base, *parts, *sums)


def group_size(devices):
    size = 1
    while 4 * size * size <= 2 * devices and devices % (2 * size) == 0:
        size *= 2
    return size


def body(conc, influx, numbers, cross, kinetics):
    _, planes, columns, _ = conc.shape
    across, along = lax.axis_size("gx"), lax.axis_size("gy")
    group = group_size(across)
    share = columns // group
    rank_x, rank_y = (lax.axis_index(axis).astype(jnp.int32).reshape(1) for axis in ("gx", "gy"))
    conc, influx, numbers, cross, kinetics = (
        pltpu.with_memory_space_constraint(x, pltpu.HBM) for x in (conc, influx, numbers, cross, kinetics)
    )

    def beside(value, stage):
        return lax.ppermute(value, "gy", [(i, i ^ 2**stage) for i in range(along)])

    def in_group(parts):
        pairs = [[(i, i ^ turn_of(d, group)) for i in range(across)] for d in range(group)]
        return [parts[0]] + [lax.ppermute(parts[d], "gx", pairs[d]) for d in range(1, group)]

    def over_groups(value, by):
        return lax.ppermute(value, "gx", [(i, (i + by * group) % across) for i in range(across)])

    *parts, table, conc, influx, y_table, z_table = edges(
        group, rank_x, rank_y, numbers, cross, kinetics, conc, influx
    )
    parts = in_group(parts)
    swept = sweeps(table, conc, influx)
    h, rough = swept[: SPECIES - 1], swept[SPECIES - 1 :]
    whole = group_sums(planes, share, table, h[0], parts)
    wholes = [whole] + [over_groups(whole, j) for j in range(1, across // group)]
    *u, rough_first, sums = column_parts(table, y_table, z_table, conc, influx, h)
    *outs, sums = entering(planes, share, table, sums, parts, wholes)
    gathered = [sums]
    for stage in range(along.bit_length() - 1):
        if stage:
            sums = pair_sums(planes, columns, stage - 1, table, sums, gathered[-1])
        gathered.append(beside(sums, stage))
    outs = in_group(outs)
    base, weights, fades = finish(table, z_table, conc, u, [rough_first, *rough])
    return spread(share, table, weights, fades, base, gathered, outs)


def solution(mesh):
    placed = (P(None, "gx", "gy", None), P("gx", "gy", None), P(), P(), P())
    return jax.shard_map(
        body, mesh=mesh, in_specs=placed, out_specs=P(None, "gx", "gy", None), check_vma=False
    )
```
